32 devices in a mesh: row: 4 (over y, core), col: 2 (over x), layer: 4 (over z).
Axes of the slice: x: 2, y: 2, z: 4, core: 2. Of those that a mesh axis runs over, the one named last changes fastest.
Arguments:
- a_blocks: bfloat16 [768, 128, 128], P(('row', 'col', 'layer')), may hold values from -0.5 to 0.5
- a_rows: int32 [768], P(('row', 'col', 'layer')), may hold values from 0 to 31, as said below
- a_cols: int32 [768], P(('row', 'col', 'layer')), may hold values from 0 to 31, as said below
- s_blocks: bfloat16 [32, 4, 128, 128], P(('row', 'layer'), 'col'), may hold values from -6 to 6
- s_cols: int32 [32, 4], P(('row', 'layer'), 'col'), may hold values from 0 to 31, as said below
- c_cols: int32 [32, 4], P('row', 'col'), may hold values from 0 to 31, as said below
Outputs:
- c_blocks: bfloat16 [32, 4, 128, 128], P(('row', 'layer'), 'col')
The draws below stay inside these ranges and needn't reach their ends.
Inputs may be any that keep to these rules, and one draw needn't show every extreme that they name: The pairs (a_rows[n], a_cols[n]) are all distinct. The blocks held by device (r, c, l) have block rows in [r * 32 / 4, (r + 1) * 32 / 4) and block columns k with (k // (32 / (4 * 4))) % 4 == l. `a_cols`: see a_rows. `s_cols`: in each row, the entries t with t // 2 == c are distinct block columns in [c * 32 / 2, (c + 1) * 32 / 2). `c_cols`: in each row, the entries t with t // 2 == c are distinct block columns in [c * 32 / 2, (c + 1) * 32 / 2).
All inputs are finite; a program needn't handle non-finite values.
Results may differ from the reference program's by a relative error of at most 0.001.
Values may be sent and summed in bfloat16 or wider, within the bound.
No kernel may reach another device: no remote copies, remote signals or barrier semaphores. Data moves between devices by JAX's collectives and lax.ppermute only.
A program may use at most 192 MiB of HBM per device.

```python
import math
import jax
import jax.numpy as jnp
from jax import lax

BS = 128
BROWS_DEV = 1
NB = 32
XPER = 24
S_PER_RANGE = 2
C_PER_RANGE = 2
N_ROW = 4
N_COL = 2
N_LAYER = 4
DEVICES = 32


def block_positions(key):
    base_key = jax.random.fold_in(key, 7)
    rows_group = NB // N_ROW
    span_layer = NB // N_LAYER
    per_device = BROWS_DEV * XPER
    wanted = N_COL * per_device
    piece_rows = NB // (N_ROW * N_LAYER)
    key_list = jax.random.split(base_key, N_ROW * N_LAYER)
    picked = jax.vmap(lambda one_key: jax.random.permutation(one_key, rows_group * span_layer)[:wanted])(key_list)
    picked = picked.reshape(N_ROW, N_LAYER, N_COL, per_device).astype(jnp.int32)
    local_row = picked // span_layer
    panel_index = picked % span_layer
    row_index = jnp.arange(N_ROW, dtype=jnp.int32).reshape(N_ROW, 1, 1, 1)
    layer_index = jnp.arange(N_LAYER, dtype=jnp.int32).reshape(1, N_LAYER, 1, 1)
    global_row = row_index * rows_group + local_row
    global_col = (panel_index // piece_rows * N_LAYER + layer_index) * piece_rows + panel_index % piece_rows
    global_row = jnp.transpose(global_row, (0, 2, 1, 3)).reshape(-1).astype(jnp.int32)
    global_col = jnp.transpose(global_col, (0, 2, 1, 3)).reshape(-1).astype(jnp.int32)
    return (global_row, global_col)


def range_columns(key, how_many, salt):
    width_range = NB // N_COL
    key_list = jax.random.split(jax.random.fold_in(key, salt), NB * N_COL)
    picked = jax.vmap(lambda one_key: jax.random.permutation(one_key, width_range)[:how_many])(key_list)
    picked = picked.reshape(NB, N_COL, how_many).astype(jnp.int32)
    range_base = (jnp.arange(N_COL, dtype=jnp.int32) * width_range).reshape(1, N_COL, 1)
    return (picked + range_base).reshape(NB, N_COL * how_many).astype(jnp.int32)


def draw_a_rows(key, part):
    return block_positions(key)[0]


def draw_a_cols(key, part):
    return block_positions(key)[1]


def draw_s_cols(key, part):
    return range_columns(key, S_PER_RANGE, 11)


def draw_c_cols(key, part):
    return range_columns(key, C_PER_RANGE, 13)


def shard_levels(key, extent, cuts, smallest, high):
    def one(dim, blocks):
        draws = jax.random.uniform(jax.random.fold_in(jax.random.fold_in(key, 6), dim), (blocks,), jnp.float32, smallest / len(cuts), high / len(cuts))
        return jnp.repeat(jnp.exp(draws), extent[dim] // blocks).reshape((-1,) + (1,) * (len(extent) - dim - 1))

    gain = one(*cuts[0])
    for cut in cuts[1:]:
        gain = gain * one(*cut)
    return gain


def noise(key, extent, spread, most, cuts=(), kind=jnp.bfloat16):
    result = jax.random.normal(key, extent, jnp.float32) * spread
    if len(cuts) > 0:
        result = shard_levels(key, extent, cuts, -0.22, 0.18) * result
    return jnp.clip(result, min=-most, max=most).astype(kind)


def setup_inputs(seed: int = 0) -> dict:
    keys = jax.random.split(jax.random.key(seed), 7)
    a_blocks = noise(keys[0], (DEVICES * BROWS_DEV * XPER, BS, BS), BS ** -0.5, 0.5, ((0, 32),))
    a_rows = draw_a_rows(jax.random.fold_in(keys[6], 71), 0)
    a_cols = draw_a_cols(jax.random.fold_in(keys[6], 71), 0)
    s_blocks = noise(keys[3], (NB, N_COL * S_PER_RANGE, BS, BS), 1.0, 6.0, ((0, 16), (1, 2)))
    s_cols = draw_s_cols(jax.random.fold_in(keys[6], 71), 0)
    c_cols = draw_c_cols(jax.random.fold_in(keys[6], 71), 0)
    return dict(a_blocks=a_blocks, a_rows=a_rows, a_cols=a_cols, s_blocks=s_blocks, s_cols=s_cols, c_cols=c_cols)


def reference(a_blocks, a_rows, a_cols, s_blocks, s_cols, c_cols):
    block_count = a_blocks.shape[0]
    kept_width = c_cols.shape[1]
    slot_total = NB * kept_width
    group_size = math.gcd(block_count, 64)
    group_count = block_count // group_size

    def add_block_group(totals, group_index):
        offset = group_index * group_size
        left_blocks = lax.dynamic_slice_in_dim(a_blocks, offset, group_size, 0).astype(jnp.float32)
        block_rows = lax.dynamic_slice_in_dim(a_rows, offset, group_size, 0)
        block_cols = lax.dynamic_slice_in_dim(a_cols, offset, group_size, 0)
        right_blocks = jnp.take(s_blocks, block_cols, axis=0).astype(jnp.float32)
        right_cols = jnp.take(s_cols, block_cols, axis=0)
        kept_cols = jnp.take(c_cols, block_rows, axis=0)
        matches = right_cols[:, :, None] == kept_cols[:, None, :]
        landed = jnp.any(matches, axis=2)
        slot_index = jnp.sum(jnp.where(matches, jnp.arange(kept_width, dtype=jnp.int32)[None, None, :], 0), axis=2).astype(jnp.int32)
        targets = jnp.where(landed, block_rows[:, None] * kept_width + slot_index, slot_total).astype(jnp.int32)
        products = jnp.einsum("mab,msbc->msac", left_blocks, right_blocks)
        totals = totals.at[targets.reshape(-1)].add(products.reshape(-1, BS, BS), mode="drop")
        return totals, None

    zero_sum = jnp.zeros((slot_total, BS, BS), jnp.float32)
    totals, unused = lax.scan(add_block_group, zero_sum, jnp.arange(group_count, dtype=jnp.int32))
    return totals.reshape(NB, kept_width, BS, BS).astype(jnp.bfloat16)
```

```python
import functools

import jax
import jax.numpy as jnp
from jax import lax
from jax.experimental import pallas as pl
from jax.experimental.pallas import tpu as pltpu
from jax.sharding import PartitionSpec as P


def shifted(value, axis, offset):
    size = lax.axis_size(axis)
    return lax.ppermute(value, axis, [((i + offset) % size, i) for i in range(size)])


def product_kernel(sizes, *refs):
    rows, cols, layers, count, piece_rows, width, local_rows, kept = sizes
    refs = list(refs)
    a_rows, refs = refs[:cols], refs[cols:]
    a_cols, refs = refs[:cols], refs[cols:]
    s_cols, refs = refs[:rows], refs[rows:]
    c_cols, refs = refs[0], refs[1:]
    x_in, refs = refs[:cols], refs[cols:]
    s_in, refs = refs[:rows], refs[rows:]
    outs, refs = refs[:layers], refs[layers:]
    x_held, s_held, totals, x_sem, s_sem, out_sem = refs

    loads = [pltpu.make_async_copy(s_in[d], s_held.at[d], s_sem.at[d]) for d in range(rows)]
    loads += [pltpu.make_async_copy(x_in[j], x_held.at[j], x_sem.at[j]) for j in range(cols)]
    for load in loads:
        load.start()
    totals[...] = jnp.zeros_like(totals)
    here = lax.div(a_rows[0][0], local_rows)
    layer = lax.rem(lax.div(a_cols[0][0], piece_rows), layers)
    own_rows = local_rows // layers
    for load in loads:
        load.wait()

    for j in range(cols):

        def one_block(n, carry):
            row = a_rows[j][n] - here * local_rows
            inner = a_cols[j][n]
            owner = lax.div(lax.div(inner, piece_rows), layers)
            piece = lax.rem(owner - here + rows, rows)
            inner = lax.rem(inner, piece_rows)
            goal = lax.rem(lax.div(row, own_rows) - layer + layers, layers)
            goal = (goal * own_rows + lax.rem(row, own_rows)) * kept
            for s in range(width):
                wanted = s_cols[0][inner, s]
                for d in range(1, rows):
                    wanted = jnp.where(piece == d, s_cols[d][inner, s], wanted)
                for t in range(kept):

                    @pl.when(c_cols[row, t] == wanted)
                    def _():
                        totals[goal + t] += jnp.dot(
                            x_held[j, n],
                            s_held[piece, inner, s],
                            preferred_element_type=jnp.float32,
                        )

            return carry

        lax.fori_loop(0, count, one_block, 0)

    slots = own_rows * kept
    stores = [
        pltpu.make_async_copy(totals.at[pl.ds(d * slots, slots)], outs[d], out_sem.at[d])
        for d in range(layers)
    ]
    for store in stores:
        store.start()
    for store in stores:
        store.wait()


def per_device(a_blocks, a_rows, a_cols, s_blocks, s_cols, c_cols):
    rows, cols, layers = (lax.axis_size(axis) for axis in ("row", "col", "layer"))
    count, order = a_blocks.shape[:2]
    piece_rows, width = s_cols.shape
    local_rows, kept = c_cols.shape
    own_rows = local_rows // layers
    slots = own_rows * kept

    x_pieces = [a_blocks] + [shifted(a_blocks, "col", j) for j in range(1, cols)]
    row_pieces = [a_rows] + [shifted(a_rows, "col", j) for j in range(1, cols)]
    col_pieces = [a_cols] + [shifted(a_cols, "col", j) for j in range(1, cols)]
    s_pieces = [s_blocks] + [shifted(s_blocks, "row", d) for d in range(1, rows)]
    s_col_pieces = [s_cols] + [shifted(s_cols, "row", d) for d in range(1, rows)]

    scalars = pl.BlockSpec(memory_space=pltpu.SMEM)
    anywhere = pl.BlockSpec(memory_space=pl.ANY)
    sizes = (rows, cols, layers, count, piece_rows, width, local_rows, kept)
    held_bytes = 2 * order * order * (cols * count + rows * piece_rows * width)
    total_bytes = 4 * order * order * local_rows * kept
    pairs = cols * count * width
    parts = pl.pallas_call(
        functools.partial(product_kernel, sizes),
        out_shape=[jax.ShapeDtypeStruct((slots, order, order), jnp.float32)] * layers,
        in_specs=[scalars] * (2 * cols + rows + 1) + [anywhere] * (cols + rows),
        out_specs=[anywhere] * layers,
        scratch_shapes=[
            pltpu.VMEM((cols, count, order, order), jnp.bfloat16),
            pltpu.VMEM((rows, piece_rows, width, order, order), jnp.bfloat16),
            pltpu.VMEM((layers * slots, order, order), jnp.float32),
            pltpu.SemaphoreType.DMA((cols,)),
            pltpu.SemaphoreType.DMA((rows,)),
            pltpu.SemaphoreType.DMA((layers,)),
        ],
        compiler_params=pltpu.CompilerParams(
            vmem_limit_bytes=held_bytes + total_bytes + 4 * 2**20
        ),
        cost_estimate=pl.CostEstimate(
            flops=2 * order**3 * pairs // 4,
            bytes_accessed=held_bytes + total_bytes,
            transcendentals=0,
        ),
        name="products",
    )(*row_pieces, *col_pieces, *s_col_pieces, c_cols, *x_pieces, *s_pieces)

    result = parts[0]
    for d in range(1, layers):
        result = result + shifted(parts[d], "layer", layers - d)
    return result.reshape(own_rows, kept, order, order).astype(jnp.bfloat16)


def solution(mesh):
    placed = (
        P(("row", "col", "layer"), None, None),
        P(("row", "col", "layer")),
        P(("row", "col", "layer")),
        P(("row", "layer"), "col", None, None),
        P(("row", "layer"), "col"),
        P("row", "col"),
    )
    return jax.shard_map(
        per_device,
        mesh=mesh,
        in_specs=placed,
        out_specs=P(("row", "layer"), "col", None, None),
        check_vma=False,
    )
```

```python
import functools

import jax
import jax.numpy as jnp
from jax import lax
from jax.experimental import pallas as pl
from jax.experimental.pallas import tpu as pltpu
from jax.sharding import PartitionSpec as P

CHUNKS = 2
GROUP = 4
MIB = 2**20


def shifted(value, axis, offset):
    size = lax.axis_size(axis)
    return lax.ppermute(value, axis, [((i + offset) % size, i) for i in range(size)])


def plan_kernel(sizes, *refs):
    rows, cols, layers, count, piece_rows, width, local_rows, kept = sizes
    row_packs, col_packs = (refs[0],) + refs[1:rows], (refs[0],) + refs[rows : rows + cols - 1]
    c_cols, pairs, tally, panel_cols = refs[rows + cols - 1 :]
    piece = piece_rows * width
    for d in range(rows):
        for q in range(piece):
            panel_cols[d * piece + q] = row_packs[d][2 * count + q]
    here = lax.div(refs[0][0], local_rows)
    layer = lax.rem(lax.div(refs[0][count], piece_rows), layers)
    own_rows = local_rows // layers
    total = jnp.int32(0)
    for j in range(cols):

        def one_block(n, total):
            row = col_packs[j][n] - here * local_rows
            inner = col_packs[j][count + n]
            owner = lax.div(inner, piece_rows * layers)
            inner = lax.rem(inner, piece_rows)
            right = (lax.rem(owner - here + rows, rows) * piece_rows + inner) * width
            goal = lax.rem(lax.div(row, own_rows) - layer + layers, layers)
            goal = (goal * own_rows + lax.rem(row, own_rows)) * kept
            for s in range(width):
                wanted = panel_cols[right + s]
                hit, slot = jnp.int32(0), goal
                for t in range(kept):
                    same = (c_cols[row, t] == wanted).astype(jnp.int32)
                    hit += same
                    slot += t * same
                pairs[0, total] = j * count + n
                pairs[1, total] = right + s
                pairs[2, total] = slot
                total += hit
            return total

        total = lax.fori_loop(0, count, one_block, total)
    for g in range(GROUP):
        pairs[0, total + g] = 0
        pairs[1, total + g] = 0
        pairs[2, total + g] = local_rows * kept
    tally[0] = total


def product_kernel(sizes, first, *refs):
    rows, cols, layers, count, slots, height = sizes
    pairs, tally, refs = refs[0], refs[1], refs[2:]
    x_in, refs = refs[:cols], refs[cols:]
    s_in, refs = refs[:rows], refs[rows:]
    own, sent, refs = refs[0], refs[1:layers], refs[layers:]
    x_held, s_held, totals, x_sem, s_sem = refs

    piece = s_held.shape[0] // rows
    loads = [
        pltpu.make_async_copy(s_in[d], s_held.at[pl.ds(d * piece, piece)], s_sem.at[d])
        for d in range(rows)
    ]
    loads.append(
        pltpu.make_async_copy(
            x_in[0].at[:, pl.ds(first, height), :], x_held.at[pl.ds(0, count)], x_sem.at[0]
        )
    )
    loads += [
        pltpu.make_async_copy(x_in[j], x_held.at[pl.ds(j * count, count)], x_sem.at[j])
        for j in range(1, cols)
    ]
    for load in loads:
        load.start()
    totals[...] = jnp.zeros_like(totals)
    for load in loads:
        load.wait()

    def one_group(group, carry):
        base = group * GROUP
        products = [
            jnp.dot(
                x_held[pairs[0, base + g]],
                s_held[pairs[1, base + g]],
                preferred_element_type=jnp.float32,
            )
            for g in range(GROUP)
        ]
        for g in range(GROUP):
            totals[pairs[2, base + g]] += products[g]
        return carry

    lax.fori_loop(0, lax.div(tally[0] + GROUP - 1, GROUP), one_group, 0)

    own[...] = totals[:slots]
    half = height // 2
    for d in range(1, layers):
        code = sent[d - 1]
        code[slots * half :] = jnp.zeros((code.shape[0] - slots * half, code.shape[1]), jnp.int32)
        for u in range(slots):
            value = totals[d * slots + u]
            peak = jnp.max(jnp.abs(value), axis=0, keepdims=True)
            power = jnp.floor(jnp.log2(jnp.maximum(peak, 1e-30)) + 1e-3) + 1.0
            whole = jnp.floor(value * jnp.exp2(15.0 - power) + 0.5).astype(jnp.int32)
            code[pl.ds(u * half, half)] = (whole[:half] << 16) | (whole[half:] & 0xFFFF)
            code[pl.ds(slots * half + u, 1)] = power.astype(jnp.int32)


def finish_kernel(sizes, *refs):
    layers, chunks, slots, height = sizes
    result = refs[-1]
    kept = result.shape[1]
    half = height // 2
    for c in range(chunks):
        own, codes = refs[c * layers], refs[c * layers + 1 : (c + 1) * layers]
        for u in range(slots):
            high, low = own[u, :half], own[u, half:]
            for code in codes:
                word = code[pl.ds(u * half, half)]
                power = code[pl.ds(slots * half + u, 1)].astype(jnp.float32)
                scale = jnp.exp2(power - 15.0)
                high += (word >> 16).astype(jnp.float32) * scale
                low += ((word << 16) >> 16).astype(jnp.float32) * scale
            at = c * height
            result[u // kept, u % kept, at : at + half] = high.astype(jnp.bfloat16)
            result[u // kept, u % kept, at + half : at + height] = low.astype(jnp.bfloat16)


def per_device(a_blocks, a_rows, a_cols, s_blocks, s_cols, c_cols):
    rows, cols, layers = (lax.axis_size(axis) for axis in ("row", "col", "layer"))
    count, order = a_blocks.shape[:2]
    piece_rows, width = s_cols.shape
    local_rows, kept = c_cols.shape
    own_rows = local_rows // layers
    slots = own_rows * kept
    height = order // CHUNKS
    panel = rows * piece_rows * width

    x_pieces = []
    for c in range(CHUNKS):
        part = lax.slice_in_dim(a_blocks, c * height, (c + 1) * height, axis=1)
        x_pieces.append([shifted(part, "col", j) for j in range(1, cols)])
    pack = jnp.concatenate([a_rows, a_cols, s_cols.reshape(-1)])
    row_packs = [shifted(pack, "row", d) for d in range(1, rows)]
    col_packs = [shifted(pack, "col", j) for j in range(1, cols)]
    flat_s = s_blocks.reshape(piece_rows * width, order, order)
    s_pieces = [flat_s] + [shifted(flat_s, "row", d) for d in range(1, rows)]

    scalars = pl.BlockSpec(memory_space=pltpu.SMEM)
    anywhere = pl.BlockSpec(memory_space=pl.ANY)
    vector = pl.BlockSpec(memory_space=pltpu.VMEM)
    most = cols * count * width
    pairs, tally = pl.pallas_call(
        functools.partial(
            plan_kernel, (rows, cols, layers, count, piece_rows, width, local_rows, kept)
        ),
        out_shape=[
            jax.ShapeDtypeStruct((3, most + GROUP), jnp.int32),
            jax.ShapeDtypeStruct((1,), jnp.int32),
        ],
        in_specs=[scalars] * (rows + cols),
        out_specs=[scalars] * 2,
        scratch_shapes=[pltpu.SMEM((panel,), jnp.int32)],
        name="plan",
    )(pack, *row_packs, *col_packs, c_cols)

    held_bytes = 2 * order * (cols * count * height + panel * order)
    total_bytes = 4 * order * height * (local_rows * kept + 1)
    code_rows = slots * (height // 2) + (slots + 7) // 8 * 8
    parts = []
    for c in range(CHUNKS):
        parts.append(
            pl.pallas_call(
                functools.partial(
                    product_kernel, (rows, cols, layers, count, slots, height), c * height
                ),
                out_shape=[jax.ShapeDtypeStruct((slots, height, order), jnp.float32)]
                + [jax.ShapeDtypeStruct((code_rows, order), jnp.int32)] * (layers - 1),
                in_specs=[scalars] * 2 + [anywhere] * (cols + rows),
                out_specs=[vector] * layers,
                scratch_shapes=[
                    pltpu.VMEM((cols * count, height, order), jnp.bfloat16),
                    pltpu.VMEM((panel, order, order), jnp.bfloat16),
                    pltpu.VMEM((layers * slots + 1, height, order), jnp.float32),
                    pltpu.SemaphoreType.DMA((cols,)),
                    pltpu.SemaphoreType.DMA((rows,)),
                ],
                compiler_params=pltpu.CompilerParams(
                    vmem_limit_bytes=held_bytes + 2 * total_bytes + 4 * MIB
                ),
                cost_estimate=pl.CostEstimate(
                    flops=2 * order**2 * height * most // 4,
                    bytes_accessed=held_bytes + total_bytes,
                    transcendentals=0,
                ),
                name=f"products_{c}",
            )(pairs, tally, a_blocks, *x_pieces[c], *s_pieces)
        )

    final = []
    for part in parts:
        final.append(part[0])
        final += [shifted(part[d], "layer", layers - d) for d in range(1, layers)]
    return pl.pallas_call(
        functools.partial(finish_kernel, (layers, CHUNKS, slots, height)),
        out_shape=jax.ShapeDtypeStruct((own_rows, kept, order, order), jnp.bfloat16),
        in_specs=[vector] * len(final),
        out_specs=vector,
        compiler_params=pltpu.CompilerParams(
            vmem_limit_bytes=16 * slots * order * order + 4 * MIB
        ),
        name="finish",
    )(*final)


def solution(mesh):
    placed = (
        P(("row", "col", "layer"), None, None),
        P(("row", "col", "layer")),
        P(("row", "col", "layer")),
        P(("row", "layer"), "col", None, None),
        P(("row", "layer"), "col"),
        P("row", "col"),
    )
    return jax.shard_map(
        per_device,
        mesh=mesh,
        in_specs=placed,
        out_specs=P(("row", "layer"), "col", None, None),
        check_vma=False,
    )
```

```python
import functools

import jax
import jax.numpy as jnp
from jax import lax
from jax.experimental import pallas as pl
from jax.experimental.pallas import tpu as pltpu
from jax.sharding import PartitionSpec as P

CHUNKS = 2
GROUP = 4
LANES = 128
MIB = 2**20


def shifted(value, axis, offset):
    size = lax.axis_size(axis)
    return lax.ppermute(value, axis, [((i + offset) % size, i) for i in range(size)])


def note_rows(how_many):
    digits = (how_many + LANES - 1) // LANES
    return (2 * digits + 15) // 16 * 16, digits


def write_notes(payload, start, values):
    height, digits = note_rows(len(values))
    row = lax.broadcasted_iota(jnp.int32, (height, LANES), 0)
    lane = lax.broadcasted_iota(jnp.int32, (height, LANES), 1)
    tile = jnp.zeros((height, LANES), jnp.int32)
    for p, value in enumerate(values):
        high = value >> 7
        here = lane == p % LANES
        tile = jnp.where(here & (row == p // LANES), value & 127, tile)
        tile = jnp.where(here & (row == digits + p // LANES), high, tile)
    payload[start : start + height] = tile.astype(jnp.float32).astype(jnp.bfloat16)


def read_notes(payload, start, how_many, whole, notes, sem):
    height, _ = note_rows(how_many)
    whole[...] = payload[start : start + height].astype(jnp.float32).astype(jnp.int32)
    copy = pltpu.make_async_copy(whole, notes, sem)
    copy.start()
    return copy


def note(notes, how_many, p):
    _, digits = note_rows(how_many)
    if isinstance(p, int) or digits > 1:
        row, lane = (p // LANES, p % LANES) if isinstance(p, int) else (p >> 7, p & 127)
    else:
        row, lane = 0, p
    return notes[row, lane] + (notes[digits + row, lane] << 7)


def pack_kernel(sizes, rights, goals, s_cols, x_in, s_in, x_out, s_out, x_sem, s_sem):
    count, height, order, piece_rows, width = sizes
    piece = piece_rows * width
    loads = [
        pltpu.make_async_copy(
            x_in.at[n, pl.ds(0, height)], x_out.at[pl.ds(n * height, height)], x_sem.at[n]
        )
        for n in range(count)
    ]
    loads += [
        pltpu.make_async_copy(s_in.at[q], s_out.at[pl.ds(q * order, order)], s_sem.at[q])
        for q in range(piece)
    ]
    for load in loads:
        load.start()
    write_notes(
        x_out, count * height, [rights[n] for n in range(count)] + [goals[n] for n in range(count)]
    )
    write_notes(
        s_out, piece * order, [s_cols[q, s] for q in range(piece_rows) for s in range(width)]
    )
    for load in loads:
        load.wait()


def list_pairs(sizes, target, panel_cols, kept_cols, pairs, tally, j):
    count, width, kept, trash = sizes

    def one_block(n, total):
        right, goal = target(n)
        for s in range(width):
            wanted = panel_cols[right + s]
            hit, slot = jnp.int32(0), goal
            for t in range(kept):
                same = (kept_cols[goal + t] == wanted).astype(jnp.int32)
                hit += same
                slot += t * same
            pairs[j, 0, total] = n
            pairs[j, 1, total] = right + s
            pairs[j, 2, total] = slot
            total += hit
        return total

    total = lax.fori_loop(0, count, one_block, jnp.int32(0))
    for g in range(GROUP):
        pairs[j, 0, total + g] = 0
        pairs[j, 1, total + g] = 0
        pairs[j, 2, total + g] = trash
    tally[j] = total


def add_products(left, panel, totals, pairs, tally, j):
    def one_group(group, carry):
        base = group * GROUP
        products = [
            jnp.dot(
                left(pairs[j, 0, base + g]),
                panel[pairs[j, 1, base + g]],
                preferred_element_type=jnp.float32,
            )
            for g in range(GROUP)
        ]
        for g in range(GROUP):
            totals[pairs[j, 2, base + g]] += products[g]
        return carry

    lax.fori_loop(0, lax.div(tally[j] + GROUP - 1, GROUP), one_group, 0)


def own_kernel(sizes, *refs):
    rows, layers, count, piece_rows, width, local_rows, kept, order = sizes
    layer, rights, goals, s_cols, c_cols, x_in, s_in = refs[:7]
    s_other = refs[7 : 6 + rows]
    totals, panel, panel_cols, kept_cols = refs[6 + rows : 10 + rows]
    whole, notes, pairs, tally, s_sem, note_sem = refs[10 + rows :]
    piece = piece_rows * width
    loads = [pltpu.make_async_copy(s_in, panel.at[pl.ds(0, piece)], s_sem.at[0])]
    for d in range(1, rows):
        loads += [
            pltpu.make_async_copy(
                s_other[d - 1].at[pl.ds(q * order, order)],
                panel.at[d * piece + q],
                s_sem.at[d * piece + q],
            )
            for q in range(piece)
        ]
    for load in loads:
        load.start()
    reads = [
        read_notes(s_other[d], piece * order, piece, whole.at[d], notes.at[d], note_sem.at[d])
        for d in range(rows - 1)
    ]
    totals[...] = jnp.zeros_like(totals)
    own_rows = local_rows // layers
    for g in range(layers):
        base = lax.rem(layer[0] + g, layers) * own_rows
        for i in range(own_rows):
            for t in range(kept):
                kept_cols[(g * own_rows + i) * kept + t] = c_cols[base + i, t]
    for read in reads:
        read.wait()
    for q in range(piece):
        panel_cols[q] = s_cols[q // width, q % width]
        for d in range(1, rows):
            panel_cols[d * piece + q] = note(notes.at[d - 1], piece, q)
    trash = local_rows * kept
    list_pairs(
        (count, width, kept, trash),
        lambda n: (rights[n], goals[n]),
        panel_cols,
        kept_cols,
        pairs,
        tally,
        0,
    )
    for load in loads:
        load.wait()
    add_products(lambda n: x_in[n], panel, totals, pairs, tally, 0)


def peer_kernel(sizes, first, *refs):
    cols, layers, count, width, kept, slots, height = sizes
    if first == 0:
        panel_cols, kept_cols, refs = refs[0], refs[1], refs[2:]
    else:
        pairs, tally, refs = refs[0], refs[1], refs[2:]
    x_in, refs = refs[: cols - 1], refs[cols - 1 :]
    panel, before, own, sent, refs = refs[0], refs[1], refs[2], refs[3 : 2 + layers], refs[2 + layers :]
    if first == 0:
        pairs, tally, totals, whole, notes, note_sem = refs
        reads = [
            read_notes(x_in[j], count * height, 2 * count, whole.at[j], notes.at[j], note_sem.at[j])
            for j in range(cols - 1)
        ]
    else:
        (totals,) = refs
    totals[...] = before[:, first : first + height]
    if first == 0:
        for j in range(cols - 1):
            reads[j].wait()
            list_pairs(
                (count, width, kept, layers * slots),
                lambda n: (
                    note(notes.at[j], 2 * count, n),
                    note(notes.at[j], 2 * count, count + n),
                ),
                panel_cols,
                kept_cols,
                pairs,
                tally,
                j,
            )

    for j in range(cols - 1):

        def left(n):
            return x_in[j][pl.ds(pl.multiple_of(n * height, height), height)]

        add_products(left, panel, totals, pairs, tally, j)

    own[...] = totals[:slots]
    half = height // 2
    for d in range(1, layers):
        code = sent[d - 1]
        code[slots * half :] = jnp.zeros((code.shape[0] - slots * half, code.shape[1]), jnp.int32)
        for u in range(slots):
            value = totals[d * slots + u]
            peak = jnp.max(jnp.abs(value), axis=0, keepdims=True)
            power = jnp.floor(jnp.log2(jnp.maximum(peak, 1e-30)) + 1e-3) + 1.0
            whole_value = jnp.floor(value * jnp.exp2(15.0 - power) + 0.5).astype(jnp.int32)
            code[pl.ds(u * half, half)] = (whole_value[:half] << 16) | (whole_value[half:] & 0xFFFF)
            code[pl.ds(slots * half + u, 1)] = power.astype(jnp.int32)


def finish_kernel(sizes, *refs):
    layers, chunks, slots, height = sizes
    result = refs[-1]
    kept = result.shape[1]
    half = height // 2
    for c in range(chunks):
        own, codes = refs[c * layers], refs[c * layers + 1 : (c + 1) * layers]
        for u in range(slots):
            high, low = own[u, :half], own[u, half:]
            for code in codes:
                word = code[pl.ds(u * half, half)]
                power = code[pl.ds(slots * half + u, 1)].astype(jnp.float32)
                scale = jnp.exp2(power - 15.0)
                high += (word >> 16).astype(jnp.float32) * scale
                low += ((word << 16) >> 16).astype(jnp.float32) * scale
            at = c * height
            result[u // kept, u % kept, at : at + half] = high.astype(jnp.bfloat16)
            result[u // kept, u % kept, at + half : at + height] = low.astype(jnp.bfloat16)


def per_device(a_blocks, a_rows, a_cols, s_blocks, s_cols, c_cols):
    rows, cols, layers = (lax.axis_size(axis) for axis in ("row", "col", "layer"))
    count, order = a_blocks.shape[:2]
    piece_rows, width = s_cols.shape
    local_rows, kept = c_cols.shape
    own_rows = local_rows // layers
    slots = own_rows * kept
    height = order // CHUNKS
    piece = piece_rows * width
    panel_size = rows * piece

    row_at, layer_at = lax.axis_index("row"), lax.axis_index("layer")
    owner = a_cols // (piece_rows * layers)
    rights = ((owner - row_at + rows) % rows * piece_rows + a_cols % piece_rows) * width
    local = a_rows - row_at * local_rows
    goals = (local // own_rows - layer_at + layers) % layers * own_rows + local % own_rows
    goals = goals * kept
    flat_s = s_blocks.reshape(piece, order, order)

    scalars = pl.BlockSpec(memory_space=pltpu.SMEM)
    anywhere = pl.BlockSpec(memory_space=pl.ANY)
    vector = pl.BlockSpec(memory_space=pltpu.VMEM)
    x_note_rows, _ = note_rows(2 * count)
    s_note_rows, _ = note_rows(piece)

    x_first, s_sent = pl.pallas_call(
        functools.partial(pack_kernel, (count, height, order, piece_rows, width)),
        out_shape=[
            jax.ShapeDtypeStruct((count * height + x_note_rows, order), jnp.bfloat16),
            jax.ShapeDtypeStruct((piece * order + s_note_rows, order), jnp.bfloat16),
        ],
        in_specs=[scalars] * 3 + [anywhere] * 2,
        out_specs=[vector] * 2,
        scratch_shapes=[pltpu.SemaphoreType.DMA((count,)), pltpu.SemaphoreType.DMA((piece,))],
        name="pack",
    )(rights, goals, s_cols, a_blocks, flat_s)
    x_pieces = [[shifted(x_first, "col", j) for j in range(1, cols)]]
    s_pieces = [shifted(s_sent, "row", d) for d in range(1, rows)]
    for c in range(1, CHUNKS):
        part = lax.slice_in_dim(a_blocks, c * height, (c + 1) * height, axis=1)
        part = part.reshape(count * height, order)
        x_pieces.append([shifted(part, "col", j) for j in range(1, cols)])

    all_slots = layers * slots
    block_bytes = order * order
    totals, panel, panel_cols, kept_cols = pl.pallas_call(
        functools.partial(
            own_kernel, (rows, layers, count, piece_rows, width, local_rows, kept, order)
        ),
        out_shape=[
            jax.ShapeDtypeStruct((all_slots + 1, order, order), jnp.float32),
            jax.ShapeDtypeStruct((panel_size, order, order), jnp.bfloat16),
            jax.ShapeDtypeStruct((panel_size,), jnp.int32),
            jax.ShapeDtypeStruct((all_slots,), jnp.int32),
        ],
        in_specs=[scalars] * 5 + [vector] * (1 + rows),
        out_specs=[vector] * 2 + [scalars] * 2,
        scratch_shapes=[
            pltpu.VMEM((rows - 1, s_note_rows, LANES), jnp.int32),
            pltpu.SMEM((rows - 1, s_note_rows, LANES), jnp.int32),
            pltpu.SMEM((1, 3, count * width + GROUP), jnp.int32),
            pltpu.SMEM((1,), jnp.int32),
            pltpu.SemaphoreType.DMA((panel_size,)),
            pltpu.SemaphoreType.DMA((rows - 1,)),
        ],
        compiler_params=pltpu.CompilerParams(
            vmem_limit_bytes=block_bytes * (4 * all_slots + 4 * panel_size + 2 * count) + 4 * MIB
        ),
        cost_estimate=pl.CostEstimate(
            flops=2 * order**3 * count * width // 4,
            bytes_accessed=block_bytes * (4 * all_slots + 4 * panel_size + 2 * count),
            transcendentals=0,
        ),
        name="own_products",
    )(layer_at.reshape(1), rights, goals, s_cols, c_cols, a_blocks, flat_s, *s_pieces)

    code_rows = slots * (height // 2) + (slots + 7) // 8 * 8
    pair_shapes = [(cols - 1, 3, count * width + GROUP), (cols - 1,)]
    parts, plan = [], []
    for c in range(CHUNKS):
        out_shape = [jax.ShapeDtypeStruct((slots, height, order), jnp.float32)]
        out_shape += [jax.ShapeDtypeStruct((code_rows, order), jnp.int32)] * (layers - 1)
        out_specs = [vector] * layers
        scratch = [pltpu.VMEM((all_slots + 1, height, order), jnp.float32)]
        if c == 0:
            out_shape += [jax.ShapeDtypeStruct(shape, jnp.int32) for shape in pair_shapes]
            out_specs += [scalars] * 2
            scratch += [
                pltpu.VMEM((cols - 1, x_note_rows, LANES), jnp.int32),
                pltpu.SMEM((cols - 1, x_note_rows, LANES), jnp.int32),
                pltpu.SemaphoreType.DMA((cols - 1,)),
            ]
        moved = block_bytes * (8 * all_slots + 2 * panel_size + 2 * count * (cols - 1))
        out = pl.pallas_call(
            functools.partial(
                peer_kernel, (cols, layers, count, width, kept, slots, height), c * height
            ),
            out_shape=out_shape,
            in_specs=[scalars] * 2 + [vector] * (cols + 1),
            out_specs=out_specs,
            scratch_shapes=scratch,
            compiler_params=pltpu.CompilerParams(vmem_limit_bytes=moved + 4 * MIB),
            cost_estimate=pl.CostEstimate(
                flops=2 * order**2 * height * count * width // 4 * (cols - 1),
                bytes_accessed=moved // CHUNKS,
                transcendentals=0,
            ),
            name=f"peer_products_{c}",
        )(*(plan or (panel_cols, kept_cols)), *x_pieces[c], panel, totals)
        if c == 0:
            plan = out[layers:]
        parts.append(out[:layers])

    final = []
    for part in parts:
        final.append(part[0])
        final += [shifted(part[d], "layer", layers - d) for d in range(1, layers)]
    return pl.pallas_call(
        functools.partial(finish_kernel, (layers, CHUNKS, slots, height)),
        out_shape=jax.ShapeDtypeStruct((own_rows, kept, order, order), jnp.bfloat16),
        in_specs=[vector] * len(final),
        out_specs=vector,
        compiler_params=pltpu.CompilerParams(
            vmem_limit_bytes=16 * slots * order * order + 4 * MIB
        ),
        name="finish",
    )(*final)


def solution(mesh):
    placed = (
        P(("row", "col", "layer"), None, None),
        P(("row", "col", "layer")),
        P(("row", "col", "layer")),
        P(("row", "layer"), "col", None, None),
        P(("row", "layer"), "col"),
        P("row", "col"),
    )
    return jax.shard_map(
        per_device,
        mesh=mesh,
        in_specs=placed,
        out_specs=P(("row", "layer"), "col", None, None),
        check_vma=False,
    )
```

```python
import functools

import jax
import jax.numpy as jnp
from jax import lax
from jax.experimental import pallas as pl
from jax.experimental.pallas import tpu as pltpu
from jax.sharding import PartitionSpec as P

CHUNKS = 2
GROUP = 4
LANES = 128
MIB = 2**20


def shifted(value, axis, offset):
    size = lax.axis_size(axis)
    return lax.ppermute(value, axis, [((i + offset) % size, i) for i in range(size)])


def quotient(value, by):
    return value >> (by.bit_length() - 1) if by & (by - 1) == 0 else lax.div(value, by)


def remainder(value, by):
    return value & (by - 1) if by & (by - 1) == 0 else lax.rem(value, by)


def note_rows(how_many):
    digits = (how_many + LANES - 1) // LANES
    return (2 * digits + 15) // 16 * 16, digits


def write_notes(payload, start, values):
    height, digits = note_rows(len(values))
    row = lax.broadcasted_iota(jnp.int32, (height, LANES), 0)
    lane = lax.broadcasted_iota(jnp.int32, (height, LANES), 1)
    tile = jnp.zeros((height, LANES), jnp.int32)
    for p, value in enumerate(values):
        here = lane == p % LANES
        tile = jnp.where(here & (row == p // LANES), value & (LANES - 1), tile)
        tile = jnp.where(here & (row == digits + p // LANES), quotient(value, LANES), tile)
    payload[start : start + height] = tile.astype(jnp.float32).astype(jnp.bfloat16)


def read_notes(payload, start, how_many, whole, notes, sem):
    height, _ = note_rows(how_many)
    whole[...] = payload[start : start + height].astype(jnp.float32).astype(jnp.int32)
    copy = pltpu.make_async_copy(whole, notes, sem)
    copy.start()
    return copy


def note(notes, how_many, p):
    _, digits = note_rows(how_many)
    return notes[p // LANES, p % LANES] + notes[digits + p // LANES, p % LANES] * LANES


def pack_kernel(sizes, a_rows, a_cols, s_cols, s_in, index, s_out, s_sem):
    count, order, piece_rows, width = sizes
    piece = piece_rows * width
    loads = [
        pltpu.make_async_copy(s_in.at[q], s_out.at[pl.ds(q * order, order)], s_sem.at[q])
        for q in range(piece)
    ]
    for load in loads:
        load.start()
    for n in range(count):
        index[n] = a_rows[n]
        index[count + n] = a_cols[n]
    write_notes(
        s_out, piece * order, [s_cols[q, s] for q in range(piece_rows) for s in range(width)]
    )
    for load in loads:
        load.wait()


def list_pairs(sizes, index, here, layer, panel_cols, kept_cols, pairs, tally, j):
    rows, layers, count, piece_rows, width, local_rows, kept = sizes
    own_rows = local_rows // layers

    def one_block(n, total):
        row = index[n] - here * local_rows
        inner = index[count + n]
        owner = quotient(inner, piece_rows * layers)
        inner = remainder(inner, piece_rows)
        right = (remainder(owner - here + rows, rows) * piece_rows + inner) * width
        goal = remainder(quotient(row, own_rows) - layer + layers, layers)
        goal = (goal * own_rows + remainder(row, own_rows)) * kept
        for s in range(width):
            wanted = panel_cols[right + s]
            hit, slot = jnp.int32(0), goal
            for t in range(kept):
                same = (kept_cols[goal + t] == wanted).astype(jnp.int32)
                hit += same
                slot += t * same
            pairs[j, 0, total] = n
            pairs[j, 1, total] = right + s
            pairs[j, 2, total] = slot
            total += hit
        return total

    total = lax.fori_loop(0, count, one_block, jnp.int32(0))
    for g in range(GROUP):
        pairs[j, 0, total + g] = 0
        pairs[j, 1, total + g] = 0
        pairs[j, 2, total + g] = local_rows * kept
    tally[j] = total


def add_products(left, panel, totals, pairs, tally, j):
    def one_group(group, carry):
        base = group * GROUP
        products = [
            jnp.dot(
                left(pairs[j, 0, base + g]),
                panel[pairs[j, 1, base + g]],
                preferred_element_type=jnp.float32,
            )
            for g in range(GROUP)
        ]
        for g in range(GROUP):
            totals[pairs[j, 2, base + g]] += products[g]
        return carry

    lax.fori_loop(0, quotient(tally[j] + GROUP - 1, GROUP), one_group, 0)


def own_kernel(sizes, *refs):
    rows, cols, layers, count, piece_rows, width, local_rows, kept, order = sizes
    index, s_cols, c_cols, x_in, s_in = refs[:cols], *refs[cols : cols + 4]
    s_other, refs = refs[cols + 4 : cols + 3 + rows], refs[cols + 3 + rows :]
    totals, panel, pairs, tally = refs[:4]
    panel_cols, kept_cols, whole, notes, s_sem, note_sem = refs[4:]
    piece = piece_rows * width
    loads = [pltpu.make_async_copy(s_in, panel.at[pl.ds(0, piece)], s_sem.at[0])]
    for d in range(1, rows):
        loads += [
            pltpu.make_async_copy(
                s_other[d - 1].at[pl.ds(q * order, order)],
                panel.at[d * piece + q],
                s_sem.at[d * piece + q],
            )
            for q in range(piece)
        ]
    reads = [
        read_notes(s_other[d], piece * order, piece, whole.at[d], notes.at[d], note_sem.at[d])
        for d in range(rows - 1)
    ]
    for load in loads:
        load.start()
    totals[...] = jnp.zeros_like(totals)
    here = quotient(index[0][0], local_rows)
    layer = remainder(quotient(index[0][count], piece_rows), layers)
    own_rows = local_rows // layers
    for g in range(layers):
        base = remainder(layer + g, layers) * own_rows
        for i in range(own_rows):
            for t in range(kept):
                kept_cols[(g * own_rows + i) * kept + t] = c_cols[base + i, t]
    for read in reads:
        read.wait()
    for q in range(piece):
        panel_cols[q] = s_cols[q // width, q % width]
        for d in range(1, rows):
            panel_cols[d * piece + q] = note(notes.at[d - 1], piece, q)
    for j in range(cols):
        list_pairs(
            (rows, layers, count, piece_rows, width, local_rows, kept),
            index[j],
            here,
            layer,
            panel_cols,
            kept_cols,
            pairs,
            tally,
            j,
        )
    for load in loads:
        load.wait()
    add_products(lambda n: x_in[n], panel, totals, pairs, tally, 0)


def peer_kernel(sizes, first, pairs, tally, *refs):
    cols, layers, slots, height = sizes
    x_in, refs = refs[: cols - 1], refs[cols - 1 :]
    panel, before, own, sent, totals = refs[0], refs[1], refs[2], refs[3 : 2 + layers], refs[-1]
    totals[...] = before[:, first : first + height]
    for j in range(1, cols):
        add_products(lambda n: x_in[j - 1][n], panel, totals, pairs, tally, j)

    own[...] = totals[:slots]
    half = height // 2
    for d in range(1, layers):
        code = sent[d - 1]
        code[slots * half :] = jnp.zeros((code.shape[0] - slots * half, code.shape[1]), jnp.int32)
        for u in range(slots):
            value = totals[d * slots + u]
            peak = jnp.max(jnp.abs(value), axis=0, keepdims=True)
            power = jnp.floor(jnp.log2(jnp.maximum(peak, 1e-30)) + 1e-3) + 1.0
            whole = jnp.floor(value * jnp.exp2(15.0 - power) + 0.5).astype(jnp.int32)
            code[pl.ds(u * half, half)] = (whole[:half] << 16) | (whole[half:] & 0xFFFF)
            code[pl.ds(slots * half + u, 1)] = power.astype(jnp.int32)


def finish_kernel(sizes, *refs):
    layers, chunks, slots, height = sizes
    result = refs[-1]
    kept = result.shape[1]
    half = height // 2
    for c in range(chunks):
        own, codes = refs[c * layers], refs[c * layers + 1 : (c + 1) * layers]
        for u in range(slots):
            high, low = own[u, :half], own[u, half:]
            for code in codes:
                word = code[pl.ds(u * half, half)]
                power = code[pl.ds(slots * half + u, 1)].astype(jnp.float32)
                scale = jnp.exp2(power - 15.0)
                high += (word >> 16).astype(jnp.float32) * scale
                low += ((word << 16) >> 16).astype(jnp.float32) * scale
            at = c * height
            result[u // kept, u % kept, at : at + half] = high.astype(jnp.bfloat16)
            result[u // kept, u % kept, at + half : at + height] = low.astype(jnp.bfloat16)


def per_device(a_blocks, a_rows, a_cols, s_blocks, s_cols, c_cols):
    rows, cols, layers = (lax.axis_size(axis) for axis in ("row", "col", "layer"))
    count, order = a_blocks.shape[:2]
    piece_rows, width = s_cols.shape
    local_rows, kept = c_cols.shape
    own_rows = local_rows // layers
    slots = own_rows * kept
    all_slots = layers * slots
    height = order // CHUNKS
    piece = piece_rows * width
    panel_size = rows * piece
    block_size = order * order
    flat_s = s_blocks.reshape(piece, order, order)
    note_height, _ = note_rows(piece)

    scalars = pl.BlockSpec(memory_space=pltpu.SMEM)
    anywhere = pl.BlockSpec(memory_space=pl.ANY)
    vector = pl.BlockSpec(memory_space=pltpu.VMEM)

    def x_chunk(blocks, c):
        part = lax.slice_in_dim(blocks, c * height, (c + 1) * height, axis=1)
        return [shifted(part, "col", j) for j in range(1, cols)]

    x_pieces = [x_chunk(a_blocks, 0)]
    index, s_sent = pl.pallas_call(
        functools.partial(pack_kernel, (count, order, piece_rows, width)),
        out_shape=[
            jax.ShapeDtypeStruct((2 * count,), jnp.int32),
            jax.ShapeDtypeStruct((piece * order + note_height, order), jnp.bfloat16),
        ],
        in_specs=[scalars] * 3 + [anywhere],
        out_specs=[scalars, vector],
        scratch_shapes=[pltpu.SemaphoreType.DMA((piece,))],
        name="pack",
    )(a_rows, a_cols, s_cols, flat_s)
    indices = [index] + [shifted(index, "col", j) for j in range(1, cols)]
    s_pieces = [shifted(s_sent, "row", d) for d in range(1, rows)]
    later_blocks, _, s_pieces = lax.optimization_barrier((a_blocks, indices, s_pieces))
    x_pieces += [x_chunk(later_blocks, c) for c in range(1, CHUNKS)]

    moved = block_size * (4 * all_slots + 4 * panel_size + 2 * count)
    totals, panel, *plan = pl.pallas_call(
        functools.partial(
            own_kernel, (rows, cols, layers, count, piece_rows, width, local_rows, kept, order)
        ),
        out_shape=[
            jax.ShapeDtypeStruct((all_slots + 1, order, order), jnp.float32),
            jax.ShapeDtypeStruct((panel_size, order, order), jnp.bfloat16),
            jax.ShapeDtypeStruct((cols, 3, count * width + GROUP), jnp.int32),
            jax.ShapeDtypeStruct((cols,), jnp.int32),
        ],
        in_specs=[scalars] * (cols + 2) + [vector] * (1 + rows),
        out_specs=[vector] * 2 + [scalars] * 2,
        scratch_shapes=[
            pltpu.SMEM((panel_size,), jnp.int32),
            pltpu.SMEM((all_slots,), jnp.int32),
            pltpu.VMEM((rows - 1, note_height, LANES), jnp.int32),
            pltpu.SMEM((rows - 1, note_height, LANES), jnp.int32),
            pltpu.SemaphoreType.DMA((panel_size,)),
            pltpu.SemaphoreType.DMA((rows - 1,)),
        ],
        compiler_params=pltpu.CompilerParams(vmem_limit_bytes=moved + 4 * MIB),
        cost_estimate=pl.CostEstimate(
            flops=2 * order**3 * count * width // 4, bytes_accessed=moved, transcendentals=0
        ),
        name="own_products",
    )(*indices, s_cols, c_cols, a_blocks, flat_s, *s_pieces)

    code_rows = slots * (height // 2) + (slots + 7) // 8 * 8
    moved = block_size * (8 * all_slots + 2 * panel_size + 2 * count * (cols - 1))
    parts = []
    for c in range(CHUNKS):
        out_shape = [jax.ShapeDtypeStruct((slots, height, order), jnp.float32)]
        out_shape += [jax.ShapeDtypeStruct((code_rows, order), jnp.int32)] * (layers - 1)
        parts.append(
            pl.pallas_call(
                functools.partial(peer_kernel, (cols, layers, slots, height), c * height),
                out_shape=out_shape,
                in_specs=[scalars] * 2 + [vector] * (cols + 1),
                out_specs=[vector] * layers,
                scratch_shapes=[pltpu.VMEM((all_slots + 1, height, order), jnp.float32)],
                compiler_params=pltpu.CompilerParams(vmem_limit_bytes=moved + 4 * MIB),
                cost_estimate=pl.CostEstimate(
                    flops=2 * order**2 * height * count * width // 4 * (cols - 1),
                    bytes_accessed=moved // CHUNKS,
                    transcendentals=0,
                ),
                name=f"peer_products_{c}",
            )(*plan, *x_pieces[c], panel, totals)
        )

    final = []
    for part in parts:
        final.append(part[0])
        final += [shifted(part[d], "layer", layers - d) for d in range(1, layers)]
    return pl.pallas_call(
        functools.partial(finish_kernel, (layers, CHUNKS, slots, height)),
        out_shape=jax.ShapeDtypeStruct((own_rows, kept, order, order), jnp.bfloat16),
        in_specs=[vector] * len(final),
        out_specs=vector,
        compiler_params=pltpu.CompilerParams(
            vmem_limit_bytes=16 * slots * order * order + 4 * MIB
        ),
        name="finish",
    )(*final)


def solution(mesh):
    placed = (
        P(("row", "col", "layer"), None, None),
        P(("row", "col", "layer")),
        P(("row", "col", "layer")),
        P(("row", "layer"), "col", None, None),
        P(("row", "layer"), "col"),
        P("row", "col"),
    )
    return jax.shard_map(
        per_device,
        mesh=mesh,
        in_specs=placed,
        out_specs=P(("row", "layer"), "col", None, None),
        check_vma=False,
    )
```

```python
import functools

import jax
import jax.numpy as jnp
from jax import lax
from jax.experimental import pallas as pl
from jax.experimental.pallas import tpu as pltpu
from jax.sharding import PartitionSpec as P

CHUNKS = 2
GROUP = 4
LANES = 128
MIB = 2**20


def shifted(value, axis, offset):
    size = lax.axis_size(axis)
    return lax.ppermute(value, axis, [((i + offset) % size, i) for i in range(size)])


def quotient(value, by):
    return value >> (by.bit_length() - 1) if by & (by - 1) == 0 else lax.div(value, by)


def remainder(value, by):
    return value & (by - 1) if by & (by - 1) == 0 else lax.rem(value, by)


def note_rows(how_many):
    digits = (how_many + LANES - 1) // LANES
    return (2 * digits + 15) // 16 * 16, digits


def with_notes(payload, values):
    (how_many,) = values.shape
    height, digits = note_rows(how_many)
    values = jnp.pad(values, (0, digits * LANES - how_many)).reshape(digits, LANES)
    tile = jnp.concatenate([values & (LANES - 1), values >> (LANES.bit_length() - 1)])
    tile = jnp.pad(tile, ((0, height - 2 * digits), (0, 0)))
    return jnp.concatenate([payload, tile.astype(payload.dtype)])


def read_notes(payload, start, how_many, whole, notes, sem):
    height, _ = note_rows(how_many)
    whole[...] = payload[start : start + height].astype(jnp.float32).astype(jnp.int32)
    copy = pltpu.make_async_copy(whole, notes, sem)
    copy.start()
    return copy


def note(notes, how_many, p):
    _, digits = note_rows(how_many)
    return notes[p // LANES, p % LANES] + notes[digits + p // LANES, p % LANES] * LANES


def list_pairs(sizes, row_of, col_of, context, panel_cols, kept_cols, pairs, tally, j):
    rows, layers, count, piece_rows, width, local_rows, kept = sizes
    own_rows = local_rows // layers
    here, layer = context[0], context[1]

    def one_block(n, total):
        row = row_of(n) - here * local_rows
        inner = col_of(n)
        owner = quotient(inner, piece_rows * layers)
        inner = remainder(inner, piece_rows)
        right = (remainder(owner - here + rows, rows) * piece_rows + inner) * width
        goal = remainder(quotient(row, own_rows) - layer + layers, layers)
        goal = (goal * own_rows + remainder(row, own_rows)) * kept
        for s in range(width):
            wanted = panel_cols[right + s]
            hit, slot = jnp.int32(0), goal
            for t in range(kept):
                same = (kept_cols[goal + t] == wanted).astype(jnp.int32)
                hit += same
                slot += t * same
            pairs[j, 0, total] = n
            pairs[j, 1, total] = right + s
            pairs[j, 2, total] = slot
            total += hit
        return total

    total = lax.fori_loop(0, count, one_block, jnp.int32(0))
    for g in range(GROUP):
        pairs[j, 0, total + g] = 0
        pairs[j, 1, total + g] = 0
        pairs[j, 2, total + g] = local_rows * kept
    tally[j] = total


def add_products(left, panel, totals, pairs, tally, j):
    def one_group(group, carry):
        base = group * GROUP
        products = [
            jnp.dot(
                left(pairs[j, 0, base + g]),
                panel[pairs[j, 1, base + g]],
                preferred_element_type=jnp.float32,
            )
            for g in range(GROUP)
        ]
        for g in range(GROUP):
            totals[pairs[j, 2, base + g]] += products[g]
        return carry

    lax.fori_loop(0, quotient(tally[j] + GROUP - 1, GROUP), one_group, 0)


def own_kernel(sizes, *refs):
    rows, layers, count, piece_rows, width, local_rows, kept, order = sizes
    a_rows, a_cols, s_cols, c_cols, x_in, s_in = refs[:6]
    s_other, refs = refs[6 : 5 + rows], refs[5 + rows :]
    totals, panel, panel_cols, kept_cols, context = refs[:5]
    pairs, tally, whole, notes, s_sem, note_sem = refs[5:]
    piece = piece_rows * width
    loads = [pltpu.make_async_copy(s_in, panel.at[pl.ds(0, piece)], s_sem.at[0])]
    for d in range(1, rows):
        loads += [
            pltpu.make_async_copy(
                s_other[d - 1].at[pl.ds(q * order, order)],
                panel.at[d * piece + q],
                s_sem.at[d * piece + q],
            )
            for q in range(piece)
        ]
    reads = [
        read_notes(s_other[d], piece * order, piece, whole.at[d], notes.at[d], note_sem.at[d])
        for d in range(rows - 1)
    ]
    for load in loads:
        load.start()
    totals[...] = jnp.zeros_like(totals)
    layer = remainder(quotient(a_cols[0], piece_rows), layers)
    context[0] = quotient(a_rows[0], local_rows)
    context[1] = layer
    own_rows = local_rows // layers
    for g in range(layers):
        base = remainder(layer + g, layers) * own_rows
        for i in range(own_rows):
            for t in range(kept):
                kept_cols[(g * own_rows + i) * kept + t] = c_cols[base + i, t]
    for read in reads:
        read.wait()
    for q in range(piece):
        panel_cols[q] = s_cols[q // width, q % width]
        for d in range(1, rows):
            panel_cols[d * piece + q] = note(notes.at[d - 1], piece, q)
    list_pairs(
        (rows, layers, count, piece_rows, width, local_rows, kept),
        lambda n: a_rows[n],
        lambda n: a_cols[n],
        context,
        panel_cols,
        kept_cols,
        pairs,
        tally,
        0,
    )
    for load in loads:
        load.wait()
    add_products(lambda n: x_in[n], panel, totals, pairs, tally, 0)


def peer_kernel(sizes, first, context, *refs):
    rows, cols, layers, count, piece_rows, width, local_rows, kept, height = sizes
    slots = local_rows * kept // layers
    if first == 0:
        panel_cols, kept_cols, *refs = refs
    else:
        pairs, tally, *refs = refs
    x_in, refs = refs[: cols - 1], refs[cols - 1 :]
    panel, before, own, sent, *refs = refs
    if first == 0:
        pairs, tally, totals, whole, notes, note_sem = refs
        reads = [
            read_notes(x_in[j], count * height, 2 * count, whole.at[j], notes.at[j], note_sem.at[j])
            for j in range(cols - 1)
        ]
    else:
        (totals,) = refs
    totals[...] = before[:, first : first + height]
    if first == 0:
        for j in range(cols - 1):
            reads[j].wait()
            list_pairs(
                (rows, layers, count, piece_rows, width, local_rows, kept),
                lambda n: note(notes.at[j], 2 * count, n),
                lambda n: note(notes.at[j], 2 * count, count + n),
                context,
                panel_cols,
                kept_cols,
                pairs,
                tally,
                j,
            )

    for j in range(cols - 1):

        def left(n):
            return x_in[j][pl.ds(pl.multiple_of(n * height, height), height)]

        add_products(left, panel, totals, pairs, tally, j)

    own[...] = totals[:slots]
    half = height // 2
    for d in range(1, layers):
        code = sent.at[remainder(context[1] + d, layers)]
        spare = code.shape[0] - slots * half
        code[slots * half :] = jnp.zeros((spare, code.shape[1]), jnp.int32)
        for u in range(slots):
            value = totals[d * slots + u]
            peak = jnp.max(jnp.abs(value), axis=0, keepdims=True)
            power = jnp.floor(jnp.log2(jnp.maximum(peak, 1e-30)) + 1e-3) + 1.0
            word = jnp.floor(value * jnp.exp2(15.0 - power) + 0.5).astype(jnp.int32)
            code[pl.ds(u * half, half)] = (word[:half] << 16) | (word[half:] & 0xFFFF)
            code[pl.ds(slots * half + u, 1)] = power.astype(jnp.int32)


def finish_kernel(sizes, context, *refs):
    layers, chunks, slots, height = sizes
    result = refs[-1]
    kept = result.shape[1]
    half = height // 2
    for c in range(chunks):
        own, codes = refs[2 * c], refs[2 * c + 1]
        for u in range(slots):
            high, low = own[u, :half], own[u, half:]
            for d in range(1, layers):
                code = codes.at[remainder(context[1] + d, layers)]
                word = code[pl.ds(u * half, half)]
                power = code[pl.ds(slots * half + u, 1)].astype(jnp.float32)
                scale = jnp.exp2(power - 15.0)
                high += (word >> 16).astype(jnp.float32) * scale
                low += ((word << 16) >> 16).astype(jnp.float32) * scale
            at = c * height
            result[u // kept, u % kept, at : at + half] = high.astype(jnp.bfloat16)
            result[u // kept, u % kept, at + half : at + height] = low.astype(jnp.bfloat16)


def per_device(a_blocks, a_rows, a_cols, s_blocks, s_cols, c_cols):
    rows, cols, layers = (lax.axis_size(axis) for axis in ("row", "col", "layer"))
    count, order = a_blocks.shape[:2]
    piece_rows, width = s_cols.shape
    local_rows, kept = c_cols.shape
    own_rows = local_rows // layers
    slots = own_rows * kept
    all_slots = layers * slots
    height = order // CHUNKS
    piece = piece_rows * width
    panel_size = rows * piece
    block_size = order * order
    flat_s = s_blocks.reshape(piece, order, order)
    x_note_rows, _ = note_rows(2 * count)
    s_note_rows, _ = note_rows(piece)

    scalars = pl.BlockSpec(memory_space=pltpu.SMEM)
    vector = pl.BlockSpec(memory_space=pltpu.VMEM)

    def x_chunk(blocks, c):
        part = lax.slice_in_dim(blocks, c * height, (c + 1) * height, axis=1)
        return part.reshape(count * height, order)

    x_first = with_notes(x_chunk(a_blocks, 0), jnp.concatenate([a_rows, a_cols]))
    x_pieces = [[shifted(x_first, "col", j) for j in range(1, cols)]]
    s_sent = with_notes(flat_s.reshape(piece * order, order), s_cols.reshape(-1))
    s_pieces = [shifted(s_sent, "row", d) for d in range(1, rows)]
    later_blocks, _ = lax.optimization_barrier((a_blocks, x_first))
    for c in range(1, CHUNKS):
        part = x_chunk(later_blocks, c)
        x_pieces.append([shifted(part, "col", j) for j in range(1, cols)])

    moved = block_size * (4 * all_slots + 4 * panel_size + 2 * count)
    totals, panel, panel_cols, kept_cols, context = pl.pallas_call(
        functools.partial(
            own_kernel, (rows, layers, count, piece_rows, width, local_rows, kept, order)
        ),
        out_shape=[
            jax.ShapeDtypeStruct((all_slots + 1, order, order), jnp.float32),
            jax.ShapeDtypeStruct((panel_size, order, order), jnp.bfloat16),
            jax.ShapeDtypeStruct((panel_size,), jnp.int32),
            jax.ShapeDtypeStruct((all_slots,), jnp.int32),
            jax.ShapeDtypeStruct((2,), jnp.int32),
        ],
        in_specs=[scalars] * 4 + [vector] * (1 + rows),
        out_specs=[vector] * 2 + [scalars] * 3,
        scratch_shapes=[
            pltpu.SMEM((1, 3, count * width + GROUP), jnp.int32),
            pltpu.SMEM((1,), jnp.int32),
            pltpu.VMEM((rows - 1, s_note_rows, LANES), jnp.int32),
            pltpu.SMEM((rows - 1, s_note_rows, LANES), jnp.int32),
            pltpu.SemaphoreType.DMA((panel_size,)),
            pltpu.SemaphoreType.DMA((rows - 1,)),
        ],
        compiler_params=pltpu.CompilerParams(vmem_limit_bytes=moved + 4 * MIB),
        cost_estimate=pl.CostEstimate(
            flops=2 * order**3 * count * width // 4, bytes_accessed=moved, transcendentals=0
        ),
        name="own_products",
    )(a_rows, a_cols, s_cols, c_cols, a_blocks, flat_s, *s_pieces)

    code_rows = slots * (height // 2) + (slots + 7) // 8 * 8
    moved = block_size * (8 * all_slots + 2 * panel_size + 2 * count * (cols - 1))
    pair_shapes = [(cols - 1, 3, count * width + GROUP), (cols - 1,)]
    final, plan = [], []
    for c in range(CHUNKS):
        out_shape = [
            jax.ShapeDtypeStruct((slots, height, order), jnp.float32),
            jax.ShapeDtypeStruct((layers, code_rows, order), jnp.int32),
        ]
        out_specs = [vector] * 2
        scratch = [pltpu.VMEM((all_slots + 1, height, order), jnp.float32)]
        if c == 0:
            out_shape += [jax.ShapeDtypeStruct(shape, jnp.int32) for shape in pair_shapes]
            out_specs += [scalars] * 2
            scratch += [
                pltpu.VMEM((cols - 1, x_note_rows, LANES), jnp.int32),
                pltpu.SMEM((cols - 1, x_note_rows, LANES), jnp.int32),
                pltpu.SemaphoreType.DMA((cols - 1,)),
            ]
        own, sent, *made = pl.pallas_call(
            functools.partial(
                peer_kernel,
                (rows, cols, layers, count, piece_rows, width, local_rows, kept, height),
                c * height,
            ),
            out_shape=out_shape,
            in_specs=[scalars] * 3 + [vector] * (cols + 1),
            out_specs=out_specs,
            scratch_shapes=scratch,
            compiler_params=pltpu.CompilerParams(vmem_limit_bytes=moved + 4 * MIB),
            cost_estimate=pl.CostEstimate(
                flops=2 * order**2 * height * count * width // 4 * (cols - 1),
                bytes_accessed=moved // CHUNKS,
                transcendentals=0,
            ),
            name=f"peer_products_{c}",
        )(context, *(plan or (panel_cols, kept_cols)), *x_pieces[c], panel, totals)
        plan = plan or made
        final += [own, lax.all_to_all(sent, "layer", 0, 0, tiled=True)]

    return pl.pallas_call(
        functools.partial(finish_kernel, (layers, CHUNKS, slots, height)),
        out_shape=jax.ShapeDtypeStruct((own_rows, kept, order, order), jnp.bfloat16),
        in_specs=[scalars] + [vector] * len(final),
        out_specs=vector,
        compiler_params=pltpu.CompilerParams(
            vmem_limit_bytes=16 * slots * order * order + 4 * MIB
        ),
        name="finish",
    )(context, *final)


def solution(mesh):
    placed = (
        P(("row", "col", "layer"), None, None),
        P(("row", "col", "layer")),
        P(("row", "col", "layer")),
        P(("row", "layer"), "col", None, None),
        P(("row", "layer"), "col"),
        P("row", "col"),
    )
    return jax.shard_map(
        per_device,
        mesh=mesh,
        in_specs=placed,
        out_specs=P(("row", "layer"), "col", None, None),
        check_vma=False,
    )
```

```python
import functools

import jax
import jax.numpy as jnp
from jax import lax
from jax.experimental import pallas as pl
from jax.experimental.pallas import tpu as pltpu
from jax.sharding import PartitionSpec as P

CHUNKS = 2
GROUP = 4
LANES = 128
MIB = 2**20


def flipped(value, axis, bits):
    return lax.ppermute(value, axis, [(i, i ^ bits) for i in range(lax.axis_size(axis))])


def gathered(value, axis):
    values = {0: value}
    bit = lax.axis_size(axis) // 2
    while bit:
        values |= {d ^ bit: flipped(held, axis, bit) for d, held in values.items()}
        bit //= 2
    return [values[d] for d in range(len(values))]


def shifted(value, axis, offset):
    size = lax.axis_size(axis)
    return lax.ppermute(value, axis, [((i + offset) % size, i) for i in range(size)])


def quotient(value, by):
    return value >> (by.bit_length() - 1) if by & (by - 1) == 0 else lax.div(value, by)


def remainder(value, by):
    return value & (by - 1) if by & (by - 1) == 0 else lax.rem(value, by)


def note_rows(how_many):
    digits = (how_many + LANES - 1) // LANES
    return (2 * digits + 15) // 16 * 16, digits


def with_notes(payload, values):
    (how_many,) = values.shape
    height, digits = note_rows(how_many)
    values = jnp.pad(values, (0, digits * LANES - how_many)).reshape(digits, LANES)
    tile = jnp.concatenate([values & (LANES - 1), values >> (LANES.bit_length() - 1)])
    tile = jnp.pad(tile, ((0, height - 2 * digits), (0, 0)))
    return jnp.concatenate([payload, tile.astype(payload.dtype)])


def read_notes(payload, start, how_many, whole, notes, sem):
    height, _ = note_rows(how_many)
    whole[...] = payload[start : start + height].astype(jnp.float32).astype(jnp.int32)
    copy = pltpu.make_async_copy(whole, notes, sem)
    copy.start()
    return copy


def note(notes, how_many, p):
    _, digits = note_rows(how_many)
    return notes[p // LANES, p % LANES] + notes[digits + p // LANES, p % LANES] * LANES


def list_pairs(sizes, a_rows, a_cols, context, panel_cols, kept_cols, pairs, tally, j):
    rows, layers, count, piece_rows, width, local_rows, kept = sizes
    own_rows = local_rows // layers
    here, layer = context[0], context[1]

    def one_block(n, total):
        row = a_rows[n] - here * local_rows
        inner = a_cols[n]
        owner = quotient(inner, piece_rows * layers)
        inner = remainder(inner, piece_rows)
        right = ((owner ^ here) * piece_rows + inner) * width
        goal = remainder(quotient(row, own_rows) - layer + layers, layers)
        goal = (goal * own_rows + remainder(row, own_rows)) * kept
        for s in range(width):
            wanted = panel_cols[right + s]
            hit, slot = jnp.int32(0), goal
            for t in range(kept):
                same = (kept_cols[goal + t] == wanted).astype(jnp.int32)
                hit += same
                slot += t * same
            pairs[j, 0, total] = n
            pairs[j, 1, total] = right + s
            pairs[j, 2, total] = slot
            total += hit
        return total

    total = lax.fori_loop(0, count, one_block, jnp.int32(0))
    for g in range(GROUP):
        pairs[j, 0, total + g] = 0
        pairs[j, 1, total + g] = 0
        pairs[j, 2, total + g] = local_rows * kept
    tally[j] = total


def add_products(left, panel, totals, pairs, tally, j):
    def one_group(group, carry):
        base = group * GROUP
        products = [
            jnp.dot(
                left(pairs[j, 0, base + g]),
                panel[pairs[j, 1, base + g]],
                preferred_element_type=jnp.float32,
            )
            for g in range(GROUP)
        ]
        for g in range(GROUP):
            totals[pairs[j, 2, base + g]] += products[g]
        return carry

    lax.fori_loop(0, quotient(tally[j] + GROUP - 1, GROUP), one_group, 0)


def own_kernel(sizes, *refs):
    rows, cols, layers, count, piece_rows, width, local_rows, kept, order = sizes
    a_rows, a_cols, refs = refs[:cols], refs[cols : 2 * cols], refs[2 * cols :]
    s_cols, c_cols, x_in, s_in = refs[:4]
    s_other, refs = refs[4 : 3 + rows], refs[3 + rows :]
    totals, panel, pairs, tally = refs[:4]
    panel_cols, kept_cols, context, whole, notes, s_sem, note_sem = refs[4:]
    piece = piece_rows * width
    loads = [pltpu.make_async_copy(s_in, panel.at[pl.ds(0, piece)], s_sem.at[0])]
    for d in range(1, rows):
        loads += [
            pltpu.make_async_copy(
                s_other[d - 1].at[pl.ds(q * order, order)],
                panel.at[d * piece + q],
                s_sem.at[d * piece + q],
            )
            for q in range(piece)
        ]
    reads = [
        read_notes(s_other[d], piece * order, piece, whole.at[d], notes.at[d], note_sem.at[d])
        for d in range(rows - 1)
    ]
    for load in loads:
        load.start()
    totals[...] = jnp.zeros_like(totals)
    layer = remainder(quotient(a_cols[0][0], piece_rows), layers)
    context[0] = quotient(a_rows[0][0], local_rows)
    context[1] = layer
    own_rows = local_rows // layers
    for g in range(layers):
        base = remainder(layer + g, layers) * own_rows
        for i in range(own_rows):
            for t in range(kept):
                kept_cols[(g * own_rows + i) * kept + t] = c_cols[base + i, t]
    for read in reads:
        read.wait()
    for q in range(piece):
        panel_cols[q] = s_cols[q // width, q % width]
        for d in range(1, rows):
            panel_cols[d * piece + q] = note(notes.at[d - 1], piece, q)
    for j in range(cols):
        list_pairs(
            (rows, layers, count, piece_rows, width, local_rows, kept),
            a_rows[j],
            a_cols[j],
            context,
            panel_cols,
            kept_cols,
            pairs,
            tally,
            j,
        )
    for load in loads:
        load.wait()
    add_products(lambda n: x_in[n], panel, totals, pairs, tally, 0)


def peer_kernel(sizes, first, pairs, tally, *refs):
    cols, layers, slots, height = sizes
    x_in, refs = refs[: cols - 1], refs[cols - 1 :]
    panel, before, own, sent, totals = refs[0], refs[1], refs[2], refs[3 : 2 + layers], refs[-1]
    totals[...] = before[:, first : first + height]
    for j in range(1, cols):
        add_products(lambda n: x_in[j - 1][n], panel, totals, pairs, tally, j)

    own[...] = totals[:slots]
    half = height // 2
    for d in range(1, layers):
        code = sent[d - 1]
        spare = code.shape[0] - slots * half
        code[slots * half :] = jnp.zeros((spare, code.shape[1]), jnp.int32)
        for u in range(slots):
            value = totals[d * slots + u]
            peak = jnp.max(jnp.abs(value), axis=0, keepdims=True)
            power = jnp.floor(jnp.log2(jnp.maximum(peak, 1e-30)) + 1e-3) + 1.0
            word = jnp.floor(value * jnp.exp2(15.0 - power) + 0.5).astype(jnp.int32)
            code[pl.ds(u * half, half)] = (word[:half] << 16) | (word[half:] & 0xFFFF)
            code[pl.ds(slots * half + u, 1)] = power.astype(jnp.int32)


def finish_kernel(sizes, *refs):
    layers, chunks, slots, height = sizes
    result = refs[-1]
    kept = result.shape[1]
    half = height // 2
    for c in range(chunks):
        own, codes = refs[c * layers], refs[c * layers + 1 : (c + 1) * layers]
        for u in range(slots):
            high, low = own[u, :half], own[u, half:]
            for code in codes:
                word = code[pl.ds(u * half, half)]
                power = code[pl.ds(slots * half + u, 1)].astype(jnp.float32)
                scale = jnp.exp2(power - 15.0)
                high += (word >> 16).astype(jnp.float32) * scale
                low += ((word << 16) >> 16).astype(jnp.float32) * scale
            at = c * height
            result[u // kept, u % kept, at : at + half] = high.astype(jnp.bfloat16)
            result[u // kept, u % kept, at + half : at + height] = low.astype(jnp.bfloat16)


def per_device(a_blocks, a_rows, a_cols, s_blocks, s_cols, c_cols):
    rows, cols, layers = (lax.axis_size(axis) for axis in ("row", "col", "layer"))
    count, order = a_blocks.shape[:2]
    piece_rows, width = s_cols.shape
    local_rows, kept = c_cols.shape
    own_rows = local_rows // layers
    slots = own_rows * kept
    all_slots = layers * slots
    height = order // CHUNKS
    piece = piece_rows * width
    panel_size = rows * piece
    block_size = order * order
    flat_s = s_blocks.reshape(piece, order, order)
    note_height, _ = note_rows(piece)

    scalars = pl.BlockSpec(memory_space=pltpu.SMEM)
    vector = pl.BlockSpec(memory_space=pltpu.VMEM)

    def x_chunk(blocks, c):
        return lax.slice_in_dim(blocks, c * height, (c + 1) * height, axis=1)

    row_pieces = [a_rows] + [shifted(a_rows, "col", j) for j in range(1, cols)]
    col_pieces = [a_cols] + [shifted(a_cols, "col", j) for j in range(1, cols)]
    x_first, row_pieces, col_pieces = lax.optimization_barrier(
        (x_chunk(a_blocks, 0), row_pieces, col_pieces)
    )
    x_pieces = [[shifted(x_first, "col", j) for j in range(1, cols)]]
    s_sent = with_notes(flat_s.reshape(piece * order, order), s_cols.reshape(-1))
    s_pieces = gathered(s_sent, "row")[1:]
    for c in range(1, CHUNKS):
        part = x_chunk(a_blocks, c)
        x_pieces.append([shifted(part, "col", j) for j in range(1, cols)])

    moved = block_size * (4 * all_slots + 4 * panel_size + 2 * count)
    totals, panel, *plan = pl.pallas_call(
        functools.partial(
            own_kernel, (rows, cols, layers, count, piece_rows, width, local_rows, kept, order)
        ),
        out_shape=[
            jax.ShapeDtypeStruct((all_slots + 1, order, order), jnp.float32),
            jax.ShapeDtypeStruct((panel_size, order, order), jnp.bfloat16),
            jax.ShapeDtypeStruct((cols, 3, count * width + GROUP), jnp.int32),
            jax.ShapeDtypeStruct((cols,), jnp.int32),
        ],
        in_specs=[scalars] * (2 * cols + 2) + [vector] * (1 + rows),
        out_specs=[vector] * 2 + [scalars] * 2,
        scratch_shapes=[
            pltpu.SMEM((panel_size,), jnp.int32),
            pltpu.SMEM((all_slots,), jnp.int32),
            pltpu.SMEM((2,), jnp.int32),
            pltpu.VMEM((rows - 1, note_height, LANES), jnp.int32),
            pltpu.SMEM((rows - 1, note_height, LANES), jnp.int32),
            pltpu.SemaphoreType.DMA((panel_size,)),
            pltpu.SemaphoreType.DMA((rows - 1,)),
        ],
        compiler_params=pltpu.CompilerParams(vmem_limit_bytes=moved + 4 * MIB),
        cost_estimate=pl.CostEstimate(
            flops=2 * order**3 * count * width // 4, bytes_accessed=moved, transcendentals=0
        ),
        name="own_products",
    )(*row_pieces, *col_pieces, s_cols, c_cols, a_blocks, flat_s, *s_pieces)

    code_rows = slots * (height // 2) + (slots + 7) // 8 * 8
    moved = block_size * (8 * all_slots + 2 * panel_size + 2 * count * (cols - 1))
    final = []
    for c in range(CHUNKS):
        out_shape = [jax.ShapeDtypeStruct((slots, height, order), jnp.float32)]
        out_shape += [jax.ShapeDtypeStruct((code_rows, order), jnp.int32)] * (layers - 1)
        own, *sent = pl.pallas_call(
            functools.partial(peer_kernel, (cols, layers, slots, height), c * height),
            out_shape=out_shape,
            in_specs=[scalars] * 2 + [vector] * (cols + 1),
            out_specs=[vector] * layers,
            scratch_shapes=[pltpu.VMEM((all_slots + 1, height, order), jnp.float32)],
            compiler_params=pltpu.CompilerParams(vmem_limit_bytes=moved + 4 * MIB),
            cost_estimate=pl.CostEstimate(
                flops=2 * order**2 * height * count * width // 4 * (cols - 1),
                bytes_accessed=moved // CHUNKS,
                transcendentals=0,
            ),
            name=f"peer_products_{c}",
        )(*plan, *x_pieces[c], panel, totals)
        final.append(own)
        final += [shifted(sent[d - 1], "layer", layers - d) for d in range(1, layers)]

    return pl.pallas_call(
        functools.partial(finish_kernel, (layers, CHUNKS, slots, height)),
        out_shape=jax.ShapeDtypeStruct((own_rows, kept, order, order), jnp.bfloat16),
        in_specs=[vector] * len(final),
        out_specs=vector,
        compiler_params=pltpu.CompilerParams(
            vmem_limit_bytes=16 * slots * order * order + 4 * MIB
        ),
        name="finish",
    )(*final)


def solution(mesh):
    placed = (
        P(("row", "col", "layer"), None, None),
        P(("row", "col", "layer")),
        P(("row", "col", "layer")),
        P(("row", "layer"), "col", None, None),
        P(("row", "layer"), "col"),
        P("row", "col"),
    )
    return jax.shard_map(
        per_device,
        mesh=mesh,
        in_specs=placed,
        out_specs=P(("row", "layer"), "col", None, None),
        check_vma=False,
    )
```

```python
import functools

import jax
import jax.numpy as jnp
from jax import lax
from jax.experimental import pallas as pl
from jax.experimental.pallas import tpu as pltpu
from jax.sharding import PartitionSpec as P

CHUNKS = 2
GROUP = 4
LANES = 128
MIB = 2**20


def flipped(value, axis, bits):
    return lax.ppermute(value, axis, [(i, i ^ bits) for i in range(lax.axis_size(axis))])


def gathered(value, axis):
    values = {0: value}
    bit = lax.axis_size(axis) // 2
    while bit:
        values |= {d ^ bit: flipped(held, axis, bit) for d, held in values.items()}
        bit //= 2
    return [values[d] for d in range(len(values))]


def shifted(value, axis, offset):
    size = lax.axis_size(axis)
    return lax.ppermute(value, axis, [((i + offset) % size, i) for i in range(size)])


def quotient(value, by):
    return value >> (by.bit_length() - 1) if by & (by - 1) == 0 else lax.div(value, by)


def remainder(value, by):
    return value & (by - 1) if by & (by - 1) == 0 else lax.rem(value, by)


def note_rows(how_many):
    digits = (how_many + LANES - 1) // LANES
    return (2 * digits + 15) // 16 * 16, digits


def with_notes(payload, values):
    (how_many,) = values.shape
    height, digits = note_rows(how_many)
    values = jnp.pad(values, (0, digits * LANES - how_many)).reshape(digits, LANES)
    tile = jnp.concatenate([remainder(values, LANES), quotient(values, LANES)])
    tile = jnp.pad(tile, ((0, height - 2 * digits), (0, 0)))
    return jnp.concatenate([payload, tile.astype(payload.dtype)])


def read_notes(payload, start, how_many, whole, notes, sem):
    height, _ = note_rows(how_many)
    whole[...] = payload[start : start + height].astype(jnp.float32).astype(jnp.int32)
    copy = pltpu.make_async_copy(whole, notes, sem)
    copy.start()
    return copy


def note(notes, how_many, p):
    _, digits = note_rows(how_many)
    return notes[p // LANES, p % LANES] + notes[digits + p // LANES, p % LANES] * LANES


def positions(sizes, a_rows, a_cols, row_at, layer_at):
    layers, piece_rows, width, local_rows, kept = sizes
    own_rows = local_rows // layers
    owner = quotient(a_cols, piece_rows * layers)
    rights = ((owner ^ row_at) * piece_rows + remainder(a_cols, piece_rows)) * width
    local = a_rows - row_at * local_rows
    goals = remainder(quotient(local, own_rows) - layer_at + layers, layers) * own_rows
    return rights, (goals + remainder(local, own_rows)) * kept


def pack_kernel(sizes, a_rows, a_cols, x_in, x_out, tile, sem):
    count, height = sizes
    spot = x_out.at[pl.ds(0, count * height)].reshape(count, height, x_out.shape[1])
    load = pltpu.make_async_copy(x_in.at[:, pl.ds(0, height), :], spot, sem)
    load.start()
    tile[...] = jnp.zeros_like(tile)
    for p, value in enumerate((a_rows[...], a_cols[...])):
        tile[2 * p : 2 * p + 1, :count] = remainder(value, LANES)
        tile[2 * p + 1 : 2 * p + 2, :count] = quotient(value, LANES)
    x_out[count * height :] = tile[...].astype(jnp.float32).astype(jnp.bfloat16)
    load.wait()


def list_pairs(sizes, index, row, panel_cols, kept_cols, pairs, tally, j):
    count, width, kept, trash = sizes
    total = jnp.int32(0)
    for n in range(count):
        right, goal = index[row, n], index[row + 1, n]
        for s in range(width):
            wanted = panel_cols[right + s]
            hit, slot = jnp.int32(0), goal
            for t in range(kept):
                same = (kept_cols[goal + t] == wanted).astype(jnp.int32)
                hit += same
                slot += t * same
            pairs[j, 0, total] = n
            pairs[j, 1, total] = right + s
            pairs[j, 2, total] = slot
            total += hit
    for g in range(GROUP):
        pairs[j, 0, total + g] = 0
        pairs[j, 1, total + g] = 0
        pairs[j, 2, total + g] = trash
    tally[j] = total


def add_products(left, panel, totals, pairs, tally, j):
    def one_group(group, carry):
        base = group * GROUP
        products = [
            jnp.dot(
                left(pairs[j, 0, base + g]),
                panel[pairs[j, 1, base + g]],
                preferred_element_type=jnp.float32,
            )
            for g in range(GROUP)
        ]
        for g in range(GROUP):
            totals[pairs[j, 2, base + g]] += products[g]
        return carry

    lax.fori_loop(0, quotient(tally[j] + GROUP - 1, GROUP), one_group, 0)


def own_kernel(sizes, *refs):
    rows, layers, count, piece_rows, width, local_rows, kept, order = sizes
    place, index, s_cols, c_cols, x_in, s_in = refs[:6]
    s_other, refs = refs[6 : 5 + rows], refs[5 + rows :]
    totals, panel, panel_cols, kept_cols = refs[:4]
    pairs, tally, whole, notes, s_sem, note_sem = refs[4:]
    piece = piece_rows * width
    loads = [pltpu.make_async_copy(s_in, panel.at[pl.ds(0, piece)], s_sem.at[0])]
    for d in range(1, rows):
        loads += [
            pltpu.make_async_copy(
                s_other[d - 1].at[pl.ds(q * order, order)],
                panel.at[d * piece + q],
                s_sem.at[d * piece + q],
            )
            for q in range(piece)
        ]
    reads = [
        read_notes(s_other[d], piece * order, piece, whole.at[d], notes.at[d], note_sem.at[d])
        for d in range(rows - 1)
    ]
    for load in loads:
        load.start()
    totals[...] = jnp.zeros_like(totals)
    own_rows = local_rows // layers
    for g in range(layers):
        base = remainder(place[1] + g, layers) * own_rows
        for i in range(own_rows):
            for t in range(kept):
                kept_cols[(g * own_rows + i) * kept + t] = c_cols[base + i, t]
    for read in reads:
        read.wait()
    for q in range(piece):
        panel_cols[q] = s_cols[q // width, q % width]
        for d in range(1, rows):
            panel_cols[d * piece + q] = note(notes.at[d - 1], piece, q)
    sizes = (count, width, kept, local_rows * kept)
    list_pairs(sizes, index, 0, panel_cols, kept_cols, pairs, tally, 0)
    for load in loads:
        load.wait()
    add_products(lambda n: x_in[n], panel, totals, pairs, tally, 0)


def peer_kernel(sizes, first, *refs):
    cols, layers, count, piece_rows, width, local_rows, kept, height = sizes
    slots = local_rows * kept // layers
    if first == 0:
        place, panel_cols, kept_cols, *refs = refs
    else:
        pairs, tally, *refs = refs
    x_in, refs = refs[: cols - 1], refs[cols - 1 :]
    panel, before, own, sent, refs = refs[0], refs[1], refs[2], refs[3 : 2 + layers], refs[2 + layers :]
    if first == 0:
        pairs, tally, totals, whole, index, note_sem = refs
        copies = []
        for j in range(cols - 1):
            digits = x_in[j][pl.ds(count * height, 16)].astype(jnp.float32).astype(jnp.int32)
            rights, goals = positions(
                (layers, piece_rows, width, local_rows, kept),
                digits[0:1] + digits[1:2] * LANES,
                digits[2:3] + digits[3:4] * LANES,
                place[0],
                place[1],
            )
            whole[j, 0:1] = rights
            whole[j, 1:2] = goals
            copies.append(pltpu.make_async_copy(whole.at[j], index.at[j], note_sem.at[j]))
            copies[-1].start()
    else:
        (totals,) = refs
    totals[...] = before[:, first : first + height]
    if first == 0:
        for j in range(cols - 1):
            copies[j].wait()
            list_pairs(
                (count, width, kept, layers * slots),
                index.at[j],
                0,
                panel_cols,
                kept_cols,
                pairs,
                tally,
                j,
            )

    for j in range(cols - 1):

        def left(n):
            return x_in[j][pl.ds(pl.multiple_of(n * height, height), height)]

        add_products(left, panel, totals, pairs, tally, j)

    own[...] = totals[:slots]
    half = height // 2
    for d in range(1, layers):
        code = sent[d - 1]
        spare = code.shape[0] - slots * half
        code[slots * half :] = jnp.zeros((spare, code.shape[1]), jnp.int32)
        for u in range(slots):
            value = totals[d * slots + u]
            peak = jnp.max(jnp.abs(value), axis=0, keepdims=True)
            power = jnp.floor(jnp.log2(jnp.maximum(peak, 1e-30)) + 1e-3) + 1.0
            word = jnp.floor(value * jnp.exp2(15.0 - power) + 0.5).astype(jnp.int32)
            code[pl.ds(u * half, half)] = (word[:half] << 16) | (word[half:] & 0xFFFF)
            code[pl.ds(slots * half + u, 1)] = power.astype(jnp.int32)


def finish_kernel(sizes, *refs):
    layers, chunks, slots, height = sizes
    result = refs[-1]
    kept = result.shape[1]
    half = height // 2
    for c in range(chunks):
        own, codes = refs[c * layers], refs[c * layers + 1 : (c + 1) * layers]
        for u in range(slots):
            high, low = own[u, :half], own[u, half:]
            for code in codes:
                word = code[pl.ds(u * half, half)]
                power = code[pl.ds(slots * half + u, 1)].astype(jnp.float32)
                scale = jnp.exp2(power - 15.0)
                high += (word >> 16).astype(jnp.float32) * scale
                low += ((word << 16) >> 16).astype(jnp.float32) * scale
            at = c * height
            result[u // kept, u % kept, at : at + half] = high.astype(jnp.bfloat16)
            result[u // kept, u % kept, at + half : at + height] = low.astype(jnp.bfloat16)


def per_device(a_blocks, a_rows, a_cols, s_blocks, s_cols, c_cols):
    rows, cols, layers = (lax.axis_size(axis) for axis in ("row", "col", "layer"))
    count, order = a_blocks.shape[:2]
    piece_rows, width = s_cols.shape
    local_rows, kept = c_cols.shape
    own_rows = local_rows // layers
    slots = own_rows * kept
    all_slots = layers * slots
    height = order // CHUNKS
    piece = piece_rows * width
    panel_size = rows * piece
    block_size = order * order
    flat_s = s_blocks.reshape(piece, order, order)
    note_height, _ = note_rows(piece)

    scalars = pl.BlockSpec(memory_space=pltpu.SMEM)
    vector = pl.BlockSpec(memory_space=pltpu.VMEM)
    anywhere = pl.BlockSpec(memory_space=pl.ANY)

    x_first = pl.pallas_call(
        functools.partial(pack_kernel, (count, height)),
        out_shape=jax.ShapeDtypeStruct((count * height + 16, order), jnp.bfloat16),
        in_specs=[vector] * 2 + [anywhere],
        out_specs=vector,
        scratch_shapes=[pltpu.VMEM((16, LANES), jnp.int32), pltpu.SemaphoreType.DMA],
        name="pack",
    )(a_rows.reshape(1, count), a_cols.reshape(1, count), a_blocks)
    x_pieces = [[shifted(x_first, "col", j) for j in range(1, cols)]]
    s_sent = with_notes(flat_s.reshape(piece * order, order), s_cols.reshape(-1))
    s_pieces = gathered(s_sent, "row")[1:]
    later_blocks, later_rows, later_cols, _ = lax.optimization_barrier(
        (a_blocks, a_rows, a_cols, x_first)
    )
    for c in range(1, CHUNKS):
        part = lax.slice_in_dim(later_blocks, c * height, (c + 1) * height, axis=1)
        part = part.reshape(count * height, order)
        x_pieces.append([shifted(part, "col", j) for j in range(1, cols)])

    place = jnp.stack([lax.axis_index("row"), lax.axis_index("layer")])
    index = jnp.stack(
        positions(
            (layers, piece_rows, width, local_rows, kept),
            later_rows,
            later_cols,
            lax.axis_index("row"),
            lax.axis_index("layer"),
        )
    )
    moved = block_size * (4 * all_slots + 4 * panel_size + 2 * count)
    totals, panel, panel_cols, kept_cols = pl.pallas_call(
        functools.partial(
            own_kernel, (rows, layers, count, piece_rows, width, local_rows, kept, order)
        ),
        out_shape=[
            jax.ShapeDtypeStruct((all_slots + 1, order, order), jnp.float32),
            jax.ShapeDtypeStruct((panel_size, order, order), jnp.bfloat16),
            jax.ShapeDtypeStruct((panel_size,), jnp.int32),
            jax.ShapeDtypeStruct((all_slots,), jnp.int32),
        ],
        in_specs=[scalars] * 4 + [vector] * (1 + rows),
        out_specs=[vector] * 2 + [scalars] * 2,
        scratch_shapes=[
            pltpu.SMEM((1, 3, count * width + GROUP), jnp.int32),
            pltpu.SMEM((1,), jnp.int32),
            pltpu.VMEM((rows - 1, note_height, LANES), jnp.int32),
            pltpu.SMEM((rows - 1, note_height, LANES), jnp.int32),
            pltpu.SemaphoreType.DMA((panel_size,)),
            pltpu.SemaphoreType.DMA((rows - 1,)),
        ],
        compiler_params=pltpu.CompilerParams(vmem_limit_bytes=moved + 4 * MIB),
        cost_estimate=pl.CostEstimate(
            flops=2 * order**3 * count * width // 4, bytes_accessed=moved, transcendentals=0
        ),
        name="own_products",
    )(place, index, s_cols, c_cols, a_blocks, flat_s, *s_pieces)

    code_rows = slots * (height // 2) + (slots + 7) // 8 * 8
    moved = block_size * (8 * all_slots + 2 * panel_size + 2 * count * (cols - 1))
    pair_shapes = [(cols - 1, 3, count * width + GROUP), (cols - 1,)]
    final, plan = [], []
    for c in range(CHUNKS):
        out_shape = [jax.ShapeDtypeStruct((slots, height, order), jnp.float32)]
        out_shape += [jax.ShapeDtypeStruct((code_rows, order), jnp.int32)] * (layers - 1)
        out_specs = [vector] * layers
        scratch = [pltpu.VMEM((all_slots + 1, height, order), jnp.float32)]
        if c == 0:
            out_shape += [jax.ShapeDtypeStruct(shape, jnp.int32) for shape in pair_shapes]
            out_specs += [scalars] * 2
            scratch += [
                pltpu.VMEM((cols - 1, 2, LANES), jnp.int32),
                pltpu.SMEM((cols - 1, 2, LANES), jnp.int32),
                pltpu.SemaphoreType.DMA((cols - 1,)),
            ]
        given = plan or (place, panel_cols, kept_cols)
        out = pl.pallas_call(
            functools.partial(
                peer_kernel,
                (cols, layers, count, piece_rows, width, local_rows, kept, height),
                c * height,
            ),
            out_shape=out_shape,
            in_specs=[scalars] * len(given) + [vector] * (cols + 1),
            out_specs=out_specs,
            scratch_shapes=scratch,
            compiler_params=pltpu.CompilerParams(vmem_limit_bytes=moved + 4 * MIB),
            cost_estimate=pl.CostEstimate(
                flops=2 * order**2 * height * count * width // 4 * (cols - 1),
                bytes_accessed=moved // CHUNKS,
                transcendentals=0,
            ),
            name=f"peer_products_{c}",
        )(*given, *x_pieces[c], panel, totals)
        plan = plan or out[layers:]
        final.append(out[0])
        final += [shifted(out[d], "layer", layers - d) for d in range(1, layers)]

    return pl.pallas_call(
        functools.partial(finish_kernel, (layers, CHUNKS, slots, height)),
        out_shape=jax.ShapeDtypeStruct((own_rows, kept, order, order), jnp.bfloat16),
        in_specs=[vector] * len(final),
        out_specs=vector,
        compiler_params=pltpu.CompilerParams(
            vmem_limit_bytes=16 * slots * order * order + 4 * MIB
        ),
        name="finish",
    )(*final)


def solution(mesh):
    placed = (
        P(("row", "col", "layer"), None, None),
        P(("row", "col", "layer")),
        P(("row", "col", "layer")),
        P(("row", "layer"), "col", None, None),
        P(("row", "layer"), "col"),
        P("row", "col"),
    )
    return jax.shard_map(
        per_device,
        mesh=mesh,
        in_specs=placed,
        out_specs=P(("row", "layer"), "col", None, None),
        check_vma=False,
    )
```

```python
import functools

import jax
import jax.numpy as jnp
from jax import lax
from jax.experimental import pallas as pl
from jax.experimental.pallas import tpu as pltpu
from jax.sharding import PartitionSpec as P

CHUNKS = 2
GROUP = 4
LANES = 128
MIB = 2**20


def flipped(value, axis, bits):
    return lax.ppermute(value, axis, [(i, i ^ bits) for i in range(lax.axis_size(axis))])


def gathered(value, axis):
    values = {0: value}
    bit = lax.axis_size(axis) // 2
    while bit:
        values |= {d ^ bit: flipped(held, axis, bit) for d, held in values.items()}
        bit //= 2
    return [values[d] for d in range(len(values))]


def shifted(value, axis, offset):
    size = lax.axis_size(axis)
    return lax.ppermute(value, axis, [((i + offset) % size, i) for i in range(size)])


def quotient(value, by):
    return value >> (by.bit_length() - 1) if by & (by - 1) == 0 else lax.div(value, by)


def remainder(value, by):
    return value & (by - 1) if by & (by - 1) == 0 else lax.rem(value, by)


def note_rows(how_many):
    digits = (how_many + LANES - 1) // LANES
    return (2 * digits + 15) // 16 * 16, digits


def with_notes(payload, values):
    (how_many,) = values.shape
    height, digits = note_rows(how_many)
    values = jnp.pad(values, (0, digits * LANES - how_many)).reshape(digits, LANES)
    tile = jnp.concatenate([remainder(values, LANES), quotient(values, LANES)])
    tile = jnp.pad(tile, ((0, height - 2 * digits), (0, 0)))
    return jnp.concatenate([payload, tile.astype(payload.dtype)])


def read_notes(payload, start, how_many, whole, notes, sem):
    height, _ = note_rows(how_many)
    whole[...] = payload[start : start + height].astype(jnp.float32).astype(jnp.int32)
    copy = pltpu.make_async_copy(whole, notes, sem)
    copy.start()
    return copy


def note(notes, how_many, p):
    _, digits = note_rows(how_many)
    return notes[p // LANES, p % LANES] + notes[digits + p // LANES, p % LANES] * LANES


def positions(sizes, a_rows, a_cols, row_at, layer_at):
    layers, piece_rows, width, local_rows, kept = sizes
    own_rows = local_rows // layers
    owner = quotient(a_cols, piece_rows * layers)
    rights = ((owner ^ row_at) * piece_rows + remainder(a_cols, piece_rows)) * width
    local = a_rows - row_at * local_rows
    goals = (quotient(local, own_rows) ^ layer_at) * own_rows
    return rights, (goals + remainder(local, own_rows)) * kept


def pack_kernel(sizes, a_rows, a_cols, x_in, x_out, tile):
    count, height = sizes
    x_out[:count] = x_in[:, :height]
    tile[...] = jnp.zeros_like(tile)
    for p, value in enumerate((a_rows[...], a_cols[...])):
        tile[2 * p : 2 * p + 1, :count] = remainder(value, LANES)
        tile[2 * p + 1 : 2 * p + 2, :count] = quotient(value, LANES)
    x_out[count, :16] = tile[...].astype(jnp.float32).astype(jnp.bfloat16)
    x_out[count, 16:] = jnp.zeros((height - 16, LANES), jnp.bfloat16)


def list_pairs(sizes, index, row, panel_cols, kept_cols, pairs, tally, j):
    count, width, kept, trash = sizes
    total = jnp.int32(0)
    for n in range(count):
        right, goal = index[row, n], index[row + 1, n]
        for s in range(width):
            wanted = panel_cols[right + s]
            hit, slot = jnp.int32(0), goal
            for t in range(kept):
                same = (kept_cols[goal + t] == wanted).astype(jnp.int32)
                hit += same
                slot += t * same
            pairs[j, 0, total] = n
            pairs[j, 1, total] = right + s
            pairs[j, 2, total] = slot
            total += hit
    for g in range(GROUP):
        pairs[j, 0, total + g] = 0
        pairs[j, 1, total + g] = 0
        pairs[j, 2, total + g] = trash
    tally[j] = total


def add_products(left, panel, totals, pairs, tally, j):
    def one_group(group, carry):
        base = group * GROUP
        products = [
            jnp.dot(
                left(pairs[j, 0, base + g]),
                panel[pairs[j, 1, base + g]],
                preferred_element_type=jnp.float32,
            )
            for g in range(GROUP)
        ]
        for g in range(GROUP):
            totals[pairs[j, 2, base + g]] += products[g]
        return carry

    lax.fori_loop(0, quotient(tally[j] + GROUP - 1, GROUP), one_group, 0)


def own_kernel(sizes, *refs):
    rows, layers, count, piece_rows, width, local_rows, kept, order = sizes
    place, index, s_cols, c_cols, x_in, s_in = refs[:6]
    s_other, refs = refs[6 : 5 + rows], refs[5 + rows :]
    totals, panel, panel_cols, kept_cols = refs[:4]
    pairs, tally, whole, notes, note_sem = refs[4:]
    piece = piece_rows * width
    reads = [
        read_notes(s_other[d], piece * order, piece, whole.at[d], notes.at[d], note_sem.at[d])
        for d in range(rows - 1)
    ]
    totals[...] = jnp.zeros_like(totals)
    panel[:piece] = s_in[...]
    for d in range(1, rows):
        for q in range(piece):
            panel[d * piece + q] = s_other[d - 1][q * order : (q + 1) * order]
    own_rows = local_rows // layers
    for g in range(layers):
        base = (place[1] ^ g) * own_rows
        for i in range(own_rows):
            for t in range(kept):
                kept_cols[(g * own_rows + i) * kept + t] = c_cols[base + i, t]
    for read in reads:
        read.wait()
    for q in range(piece):
        panel_cols[q] = s_cols[q // width, q % width]
        for d in range(1, rows):
            panel_cols[d * piece + q] = note(notes.at[d - 1], piece, q)
    sizes = (count, width, kept, local_rows * kept)
    list_pairs(sizes, index, 0, panel_cols, kept_cols, pairs, tally, 0)
    add_products(lambda n: x_in[n], panel, totals, pairs, tally, 0)


def peer_kernel(sizes, first, *refs):
    cols, layers, count, piece_rows, width, local_rows, kept, height = sizes
    slots = local_rows * kept // layers
    if first == 0:
        place, panel_cols, kept_cols, *refs = refs
    else:
        pairs, tally, *refs = refs
    x_in, refs = refs[: cols - 1], refs[cols - 1 :]
    panel, before, own, sent, refs = refs[0], refs[1], refs[2], refs[3 : 2 + layers], refs[2 + layers :]
    if first == 0:
        pairs, tally, totals, whole, index, note_sem = refs
        copies = []
        for j in range(cols - 1):
            digits = x_in[j][count, :16].astype(jnp.float32).astype(jnp.int32)
            rights, goals = positions(
                (layers, piece_rows, width, local_rows, kept),
                digits[0:1] + digits[1:2] * LANES,
                digits[2:3] + digits[3:4] * LANES,
                place[0],
                place[1],
            )
            whole[j, 0:1] = rights
            whole[j, 1:2] = goals
            copies.append(pltpu.make_async_copy(whole.at[j], index.at[j], note_sem.at[j]))
            copies[-1].start()
    else:
        (totals,) = refs
    totals[...] = before[:, first : first + height]
    if first == 0:
        for j in range(cols - 1):
            copies[j].wait()
            list_pairs(
                (count, width, kept, layers * slots),
                index.at[j],
                0,
                panel_cols,
                kept_cols,
                pairs,
                tally,
                j,
            )

    for j in range(cols - 1):
        add_products(lambda n: x_in[j][n], panel, totals, pairs, tally, j)

    own[...] = totals[:slots]
    half = height // 2
    for d in range(1, layers):
        code = sent[d - 1]
        spare = code.shape[0] - slots * half
        code[slots * half :] = jnp.zeros((spare, code.shape[1]), jnp.int32)
        for u in range(slots):
            value = totals[d * slots + u]
            peak = jnp.max(jnp.abs(value), axis=0, keepdims=True)
            power = jnp.floor(jnp.log2(jnp.maximum(peak, 1e-30)) + 1e-3) + 1.0
            word = jnp.floor(value * jnp.exp2(15.0 - power) + 0.5).astype(jnp.int32)
            code[pl.ds(u * half, half)] = (word[:half] << 16) | (word[half:] & 0xFFFF)
            code[pl.ds(slots * half + u, 1)] = power.astype(jnp.int32)


def finish_kernel(sizes, *refs):
    layers, chunks, slots, height = sizes
    result = refs[-1]
    kept = result.shape[1]
    half = height // 2
    for c in range(chunks):
        own, codes = refs[c * layers], refs[c * layers + 1 : (c + 1) * layers]
        for u in range(slots):
            high, low = own[u, :half], own[u, half:]
            for code in codes:
                word = code[pl.ds(u * half, half)]
                power = code[pl.ds(slots * half + u, 1)].astype(jnp.float32)
                scale = jnp.exp2(power - 15.0)
                high += (word >> 16).astype(jnp.float32) * scale
                low += ((word << 16) >> 16).astype(jnp.float32) * scale
            at = c * height
            result[u // kept, u % kept, at : at + half] = high.astype(jnp.bfloat16)
            result[u // kept, u % kept, at + half : at + height] = low.astype(jnp.bfloat16)


def per_device(a_blocks, a_rows, a_cols, s_blocks, s_cols, c_cols):
    rows, cols, layers = (lax.axis_size(axis) for axis in ("row", "col", "layer"))
    count, order = a_blocks.shape[:2]
    piece_rows, width = s_cols.shape
    local_rows, kept = c_cols.shape
    own_rows = local_rows // layers
    slots = own_rows * kept
    all_slots = layers * slots
    height = order // CHUNKS
    piece = piece_rows * width
    panel_size = rows * piece
    block_size = order * order
    flat_s = s_blocks.reshape(piece, order, order)
    note_height, _ = note_rows(piece)

    scalars = pl.BlockSpec(memory_space=pltpu.SMEM)
    vector = pl.BlockSpec(memory_space=pltpu.VMEM)
    anywhere = pl.BlockSpec(memory_space=pl.ANY)

    x_first = pl.pallas_call(
        functools.partial(pack_kernel, (count, height)),
        out_shape=jax.ShapeDtypeStruct((count + 1, height, order), jnp.bfloat16),
        in_specs=[vector] * 3,
        out_specs=vector,
        scratch_shapes=[pltpu.VMEM((16, LANES), jnp.int32)],
        compiler_params=pltpu.CompilerParams(
            vmem_limit_bytes=2 * block_size * (2 * count + 1) + 4 * MIB
        ),
        name="pack",
    )(a_rows.reshape(1, count), a_cols.reshape(1, count), a_blocks)
    x_pieces = [[shifted(x_first, "col", j) for j in range(1, cols)]]
    later_s, later_blocks, later_rows, later_cols, _ = lax.optimization_barrier(
        (flat_s, a_blocks, a_rows, a_cols, x_first)
    )
    for c in range(1, CHUNKS):
        part = lax.slice_in_dim(later_blocks, c * height, (c + 1) * height, axis=1)
        x_pieces.append([shifted(part, "col", j) for j in range(1, cols)])
    s_sent = with_notes(later_s.reshape(piece * order, order), s_cols.reshape(-1))
    s_pieces = gathered(s_sent, "row")[1:]

    place = jnp.stack([lax.axis_index("row"), lax.axis_index("layer")])
    index = jnp.stack(
        positions(
            (layers, piece_rows, width, local_rows, kept),
            later_rows,
            later_cols,
            lax.axis_index("row"),
            lax.axis_index("layer"),
        )
    )
    moved = block_size * (4 * all_slots + 4 * panel_size + 2 * count)
    totals, panel, panel_cols, kept_cols = pl.pallas_call(
        functools.partial(
            own_kernel, (rows, layers, count, piece_rows, width, local_rows, kept, order)
        ),
        out_shape=[
            jax.ShapeDtypeStruct((all_slots + 1, order, order), jnp.float32),
            jax.ShapeDtypeStruct((panel_size, order, order), jnp.bfloat16),
            jax.ShapeDtypeStruct((panel_size,), jnp.int32),
            jax.ShapeDtypeStruct((all_slots,), jnp.int32),
        ],
        in_specs=[scalars] * 4 + [vector] * (1 + rows),
        out_specs=[vector] * 2 + [scalars] * 2,
        scratch_shapes=[
            pltpu.SMEM((1, 3, count * width + GROUP), jnp.int32),
            pltpu.SMEM((1,), jnp.int32),
            pltpu.VMEM((rows - 1, note_height, LANES), jnp.int32),
            pltpu.SMEM((rows - 1, note_height, LANES), jnp.int32),
            pltpu.SemaphoreType.DMA((rows - 1,)),
        ],
        compiler_params=pltpu.CompilerParams(vmem_limit_bytes=moved + 4 * MIB),
        cost_estimate=pl.CostEstimate(
            flops=2 * order**3 * count * width // 4, bytes_accessed=moved, transcendentals=0
        ),
        name="own_products",
    )(place, index, s_cols, c_cols, a_blocks, flat_s, *s_pieces)

    code_rows = slots * (height // 2) + (slots + 7) // 8 * 8
    moved = block_size * (8 * all_slots + 2 * panel_size + 2 * count * (cols - 1))
    pair_shapes = [(cols - 1, 3, count * width + GROUP), (cols - 1,)]
    final, plan = [], []
    order_out = sorted(range(1, layers), key=lambda d: (1 - d % 2, d))
    for c in range(CHUNKS):
        out_shape = [jax.ShapeDtypeStruct((slots, height, order), jnp.float32)]
        out_shape += [jax.ShapeDtypeStruct((code_rows, order), jnp.int32)] * (layers - 1)
        out_specs = [vector] * layers
        scratch = [pltpu.VMEM((all_slots + 1, height, order), jnp.float32)]
        if c == 0:
            out_shape += [jax.ShapeDtypeStruct(shape, jnp.int32) for shape in pair_shapes]
            out_specs += [scalars] * 2
            scratch += [
                pltpu.VMEM((cols - 1, 2, LANES), jnp.int32),
                pltpu.SMEM((cols - 1, 2, LANES), jnp.int32),
                pltpu.SemaphoreType.DMA((cols - 1,)),
            ]
        given = plan or (place, panel_cols, kept_cols)
        out = pl.pallas_call(
            functools.partial(
                peer_kernel,
                (cols, layers, count, piece_rows, width, local_rows, kept, height),
                c * height,
            ),
            out_shape=out_shape,
            in_specs=[scalars] * len(given) + [vector] * (cols + 1),
            out_specs=out_specs,
            scratch_shapes=scratch,
            compiler_params=pltpu.CompilerParams(vmem_limit_bytes=moved + 4 * MIB),
            cost_estimate=pl.CostEstimate(
                flops=2 * order**2 * height * count * width // 4 * (cols - 1),
                bytes_accessed=moved // CHUNKS,
                transcendentals=0,
            ),
            name=f"peer_products_{c}",
        )(*given, *x_pieces[c], panel, totals)
        plan = plan or out[layers:]
        final.append(out[0])
        final += [flipped(out[d], "layer", d) for d in order_out]

    return pl.pallas_call(
        functools.partial(finish_kernel, (layers, CHUNKS, slots, height)),
        out_shape=jax.ShapeDtypeStruct((own_rows, kept, order, order), jnp.bfloat16),
        in_specs=[vector] * len(final),
        out_specs=vector,
        compiler_params=pltpu.CompilerParams(
            vmem_limit_bytes=16 * slots * order * order + 4 * MIB
        ),
        name="finish",
    )(*final)


def solution(mesh):
    placed = (
        P(("row", "col", "layer"), None, None),
        P(("row", "col", "layer")),
        P(("row", "col", "layer")),
        P(("row", "layer"), "col", None, None),
        P(("row", "layer"), "col"),
        P("row", "col"),
    )
    return jax.shard_map(
        per_device,
        mesh=mesh,
        in_specs=placed,
        out_specs=P(("row", "layer"), "col", None, None),
        check_vma=False,
    )
```

```python
import functools

import jax
import jax.numpy as jnp
from jax import lax
from jax.experimental import pallas as pl
from jax.experimental.pallas import tpu as pltpu
from jax.sharding import PartitionSpec as P

GROUP = 4
LANES = 128
MIB = 2**20
HBM = pltpu.MemorySpace.HBM


def row_ranges(order):
    first = order * 5 // 8
    return [(0, first), (first, order - first)]


def in_hbm(*values):
    return [pltpu.with_memory_space_constraint(value, HBM) for value in values]


def flipped(value, axis, bits):
    return lax.ppermute(value, axis, [(i, i ^ bits) for i in range(lax.axis_size(axis))])


def gathered(value, axis):
    values = {0: value}
    bit = lax.axis_size(axis) // 2
    while bit:
        values |= {d ^ bit: flipped(held, axis, bit) for d, held in values.items()}
        bit //= 2
    return [values[d] for d in range(len(values))]


def shifted(value, axis, offset):
    size = lax.axis_size(axis)
    return lax.ppermute(value, axis, [((i + offset) % size, i) for i in range(size)])


def quotient(value, by):
    return value >> (by.bit_length() - 1) if by & (by - 1) == 0 else lax.div(value, by)


def remainder(value, by):
    return value & (by - 1) if by & (by - 1) == 0 else lax.rem(value, by)


def write_digits(tile, at, value):
    height, width = value.shape
    tile[at : at + height, :width] = remainder(value, LANES)
    tile[at + height : at + 2 * height, :width] = quotient(value, LANES)


def positions(sizes, a_rows, a_cols, row_at, layer_at):
    layers, piece_rows, width, local_rows, kept = sizes
    own_rows = local_rows // layers
    owner = quotient(a_cols, piece_rows * layers)
    rights = ((owner ^ row_at) * piece_rows + remainder(a_cols, piece_rows)) * width
    local = a_rows - row_at * local_rows
    goals = remainder(quotient(local, own_rows) - layer_at + layers, layers) * own_rows
    return rights, (goals + remainder(local, own_rows)) * kept


def pack_kernel(sizes, a_rows, a_cols, x_in, s_cols, s_in, *refs):
    count, piece, order, ranges = sizes
    s_out, x_out, refs = refs[0], refs[1 : 1 + len(ranges)], refs[1 + len(ranges) :]
    rows, cols, s_held, x_tile, s_tile, sem = refs
    small = [(a_rows, rows), (a_cols, cols), (s_cols, s_held)]
    large = [(x_in.at[:, pl.ds(*span)], out.at[pl.ds(0, count)]) for span, out in zip(ranges, x_out)]
    large += [(s_in.at[q], s_out.at[pl.ds(q * order, order)]) for q in range(piece)]
    loads = [
        pltpu.make_async_copy(source, goal, sem.at[p])
        for p, (source, goal) in enumerate(small + large)
    ]
    for load in loads:
        load.start()
    x_tile[...] = jnp.zeros_like(x_tile)
    s_tile[...] = jnp.zeros_like(s_tile)
    height = ranges[0][1]
    x_out[0][count, 16:] = jnp.zeros((height - 16, LANES), jnp.bfloat16)
    for load in loads[:3]:
        load.wait()
    write_digits(x_tile, 0, rows[...])
    write_digits(x_tile, 2, cols[...])
    write_digits(s_tile, 0, s_held[...])
    x_out[0][count, :16] = x_tile[...].astype(jnp.float32).astype(jnp.bfloat16)
    s_out[piece * order :] = s_tile[...].astype(jnp.float32).astype(jnp.bfloat16)
    for load in loads[3:]:
        load.wait()


def place_kernel(sizes, place, a_rows, a_cols, c_cols, index, kept_cols, rows, cols, held, sem):
    layers, count, piece_rows, width, local_rows, kept = sizes
    loads = [
        pltpu.make_async_copy(source, goal, sem.at[p])
        for p, (source, goal) in enumerate(((a_rows, rows), (a_cols, cols), (c_cols, held)))
    ]
    for load in loads:
        load.start()
    for load in loads:
        load.wait()
    own_rows = local_rows // layers
    for n in range(count):
        index[0, n], index[1, n] = positions(
            (layers, piece_rows, width, local_rows, kept), rows[0, n], cols[0, n], place[0], place[1]
        )
    for g in range(layers):
        base = remainder(place[1] + g, layers) * own_rows
        for i in range(own_rows):
            for t in range(kept):
                kept_cols[(g * own_rows + i) * kept + t] = held[t, base + i]


def list_pairs(sizes, index, panel_cols, kept_cols, pairs):
    count, width, kept, trash = sizes
    total = jnp.int32(0)
    for n in range(count):
        right, goal = index[0, n], index[1, n]
        for s in range(width):
            wanted = panel_cols[right + s]
            hit, slot = jnp.int32(0), goal
            for t in range(kept):
                same = (kept_cols[goal + t] == wanted).astype(jnp.int32)
                hit += same
                slot += t * same
            pairs[0, total] = n
            pairs[1, total] = right + s
            pairs[2, total] = slot
            total += hit
    for g in range(GROUP):
        pairs[0, total + g] = 0
        pairs[1, total + g] = 0
        pairs[2, total + g] = trash
    pairs[0, count * width + GROUP] = total


def add_products(left, panel, totals, pairs):
    def one_group(group, carry):
        base = group * GROUP
        products = [
            jnp.dot(
                left[pairs[0, base + g]],
                panel[pairs[1, base + g]],
                preferred_element_type=jnp.float32,
            )
            for g in range(GROUP)
        ]
        for g in range(GROUP):
            totals[pairs[2, base + g]] += products[g]
        return carry

    total = pairs[0, pairs.shape[1] - 1]
    lax.fori_loop(0, quotient(total + GROUP - 1, GROUP), one_group, 0)


def own_kernel(sizes, ranges, *refs):
    rows, count, piece_rows, width, kept, order = sizes
    index, kept_cols, refs = refs[0], refs[1], refs[2:]
    x_in, s_in, refs = refs[: len(ranges)], refs[len(ranges) :][:rows], refs[len(ranges) + rows :]
    totals, panel, panel_cols, pairs, whole, notes, sem = refs
    piece = piece_rows * width
    for d in range(rows):
        tile = s_in[d][piece * order :].astype(jnp.float32).astype(jnp.int32)
        whole[d] = tile[:piece_rows] + tile[piece_rows : 2 * piece_rows] * LANES
    copy = pltpu.make_async_copy(whole, notes, sem)
    copy.start()
    totals[...] = jnp.zeros_like(totals)
    for d in range(rows):
        for q in range(piece):
            panel[d * piece + q] = s_in[d][q * order : (q + 1) * order]
    copy.wait()
    for d in range(rows):
        for q in range(piece):
            panel_cols[d * piece + q] = notes[d, q // width, q % width]
    list_pairs((count, width, kept, totals.shape[0] - 1), index, panel_cols, kept_cols, pairs)
    for (first, height), blocks in zip(ranges, x_in):
        add_products(blocks, panel, totals.at[:, pl.ds(first, height)], pairs)


def peer_kernel(sizes, span, *refs):
    cols, layers, count, piece_rows, width, local_rows, kept = sizes
    first, height = span
    slots = local_rows * kept // layers
    if first == 0:
        place, panel_cols, kept_cols, *refs = refs
    else:
        pairs, *refs = refs
    x_in, refs = refs[: cols - 1], refs[cols - 1 :]
    panel, before, own, sent, refs = refs[0], refs[1], refs[2], refs[3 : 2 + layers], refs[2 + layers :]
    if first == 0:
        pairs, totals, whole, index, sem = refs
        copies = []
        for j in range(cols - 1):
            digits = x_in[j][count, :16].astype(jnp.float32).astype(jnp.int32)
            whole[j, 0:1], whole[j, 1:2] = positions(
                (layers, piece_rows, width, local_rows, kept),
                digits[0:1] + digits[1:2] * LANES,
                digits[2:3] + digits[3:4] * LANES,
                place[0],
                place[1],
            )
            copies.append(pltpu.make_async_copy(whole.at[j], index.at[j], sem.at[j]))
            copies[j].start()
    else:
        (totals,) = refs
    totals[...] = before[:, first : first + height]
    if first == 0:
        for j in range(cols - 1):
            copies[j].wait()
            list_pairs(
                (count, width, kept, layers * slots),
                index.at[j],
                panel_cols,
                kept_cols,
                pairs.at[j],
            )
    for j in range(cols - 1):
        add_products(x_in[j], panel, totals, pairs.at[j])

    own[...] = totals[:slots]
    half = height // 2
    for d in range(1, layers):
        code = sent[d - 1]
        spare = code.shape[0] - slots * half
        code[slots * half :] = jnp.zeros((spare, code.shape[1]), jnp.int32)
        for u in range(slots):
            value = totals[d * slots + u]
            peak = jnp.max(jnp.abs(value), axis=0, keepdims=True)
            power = jnp.floor(jnp.log2(jnp.maximum(peak, 1e-30)) + 1e-3) + 1.0
            word = jnp.floor(value * jnp.exp2(15.0 - power) + 0.5).astype(jnp.int32)
            code[pl.ds(u * half, half)] = (word[:half] << 16) | (word[half:] & 0xFFFF)
            code[pl.ds(slots * half + u, 1)] = power.astype(jnp.int32)


def finish_kernel(sizes, span, *refs):
    layers, slots = sizes
    first, height = span
    half = height // 2
    before, own, codes, result = refs[: first > 0], refs[-layers - 1], refs[-layers:-1], refs[-1]
    kept = result.shape[1]
    for done in before:
        result[:, :, :first] = done[...]
    for u in range(slots):
        high, low = own[u, :half], own[u, half:]
        for code in codes:
            word = code[pl.ds(u * half, half)]
            power = code[pl.ds(slots * half + u, 1)].astype(jnp.float32)
            scale = jnp.exp2(power - 15.0)
            high += (word >> 16).astype(jnp.float32) * scale
            low += ((word << 16) >> 16).astype(jnp.float32) * scale
        result[u // kept, u % kept, first : first + half] = high.astype(jnp.bfloat16)
        result[u // kept, u % kept, first + half : first + height] = low.astype(jnp.bfloat16)


def per_device(a_blocks, a_rows, a_cols, s_blocks, s_cols, c_cols):
    rows, cols, layers = (lax.axis_size(axis) for axis in ("row", "col", "layer"))
    count, order = a_blocks.shape[:2]
    piece_rows, width = s_cols.shape
    local_rows, kept = c_cols.shape
    own_rows = local_rows // layers
    slots = own_rows * kept
    all_slots = layers * slots
    ranges = row_ranges(order)
    piece = piece_rows * width
    panel_size = rows * piece
    block_size = order * order
    flat_s = s_blocks.reshape(piece, order, order)
    note_height = (2 * piece_rows + 15) // 16 * 16
    first_height = ranges[0][1]

    scalars = pl.BlockSpec(memory_space=pltpu.SMEM)
    vector = pl.BlockSpec(memory_space=pltpu.VMEM)
    far = pl.BlockSpec(memory_space=HBM)

    s_sent, *x_sent = pl.pallas_call(
        functools.partial(pack_kernel, (count, piece, order, ranges)),
        out_shape=[jax.ShapeDtypeStruct((piece * order + note_height, order), jnp.bfloat16)]
        + [
            jax.ShapeDtypeStruct((count + (at == 0), height, order), jnp.bfloat16)
            for at, height in ranges
        ],
        in_specs=[far] * 5,
        out_specs=[vector] * (1 + len(ranges)),
        scratch_shapes=[
            pltpu.VMEM((1, count), jnp.int32),
            pltpu.VMEM((1, count), jnp.int32),
            pltpu.VMEM((piece_rows, width), jnp.int32),
            pltpu.VMEM((16, LANES), jnp.int32),
            pltpu.VMEM((note_height, LANES), jnp.int32),
            pltpu.SemaphoreType.DMA((3 + piece + len(ranges),)),
        ],
        compiler_params=pltpu.CompilerParams(
            vmem_limit_bytes=2 * block_size * (2 * count + piece) + 4 * MIB
        ),
        name="pack",
    )(*in_hbm(a_rows.reshape(1, count), a_cols.reshape(1, count), a_blocks, s_cols, flat_s))
    x_pieces = [[shifted(part, "col", j) for j in range(1, cols)] for part in x_sent]
    s_pieces = gathered(s_sent, "row")

    place = jnp.stack([lax.axis_index("row"), lax.axis_index("layer")])
    index, kept_cols = pl.pallas_call(
        functools.partial(place_kernel, (layers, count, piece_rows, width, local_rows, kept)),
        out_shape=[
            jax.ShapeDtypeStruct((2, count), jnp.int32),
            jax.ShapeDtypeStruct((all_slots,), jnp.int32),
        ],
        in_specs=[scalars] + [far] * 3,
        out_specs=[scalars] * 2,
        scratch_shapes=[
            pltpu.SMEM((1, count), jnp.int32),
            pltpu.SMEM((1, count), jnp.int32),
            pltpu.SMEM((kept, local_rows), jnp.int32),
            pltpu.SemaphoreType.DMA((3,)),
        ],
        cost_estimate=pl.CostEstimate(flops=0, bytes_accessed=16 * MIB, transcendentals=0),
        name="place",
    )(place, *in_hbm(a_rows.reshape(1, count), a_cols.reshape(1, count), c_cols.T))

    moved = block_size * (4 * all_slots + 4 * panel_size + 2 * count)
    totals, panel, panel_cols = pl.pallas_call(
        functools.partial(own_kernel, (rows, count, piece_rows, width, kept, order), ranges),
        out_shape=[
            jax.ShapeDtypeStruct((all_slots + 1, order, order), jnp.float32),
            jax.ShapeDtypeStruct((panel_size, order, order), jnp.bfloat16),
            jax.ShapeDtypeStruct((panel_size,), jnp.int32),
        ],
        in_specs=[scalars] * 2 + [vector] * (len(ranges) + rows),
        out_specs=[vector] * 2 + [scalars],
        scratch_shapes=[
            pltpu.SMEM((3, count * width + GROUP + 1), jnp.int32),
            pltpu.VMEM((rows, piece_rows, LANES), jnp.int32),
            pltpu.SMEM((rows, piece_rows, LANES), jnp.int32),
            pltpu.SemaphoreType.DMA,
        ],
        compiler_params=pltpu.CompilerParams(vmem_limit_bytes=moved + 4 * MIB),
        cost_estimate=pl.CostEstimate(
            flops=2 * order**3 * count * width // 4, bytes_accessed=moved, transcendentals=0
        ),
        name="own_products",
    )(index, kept_cols, *x_sent, *s_pieces)

    moved = block_size * (8 * all_slots + 2 * panel_size + 2 * count * (cols - 1))
    finished, plan = [], []
    for (at, height), pieces in zip(ranges, x_pieces):
        code_rows = slots * (height // 2) + (slots + 7) // 8 * 8
        out_shape = [jax.ShapeDtypeStruct((slots, height, order), jnp.float32)]
        out_shape += [jax.ShapeDtypeStruct((code_rows, order), jnp.int32)] * (layers - 1)
        out_specs = [vector] * layers
        scratch = [pltpu.VMEM((all_slots + 1, height, order), jnp.float32)]
        if at == 0:
            out_shape.append(
                jax.ShapeDtypeStruct((cols - 1, 3, count * width + GROUP + 1), jnp.int32)
            )
            out_specs.append(scalars)
            scratch += [
                pltpu.VMEM((cols - 1, 2, LANES), jnp.int32),
                pltpu.SMEM((cols - 1, 2, LANES), jnp.int32),
                pltpu.SemaphoreType.DMA((cols - 1,)),
            ]
        given = plan or (place, panel_cols, kept_cols)
        out = pl.pallas_call(
            functools.partial(
                peer_kernel,
                (cols, layers, count, piece_rows, width, local_rows, kept),
                (at, height),
            ),
            out_shape=out_shape,
            in_specs=[scalars] * len(given) + [vector] * (cols + 1),
            out_specs=out_specs,
            scratch_shapes=scratch,
            compiler_params=pltpu.CompilerParams(vmem_limit_bytes=moved + 4 * MIB),
            cost_estimate=pl.CostEstimate(
                flops=2 * order**2 * height * count * width // 4 * (cols - 1),
                bytes_accessed=moved // 2,
                transcendentals=0,
            ),
            name=f"peer_products_{at}",
        )(*given, *pieces, panel, totals)
        plan = plan or out[layers:]
        codes = [shifted(out[d], "layer", layers - d) for d in range(1, layers)]
        finished = [
            pl.pallas_call(
                functools.partial(finish_kernel, (layers, slots), (at, height)),
                out_shape=jax.ShapeDtypeStruct((own_rows, kept, at + height, order), jnp.bfloat16),
                in_specs=[vector] * (len(finished) + layers),
                out_specs=vector,
                compiler_params=pltpu.CompilerParams(
                    vmem_limit_bytes=16 * slots * block_size + 4 * MIB
                ),
                name=f"finish_{at}",
            )(*finished, out[0], *codes)
        ]
    return finished[0]


def solution(mesh):
    placed = (
        P(("row", "col", "layer"), None, None),
        P(("row", "col", "layer")),
        P(("row", "col", "layer")),
        P(("row", "layer"), "col", None, None),
        P(("row", "layer"), "col"),
        P("row", "col"),
    )
    return jax.shard_map(
        per_device,
        mesh=mesh,
        in_specs=placed,
        out_specs=P(("row", "layer"), "col", None, None),
        check_vma=False,
    )
```

```python
import functools

import jax
import jax.numpy as jnp
from jax import lax
from jax.experimental import pallas as pl
from jax.experimental.pallas import tpu as pltpu
from jax.sharding import PartitionSpec as P

GROUP = 4
LANES = 128
MIB = 2**20
HBM = pltpu.MemorySpace.HBM


def row_ranges(order):
    first = order * 5 // 8
    return [(0, first), (first, order - first)]


def in_hbm(*values):
    return [pltpu.with_memory_space_constraint(value, HBM) for value in values]


def flipped(value, axis, bits):
    return lax.ppermute(value, axis, [(i, i ^ bits) for i in range(lax.axis_size(axis))])


def gathered(value, axis):
    values = {0: value}
    bit = lax.axis_size(axis) // 2
    while bit:
        values |= {d ^ bit: flipped(held, axis, bit) for d, held in values.items()}
        bit //= 2
    return [values[d] for d in range(len(values))]


def shifted(value, axis, offset):
    size = lax.axis_size(axis)
    return lax.ppermute(value, axis, [((i + offset) % size, i) for i in range(size)])


def quotient(value, by):
    return value >> (by.bit_length() - 1) if by & (by - 1) == 0 else lax.div(value, by)


def remainder(value, by):
    return value & (by - 1) if by & (by - 1) == 0 else lax.rem(value, by)


def write_digits(tile, at, value):
    height, width = value.shape
    tile[at : at + height, :width] = remainder(value, LANES)
    tile[at + height : at + 2 * height, :width] = quotient(value, LANES)


def pack_kernel(sizes, a_rows, a_cols, c_cols, x_in, s_cols, s_in, *refs):
    layers, count, piece_rows, width, local_rows, kept, order, ranges = sizes
    known, s_out, x_out, refs = refs[0], refs[1], refs[2 : 2 + len(ranges)], refs[2 + len(ranges) :]
    rows, cols, kept_held, s_held, x_tile, s_tile, sem = refs
    piece = piece_rows * width
    small = [(a_rows, rows), (a_cols, cols), (c_cols, kept_held), (s_cols, s_held)]
    large = [(x_in.at[:, pl.ds(*span)], out.at[pl.ds(0, count)]) for span, out in zip(ranges, x_out)]
    large += [(s_in.at[q], s_out.at[pl.ds(q * order, order)]) for q in range(piece)]
    loads = [
        pltpu.make_async_copy(source, goal, sem.at[p])
        for p, (source, goal) in enumerate(small + large)
    ]
    for load in loads:
        load.start()
    known[...] = jnp.zeros_like(known)
    x_tile[...] = jnp.zeros_like(x_tile)
    s_tile[...] = jnp.zeros_like(s_tile)
    x_out[0][count, 16:] = jnp.zeros((ranges[0][1] - 16, LANES), jnp.bfloat16)
    for load in loads[: len(small)]:
        load.wait()
    own_rows = local_rows // layers
    row, col = rows[...], cols[...]
    here = quotient(row[:, :1], local_rows)
    layer = remainder(quotient(col[:, :1], piece_rows), layers)
    owner = quotient(col, piece_rows * layers)
    local = row - here * local_rows
    goal = remainder(quotient(local, own_rows) - layer + layers, layers) * own_rows
    place = (
        ((owner ^ here) * piece_rows + remainder(col, piece_rows)) * width,
        (goal + remainder(local, own_rows)) * kept,
        local,
    )
    for p, value in enumerate(place):
        known[p : p + 1, :count] = value
        write_digits(x_tile, 2 * p, value)
    known[8 : 8 + kept, :local_rows] = kept_held[...]
    write_digits(s_tile, 0, s_held[...])
    x_out[0][count, :16] = x_tile[...].astype(jnp.float32).astype(jnp.bfloat16)
    s_out[piece * order :] = s_tile[...].astype(jnp.float32).astype(jnp.bfloat16)
    for load in loads[len(small) :]:
        load.wait()


def match(sizes, place, panel_cols, kept_cols, codes):
    width, local_rows, kept = sizes
    right, goal, local = place
    wanted, held = [jnp.zeros_like(right)] * width, [jnp.zeros_like(right)] * kept
    for p in range(panel_cols.shape[0]):
        for s in range(width):
            wanted[s] = jnp.where(right == p * width, panel_cols[p : p + 1, s : s + 1], wanted[s])
    for i in range(local_rows):
        for t in range(kept):
            held[t] = jnp.where(local == i, kept_cols[t : t + 1, i : i + 1], held[t])
    codes[0:1] = right
    for s in range(width):
        slot = jnp.full_like(right, -1)
        for t in range(kept):
            slot = jnp.where(held[t] == wanted[s], goal + t, slot)
        codes[1 + s : 2 + s] = slot


def list_pairs(sizes, codes, pairs):
    count, width, trash = sizes
    total = jnp.int32(0)
    for n in range(count):
        right = codes[0, n]
        for s in range(width):
            slot = codes[1 + s, n]
            pairs[0, total] = n
            pairs[1, total] = right + s
            pairs[2, total] = slot
            total += (slot >= 0).astype(jnp.int32)
    for g in range(GROUP):
        pairs[0, total + g] = 0
        pairs[1, total + g] = 0
        pairs[2, total + g] = trash
    return total


def add_products(left, panel, totals, pairs, total):
    def one_group(group, carry):
        base = group * GROUP
        products = [
            jnp.dot(
                left[pairs[0, base + g]],
                panel[pairs[1, base + g]],
                preferred_element_type=jnp.float32,
            )
            for g in range(GROUP)
        ]
        for g in range(GROUP):
            totals[pairs[2, base + g]] += products[g]
        return carry

    lax.fori_loop(0, quotient(total + GROUP - 1, GROUP), one_group, 0)


def own_kernel(sizes, ranges, known, *refs):
    rows, count, piece_rows, width, local_rows, kept, order = sizes
    x_in, s_in, refs = refs[: len(ranges)], refs[len(ranges) :][:rows], refs[len(ranges) + rows :]
    totals, panel, panel_cols, codes, numbers, pairs, sem = refs
    piece = piece_rows * width
    for d in range(rows):
        tile = s_in[d][piece * order :].astype(jnp.float32).astype(jnp.int32)
        panel_cols[d * piece_rows : (d + 1) * piece_rows] = (
            tile[:piece_rows] + tile[piece_rows : 2 * piece_rows] * LANES
        )
    place = known[0:1], known[1:2], known[2:3]
    match((width, local_rows, kept), place, panel_cols[...], known[8 : 8 + kept], codes)
    copy = pltpu.make_async_copy(codes, numbers, sem)
    copy.start()
    totals[...] = jnp.zeros_like(totals)
    for d in range(rows):
        for q in range(piece):
            panel[d * piece + q] = s_in[d][q * order : (q + 1) * order]
    copy.wait()
    total = list_pairs((count, width, totals.shape[0] - 1), numbers, pairs)
    for (first, height), blocks in zip(ranges, x_in):
        add_products(blocks, panel, totals.at[:, pl.ds(first, height)], pairs, total)


def peer_kernel(sizes, span, *refs):
    cols, layers, count, width, local_rows, kept = sizes
    first, height = span
    slots = local_rows * kept // layers
    if first == 0:
        known, panel_cols, *refs = refs
    else:
        codes, *refs = refs
    x_in, refs = refs[: cols - 1], refs[cols - 1 :]
    panel, before, own, sent, refs = refs[0], refs[1], refs[2], refs[3 : 2 + layers], refs[2 + layers :]
    if first == 0:
        codes, *refs = refs
        for j in range(cols - 1):
            digits = x_in[j][count, :16].astype(jnp.float32).astype(jnp.int32)
            place = [digits[p : p + 1] + digits[p + 1 : p + 2] * LANES for p in (0, 2, 4)]
            match(
                (width, local_rows, kept), place, panel_cols[...], known[8 : 8 + kept], codes.at[j]
            )
    totals, numbers, pairs, sem = refs
    copy = pltpu.make_async_copy(codes, numbers, sem)
    copy.start()
    totals[...] = before[:, first : first + height]
    copy.wait()
    for j in range(cols - 1):
        total = list_pairs((count, width, layers * slots), numbers.at[j], pairs)
        add_products(x_in[j], panel, totals, pairs, total)

    own[...] = totals[:slots]
    half = height // 2
    for d in range(1, layers):
        code = sent[d - 1]
        spare = code.shape[0] - slots * half
        code[slots * half :] = jnp.zeros((spare, code.shape[1]), jnp.int32)
        for u in range(slots):
            value = totals[d * slots + u]
            peak = jnp.max(jnp.abs(value), axis=0, keepdims=True)
            power = jnp.floor(jnp.log2(jnp.maximum(peak, 1e-30)) + 1e-3) + 1.0
            word = jnp.floor(value * jnp.exp2(15.0 - power) + 0.5).astype(jnp.int32)
            code[pl.ds(u * half, half)] = (word[:half] << 16) | (word[half:] & 0xFFFF)
            code[pl.ds(slots * half + u, 1)] = power.astype(jnp.int32)


def finish_kernel(sizes, span, *refs):
    layers, slots = sizes
    first, height = span
    half = height // 2
    before, own, codes, result = refs[: first > 0], refs[-layers - 1], refs[-layers:-1], refs[-1]
    kept = result.shape[1]
    for done in before:
        result[:, :, :first] = done[...]
    for u in range(slots):
        high, low = own[u, :half], own[u, half:]
        for code in codes:
            word = code[pl.ds(u * half, half)]
            power = code[pl.ds(slots * half + u, 1)].astype(jnp.float32)
            scale = jnp.exp2(power - 15.0)
            high += (word >> 16).astype(jnp.float32) * scale
            low += ((word << 16) >> 16).astype(jnp.float32) * scale
        result[u // kept, u % kept, first : first + half] = high.astype(jnp.bfloat16)
        result[u // kept, u % kept, first + half : first + height] = low.astype(jnp.bfloat16)


def per_device(a_blocks, a_rows, a_cols, s_blocks, s_cols, c_cols):
    rows, cols, layers = (lax.axis_size(axis) for axis in ("row", "col", "layer"))
    count, order = a_blocks.shape[:2]
    piece_rows, width = s_cols.shape
    local_rows, kept = c_cols.shape
    own_rows = local_rows // layers
    slots = own_rows * kept
    all_slots = layers * slots
    ranges = row_ranges(order)
    piece = piece_rows * width
    panel_size = rows * piece
    block_size = order * order
    flat_s = s_blocks.reshape(piece, order, order)
    note_height = (2 * piece_rows + 15) // 16 * 16
    code_height = (1 + width + 7) // 8 * 8

    vector = pl.BlockSpec(memory_space=pltpu.VMEM)
    far = pl.BlockSpec(memory_space=HBM)

    known, s_sent, *x_sent = pl.pallas_call(
        functools.partial(
            pack_kernel, (layers, count, piece_rows, width, local_rows, kept, order, ranges)
        ),
        out_shape=[
            jax.ShapeDtypeStruct((16, LANES), jnp.int32),
            jax.ShapeDtypeStruct((piece * order + note_height, order), jnp.bfloat16),
        ]
        + [
            jax.ShapeDtypeStruct((count + (at == 0), height, order), jnp.bfloat16)
            for at, height in ranges
        ],
        in_specs=[far] * 6,
        out_specs=[vector] * (2 + len(ranges)),
        scratch_shapes=[
            pltpu.VMEM((1, count), jnp.int32),
            pltpu.VMEM((1, count), jnp.int32),
            pltpu.VMEM((kept, local_rows), jnp.int32),
            pltpu.VMEM((piece_rows, width), jnp.int32),
            pltpu.VMEM((16, LANES), jnp.int32),
            pltpu.VMEM((note_height, LANES), jnp.int32),
            pltpu.SemaphoreType.DMA((4 + piece + len(ranges),)),
        ],
        compiler_params=pltpu.CompilerParams(
            vmem_limit_bytes=2 * block_size * (2 * count + piece) + 4 * MIB
        ),
        name="pack",
    )(
        *in_hbm(
            a_rows.reshape(1, count), a_cols.reshape(1, count), c_cols.T, a_blocks, s_cols, flat_s
        )
    )
    x_pieces = [[shifted(part, "col", j) for j in range(1, cols)] for part in x_sent]
    s_pieces = gathered(s_sent, "row")

    moved = block_size * (4 * all_slots + 4 * panel_size + 2 * count)
    totals, panel, panel_cols = pl.pallas_call(
        functools.partial(
            own_kernel, (rows, count, piece_rows, width, local_rows, kept, order), ranges
        ),
        out_shape=[
            jax.ShapeDtypeStruct((all_slots + 1, order, order), jnp.float32),
            jax.ShapeDtypeStruct((panel_size, order, order), jnp.bfloat16),
            jax.ShapeDtypeStruct((rows * piece_rows, LANES), jnp.int32),
        ],
        in_specs=[vector] * (1 + len(ranges) + rows),
        out_specs=[vector] * 3,
        scratch_shapes=[
            pltpu.VMEM((code_height, LANES), jnp.int32),
            pltpu.SMEM((code_height, LANES), jnp.int32),
            pltpu.SMEM((3, count * width + GROUP), jnp.int32),
            pltpu.SemaphoreType.DMA,
        ],
        compiler_params=pltpu.CompilerParams(vmem_limit_bytes=moved + 4 * MIB),
        cost_estimate=pl.CostEstimate(
            flops=2 * order**3 * count * width // 4, bytes_accessed=moved, transcendentals=0
        ),
        name="own_products",
    )(known, *x_sent, *s_pieces)

    moved = block_size * (8 * all_slots + 2 * panel_size + 2 * count * (cols - 1))
    code_shape = (cols - 1, code_height, LANES)
    finished, plan = [], []
    for (at, height), pieces in zip(ranges, x_pieces):
        code_rows = slots * (height // 2) + (slots + 7) // 8 * 8
        out_shape = [jax.ShapeDtypeStruct((slots, height, order), jnp.float32)]
        out_shape += [jax.ShapeDtypeStruct((code_rows, order), jnp.int32)] * (layers - 1)
        if at == 0:
            out_shape.append(jax.ShapeDtypeStruct(code_shape, jnp.int32))
        given = plan or (known, panel_cols)
        out = pl.pallas_call(
            functools.partial(
                peer_kernel, (cols, layers, count, width, local_rows, kept), (at, height)
            ),
            out_shape=out_shape,
            in_specs=[vector] * (len(given) + cols + 1),
            out_specs=[vector] * len(out_shape),
            scratch_shapes=[
                pltpu.VMEM((all_slots + 1, height, order), jnp.float32),
                pltpu.SMEM(code_shape, jnp.int32),
                pltpu.SMEM((3, count * width + GROUP), jnp.int32),
                pltpu.SemaphoreType.DMA,
            ],
            compiler_params=pltpu.CompilerParams(vmem_limit_bytes=moved + 4 * MIB),
            cost_estimate=pl.CostEstimate(
                flops=2 * order**2 * height * count * width // 4 * (cols - 1),
                bytes_accessed=moved // 2,
                transcendentals=0,
            ),
            name=f"peer_products_{at}",
        )(*given, *pieces, panel, totals)
        plan = plan or out[layers:]
        codes = [shifted(out[d], "layer", layers - d) for d in range(1, layers)]
        finished = [
            pl.pallas_call(
                functools.partial(finish_kernel, (layers, slots), (at, height)),
                out_shape=jax.ShapeDtypeStruct((own_rows, kept, at + height, order), jnp.bfloat16),
                in_specs=[vector] * (len(finished) + layers),
                out_specs=vector,
                compiler_params=pltpu.CompilerParams(
                    vmem_limit_bytes=16 * slots * block_size + 4 * MIB
                ),
                name=f"finish_{at}",
            )(*finished, out[0], *codes)
        ]
    return finished[0]


def solution(mesh):
    placed = (
        P(("row", "col", "layer"), None, None),
        P(("row", "col", "layer")),
        P(("row", "col", "layer")),
        P(("row", "layer"), "col", None, None),
        P(("row", "layer"), "col"),
        P("row", "col"),
    )
    return jax.shard_map(
        per_device,
        mesh=mesh,
        in_specs=placed,
        out_specs=P(("row", "layer"), "col", None, None),
        check_vma=False,
    )
```

```python
import functools

import jax
import jax.numpy as jnp
from jax import lax
from jax.experimental import pallas as pl
from jax.experimental.pallas import tpu as pltpu
from jax.sharding import PartitionSpec as P

GROUP = 4
LANES = 128
MIB = 2**20
HBM = pltpu.MemorySpace.HBM


def row_ranges(order):
    first = order * 5 // 8
    return [(0, first), (first, order - first)]


def in_hbm(*values):
    return [pltpu.with_memory_space_constraint(value, HBM) for value in values]


def flipped(value, axis, bits):
    return lax.ppermute(value, axis, [(i, i ^ bits) for i in range(lax.axis_size(axis))])


def gathered(value, axis):
    values = {0: value}
    bit = lax.axis_size(axis) // 2
    while bit:
        values |= {d ^ bit: flipped(held, axis, bit) for d, held in values.items()}
        bit //= 2
    return [values[d] for d in range(len(values))]


def shifted(value, axis, offset):
    size = lax.axis_size(axis)
    return lax.ppermute(value, axis, [((i + offset) % size, i) for i in range(size)])


def quotient(value, by):
    return value >> (by.bit_length() - 1) if by & (by - 1) == 0 else lax.div(value, by)


def remainder(value, by):
    return value & (by - 1) if by & (by - 1) == 0 else lax.rem(value, by)


def write_digits(tile, at, value):
    height, width = value.shape
    tile[at : at + height, :width] = remainder(value, LANES)
    tile[at + height : at + 2 * height, :width] = quotient(value, LANES)


def pack_kernel(sizes, a_rows, a_cols, c_cols, x_in, s_cols, s_in, *refs):
    layers, count, piece_rows, width, local_rows, kept, order, ranges = sizes
    known, s_out, x_out, refs = refs[0], refs[1], refs[2 : 2 + len(ranges)], refs[2 + len(ranges) :]
    rows, cols, kept_held, s_held, x_tile, s_tile, sem = refs
    piece = piece_rows * width
    small = [(a_rows, rows), (a_cols, cols), (c_cols, kept_held), (s_cols, s_held)]
    large = [
        (
            x_in.at[:, pl.ds(first, height)],
            out.at[pl.ds(0, count * height)].reshape(count, height, order),
        )
        for (first, height), out in zip(ranges, x_out)
    ]
    large += [(s_in.at[q], s_out.at[pl.ds(q * order, order)]) for q in range(piece)]
    loads = [
        pltpu.make_async_copy(source, goal, sem.at[p])
        for p, (source, goal) in enumerate(small + large)
    ]
    for load in loads:
        load.start()
    known[...] = jnp.zeros_like(known)
    x_tile[...] = jnp.zeros_like(x_tile)
    s_tile[...] = jnp.zeros_like(s_tile)
    for load in loads[: len(small)]:
        load.wait()
    own_rows = local_rows // layers
    row, col = rows[...], cols[...]
    here = quotient(row[:, :1], local_rows)
    layer = remainder(quotient(col[:, :1], piece_rows), layers)
    owner = quotient(col, piece_rows * layers)
    local = row - here * local_rows
    goal = remainder(quotient(local, own_rows) - layer + layers, layers) * own_rows
    place = (
        ((owner ^ here) * piece_rows + remainder(col, piece_rows)) * width,
        (goal + remainder(local, own_rows)) * kept,
        local,
    )
    for p, value in enumerate(place):
        known[p : p + 1, :count] = value
        write_digits(x_tile, 2 * p, value)
    known[8 : 8 + kept, :local_rows] = kept_held[...]
    write_digits(s_tile, 0, s_held[...])
    x_out[0][count * ranges[0][1] :] = x_tile[...].astype(jnp.float32).astype(jnp.bfloat16)
    s_out[piece * order :] = s_tile[...].astype(jnp.float32).astype(jnp.bfloat16)
    for load in loads[len(small) :]:
        load.wait()


def match(sizes, place, panel_cols, kept_cols, codes):
    width, local_rows, kept = sizes
    right, goal, local = place
    wanted, held = [jnp.zeros_like(right)] * width, [jnp.zeros_like(right)] * kept
    for p in range(panel_cols.shape[0]):
        for s in range(width):
            wanted[s] = jnp.where(right == p * width, panel_cols[p : p + 1, s : s + 1], wanted[s])
    for i in range(local_rows):
        for t in range(kept):
            held[t] = jnp.where(local == i, kept_cols[t : t + 1, i : i + 1], held[t])
    codes[0:1] = right
    for s in range(width):
        slot = jnp.full_like(right, -1)
        for t in range(kept):
            slot = jnp.where(held[t] == wanted[s], goal + t, slot)
        codes[1 + s : 2 + s] = slot


def list_pairs(sizes, codes, pairs):
    count, width, trash = sizes
    total = jnp.int32(0)
    for n in range(count):
        right = codes[0, n]
        for s in range(width):
            slot = codes[1 + s, n]
            pairs[0, total] = n
            pairs[1, total] = right + s
            pairs[2, total] = slot
            total += (slot >= 0).astype(jnp.int32)
    for g in range(GROUP):
        pairs[0, total + g] = 0
        pairs[1, total + g] = 0
        pairs[2, total + g] = trash
    return total


def add_products(left, panel, totals, pairs, total):
    height = totals.shape[1]

    def block(n):
        return left[pl.ds(pl.multiple_of(n * height, height), height)]

    def one_group(group, carry):
        base = group * GROUP
        products = [
            jnp.dot(
                block(pairs[0, base + g]),
                panel[pairs[1, base + g]],
                preferred_element_type=jnp.float32,
            )
            for g in range(GROUP)
        ]
        for g in range(GROUP):
            totals[pairs[2, base + g]] += products[g]
        return carry

    lax.fori_loop(0, quotient(total + GROUP - 1, GROUP), one_group, 0)


def own_kernel(sizes, ranges, known, *refs):
    rows, count, piece_rows, width, local_rows, kept, order = sizes
    x_in, s_in, refs = refs[: len(ranges)], refs[len(ranges) :][:rows], refs[len(ranges) + rows :]
    totals, panel, panel_cols, codes, numbers, pairs, sem = refs
    piece = piece_rows * width
    for d in range(rows):
        tile = s_in[d][piece * order :].astype(jnp.float32).astype(jnp.int32)
        panel_cols[d * piece_rows : (d + 1) * piece_rows] = (
            tile[:piece_rows] + tile[piece_rows : 2 * piece_rows] * LANES
        )
    place = known[0:1], known[1:2], known[2:3]
    match((width, local_rows, kept), place, panel_cols[...], known[8 : 8 + kept], codes)
    copy = pltpu.make_async_copy(codes, numbers, sem)
    copy.start()
    totals[...] = jnp.zeros_like(totals)
    for d in range(rows):
        for q in range(piece):
            panel[d * piece + q] = s_in[d][q * order : (q + 1) * order]
    copy.wait()
    total = list_pairs((count, width, totals.shape[0] - 1), numbers, pairs)
    for (first, height), blocks in zip(ranges, x_in):
        add_products(blocks, panel, totals.at[:, pl.ds(first, height)], pairs, total)


def peer_kernel(sizes, span, *refs):
    cols, layers, count, width, local_rows, kept = sizes
    first, height = span
    slots = local_rows * kept // layers
    if first == 0:
        known, panel_cols, *refs = refs
    else:
        codes, *refs = refs
    x_in, refs = refs[: cols - 1], refs[cols - 1 :]
    panel, before, own, sent, refs = refs[0], refs[1], refs[2], refs[3 : 2 + layers], refs[2 + layers :]
    if first == 0:
        codes, *refs = refs
        for j in range(cols - 1):
            digits = x_in[j][count * height :].astype(jnp.float32).astype(jnp.int32)
            place = [digits[p : p + 1] + digits[p + 1 : p + 2] * LANES for p in (0, 2, 4)]
            match(
                (width, local_rows, kept), place, panel_cols[...], known[8 : 8 + kept], codes.at[j]
            )
    totals, numbers, pairs, sem = refs
    copy = pltpu.make_async_copy(codes, numbers, sem)
    copy.start()
    totals[...] = before[:, first : first + height]
    copy.wait()
    for j in range(cols - 1):
        total = list_pairs((count, width, layers * slots), numbers.at[j], pairs)
        add_products(x_in[j], panel, totals, pairs, total)

    own[...] = totals[:slots]
    half = height // 2
    for d in range(1, layers):
        code = sent[d - 1]
        spare = code.shape[0] - slots * half
        code[slots * half :] = jnp.zeros((spare, code.shape[1]), jnp.int32)
        for u in range(slots):
            value = totals[d * slots + u]
            peak = jnp.max(jnp.abs(value), axis=0, keepdims=True)
            power = jnp.floor(jnp.log2(jnp.maximum(peak, 1e-30)) + 1e-3) + 1.0
            word = jnp.floor(value * jnp.exp2(15.0 - power) + 0.5).astype(jnp.int32)
            code[pl.ds(u * half, half)] = (word[:half] << 16) | (word[half:] & 0xFFFF)
            code[pl.ds(slots * half + u, 1)] = power.astype(jnp.int32)


def finish_kernel(sizes, span, *refs):
    layers, slots = sizes
    first, height = span
    half = height // 2
    before, own, codes, result = refs[: first > 0], refs[-layers - 1], refs[-layers:-1], refs[-1]
    kept = result.shape[1]
    for done in before:
        result[:, :, :first] = done[...]
    for u in range(slots):
        high, low = own[u, :half], own[u, half:]
        for code in codes:
            word = code[pl.ds(u * half, half)]
            power = code[pl.ds(slots * half + u, 1)].astype(jnp.float32)
            scale = jnp.exp2(power - 15.0)
            high += (word >> 16).astype(jnp.float32) * scale
            low += ((word << 16) >> 16).astype(jnp.float32) * scale
        result[u // kept, u % kept, first : first + half] = high.astype(jnp.bfloat16)
        result[u // kept, u % kept, first + half : first + height] = low.astype(jnp.bfloat16)


def per_device(a_blocks, a_rows, a_cols, s_blocks, s_cols, c_cols):
    rows, cols, layers = (lax.axis_size(axis) for axis in ("row", "col", "layer"))
    count, order = a_blocks.shape[:2]
    piece_rows, width = s_cols.shape
    local_rows, kept = c_cols.shape
    own_rows = local_rows // layers
    slots = own_rows * kept
    all_slots = layers * slots
    ranges = row_ranges(order)
    piece = piece_rows * width
    panel_size = rows * piece
    block_size = order * order
    flat_s = s_blocks.reshape(piece, order, order)
    note_height = (2 * piece_rows + 15) // 16 * 16
    code_height = (1 + width + 7) // 8 * 8

    vector = pl.BlockSpec(memory_space=pltpu.VMEM)
    far = pl.BlockSpec(memory_space=HBM)

    known, s_sent, *x_sent = pl.pallas_call(
        functools.partial(
            pack_kernel, (layers, count, piece_rows, width, local_rows, kept, order, ranges)
        ),
        out_shape=[
            jax.ShapeDtypeStruct((16, LANES), jnp.int32),
            jax.ShapeDtypeStruct((piece * order + note_height, order), jnp.bfloat16),
        ]
        + [
            jax.ShapeDtypeStruct((count * height + 16 * (at == 0), order), jnp.bfloat16)
            for at, height in ranges
        ],
        in_specs=[far] * 6,
        out_specs=[vector] * (2 + len(ranges)),
        scratch_shapes=[
            pltpu.VMEM((1, count), jnp.int32),
            pltpu.VMEM((1, count), jnp.int32),
            pltpu.VMEM((kept, local_rows), jnp.int32),
            pltpu.VMEM((piece_rows, width), jnp.int32),
            pltpu.VMEM((16, LANES), jnp.int32),
            pltpu.VMEM((note_height, LANES), jnp.int32),
            pltpu.SemaphoreType.DMA((4 + piece + len(ranges),)),
        ],
        compiler_params=pltpu.CompilerParams(
            vmem_limit_bytes=2 * block_size * (2 * count + piece) + 4 * MIB
        ),
        name="pack",
    )(
        *in_hbm(
            a_rows.reshape(1, count), a_cols.reshape(1, count), c_cols.T, a_blocks, s_cols, flat_s
        )
    )
    x_pieces = [[shifted(part, "col", j) for j in range(1, cols)] for part in x_sent]
    s_pieces = gathered(s_sent, "row")

    moved = block_size * (4 * all_slots + 4 * panel_size + 2 * count)
    totals, panel, panel_cols = pl.pallas_call(
        functools.partial(
            own_kernel, (rows, count, piece_rows, width, local_rows, kept, order), ranges
        ),
        out_shape=[
            jax.ShapeDtypeStruct((all_slots + 1, order, order), jnp.float32),
            jax.ShapeDtypeStruct((panel_size, order, order), jnp.bfloat16),
            jax.ShapeDtypeStruct((rows * piece_rows, LANES), jnp.int32),
        ],
        in_specs=[vector] * (1 + len(ranges) + rows),
        out_specs=[vector] * 3,
        scratch_shapes=[
            pltpu.VMEM((code_height, LANES), jnp.int32),
            pltpu.SMEM((code_height, LANES), jnp.int32),
            pltpu.SMEM((3, count * width + GROUP), jnp.int32),
            pltpu.SemaphoreType.DMA,
        ],
        compiler_params=pltpu.CompilerParams(vmem_limit_bytes=moved + 4 * MIB),
        cost_estimate=pl.CostEstimate(
            flops=2 * order**3 * count * width // 4, bytes_accessed=moved, transcendentals=0
        ),
        name="own_products",
    )(known, *x_sent, *s_pieces)

    moved = block_size * (8 * all_slots + 2 * panel_size + 2 * count * (cols - 1))
    code_shape = (cols - 1, code_height, LANES)
    finished, plan = [], []
    for (at, height), pieces in zip(ranges, x_pieces):
        code_rows = slots * (height // 2) + (slots + 7) // 8 * 8
        out_shape = [jax.ShapeDtypeStruct((slots, height, order), jnp.float32)]
        out_shape += [jax.ShapeDtypeStruct((code_rows, order), jnp.int32)] * (layers - 1)
        if at == 0:
            out_shape.append(jax.ShapeDtypeStruct(code_shape, jnp.int32))
        given = plan or (known, panel_cols)
        out = pl.pallas_call(
            functools.partial(
                peer_kernel, (cols, layers, count, width, local_rows, kept), (at, height)
            ),
            out_shape=out_shape,
            in_specs=[vector] * (len(given) + cols + 1),
            out_specs=[vector] * len(out_shape),
            scratch_shapes=[
                pltpu.VMEM((all_slots + 1, height, order), jnp.float32),
                pltpu.SMEM(code_shape, jnp.int32),
                pltpu.SMEM((3, count * width + GROUP), jnp.int32),
                pltpu.SemaphoreType.DMA,
            ],
            compiler_params=pltpu.CompilerParams(vmem_limit_bytes=moved + 4 * MIB),
            cost_estimate=pl.CostEstimate(
                flops=2 * order**2 * height * count * width // 4 * (cols - 1),
                bytes_accessed=moved // 2,
                transcendentals=0,
            ),
            name=f"peer_products_{at}",
        )(*given, *pieces, panel, totals)
        plan = plan or out[layers:]
        turn = range(layers - 1, 0, -1) if at == 0 else [*range(layers - 2, 0, -1), layers - 1]
        codes = [shifted(out[d], "layer", layers - d) for d in turn]
        finished = [
            pl.pallas_call(
                functools.partial(finish_kernel, (layers, slots), (at, height)),
                out_shape=jax.ShapeDtypeStruct((own_rows, kept, at + height, order), jnp.bfloat16),
                in_specs=[vector] * (len(finished) + layers),
                out_specs=vector,
                compiler_params=pltpu.CompilerParams(
                    vmem_limit_bytes=16 * slots * block_size + 4 * MIB
                ),
                name=f"finish_{at}",
            )(*finished, out[0], *codes)
        ]
    return finished[0]


def solution(mesh):
    placed = (
        P(("row", "col", "layer"), None, None),
        P(("row", "col", "layer")),
        P(("row", "col", "layer")),
        P(("row", "layer"), "col", None, None),
        P(("row", "layer"), "col"),
        P("row", "col"),
    )
    return jax.shard_map(
        per_device,
        mesh=mesh,
        in_specs=placed,
        out_specs=P(("row", "layer"), "col", None, None),
        check_vma=False,
    )
```

```python
import functools

import jax
import jax.numpy as jnp
from jax import lax
from jax.experimental import pallas as pl
from jax.experimental.pallas import tpu as pltpu
from jax.sharding import PartitionSpec as P

GROUP = 4
LANES = 128
MIB = 2**20
HBM = pltpu.MemorySpace.HBM


def row_ranges(order):
    first = order * 5 // 8
    return [(0, first), (first, order - first)]


def in_hbm(*values):
    return [pltpu.with_memory_space_constraint(value, HBM) for value in values]


def flipped(value, axis, bits):
    return lax.ppermute(value, axis, [(i, i ^ bits) for i in range(lax.axis_size(axis))])


def gathered(value, axis):
    values = {0: value}
    bit = lax.axis_size(axis) // 2
    while bit:
        values |= {d ^ bit: flipped(held, axis, bit) for d, held in values.items()}
        bit //= 2
    return [values[d] for d in range(len(values))]


def shifted(value, axis, offset):
    size = lax.axis_size(axis)
    return lax.ppermute(value, axis, [((i + offset) % size, i) for i in range(size)])


def quotient(value, by):
    return value >> (by.bit_length() - 1) if by & (by - 1) == 0 else lax.div(value, by)


def remainder(value, by):
    return value & (by - 1) if by & (by - 1) == 0 else lax.rem(value, by)


def write_digits(tile, at, value):
    height, width = value.shape
    tile[at : at + height, :width] = remainder(value, LANES)
    tile[at + height : at + 2 * height, :width] = quotient(value, LANES)


def pack_kernel(sizes, a_rows, a_cols, c_cols, x_in, s_cols, s_in, *refs):
    layers, count, piece_rows, width, local_rows, kept, order, ranges = sizes
    known, s_out, x_out, refs = refs[0], refs[1], refs[2 : 2 + len(ranges)], refs[2 + len(ranges) :]
    rows, cols, kept_held, s_held, x_tile, s_tile, sem = refs
    piece = piece_rows * width
    small = [(a_rows, rows), (a_cols, cols), (c_cols, kept_held), (s_cols, s_held)]
    large = [
        (
            x_in.at[:, pl.ds(first, height)],
            out.at[pl.ds(0, count * height)].reshape(count, height, order),
        )
        for (first, height), out in zip(ranges, x_out)
    ]
    large += [(s_in.at[q], s_out.at[pl.ds(q * order, order)]) for q in range(piece)]
    loads = [
        pltpu.make_async_copy(source, goal, sem.at[p])
        for p, (source, goal) in enumerate(small + large)
    ]
    for load in loads:
        load.start()
    known[...] = jnp.zeros_like(known)
    x_tile[...] = jnp.zeros_like(x_tile)
    s_tile[...] = jnp.zeros_like(s_tile)
    for load in loads[: len(small)]:
        load.wait()
    own_rows = local_rows // layers
    row, col = rows[...], cols[...]
    here = quotient(row[:, :1], local_rows)
    layer = remainder(quotient(col[:, :1], piece_rows), layers)
    owner = quotient(col, piece_rows * layers)
    local = row - here * local_rows
    goal = remainder(quotient(local, own_rows) - layer + layers, layers) * own_rows
    place = (
        ((owner ^ here) * piece_rows + remainder(col, piece_rows)) * width,
        (goal + remainder(local, own_rows)) * kept,
        local,
    )
    for p, value in enumerate(place):
        known[p : p + 1, :count] = value
        write_digits(x_tile, 2 * p, value)
    known[8 : 8 + kept, :local_rows] = kept_held[...]
    write_digits(s_tile, 0, s_held[...])
    x_out[0][count * ranges[0][1] :] = x_tile[...].astype(jnp.float32).astype(jnp.bfloat16)
    s_out[piece * order :] = s_tile[...].astype(jnp.float32).astype(jnp.bfloat16)
    for load in loads[len(small) :]:
        load.wait()


def match(sizes, place, panel_cols, kept_cols, codes):
    width, local_rows, kept = sizes
    right, goal, local = place
    wanted, held = [jnp.zeros_like(right)] * width, [jnp.zeros_like(right)] * kept
    for p in range(panel_cols.shape[0]):
        for s in range(width):
            wanted[s] = jnp.where(right == p * width, panel_cols[p : p + 1, s : s + 1], wanted[s])
    for i in range(local_rows):
        for t in range(kept):
            held[t] = jnp.where(local == i, kept_cols[t : t + 1, i : i + 1], held[t])
    codes[0:1] = right
    for s in range(width):
        slot = jnp.full_like(right, -1)
        for t in range(kept):
            slot = jnp.where(held[t] == wanted[s], goal + t, slot)
        codes[1 + s : 2 + s] = slot


def list_pairs(sizes, codes, pairs):
    count, width, trash = sizes
    total = jnp.int32(0)
    for n in range(count):
        right = codes[0, n]
        for s in range(width):
            slot = codes[1 + s, n]
            pairs[0, total] = n
            pairs[1, total] = right + s
            pairs[2, total] = slot
            total += (slot >= 0).astype(jnp.int32)
    for g in range(GROUP):
        pairs[0, total + g] = 0
        pairs[1, total + g] = 0
        pairs[2, total + g] = trash
    return total


def add_products(left, panel, totals, pairs, total):
    height = totals.shape[1]

    def block(n):
        return left[pl.ds(pl.multiple_of(n * height, height), height)]

    def one_group(group, carry):
        base = group * GROUP
        products = [
            jnp.dot(
                block(pairs[0, base + g]),
                panel[pairs[1, base + g]],
                preferred_element_type=jnp.float32,
            )
            for g in range(GROUP)
        ]
        for g in range(GROUP):
            totals[pairs[2, base + g]] += products[g]
        return carry

    lax.fori_loop(0, quotient(total + GROUP - 1, GROUP), one_group, 0)


def own_kernel(sizes, ranges, known, *refs):
    rows, count, piece_rows, width, local_rows, kept, order = sizes
    x_in, s_in, refs = refs[: len(ranges)], refs[len(ranges) :][:rows], refs[len(ranges) + rows :]
    totals, panel, panel_cols, codes, numbers, pairs, sem = refs
    piece = piece_rows * width
    for d in range(rows):
        tile = s_in[d][piece * order :].astype(jnp.float32).astype(jnp.int32)
        panel_cols[d * piece_rows : (d + 1) * piece_rows] = (
            tile[:piece_rows] + tile[piece_rows : 2 * piece_rows] * LANES
        )
    place = known[0:1], known[1:2], known[2:3]
    match((width, local_rows, kept), place, panel_cols[...], known[8 : 8 + kept], codes)
    copy = pltpu.make_async_copy(codes, numbers, sem)
    copy.start()
    totals[...] = jnp.zeros_like(totals)
    for d in range(rows):
        for q in range(piece):
            panel[d * piece + q] = s_in[d][q * order : (q + 1) * order]
    copy.wait()
    total = list_pairs((count, width, totals.shape[0] - 1), numbers, pairs)
    for (first, height), blocks in zip(ranges, x_in):
        add_products(blocks, panel, totals.at[:, pl.ds(first, height)], pairs, total)


def peer_kernel(sizes, span, *refs):
    cols, layers, count, width, local_rows, kept = sizes
    first, height = span
    slots = local_rows * kept // layers
    if first == 0:
        known, panel_cols, *refs = refs
    else:
        codes, *refs = refs
    x_in, refs = refs[: cols - 1], refs[cols - 1 :]
    panel, before, own, sent, refs = refs[0], refs[1], refs[2], refs[3 : 2 + layers], refs[2 + layers :]
    if first == 0:
        codes, *refs = refs
        for j in range(cols - 1):
            digits = x_in[j][count * height :].astype(jnp.float32).astype(jnp.int32)
            place = [digits[p : p + 1] + digits[p + 1 : p + 2] * LANES for p in (0, 2, 4)]
            match(
                (width, local_rows, kept), place, panel_cols[...], known[8 : 8 + kept], codes.at[j]
            )
    totals, numbers, pairs, sem = refs
    copy = pltpu.make_async_copy(codes, numbers, sem)
    copy.start()
    totals[...] = before[:, first : first + height]
    copy.wait()
    for j in range(cols - 1):
        total = list_pairs((count, width, layers * slots), numbers.at[j], pairs)
        add_products(x_in[j], panel, totals, pairs, total)

    own[...] = totals[:slots]
    half = height // 2
    for d in range(1, layers):
        code = sent[d - 1]
        spare = code.shape[0] - slots * half
        code[slots * half :] = jnp.zeros((spare, code.shape[1]), jnp.int32)
        for u in range(slots):
            value = totals[d * slots + u]
            peak = jnp.max(jnp.abs(value), axis=0, keepdims=True)
            power = jnp.floor(jnp.log2(jnp.maximum(peak, 1e-30)) + 1e-3) + 1.0
            word = jnp.floor(value * jnp.exp2(15.0 - power) + 0.5).astype(jnp.int32)
            code[pl.ds(u * half, half)] = (word[:half] << 16) | (word[half:] & 0xFFFF)
            code[pl.ds(slots * half + u, 1)] = power.astype(jnp.int32)


def finish_kernel(sizes, span, *refs):
    layers, slots = sizes
    first, height = span
    half = height // 2
    before, own, codes, result = refs[: first > 0], refs[-layers - 1], refs[-layers:-1], refs[-1]
    kept = result.shape[1]
    for done in before:
        result[:, :, :first] = done[...]
    for u in range(slots):
        high, low = own[u, :half], own[u, half:]
        for code in codes:
            word = code[pl.ds(u * half, half)]
            power = code[pl.ds(slots * half + u, 1)].astype(jnp.float32)
            scale = jnp.exp2(power - 15.0)
            high += (word >> 16).astype(jnp.float32) * scale
            low += ((word << 16) >> 16).astype(jnp.float32) * scale
        result[u // kept, u % kept, first : first + half] = high.astype(jnp.bfloat16)
        result[u // kept, u % kept, first + half : first + height] = low.astype(jnp.bfloat16)


def per_device(a_blocks, a_rows, a_cols, s_blocks, s_cols, c_cols):
    rows, cols, layers = (lax.axis_size(axis) for axis in ("row", "col", "layer"))
    count, order = a_blocks.shape[:2]
    piece_rows, width = s_cols.shape
    local_rows, kept = c_cols.shape
    own_rows = local_rows // layers
    slots = own_rows * kept
    all_slots = layers * slots
    ranges = row_ranges(order)
    piece = piece_rows * width
    panel_size = rows * piece
    block_size = order * order
    flat_s = s_blocks.reshape(piece, order, order)
    note_height = (2 * piece_rows + 15) // 16 * 16
    code_height = (1 + width + 7) // 8 * 8

    vector = pl.BlockSpec(memory_space=pltpu.VMEM)
    far = pl.BlockSpec(memory_space=HBM)

    known, s_sent, *x_sent = pl.pallas_call(
        functools.partial(
            pack_kernel, (layers, count, piece_rows, width, local_rows, kept, order, ranges)
        ),
        out_shape=[
            jax.ShapeDtypeStruct((16, LANES), jnp.int32),
            jax.ShapeDtypeStruct((piece * order + note_height, order), jnp.bfloat16),
        ]
        + [
            jax.ShapeDtypeStruct((count * height + 16 * (at == 0), order), jnp.bfloat16)
            for at, height in ranges
        ],
        in_specs=[far] * 6,
        out_specs=[vector] * (2 + len(ranges)),
        scratch_shapes=[
            pltpu.VMEM((1, count), jnp.int32),
            pltpu.VMEM((1, count), jnp.int32),
            pltpu.VMEM((kept, local_rows), jnp.int32),
            pltpu.VMEM((piece_rows, width), jnp.int32),
            pltpu.VMEM((16, LANES), jnp.int32),
            pltpu.VMEM((note_height, LANES), jnp.int32),
            pltpu.SemaphoreType.DMA((4 + piece + len(ranges),)),
        ],
        compiler_params=pltpu.CompilerParams(
            vmem_limit_bytes=2 * block_size * (2 * count + piece) + 4 * MIB
        ),
        name="pack",
    )(
        *in_hbm(
            a_rows.reshape(1, count), a_cols.reshape(1, count), c_cols.T, a_blocks, s_cols, flat_s
        )
    )
    s_pieces = gathered(s_sent, "row")
    later, _ = lax.optimization_barrier((x_sent[1:], s_pieces))
    x_pieces = [
        [shifted(part, "col", j) for j in range(1, cols)] for part in (x_sent[0], *later)
    ]

    moved = block_size * (4 * all_slots + 4 * panel_size + 2 * count)
    totals, panel, panel_cols = pl.pallas_call(
        functools.partial(
            own_kernel, (rows, count, piece_rows, width, local_rows, kept, order), ranges
        ),
        out_shape=[
            jax.ShapeDtypeStruct((all_slots + 1, order, order), jnp.float32),
            jax.ShapeDtypeStruct((panel_size, order, order), jnp.bfloat16),
            jax.ShapeDtypeStruct((rows * piece_rows, LANES), jnp.int32),
        ],
        in_specs=[vector] * (1 + len(ranges) + rows),
        out_specs=[vector] * 3,
        scratch_shapes=[
            pltpu.VMEM((code_height, LANES), jnp.int32),
            pltpu.SMEM((code_height, LANES), jnp.int32),
            pltpu.SMEM((3, count * width + GROUP), jnp.int32),
            pltpu.SemaphoreType.DMA,
        ],
        compiler_params=pltpu.CompilerParams(vmem_limit_bytes=moved + 4 * MIB),
        cost_estimate=pl.CostEstimate(
            flops=2 * order**3 * count * width // 4, bytes_accessed=moved, transcendentals=0
        ),
        name="own_products",
    )(known, *x_sent, *s_pieces)

    moved = block_size * (8 * all_slots + 2 * panel_size + 2 * count * (cols - 1))
    code_shape = (cols - 1, code_height, LANES)
    finished, plan = [], []
    for (at, height), pieces in zip(ranges, x_pieces):
        code_rows = slots * (height // 2) + (slots + 7) // 8 * 8
        out_shape = [jax.ShapeDtypeStruct((slots, height, order), jnp.float32)]
        out_shape += [jax.ShapeDtypeStruct((code_rows, order), jnp.int32)] * (layers - 1)
        if at == 0:
            out_shape.append(jax.ShapeDtypeStruct(code_shape, jnp.int32))
        given = plan or (known, panel_cols)
        out = pl.pallas_call(
            functools.partial(
                peer_kernel, (cols, layers, count, width, local_rows, kept), (at, height)
            ),
            out_shape=out_shape,
            in_specs=[vector] * (len(given) + cols + 1),
            out_specs=[vector] * len(out_shape),
            scratch_shapes=[
                pltpu.VMEM((all_slots + 1, height, order), jnp.float32),
                pltpu.SMEM(code_shape, jnp.int32),
                pltpu.SMEM((3, count * width + GROUP), jnp.int32),
                pltpu.SemaphoreType.DMA,
            ],
            compiler_params=pltpu.CompilerParams(vmem_limit_bytes=moved + 4 * MIB),
            cost_estimate=pl.CostEstimate(
                flops=2 * order**2 * height * count * width // 4 * (cols - 1),
                bytes_accessed=moved // 2,
                transcendentals=0,
            ),
            name=f"peer_products_{at}",
        )(*given, *pieces, panel, totals)
        plan = plan or out[layers:]
        codes = [shifted(out[d], "layer", layers - d) for d in range(1, layers)]
        finished = [
            pl.pallas_call(
                functools.partial(finish_kernel, (layers, slots), (at, height)),
                out_shape=jax.ShapeDtypeStruct((own_rows, kept, at + height, order), jnp.bfloat16),
                in_specs=[vector] * (len(finished) + layers),
                out_specs=vector,
                compiler_params=pltpu.CompilerParams(
                    vmem_limit_bytes=16 * slots * block_size + 4 * MIB
                ),
                name=f"finish_{at}",
            )(*finished, out[0], *codes)
        ]
    return finished[0]


def solution(mesh):
    placed = (
        P(("row", "col", "layer"), None, None),
        P(("row", "col", "layer")),
        P(("row", "col", "layer")),
        P(("row", "layer"), "col", None, None),
        P(("row", "layer"), "col"),
        P("row", "col"),
    )
    return jax.shard_map(
        per_device,
        mesh=mesh,
        in_specs=placed,
        out_specs=P(("row", "layer"), "col", None, None),
        check_vma=False,
    )
```

```python
import functools

import jax
import jax.numpy as jnp
from jax import lax
from jax.experimental import pallas as pl
from jax.experimental.pallas import tpu as pltpu
from jax.sharding import PartitionSpec as P

GROUP = 8
LANES = 128
MIB = 2**20
HBM = pltpu.MemorySpace.HBM


def row_ranges(order):
    first = order * 5 // 8
    return [(0, first), (first, order - first)]


def in_hbm(*values):
    return [pltpu.with_memory_space_constraint(value, HBM) for value in values]


def flipped(value, axis, bits):
    return lax.ppermute(value, axis, [(i, i ^ bits) for i in range(lax.axis_size(axis))])


def gathered(value, axis):
    values = {0: value}
    bit = lax.axis_size(axis) // 2
    while bit:
        values |= {d ^ bit: flipped(held, axis, bit) for d, held in values.items()}
        bit //= 2
    return [values[d] for d in range(len(values))]


def shifted(value, axis, offset):
    size = lax.axis_size(axis)
    return lax.ppermute(value, axis, [((i + offset) % size, i) for i in range(size)])


def quotient(value, by):
    return value >> (by.bit_length() - 1) if by & (by - 1) == 0 else lax.div(value, by)


def remainder(value, by):
    return value & (by - 1) if by & (by - 1) == 0 else lax.rem(value, by)


def write_digits(tile, at, value):
    height, width = value.shape
    tile[at : at + height, :width] = remainder(value, LANES)
    tile[at + height : at + 2 * height, :width] = quotient(value, LANES)


def pack_kernel(sizes, a_rows, a_cols, c_cols, x_in, s_cols, s_in, *refs):
    layers, count, piece_rows, width, local_rows, kept, order, ranges = sizes
    known, s_out, x_out, refs = refs[0], refs[1], refs[2 : 2 + len(ranges)], refs[2 + len(ranges) :]
    rows, cols, kept_held, s_held, x_tile, s_tile, sem = refs
    piece = piece_rows * width
    small = [(a_rows, rows), (a_cols, cols), (c_cols, kept_held), (s_cols, s_held)]
    large = [
        (
            x_in.at[:, pl.ds(first, height)],
            out.at[pl.ds(0, count * height)].reshape(count, height, order),
        )
        for (first, height), out in zip(ranges, x_out)
    ]
    large += [(s_in.at[q], s_out.at[pl.ds(q * order, order)]) for q in range(piece)]
    loads = [
        pltpu.make_async_copy(source, goal, sem.at[p])
        for p, (source, goal) in enumerate(small + large)
    ]
    for load in loads:
        load.start()
    known[...] = jnp.zeros_like(known)
    x_tile[...] = jnp.zeros_like(x_tile)
    s_tile[...] = jnp.zeros_like(s_tile)
    for load in loads[: len(small)]:
        load.wait()
    own_rows = local_rows // layers
    row, col = rows[...], cols[...]
    here = quotient(row[:, :1], local_rows)
    layer = remainder(quotient(col[:, :1], piece_rows), layers)
    owner = quotient(col, piece_rows * layers)
    local = row - here * local_rows
    goal = remainder(quotient(local, own_rows) - layer + layers, layers) * own_rows
    place = (
        ((owner ^ here) * piece_rows + remainder(col, piece_rows)) * width,
        (goal + remainder(local, own_rows)) * kept,
        local,
    )
    for p, value in enumerate(place):
        known[p : p + 1, :count] = value
        write_digits(x_tile, 2 * p, value)
    known[8 : 8 + kept, :local_rows] = kept_held[...]
    write_digits(s_tile, 0, s_held[...])
    x_out[0][count * ranges[0][1] :] = x_tile[...].astype(jnp.float32).astype(jnp.bfloat16)
    s_out[piece * order :] = s_tile[...].astype(jnp.float32).astype(jnp.bfloat16)
    for load in loads[len(small) :]:
        load.wait()


def match(sizes, place, panel_cols, kept_cols, codes):
    width, local_rows, kept = sizes
    right, goal, local = place
    wanted, held = [jnp.zeros_like(right)] * width, [jnp.zeros_like(right)] * kept
    for p in range(panel_cols.shape[0]):
        for s in range(width):
            wanted[s] = jnp.where(right == p * width, panel_cols[p : p + 1, s : s + 1], wanted[s])
    for i in range(local_rows):
        for t in range(kept):
            held[t] = jnp.where(local == i, kept_cols[t : t + 1, i : i + 1], held[t])
    codes[0:1] = right
    for s in range(width):
        slot = jnp.full_like(right, -1)
        for t in range(kept):
            slot = jnp.where(held[t] == wanted[s], goal + t, slot)
        codes[1 + s : 2 + s] = slot


def list_pairs(sizes, codes, pairs):
    count, width, trash = sizes
    total = jnp.int32(0)
    for n in range(count):
        right = codes[0, n]
        for s in range(width):
            slot = codes[1 + s, n]
            pairs[0, total] = n
            pairs[1, total] = right + s
            pairs[2, total] = slot
            total += (slot >= 0).astype(jnp.int32)
    for g in range(GROUP):
        pairs[0, total + g] = 0
        pairs[1, total + g] = 0
        pairs[2, total + g] = trash
    return total


def add_products(left, panel, totals, pairs, total):
    height = totals.shape[1]

    def block(n):
        return left[pl.ds(pl.multiple_of(n * height, height), height)]

    def one_group(group, carry):
        base = group * GROUP
        products = [
            jnp.dot(
                block(pairs[0, base + g]),
                panel[pairs[1, base + g]],
                preferred_element_type=jnp.float32,
            )
            for g in range(GROUP)
        ]
        for g in range(GROUP):
            totals[pairs[2, base + g]] += products[g]
        return carry

    lax.fori_loop(0, quotient(total + GROUP - 1, GROUP), one_group, 0)


def own_kernel(sizes, ranges, known, *refs):
    rows, count, piece_rows, width, local_rows, kept, order = sizes
    x_in, s_in, refs = refs[: len(ranges)], refs[len(ranges) :][:rows], refs[len(ranges) + rows :]
    totals, panel, panel_cols, codes, numbers, pairs, sem = refs
    piece = piece_rows * width
    for d in range(rows):
        tile = s_in[d][piece * order :].astype(jnp.float32).astype(jnp.int32)
        panel_cols[d * piece_rows : (d + 1) * piece_rows] = (
            tile[:piece_rows] + tile[piece_rows : 2 * piece_rows] * LANES
        )
    place = known[0:1], known[1:2], known[2:3]
    match((width, local_rows, kept), place, panel_cols[...], known[8 : 8 + kept], codes)
    copy = pltpu.make_async_copy(codes, numbers, sem)
    copy.start()
    totals[...] = jnp.zeros_like(totals)
    for d in range(rows):
        for q in range(piece):
            panel[d * piece + q] = s_in[d][q * order : (q + 1) * order]
    copy.wait()
    total = list_pairs((count, width, totals.shape[0] - 1), numbers, pairs)
    for (first, height), blocks in zip(ranges, x_in):
        add_products(blocks, panel, totals.at[:, pl.ds(first, height)], pairs, total)


def peer_kernel(sizes, span, *refs):
    cols, layers, count, width, local_rows, kept = sizes
    first, height = span
    slots = local_rows * kept // layers
    if first == 0:
        known, panel_cols, *refs = refs
    else:
        codes, *refs = refs
    x_in, refs = refs[: cols - 1], refs[cols - 1 :]
    panel, before, own, sent, refs = refs[0], refs[1], refs[2], refs[3 : 2 + layers], refs[2 + layers :]
    if first == 0:
        codes, *refs = refs
        for j in range(cols - 1):
            digits = x_in[j][count * height :].astype(jnp.float32).astype(jnp.int32)
            place = [digits[p : p + 1] + digits[p + 1 : p + 2] * LANES for p in (0, 2, 4)]
            match(
                (width, local_rows, kept), place, panel_cols[...], known[8 : 8 + kept], codes.at[j]
            )
    totals, numbers, pairs, sem = refs
    copy = pltpu.make_async_copy(codes, numbers, sem)
    copy.start()
    totals[...] = before[:, first : first + height]
    copy.wait()
    for j in range(cols - 1):
        total = list_pairs((count, width, layers * slots), numbers.at[j], pairs)
        add_products(x_in[j], panel, totals, pairs, total)

    own[...] = totals[:slots]
    half = height // 2
    sublane = lax.broadcasted_iota(jnp.int32, (8, totals.shape[2]), 0)
    for d in range(1, layers):
        code = sent[d - 1]
        for u in range(slots):
            value = totals[d * slots + u]
            peak = jnp.max(jnp.abs(value), axis=0, keepdims=True)
            power = jnp.floor(jnp.log2(jnp.maximum(peak, 1e-30)) + 1e-3) + 1.0
            whole = jnp.floor(value * jnp.exp2(15.0 - power) + 0.5).astype(jnp.int32)
            word = (whole[:half] << 16) | (whole[half:] & 0xFFFF)
            bits = ((power.astype(jnp.int32) + 128) >> sublane) & 1
            code[pl.ds(u * half, 8)] = (word[:8] & ~1) | bits
            code[pl.ds(u * half + 8, half - 8)] = word[8:]


def finish_kernel(sizes, span, *refs):
    layers, slots = sizes
    first, height = span
    half = height // 2
    sublane = lax.broadcasted_iota(jnp.int32, (8, refs[-1].shape[3]), 0)
    before, own, codes, result = refs[: first > 0], refs[-layers - 1], refs[-layers:-1], refs[-1]
    kept = result.shape[1]
    for done in before:
        result[:, :, :first] = done[...]
    for u in range(slots):
        high, low = own[u, :half], own[u, half:]
        for code in codes:
            word = code[pl.ds(u * half, half)]
            power = jnp.sum((word[:8] & 1) << sublane, axis=0, keepdims=True).astype(jnp.float32)
            scale = jnp.exp2(power - (128.0 + 15.0))
            high += (word >> 16).astype(jnp.float32) * scale
            low += ((word << 16) >> 16).astype(jnp.float32) * scale
        result[u // kept, u % kept, first : first + half] = high.astype(jnp.bfloat16)
        result[u // kept, u % kept, first + half : first + height] = low.astype(jnp.bfloat16)


def per_device(a_blocks, a_rows, a_cols, s_blocks, s_cols, c_cols):
    rows, cols, layers = (lax.axis_size(axis) for axis in ("row", "col", "layer"))
    count, order = a_blocks.shape[:2]
    piece_rows, width = s_cols.shape
    local_rows, kept = c_cols.shape
    own_rows = local_rows // layers
    slots = own_rows * kept
    all_slots = layers * slots
    ranges = row_ranges(order)
    piece = piece_rows * width
    panel_size = rows * piece
    block_size = order * order
    flat_s = s_blocks.reshape(piece, order, order)
    note_height = (2 * piece_rows + 15) // 16 * 16
    code_height = (1 + width + 7) // 8 * 8

    vector = pl.BlockSpec(memory_space=pltpu.VMEM)
    far = pl.BlockSpec(memory_space=HBM)

    known, s_sent, *x_sent = pl.pallas_call(
        functools.partial(
            pack_kernel, (layers, count, piece_rows, width, local_rows, kept, order, ranges)
        ),
        out_shape=[
            jax.ShapeDtypeStruct((16, LANES), jnp.int32),
            jax.ShapeDtypeStruct((piece * order + note_height, order), jnp.bfloat16),
        ]
        + [
            jax.ShapeDtypeStruct((count * height + 16 * (at == 0), order), jnp.bfloat16)
            for at, height in ranges
        ],
        in_specs=[far] * 6,
        out_specs=[vector] * (2 + len(ranges)),
        scratch_shapes=[
            pltpu.VMEM((1, count), jnp.int32),
            pltpu.VMEM((1, count), jnp.int32),
            pltpu.VMEM((kept, local_rows), jnp.int32),
            pltpu.VMEM((piece_rows, width), jnp.int32),
            pltpu.VMEM((16, LANES), jnp.int32),
            pltpu.VMEM((note_height, LANES), jnp.int32),
            pltpu.SemaphoreType.DMA((4 + piece + len(ranges),)),
        ],
        compiler_params=pltpu.CompilerParams(
            vmem_limit_bytes=2 * block_size * (2 * count + piece) + 4 * MIB
        ),
        name="pack",
    )(
        *in_hbm(
            a_rows.reshape(1, count), a_cols.reshape(1, count), c_cols.T, a_blocks, s_cols, flat_s
        )
    )
    s_pieces = gathered(s_sent, "row")
    later, _ = lax.optimization_barrier((x_sent[1:], s_pieces))
    x_pieces = [
        [shifted(part, "col", j) for j in range(1, cols)] for part in (x_sent[0], *later)
    ]

    moved = block_size * (4 * all_slots + 4 * panel_size + 2 * count)
    totals, panel, panel_cols = pl.pallas_call(
        functools.partial(
            own_kernel, (rows, count, piece_rows, width, local_rows, kept, order), ranges
        ),
        out_shape=[
            jax.ShapeDtypeStruct((all_slots + 1, order, order), jnp.float32),
            jax.ShapeDtypeStruct((panel_size, order, order), jnp.bfloat16),
            jax.ShapeDtypeStruct((rows * piece_rows, LANES), jnp.int32),
        ],
        in_specs=[vector] * (1 + len(ranges) + rows),
        out_specs=[vector] * 3,
        scratch_shapes=[
            pltpu.VMEM((code_height, LANES), jnp.int32),
            pltpu.SMEM((code_height, LANES), jnp.int32),
            pltpu.SMEM((3, count * width + GROUP), jnp.int32),
            pltpu.SemaphoreType.DMA,
        ],
        compiler_params=pltpu.CompilerParams(vmem_limit_bytes=moved + 4 * MIB),
        cost_estimate=pl.CostEstimate(
            flops=2 * order**3 * count * width // 4, bytes_accessed=moved, transcendentals=0
        ),
        name="own_products",
    )(known, *x_sent, *s_pieces)

    moved = block_size * (8 * all_slots + 2 * panel_size + 2 * count * (cols - 1))
    code_shape = (cols - 1, code_height, LANES)
    finished, plan = [], []
    for (at, height), pieces in zip(ranges, x_pieces):
        code_rows = slots * (height // 2)
        out_shape = [jax.ShapeDtypeStruct((slots, height, order), jnp.float32)]
        out_shape += [jax.ShapeDtypeStruct((code_rows, order), jnp.int32)] * (layers - 1)
        if at == 0:
            out_shape.append(jax.ShapeDtypeStruct(code_shape, jnp.int32))
        given = plan or (known, panel_cols)
        out = pl.pallas_call(
            functools.partial(
                peer_kernel, (cols, layers, count, width, local_rows, kept), (at, height)
            ),
            out_shape=out_shape,
            in_specs=[vector] * (len(given) + cols + 1),
            out_specs=[vector] * len(out_shape),
            scratch_shapes=[
                pltpu.VMEM((all_slots + 1, height, order), jnp.float32),
                pltpu.SMEM(code_shape, jnp.int32),
                pltpu.SMEM((3, count * width + GROUP), jnp.int32),
                pltpu.SemaphoreType.DMA,
            ],
            compiler_params=pltpu.CompilerParams(vmem_limit_bytes=moved + 4 * MIB),
            cost_estimate=pl.CostEstimate(
                flops=2 * order**2 * height * count * width // 4 * (cols - 1),
                bytes_accessed=moved // 2,
                transcendentals=0,
            ),
            name=f"peer_products_{at}",
        )(*given, *pieces, panel, totals)
        plan = plan or out[layers:]
        codes = [shifted(out[d], "layer", layers - d) for d in range(1, layers)]
        finished = [
            pl.pallas_call(
                functools.partial(finish_kernel, (layers, slots), (at, height)),
                out_shape=jax.ShapeDtypeStruct((own_rows, kept, at + height, order), jnp.bfloat16),
                in_specs=[vector] * (len(finished) + layers),
                out_specs=vector,
                compiler_params=pltpu.CompilerParams(
                    vmem_limit_bytes=16 * slots * block_size + 4 * MIB
                ),
                name=f"finish_{at}",
            )(*finished, out[0], *codes)
        ]
    return finished[0]


def solution(mesh):
    placed = (
        P(("row", "col", "layer"), None, None),
        P(("row", "col", "layer")),
        P(("row", "col", "layer")),
        P(("row", "layer"), "col", None, None),
        P(("row", "layer"), "col"),
        P("row", "col"),
    )
    return jax.shard_map(
        per_device,
        mesh=mesh,
        in_specs=placed,
        out_specs=P(("row", "layer"), "col", None, None),
        check_vma=False,
    )
```

```python
import functools

import jax
import jax.numpy as jnp
from jax import lax
from jax.experimental import pallas as pl
from jax.experimental.pallas import tpu as pltpu
from jax.sharding import PartitionSpec as P

GROUP = 8
LANES = 128
MIB = 2**20
HBM = pltpu.MemorySpace.HBM


def row_ranges(order):
    first = order * 5 // 8
    return [(0, first), (first, order - first)]


def in_hbm(*values):
    return [pltpu.with_memory_space_constraint(value, HBM) for value in values]


def flipped(value, axis, bits):
    return lax.ppermute(value, axis, [(i, i ^ bits) for i in range(lax.axis_size(axis))])


def gathered(value, axis):
    values = {0: value}
    bit = lax.axis_size(axis) // 2
    while bit:
        values |= {d ^ bit: flipped(held, axis, bit) for d, held in values.items()}
        bit //= 2
    return [values[d] for d in range(len(values))]


def shifted(value, axis, offset):
    size = lax.axis_size(axis)
    return lax.ppermute(value, axis, [((i + offset) % size, i) for i in range(size)])


def quotient(value, by):
    return value >> (by.bit_length() - 1) if by & (by - 1) == 0 else lax.div(value, by)


def remainder(value, by):
    return value & (by - 1) if by & (by - 1) == 0 else lax.rem(value, by)


def write_digits(tile, at, value):
    height, width = value.shape
    tile[at : at + height, :width] = remainder(value, LANES)
    tile[at + height : at + 2 * height, :width] = quotient(value, LANES)


def pack_kernel(sizes, a_rows, a_cols, c_cols, x_in, s_cols, s_in, *refs):
    layers, count, piece_rows, width, local_rows, kept, order, ranges = sizes
    known, s_out, x_out, refs = refs[0], refs[1], refs[2 : 2 + len(ranges)], refs[2 + len(ranges) :]
    rows, cols, kept_held, s_held, x_tile, s_tile, sem = refs
    piece = piece_rows * width
    small = [(a_rows, rows), (a_cols, cols), (c_cols, kept_held), (s_cols, s_held)]
    large = [
        (
            x_in.at[:, pl.ds(first, height)],
            out.at[pl.ds(0, count * height)].reshape(count, height, order),
        )
        for (first, height), out in zip(ranges, x_out)
    ]
    large += [(s_in.at[q], s_out.at[pl.ds(q * order, order)]) for q in range(piece)]
    loads = [
        pltpu.make_async_copy(source, goal, sem.at[p])
        for p, (source, goal) in enumerate(small + large)
    ]
    for load in loads:
        load.start()
    known[...] = jnp.zeros_like(known)
    x_tile[...] = jnp.zeros_like(x_tile)
    s_tile[...] = jnp.zeros_like(s_tile)
    for load in loads[: len(small)]:
        load.wait()
    own_rows = local_rows // layers
    row, col = rows[...], cols[...]
    here = quotient(row[:, :1], local_rows)
    layer = remainder(quotient(col[:, :1], piece_rows), layers)
    owner = quotient(col, piece_rows * layers)
    local = row - here * local_rows
    goal = (quotient(local, own_rows) ^ layer) * own_rows
    place = (
        ((owner ^ here) * piece_rows + remainder(col, piece_rows)) * width,
        (goal + remainder(local, own_rows)) * kept,
        local,
    )
    for p, value in enumerate(place):
        known[p : p + 1, :count] = value
        write_digits(x_tile, 2 * p, value)
    known[8 : 8 + kept, :local_rows] = kept_held[...]
    write_digits(s_tile, 0, s_held[...])
    x_out[0][count * ranges[0][1] :] = x_tile[...].astype(jnp.float32).astype(jnp.bfloat16)
    s_out[piece * order :] = s_tile[...].astype(jnp.float32).astype(jnp.bfloat16)
    for load in loads[len(small) :]:
        load.wait()


def match(sizes, place, panel_cols, kept_cols, codes):
    width, local_rows, kept = sizes
    right, goal, local = place
    wanted, held = [jnp.zeros_like(right)] * width, [jnp.zeros_like(right)] * kept
    for p in range(panel_cols.shape[0]):
        for s in range(width):
            wanted[s] = jnp.where(right == p * width, panel_cols[p : p + 1, s : s + 1], wanted[s])
    for i in range(local_rows):
        for t in range(kept):
            held[t] = jnp.where(local == i, kept_cols[t : t + 1, i : i + 1], held[t])
    codes[0:1] = right
    for s in range(width):
        slot = jnp.full_like(right, -1)
        for t in range(kept):
            slot = jnp.where(held[t] == wanted[s], goal + t, slot)
        codes[1 + s : 2 + s] = slot


def list_pairs(sizes, codes, pairs):
    count, width, trash = sizes
    total = jnp.int32(0)
    for n in range(count):
        right = codes[0, n]
        for s in range(width):
            slot = codes[1 + s, n]
            pairs[0, total] = n
            pairs[1, total] = right + s
            pairs[2, total] = slot
            total += (slot >= 0).astype(jnp.int32)
    for g in range(GROUP):
        pairs[0, total + g] = 0
        pairs[1, total + g] = 0
        pairs[2, total + g] = trash
    return total


def add_products(left, panel, totals, pairs, total):
    height = totals.shape[1]

    def block(n):
        return left[pl.ds(pl.multiple_of(n * height, height), height)]

    def one_group(group, carry):
        base = group * GROUP
        products = [
            jnp.dot(
                block(pairs[0, base + g]),
                panel[pairs[1, base + g]],
                preferred_element_type=jnp.float32,
            )
            for g in range(GROUP)
        ]
        for g in range(GROUP):
            totals[pairs[2, base + g]] += products[g]
        return carry

    lax.fori_loop(0, quotient(total + GROUP - 1, GROUP), one_group, 0)


def own_kernel(sizes, ranges, known, *refs):
    rows, count, piece_rows, width, local_rows, kept, order = sizes
    x_in, s_in, refs = refs[: len(ranges)], refs[len(ranges) :][:rows], refs[len(ranges) + rows :]
    totals, panel, panel_cols, codes, numbers, pairs, sem = refs
    piece = piece_rows * width
    for d in range(rows):
        tile = s_in[d][piece * order :].astype(jnp.float32).astype(jnp.int32)
        panel_cols[d * piece_rows : (d + 1) * piece_rows] = (
            tile[:piece_rows] + tile[piece_rows : 2 * piece_rows] * LANES
        )
    place = known[0:1], known[1:2], known[2:3]
    match((width, local_rows, kept), place, panel_cols[...], known[8 : 8 + kept], codes)
    copy = pltpu.make_async_copy(codes, numbers, sem)
    copy.start()
    totals[...] = jnp.zeros_like(totals)
    for d in range(rows):
        for q in range(piece):
            panel[d * piece + q] = s_in[d][q * order : (q + 1) * order]
    copy.wait()
    total = list_pairs((count, width, totals.shape[0] - 1), numbers, pairs)
    for (first, height), blocks in zip(ranges, x_in):
        add_products(blocks, panel, totals.at[:, pl.ds(first, height)], pairs, total)


def peer_kernel(sizes, span, *refs):
    cols, layers, count, width, local_rows, kept = sizes
    first, height = span
    slots = local_rows * kept // layers
    if first == 0:
        known, panel_cols, *refs = refs
    else:
        codes, *refs = refs
    x_in, refs = refs[: cols - 1], refs[cols - 1 :]
    panel, before, own, sent, refs = refs[0], refs[1], refs[2], refs[3 : 2 + layers], refs[2 + layers :]
    if first == 0:
        codes, *refs = refs
        for j in range(cols - 1):
            digits = x_in[j][count * height :].astype(jnp.float32).astype(jnp.int32)
            place = [digits[p : p + 1] + digits[p + 1 : p + 2] * LANES for p in (0, 2, 4)]
            match(
                (width, local_rows, kept), place, panel_cols[...], known[8 : 8 + kept], codes.at[j]
            )
    totals, numbers, pairs, sem = refs
    copy = pltpu.make_async_copy(codes, numbers, sem)
    copy.start()
    totals[...] = before[:, first : first + height]
    copy.wait()
    for j in range(cols - 1):
        total = list_pairs((count, width, layers * slots), numbers.at[j], pairs)
        add_products(x_in[j], panel, totals, pairs, total)

    own[...] = totals[:slots]
    half = height // 2
    sublane = lax.broadcasted_iota(jnp.int32, (8, totals.shape[2]), 0)
    for d in range(1, layers):
        code = sent[d - 1]
        for u in range(slots):
            value = totals[d * slots + u]
            peak = jnp.max(jnp.abs(value), axis=0, keepdims=True)
            power = jnp.floor(jnp.log2(jnp.maximum(peak, 1e-30)) + 1e-3) + 1.0
            whole = jnp.floor(value * jnp.exp2(15.0 - power) + 0.5).astype(jnp.int32)
            word = (whole[:half] << 16) | (whole[half:] & 0xFFFF)
            bits = ((power.astype(jnp.int32) + 128) >> sublane) & 1
            code[pl.ds(u * half, 8)] = (word[:8] & ~1) | bits
            code[pl.ds(u * half + 8, half - 8)] = word[8:]


def finish_kernel(sizes, span, *refs):
    layers, slots = sizes
    first, height = span
    half = height // 2
    sublane = lax.broadcasted_iota(jnp.int32, (8, refs[-1].shape[3]), 0)
    before, own, codes, result = refs[: first > 0], refs[-layers - 1], refs[-layers:-1], refs[-1]
    kept = result.shape[1]
    for done in before:
        result[:, :, :first] = done[...]
    for u in range(slots):
        high, low = own[u, :half], own[u, half:]
        for code in codes:
            word = code[pl.ds(u * half, half)]
            power = jnp.sum((word[:8] & 1) << sublane, axis=0, keepdims=True).astype(jnp.float32)
            scale = jnp.exp2(power - (128.0 + 15.0))
            high += (word >> 16).astype(jnp.float32) * scale
            low += ((word << 16) >> 16).astype(jnp.float32) * scale
        result[u // kept, u % kept, first : first + half] = high.astype(jnp.bfloat16)
        result[u // kept, u % kept, first + half : first + height] = low.astype(jnp.bfloat16)


def per_device(a_blocks, a_rows, a_cols, s_blocks, s_cols, c_cols):
    rows, cols, layers = (lax.axis_size(axis) for axis in ("row", "col", "layer"))
    count, order = a_blocks.shape[:2]
    piece_rows, width = s_cols.shape
    local_rows, kept = c_cols.shape
    own_rows = local_rows // layers
    slots = own_rows * kept
    all_slots = layers * slots
    ranges = row_ranges(order)
    piece = piece_rows * width
    panel_size = rows * piece
    block_size = order * order
    flat_s = s_blocks.reshape(piece, order, order)
    note_height = (2 * piece_rows + 15) // 16 * 16
    code_height = (1 + width + 7) // 8 * 8

    vector = pl.BlockSpec(memory_space=pltpu.VMEM)
    far = pl.BlockSpec(memory_space=HBM)

    known, s_sent, *x_sent = pl.pallas_call(
        functools.partial(
            pack_kernel, (layers, count, piece_rows, width, local_rows, kept, order, ranges)
        ),
        out_shape=[
            jax.ShapeDtypeStruct((16, LANES), jnp.int32),
            jax.ShapeDtypeStruct((piece * order + note_height, order), jnp.bfloat16),
        ]
        + [
            jax.ShapeDtypeStruct((count * height + 16 * (at == 0), order), jnp.bfloat16)
            for at, height in ranges
        ],
        in_specs=[far] * 6,
        out_specs=[vector] * (2 + len(ranges)),
        scratch_shapes=[
            pltpu.VMEM((1, count), jnp.int32),
            pltpu.VMEM((1, count), jnp.int32),
            pltpu.VMEM((kept, local_rows), jnp.int32),
            pltpu.VMEM((piece_rows, width), jnp.int32),
            pltpu.VMEM((16, LANES), jnp.int32),
            pltpu.VMEM((note_height, LANES), jnp.int32),
            pltpu.SemaphoreType.DMA((4 + piece + len(ranges),)),
        ],
        compiler_params=pltpu.CompilerParams(
            vmem_limit_bytes=2 * block_size * (2 * count + piece) + 4 * MIB
        ),
        name="pack",
    )(
        *in_hbm(
            a_rows.reshape(1, count), a_cols.reshape(1, count), c_cols.T, a_blocks, s_cols, flat_s
        )
    )
    s_pieces = gathered(s_sent, "row")
    later, _ = lax.optimization_barrier((x_sent[1:], s_pieces))
    x_pieces = [
        [shifted(part, "col", j) for j in range(1, cols)] for part in (x_sent[0], *later)
    ]

    moved = block_size * (4 * all_slots + 4 * panel_size + 2 * count)
    totals, panel, panel_cols = pl.pallas_call(
        functools.partial(
            own_kernel, (rows, count, piece_rows, width, local_rows, kept, order), ranges
        ),
        out_shape=[
            jax.ShapeDtypeStruct((all_slots + 1, order, order), jnp.float32),
            jax.ShapeDtypeStruct((panel_size, order, order), jnp.bfloat16),
            jax.ShapeDtypeStruct((rows * piece_rows, LANES), jnp.int32),
        ],
        in_specs=[vector] * (1 + len(ranges) + rows),
        out_specs=[vector] * 3,
        scratch_shapes=[
            pltpu.VMEM((code_height, LANES), jnp.int32),
            pltpu.SMEM((code_height, LANES), jnp.int32),
            pltpu.SMEM((3, count * width + GROUP), jnp.int32),
            pltpu.SemaphoreType.DMA,
        ],
        compiler_params=pltpu.CompilerParams(vmem_limit_bytes=moved + 4 * MIB),
        cost_estimate=pl.CostEstimate(
            flops=2 * order**3 * count * width // 4, bytes_accessed=moved, transcendentals=0
        ),
        name="own_products",
    )(known, *x_sent, *s_pieces)

    moved = block_size * (8 * all_slots + 2 * panel_size + 2 * count * (cols - 1))
    code_shape = (cols - 1, code_height, LANES)
    finished, plan = [], []
    for (at, height), pieces in zip(ranges, x_pieces):
        code_rows = slots * (height // 2)
        out_shape = [jax.ShapeDtypeStruct((slots, height, order), jnp.float32)]
        out_shape += [jax.ShapeDtypeStruct((code_rows, order), jnp.int32)] * (layers - 1)
        if at == 0:
            out_shape.append(jax.ShapeDtypeStruct(code_shape, jnp.int32))
        given = plan or (known, panel_cols)
        out = pl.pallas_call(
            functools.partial(
                peer_kernel, (cols, layers, count, width, local_rows, kept), (at, height)
            ),
            out_shape=out_shape,
            in_specs=[vector] * (len(given) + cols + 1),
            out_specs=[vector] * len(out_shape),
            scratch_shapes=[
                pltpu.VMEM((all_slots + 1, height, order), jnp.float32),
                pltpu.SMEM(code_shape, jnp.int32),
                pltpu.SMEM((3, count * width + GROUP), jnp.int32),
                pltpu.SemaphoreType.DMA,
            ],
            compiler_params=pltpu.CompilerParams(vmem_limit_bytes=moved + 4 * MIB),
            cost_estimate=pl.CostEstimate(
                flops=2 * order**2 * height * count * width // 4 * (cols - 1),
                bytes_accessed=moved // 2,
                transcendentals=0,
            ),
            name=f"peer_products_{at}",
        )(*given, *pieces, panel, totals)
        plan = plan or out[layers:]
        turn = range(layers - 1, 0, -1) if at == 0 else [*range(layers - 2, 0, -1), layers - 1]
        codes = [flipped(out[d], "layer", d) for d in turn]
        finished = [
            pl.pallas_call(
                functools.partial(finish_kernel, (layers, slots), (at, height)),
                out_shape=jax.ShapeDtypeStruct((own_rows, kept, at + height, order), jnp.bfloat16),
                in_specs=[vector] * (len(finished) + layers),
                out_specs=vector,
                compiler_params=pltpu.CompilerParams(
                    vmem_limit_bytes=16 * slots * block_size + 4 * MIB
                ),
                name=f"finish_{at}",
            )(*finished, out[0], *codes)
        ]
    return finished[0]


def solution(mesh):
    placed = (
        P(("row", "col", "layer"), None, None),
        P(("row", "col", "layer")),
        P(("row", "col", "layer")),
        P(("row", "layer"), "col", None, None),
        P(("row", "layer"), "col"),
        P("row", "col"),
    )
    return jax.shard_map(
        per_device,
        mesh=mesh,
        in_specs=placed,
        out_specs=P(("row", "layer"), "col", None, None),
        check_vma=False,
    )
```

```python
import functools

import jax
import jax.numpy as jnp
from jax import lax
from jax.experimental import pallas as pl
from jax.experimental.pallas import tpu as pltpu
from jax.sharding import PartitionSpec as P

GROUP = 8
LANES = 128
FIELD = 10
MIB = 2**20
HBM = pltpu.MemorySpace.HBM


def row_ranges(order):
    first = order * 5 // 8
    return [(0, first), (first, order - first)]


def in_hbm(*values):
    return [pltpu.with_memory_space_constraint(value, HBM) for value in values]


def flipped(value, axis, bits):
    return lax.ppermute(value, axis, [(i, i ^ bits) for i in range(lax.axis_size(axis))])


def gathered(value, axis):
    values = {0: value}
    bit = lax.axis_size(axis) // 2
    while bit:
        values |= {d ^ bit: flipped(held, axis, bit) for d, held in values.items()}
        bit //= 2
    return [values[d] for d in range(len(values))]


def shifted(value, axis, offset):
    size = lax.axis_size(axis)
    return lax.ppermute(value, axis, [((i + offset) % size, i) for i in range(size)])


def quotient(value, by):
    return value >> (by.bit_length() - 1) if by & (by - 1) == 0 else lax.div(value, by)


def remainder(value, by):
    return value & (by - 1) if by & (by - 1) == 0 else lax.rem(value, by)


def write_digits(tile, at, value):
    height, width = value.shape
    tile[at : at + height, :width] = remainder(value, LANES)
    tile[at + height : at + 2 * height, :width] = quotient(value, LANES)


def pack_kernel(sizes, a_rows, a_cols, c_cols, x_in, s_cols, s_in, *refs):
    layers, count, piece_rows, width, local_rows, kept, order, ranges = sizes
    known, s_out, x_out, refs = refs[0], refs[1], refs[2 : 2 + len(ranges)], refs[2 + len(ranges) :]
    rows, cols, kept_held, s_held, x_tile, s_tile, sem = refs
    piece = piece_rows * width
    small = [(a_rows, rows), (a_cols, cols), (c_cols, kept_held), (s_cols, s_held)]
    large = [
        (
            x_in.at[:, pl.ds(first, height)],
            out.at[pl.ds(0, count * height)].reshape(count, height, order),
        )
        for (first, height), out in zip(ranges, x_out)
    ]
    large += [(s_in.at[q], s_out.at[pl.ds(q * order, order)]) for q in range(piece)]
    loads = [
        pltpu.make_async_copy(source, goal, sem.at[p])
        for p, (source, goal) in enumerate(small + large)
    ]
    for load in loads:
        load.start()
    known[...] = jnp.zeros_like(known)
    x_tile[...] = jnp.zeros_like(x_tile)
    s_tile[...] = jnp.zeros_like(s_tile)
    for load in loads[: len(small)]:
        load.wait()
    own_rows = local_rows // layers
    row, col = rows[...], cols[...]
    here = quotient(row[:, :1], local_rows)
    layer = remainder(quotient(col[:, :1], piece_rows), layers)
    owner = quotient(col, piece_rows * layers)
    local = row - here * local_rows
    goal = (quotient(local, own_rows) ^ layer) * own_rows
    place = (
        ((owner ^ here) * piece_rows + remainder(col, piece_rows)) * width,
        (goal + remainder(local, own_rows)) * kept,
        local,
    )
    for p, value in enumerate(place):
        known[p : p + 1, :count] = value
        write_digits(x_tile, 2 * p, value)
    known[8 : 8 + kept, :local_rows] = kept_held[...]
    write_digits(s_tile, 0, s_held[...])
    x_out[0][count * ranges[0][1] :] = x_tile[...].astype(jnp.float32).astype(jnp.bfloat16)
    s_out[piece * order :] = s_tile[...].astype(jnp.float32).astype(jnp.bfloat16)
    for load in loads[len(small) :]:
        load.wait()


def match(sizes, place, panel_cols, kept_cols, codes):
    width, local_rows, kept = sizes
    right, goal, local = place
    wanted, held = [jnp.zeros_like(right)] * width, [jnp.zeros_like(right)] * kept
    for p in range(panel_cols.shape[0]):
        for s in range(width):
            wanted[s] = jnp.where(right == p * width, panel_cols[p : p + 1, s : s + 1], wanted[s])
    for i in range(local_rows):
        for t in range(kept):
            held[t] = jnp.where(local == i, kept_cols[t : t + 1, i : i + 1], held[t])
    block = lax.broadcasted_iota(jnp.int32, right.shape, 1)
    for s in range(width):
        word = jnp.full_like(right, -1)
        for t in range(kept):
            pair = ((block << FIELD) | (right + s)) << FIELD | (goal + t)
            word = jnp.where(held[t] == wanted[s], pair, word)
        codes[s : s + 1] = word


def list_pairs(sizes, codes, pairs):
    count, width, trash = sizes
    total = jnp.int32(0)
    for n in range(count):
        for s in range(width):
            word = codes[s, n]
            pairs[total] = word
            total += (word >= 0).astype(jnp.int32)
    for g in range(GROUP):
        pairs[total + g] = trash
    return total


def add_products(left, panel, totals, pairs, total):
    height = totals.shape[1]
    mask = (1 << FIELD) - 1

    def one_group(group, carry):
        words = [pairs[group * GROUP + g] for g in range(GROUP)]
        products = []
        for word in words:
            at = pl.multiple_of((word >> (2 * FIELD)) * height, height)
            products.append(
                jnp.dot(
                    left[pl.ds(at, height)],
                    panel[(word >> FIELD) & mask],
                    preferred_element_type=jnp.float32,
                )
            )
        for word, product in zip(words, products):
            totals[word & mask] += product
        return carry

    lax.fori_loop(0, quotient(total + GROUP - 1, GROUP), one_group, 0)


def own_kernel(sizes, ranges, known, *refs):
    rows, count, piece_rows, width, local_rows, kept, order = sizes
    x_in, s_in, refs = refs[: len(ranges)], refs[len(ranges) :][:rows], refs[len(ranges) + rows :]
    totals, panel, panel_cols, codes, numbers, pairs, sem = refs
    piece = piece_rows * width
    for d in range(rows):
        tile = s_in[d][piece * order :].astype(jnp.float32).astype(jnp.int32)
        panel_cols[d * piece_rows : (d + 1) * piece_rows] = (
            tile[:piece_rows] + tile[piece_rows : 2 * piece_rows] * LANES
        )
    place = known[0:1], known[1:2], known[2:3]
    match((width, local_rows, kept), place, panel_cols[...], known[8 : 8 + kept], codes)
    copy = pltpu.make_async_copy(codes, numbers, sem)
    copy.start()
    totals[...] = jnp.zeros_like(totals)
    for d in range(rows):
        for q in range(piece):
            panel[d * piece + q] = s_in[d][q * order : (q + 1) * order]
    copy.wait()
    total = list_pairs((count, width, totals.shape[0] - 1), numbers, pairs)
    for (first, height), blocks in zip(ranges, x_in):
        add_products(blocks, panel, totals.at[:, pl.ds(first, height)], pairs, total)


def peer_kernel(sizes, span, *refs):
    cols, layers, count, width, local_rows, kept = sizes
    first, height = span
    slots = local_rows * kept // layers
    if first == 0:
        known, panel_cols, *refs = refs
    else:
        codes, *refs = refs
    x_in, refs = refs[: cols - 1], refs[cols - 1 :]
    panel, before, own, sent, refs = refs[0], refs[1], refs[2], refs[3 : 2 + layers], refs[2 + layers :]
    if first == 0:
        codes, *refs = refs
        for j in range(cols - 1):
            digits = x_in[j][count * height :].astype(jnp.float32).astype(jnp.int32)
            place = [digits[p : p + 1] + digits[p + 1 : p + 2] * LANES for p in (0, 2, 4)]
            match(
                (width, local_rows, kept), place, panel_cols[...], known[8 : 8 + kept], codes.at[j]
            )
    totals, numbers, pairs, sem = refs
    copy = pltpu.make_async_copy(codes, numbers, sem)
    copy.start()
    totals[...] = before[:, first : first + height]
    copy.wait()
    for j in range(cols - 1):
        total = list_pairs((count, width, layers * slots), numbers.at[j], pairs)
        add_products(x_in[j], panel, totals, pairs, total)

    own[...] = totals[:slots]
    half = height // 2
    sublane = lax.broadcasted_iota(jnp.int32, (8, totals.shape[2]), 0)
    for d in range(1, layers):
        code = sent[d - 1]
        for u in range(slots):
            value = totals[d * slots + u]
            peak = jnp.max(jnp.abs(value), axis=0, keepdims=True)
            power = jnp.floor(jnp.log2(jnp.maximum(peak, 1e-30)) + 1e-3) + 1.0
            whole = jnp.floor(value * jnp.exp2(15.0 - power) + 0.5).astype(jnp.int32)
            word = (whole[:half] << 16) | (whole[half:] & 0xFFFF)
            bits = ((power.astype(jnp.int32) + 128) >> sublane) & 1
            code[pl.ds(u * half, 8)] = (word[:8] & ~1) | bits
            code[pl.ds(u * half + 8, half - 8)] = word[8:]


def finish_kernel(sizes, span, *refs):
    layers, slots = sizes
    first, height = span
    half = height // 2
    sublane = lax.broadcasted_iota(jnp.int32, (8, refs[-1].shape[3]), 0)
    before, own, codes, result = refs[: first > 0], refs[-layers - 1], refs[-layers:-1], refs[-1]
    kept = result.shape[1]
    for done in before:
        result[:, :, :first] = done[...]
    for u in range(slots):
        high, low = own[u, :half], own[u, half:]
        for code in codes:
            word = code[pl.ds(u * half, half)]
            power = jnp.sum((word[:8] & 1) << sublane, axis=0, keepdims=True).astype(jnp.float32)
            scale = jnp.exp2(power - (128.0 + 15.0))
            high += (word >> 16).astype(jnp.float32) * scale
            low += ((word << 16) >> 16).astype(jnp.float32) * scale
        result[u // kept, u % kept, first : first + half] = high.astype(jnp.bfloat16)
        result[u // kept, u % kept, first + half : first + height] = low.astype(jnp.bfloat16)


def per_device(a_blocks, a_rows, a_cols, s_blocks, s_cols, c_cols):
    rows, cols, layers = (lax.axis_size(axis) for axis in ("row", "col", "layer"))
    count, order = a_blocks.shape[:2]
    piece_rows, width = s_cols.shape
    local_rows, kept = c_cols.shape
    own_rows = local_rows // layers
    slots = own_rows * kept
    all_slots = layers * slots
    ranges = row_ranges(order)
    piece = piece_rows * width
    panel_size = rows * piece
    block_size = order * order
    flat_s = s_blocks.reshape(piece, order, order)
    note_height = (2 * piece_rows + 15) // 16 * 16
    code_height = (width + 7) // 8 * 8

    vector = pl.BlockSpec(memory_space=pltpu.VMEM)
    far = pl.BlockSpec(memory_space=HBM)

    known, s_sent, *x_sent = pl.pallas_call(
        functools.partial(
            pack_kernel, (layers, count, piece_rows, width, local_rows, kept, order, ranges)
        ),
        out_shape=[
            jax.ShapeDtypeStruct((16, LANES), jnp.int32),
            jax.ShapeDtypeStruct((piece * order + note_height, order), jnp.bfloat16),
        ]
        + [
            jax.ShapeDtypeStruct((count * height + 16 * (at == 0), order), jnp.bfloat16)
            for at, height in ranges
        ],
        in_specs=[far] * 6,
        out_specs=[vector] * (2 + len(ranges)),
        scratch_shapes=[
            pltpu.VMEM((1, count), jnp.int32),
            pltpu.VMEM((1, count), jnp.int32),
            pltpu.VMEM((kept, local_rows), jnp.int32),
            pltpu.VMEM((piece_rows, width), jnp.int32),
            pltpu.VMEM((16, LANES), jnp.int32),
            pltpu.VMEM((note_height, LANES), jnp.int32),
            pltpu.SemaphoreType.DMA((4 + piece + len(ranges),)),
        ],
        compiler_params=pltpu.CompilerParams(
            vmem_limit_bytes=2 * block_size * (2 * count + piece) + 4 * MIB
        ),
        name="pack",
    )(
        *in_hbm(
            a_rows.reshape(1, count), a_cols.reshape(1, count), c_cols.T, a_blocks, s_cols, flat_s
        )
    )
    s_pieces = gathered(s_sent, "row")
    later, _ = lax.optimization_barrier((x_sent[1:], s_pieces))
    x_pieces = [
        [shifted(part, "col", j) for j in range(1, cols)] for part in (x_sent[0], *later)
    ]

    moved = block_size * (4 * all_slots + 4 * panel_size + 2 * count)
    totals, panel, panel_cols = pl.pallas_call(
        functools.partial(
            own_kernel, (rows, count, piece_rows, width, local_rows, kept, order), ranges
        ),
        out_shape=[
            jax.ShapeDtypeStruct((all_slots + 1, order, order), jnp.float32),
            jax.ShapeDtypeStruct((panel_size, order, order), jnp.bfloat16),
            jax.ShapeDtypeStruct((rows * piece_rows, LANES), jnp.int32),
        ],
        in_specs=[vector] * (1 + len(ranges) + rows),
        out_specs=[vector] * 3,
        scratch_shapes=[
            pltpu.VMEM((code_height, LANES), jnp.int32),
            pltpu.SMEM((code_height, LANES), jnp.int32),
            pltpu.SMEM((count * width + GROUP,), jnp.int32),
            pltpu.SemaphoreType.DMA,
        ],
        compiler_params=pltpu.CompilerParams(vmem_limit_bytes=moved + 4 * MIB),
        cost_estimate=pl.CostEstimate(
            flops=2 * order**3 * count * width // 4, bytes_accessed=moved, transcendentals=0
        ),
        name="own_products",
    )(known, *x_sent, *s_pieces)

    moved = block_size * (8 * all_slots + 2 * panel_size + 2 * count * (cols - 1))
    code_shape = (cols - 1, code_height, LANES)
    finished, plan = [], []
    for (at, height), pieces in zip(ranges, x_pieces):
        code_rows = slots * (height // 2)
        out_shape = [jax.ShapeDtypeStruct((slots, height, order), jnp.float32)]
        out_shape += [jax.ShapeDtypeStruct((code_rows, order), jnp.int32)] * (layers - 1)
        if at == 0:
            out_shape.append(jax.ShapeDtypeStruct(code_shape, jnp.int32))
        given = plan or (known, panel_cols)
        out = pl.pallas_call(
            functools.partial(
                peer_kernel, (cols, layers, count, width, local_rows, kept), (at, height)
            ),
            out_shape=out_shape,
            in_specs=[vector] * (len(given) + cols + 1),
            out_specs=[vector] * len(out_shape),
            scratch_shapes=[
                pltpu.VMEM((all_slots + 1, height, order), jnp.float32),
                pltpu.SMEM(code_shape, jnp.int32),
                pltpu.SMEM((count * width + GROUP,), jnp.int32),
                pltpu.SemaphoreType.DMA,
            ],
            compiler_params=pltpu.CompilerParams(vmem_limit_bytes=moved + 4 * MIB),
            cost_estimate=pl.CostEstimate(
                flops=2 * order**2 * height * count * width // 4 * (cols - 1),
                bytes_accessed=moved // 2,
                transcendentals=0,
            ),
            name=f"peer_products_{at}",
        )(*given, *pieces, panel, totals)
        plan = plan or out[layers:]
        turn = range(layers - 1, 0, -1) if at == 0 else [*range(layers - 2, 0, -1), layers - 1]
        codes = [flipped(out[d], "layer", d) for d in turn]
        finished = [
            pl.pallas_call(
                functools.partial(finish_kernel, (layers, slots), (at, height)),
                out_shape=jax.ShapeDtypeStruct((own_rows, kept, at + height, order), jnp.bfloat16),
                in_specs=[vector] * (len(finished) + layers),
                out_specs=vector,
                compiler_params=pltpu.CompilerParams(
                    vmem_limit_bytes=16 * slots * block_size + 4 * MIB
                ),
                name=f"finish_{at}",
            )(*finished, out[0], *codes)
        ]
    return finished[0]


def solution(mesh):
    placed = (
        P(("row", "col", "layer"), None, None),
        P(("row", "col", "layer")),
        P(("row", "col", "layer")),
        P(("row", "layer"), "col", None, None),
        P(("row", "layer"), "col"),
        P("row", "col"),
    )
    return jax.shard_map(
        per_device,
        mesh=mesh,
        in_specs=placed,
        out_specs=P(("row", "layer"), "col", None, None),
        check_vma=False,
    )
```

```python
import functools

import jax
import jax.numpy as jnp
from jax import lax
from jax.experimental import pallas as pl
from jax.experimental.pallas import tpu as pltpu
from jax.sharding import PartitionSpec as P

GROUP = 8
LANES = 128
FIELD = 10
MIB = 2**20
HBM = pltpu.MemorySpace.HBM


def row_ranges(order):
    first = order * 5 // 8
    return [(0, first), (first, order - first)]


def in_hbm(*values):
    return [pltpu.with_memory_space_constraint(value, HBM) for value in values]


def flipped(value, axis, bits):
    return lax.ppermute(value, axis, [(i, i ^ bits) for i in range(lax.axis_size(axis))])


def gathered(value, axis):
    values = {0: value}
    bit = lax.axis_size(axis) // 2
    while bit:
        values |= {d ^ bit: flipped(held, axis, bit) for d, held in values.items()}
        bit //= 2
    return [values[d] for d in range(len(values))]


def shifted(value, axis, offset):
    size = lax.axis_size(axis)
    return lax.ppermute(value, axis, [((i + offset) % size, i) for i in range(size)])


def quotient(value, by):
    return value >> (by.bit_length() - 1) if by & (by - 1) == 0 else lax.div(value, by)


def remainder(value, by):
    return value & (by - 1) if by & (by - 1) == 0 else lax.rem(value, by)


def write_digits(tile, at, value):
    height, width = value.shape
    tile[at : at + height, :width] = remainder(value, LANES)
    tile[at + height : at + 2 * height, :width] = quotient(value, LANES)


def pack_kernel(sizes, a_rows, a_cols, c_cols, x_in, s_cols, s_in, *refs):
    layers, count, piece_rows, width, local_rows, kept, order, ranges = sizes
    known, s_out, x_out, refs = refs[0], refs[1], refs[2 : 2 + len(ranges)], refs[2 + len(ranges) :]
    rows, cols, kept_held, s_held, x_tile, s_tile, sem = refs
    piece = piece_rows * width
    small = [(a_rows, rows), (a_cols, cols), (c_cols, kept_held), (s_cols, s_held)]
    large = [
        (
            x_in.at[:, pl.ds(first, height)],
            out.at[pl.ds(0, count * height)].reshape(count, height, order),
        )
        for (first, height), out in zip(ranges, x_out)
    ]
    large += [(s_in.at[q], s_out.at[pl.ds(q * order, order)]) for q in range(piece)]
    loads = [
        pltpu.make_async_copy(source, goal, sem.at[p])
        for p, (source, goal) in enumerate(small + large)
    ]
    for load in loads:
        load.start()
    known[...] = jnp.zeros_like(known)
    x_tile[...] = jnp.zeros_like(x_tile)
    s_tile[...] = jnp.zeros_like(s_tile)
    for load in loads[: len(small)]:
        load.wait()
    own_rows = local_rows // layers
    row, col = rows[...], cols[...]
    here = quotient(row[:, :1], local_rows)
    layer = remainder(quotient(col[:, :1], piece_rows), layers)
    owner = quotient(col, piece_rows * layers)
    local = row - here * local_rows
    goal = (quotient(local, own_rows) ^ layer) * own_rows
    place = (
        ((owner ^ here) * piece_rows + remainder(col, piece_rows)) * width,
        (goal + remainder(local, own_rows)) * kept,
        local,
    )
    for p, value in enumerate(place):
        known[p : p + 1, :count] = value
        write_digits(x_tile, 2 * p, value)
    known[8 : 8 + kept, :local_rows] = kept_held[...]
    write_digits(s_tile, 0, s_held[...])
    x_out[0][count * ranges[0][1] :] = x_tile[...].astype(jnp.float32).astype(jnp.bfloat16)
    s_out[piece * order :] = s_tile[...].astype(jnp.float32).astype(jnp.bfloat16)
    for load in loads[len(small) :]:
        load.wait()


def match(sizes, place, panel_cols, kept_cols, codes):
    width, local_rows, kept = sizes
    right, goal, local = place
    wanted, held = [jnp.zeros_like(right)] * width, [jnp.zeros_like(right)] * kept
    for p in range(panel_cols.shape[0]):
        for s in range(width):
            wanted[s] = jnp.where(right == p * width, panel_cols[p : p + 1, s : s + 1], wanted[s])
    for i in range(local_rows):
        for t in range(kept):
            held[t] = jnp.where(local == i, kept_cols[t : t + 1, i : i + 1], held[t])
    block = lax.broadcasted_iota(jnp.int32, right.shape, 1)
    for s in range(width):
        word = jnp.full_like(right, -1)
        for t in range(kept):
            pair = ((block << FIELD) | (right + s)) << FIELD | (goal + t)
            word = jnp.where(held[t] == wanted[s], pair, word)
        codes[s : s + 1] = word


def list_pairs(sizes, codes, pairs):
    count, width, trash = sizes
    total = jnp.int32(0)
    for n in range(count):
        for s in range(width):
            word = codes[s, n]
            pairs[total] = word
            total += (word >= 0).astype(jnp.int32)
    for g in range(GROUP):
        pairs[total + g] = trash
    return total


def add_products(left, panel, totals, pairs, total):
    height = totals.shape[1]
    mask = (1 << FIELD) - 1

    def one_group(group, carry):
        words = [pairs[group * GROUP + g] for g in range(GROUP)]
        products = []
        for word in words:
            at = pl.multiple_of((word >> (2 * FIELD)) * height, height)
            products.append(
                jnp.dot(
                    left[pl.ds(at, height)],
                    panel[(word >> FIELD) & mask],
                    preferred_element_type=jnp.float32,
                )
            )
        for word, product in zip(words, products):
            totals[word & mask] += product
        return carry

    lax.fori_loop(0, quotient(total + GROUP - 1, GROUP), one_group, 0)


def own_kernel(sizes, ranges, known, *refs):
    rows, count, piece_rows, width, local_rows, kept, order = sizes
    x_in, s_in, refs = refs[: len(ranges)], refs[len(ranges) :][:rows], refs[len(ranges) + rows :]
    totals, panel, panel_cols, codes, numbers, pairs, sem = refs
    piece = piece_rows * width
    for d in range(rows):
        tile = s_in[d][piece * order :].astype(jnp.float32).astype(jnp.int32)
        panel_cols[d * piece_rows : (d + 1) * piece_rows] = (
            tile[:piece_rows] + tile[piece_rows : 2 * piece_rows] * LANES
        )
    place = known[0:1], known[1:2], known[2:3]
    match((width, local_rows, kept), place, panel_cols[...], known[8 : 8 + kept], codes)
    copy = pltpu.make_async_copy(codes, numbers, sem)
    copy.start()
    totals[...] = jnp.zeros_like(totals)
    for d in range(rows):
        for q in range(piece):
            panel[d * piece + q] = s_in[d][q * order : (q + 1) * order]
    copy.wait()
    total = list_pairs((count, width, totals.shape[0] - 1), numbers, pairs)
    for (first, height), blocks in zip(ranges, x_in):
        add_products(blocks, panel, totals.at[:, pl.ds(first, height)], pairs, total)


def peer_kernel(sizes, span, *refs):
    cols, layers, count, width, local_rows, kept = sizes
    first, height = span
    slots = local_rows * kept // layers
    if first == 0:
        known, panel_cols, *refs = refs
    else:
        codes, *refs = refs
    x_in, refs = refs[: cols - 1], refs[cols - 1 :]
    panel, before, own, sent, refs = refs[0], refs[1], refs[2], refs[3 : 2 + layers], refs[2 + layers :]
    if first == 0:
        codes, *refs = refs
        for j in range(cols - 1):
            digits = x_in[j][count * height :].astype(jnp.float32).astype(jnp.int32)
            place = [digits[p : p + 1] + digits[p + 1 : p + 2] * LANES for p in (0, 2, 4)]
            match(
                (width, local_rows, kept), place, panel_cols[...], known[8 : 8 + kept], codes.at[j]
            )
    totals, numbers, pairs, sem = refs
    copy = pltpu.make_async_copy(codes, numbers, sem)
    copy.start()
    totals[...] = before[:, first : first + height]
    copy.wait()
    for j in range(cols - 1):
        total = list_pairs((count, width, layers * slots), numbers.at[j], pairs)
        add_products(x_in[j], panel, totals, pairs, total)

    own[...] = totals[:slots]
    half = height // 2
    sublane = lax.broadcasted_iota(jnp.int32, (8, totals.shape[2]), 0)
    for d in range(1, layers):
        code = sent[d - 1]
        for u in range(slots):
            value = totals[d * slots + u]
            peak = jnp.max(jnp.abs(value), axis=0, keepdims=True)
            power = jnp.floor(jnp.log2(jnp.maximum(peak, 1e-30)) + 1e-3) + 1.0
            whole = jnp.floor(value * jnp.exp2(15.0 - power) + 0.5).astype(jnp.int32)
            word = (whole[:half] << 16) | (whole[half:] & 0xFFFF)
            bits = ((power.astype(jnp.int32) + 128) >> sublane) & 1
            code[pl.ds(u * half, 8)] = (word[:8] & ~1) | bits
            code[pl.ds(u * half + 8, half - 8)] = word[8:]


def finish_kernel(sizes, span, *refs):
    layers, slots = sizes
    first, height = span
    half = height // 2
    sublane = lax.broadcasted_iota(jnp.int32, (8, refs[-1].shape[3]), 0)
    before, own, codes, result = refs[: first > 0], refs[-layers - 1], refs[-layers:-1], refs[-1]
    kept = result.shape[1]
    for done in before:
        result[:, :, :first] = done[...]
    for u in range(slots):
        high, low = own[u, :half], own[u, half:]
        for code in codes:
            word = code[pl.ds(u * half, half)]
            power = jnp.sum((word[:8] & 1) << sublane, axis=0, keepdims=True).astype(jnp.float32)
            scale = jnp.exp2(power - (128.0 + 15.0))
            high += (word >> 16).astype(jnp.float32) * scale
            low += ((word << 16) >> 16).astype(jnp.float32) * scale
        result[u // kept, u % kept, first : first + half] = high.astype(jnp.bfloat16)
        result[u // kept, u % kept, first + half : first + height] = low.astype(jnp.bfloat16)


def per_device(a_blocks, a_rows, a_cols, s_blocks, s_cols, c_cols):
    rows, cols, layers = (lax.axis_size(axis) for axis in ("row", "col", "layer"))
    count, order = a_blocks.shape[:2]
    piece_rows, width = s_cols.shape
    local_rows, kept = c_cols.shape
    own_rows = local_rows // layers
    slots = own_rows * kept
    all_slots = layers * slots
    ranges = row_ranges(order)
    piece = piece_rows * width
    panel_size = rows * piece
    block_size = order * order
    flat_s = s_blocks.reshape(piece, order, order)
    note_height = (2 * piece_rows + 15) // 16 * 16
    code_height = (width + 7) // 8 * 8

    vector = pl.BlockSpec(memory_space=pltpu.VMEM)
    far = pl.BlockSpec(memory_space=HBM)

    known, s_sent, *x_sent = pl.pallas_call(
        functools.partial(
            pack_kernel, (layers, count, piece_rows, width, local_rows, kept, order, ranges)
        ),
        out_shape=[
            jax.ShapeDtypeStruct((16, LANES), jnp.int32),
            jax.ShapeDtypeStruct((piece * order + note_height, order), jnp.bfloat16),
        ]
        + [
            jax.ShapeDtypeStruct((count * height + 16 * (at == 0), order), jnp.bfloat16)
            for at, height in ranges
        ],
        in_specs=[far] * 6,
        out_specs=[vector] * (2 + len(ranges)),
        scratch_shapes=[
            pltpu.VMEM((1, count), jnp.int32),
            pltpu.VMEM((1, count), jnp.int32),
            pltpu.VMEM((kept, local_rows), jnp.int32),
            pltpu.VMEM((piece_rows, width), jnp.int32),
            pltpu.VMEM((16, LANES), jnp.int32),
            pltpu.VMEM((note_height, LANES), jnp.int32),
            pltpu.SemaphoreType.DMA((4 + piece + len(ranges),)),
        ],
        compiler_params=pltpu.CompilerParams(
            vmem_limit_bytes=2 * block_size * (2 * count + piece) + 4 * MIB
        ),
        name="pack",
    )(
        *in_hbm(
            a_rows.reshape(1, count), a_cols.reshape(1, count), c_cols.T, a_blocks, s_cols, flat_s
        )
    )
    s_pieces = gathered(s_sent, "row")
    later, _ = lax.optimization_barrier((x_sent[1:], s_pieces))
    x_pieces = [
        [shifted(part, "col", j) for j in range(1, cols)] for part in (x_sent[0], *later)
    ]

    moved = block_size * (4 * all_slots + 4 * panel_size + 2 * count)
    totals, panel, panel_cols = pl.pallas_call(
        functools.partial(
            own_kernel, (rows, count, piece_rows, width, local_rows, kept, order), ranges
        ),
        out_shape=[
            jax.ShapeDtypeStruct((all_slots + 1, order, order), jnp.float32),
            jax.ShapeDtypeStruct((panel_size, order, order), jnp.bfloat16),
            jax.ShapeDtypeStruct((rows * piece_rows, LANES), jnp.int32),
        ],
        in_specs=[vector] * (1 + len(ranges) + rows),
        out_specs=[vector] * 3,
        scratch_shapes=[
            pltpu.VMEM((code_height, LANES), jnp.int32),
            pltpu.SMEM((code_height, LANES), jnp.int32),
            pltpu.SMEM((count * width + GROUP,), jnp.int32),
            pltpu.SemaphoreType.DMA,
        ],
        compiler_params=pltpu.CompilerParams(vmem_limit_bytes=moved + 4 * MIB),
        cost_estimate=pl.CostEstimate(
            flops=2 * order**3 * count * width // 4, bytes_accessed=moved, transcendentals=0
        ),
        name="own_products",
    )(known, *x_sent, *s_pieces)

    moved = block_size * (8 * all_slots + 2 * panel_size + 2 * count * (cols - 1))
    code_shape = (cols - 1, code_height, LANES)
    finished, plan = [], []
    for (at, height), pieces in zip(ranges, x_pieces):
        code_rows = slots * (height // 2)
        out_shape = [jax.ShapeDtypeStruct((slots, height, order), jnp.float32)]
        out_shape += [jax.ShapeDtypeStruct((code_rows, order), jnp.int32)] * (layers - 1)
        if at == 0:
            out_shape.append(jax.ShapeDtypeStruct(code_shape, jnp.int32))
        given = plan or (known, panel_cols)
        out = pl.pallas_call(
            functools.partial(
                peer_kernel, (cols, layers, count, width, local_rows, kept), (at, height)
            ),
            out_shape=out_shape,
            in_specs=[vector] * (len(given) + cols + 1),
            out_specs=[vector] * len(out_shape),
            scratch_shapes=[
                pltpu.VMEM((all_slots + 1, height, order), jnp.float32),
                pltpu.SMEM(code_shape, jnp.int32),
                pltpu.SMEM((count * width + GROUP,), jnp.int32),
                pltpu.SemaphoreType.DMA,
            ],
            compiler_params=pltpu.CompilerParams(vmem_limit_bytes=moved + 4 * MIB),
            cost_estimate=pl.CostEstimate(
                flops=2 * order**2 * height * count * width // 4 * (cols - 1),
                bytes_accessed=moved // 2,
                transcendentals=0,
            ),
            name=f"peer_products_{at}",
        )(*given, *pieces, panel, totals)
        plan = plan or out[layers:]
        far = [d for d in range(layers // 2, layers)]
        turn = far + [d for d in range(1, layers) if d not in far]
        if at > 0:
            turn = turn[1:] + turn[:1]
        codes = [flipped(out[d], "layer", d) for d in turn]
        finished = [
            pl.pallas_call(
                functools.partial(finish_kernel, (layers, slots), (at, height)),
                out_shape=jax.ShapeDtypeStruct((own_rows, kept, at + height, order), jnp.bfloat16),
                in_specs=[vector] * (len(finished) + layers),
                out_specs=vector,
                compiler_params=pltpu.CompilerParams(
                    vmem_limit_bytes=16 * slots * block_size + 4 * MIB
                ),
                name=f"finish_{at}",
            )(*finished, out[0], *codes)
        ]
    return finished[0]


def solution(mesh):
    placed = (
        P(("row", "col", "layer"), None, None),
        P(("row", "col", "layer")),
        P(("row", "col", "layer")),
        P(("row", "layer"), "col", None, None),
        P(("row", "layer"), "col"),
        P("row", "col"),
    )
    return jax.shard_map(
        per_device,
        mesh=mesh,
        in_specs=placed,
        out_specs=P(("row", "layer"), "col", None, None),
        check_vma=False,
    )
```

```python
import functools

import jax
import jax.numpy as jnp
from jax import lax
from jax.experimental import pallas as pl
from jax.experimental.pallas import tpu as pltpu
from jax.sharding import PartitionSpec as P

GROUP = 8
LANES = 128
FIELD = 10
MIB = 2**20
HBM = pltpu.MemorySpace.HBM


def row_ranges(order):
    first = order * 5 // 8
    return [(0, first), (first, order - first)]


def in_hbm(*values):
    return [pltpu.with_memory_space_constraint(value, HBM) for value in values]


def flipped(value, axis, bits):
    return lax.ppermute(value, axis, [(i, i ^ bits) for i in range(lax.axis_size(axis))])


def gathered(value, axis):
    values = {0: value}
    bit = lax.axis_size(axis) // 2
    while bit:
        values |= {d ^ bit: flipped(held, axis, bit) for d, held in values.items()}
        bit //= 2
    return [values[d] for d in range(len(values))]


def shifted(value, axis, offset):
    size = lax.axis_size(axis)
    return lax.ppermute(value, axis, [((i + offset) % size, i) for i in range(size)])


def quotient(value, by):
    return value >> (by.bit_length() - 1) if by & (by - 1) == 0 else lax.div(value, by)


def remainder(value, by):
    return value & (by - 1) if by & (by - 1) == 0 else lax.rem(value, by)


def write_digits(tile, at, value):
    height, width = value.shape
    tile[at : at + height, :width] = remainder(value, LANES)
    tile[at + height : at + 2 * height, :width] = quotient(value, LANES)


def pack_first_kernel(sizes, a_rows, a_cols, c_cols, x_in, known, x_out, rows, cols, held, tile, sem):
    layers, count, piece_rows, width, local_rows, kept, order, height = sizes
    spot = x_out.at[pl.ds(0, count * height)].reshape(count, height, order)
    loads = [
        pltpu.make_async_copy(source, goal, sem.at[p])
        for p, (source, goal) in enumerate(
            ((a_rows, rows), (a_cols, cols), (c_cols, held), (x_in.at[:, pl.ds(0, height)], spot))
        )
    ]
    for load in loads:
        load.start()
    known[...] = jnp.zeros_like(known)
    tile[...] = jnp.zeros_like(tile)
    for load in loads[:3]:
        load.wait()
    own_rows = local_rows // layers
    row, col = rows[...], cols[...]
    here = quotient(row[:, :1], local_rows)
    layer = remainder(quotient(col[:, :1], piece_rows), layers)
    owner = quotient(col, piece_rows * layers)
    local = row - here * local_rows
    goal = (quotient(local, own_rows) ^ layer) * own_rows
    place = (
        ((owner ^ here) * piece_rows + remainder(col, piece_rows)) * width,
        (goal + remainder(local, own_rows)) * kept,
        local,
    )
    for p, value in enumerate(place):
        known[p : p + 1, :count] = value
        write_digits(tile, 2 * p, value)
    known[8 : 8 + kept, :local_rows] = held[...]
    x_out[count * height :] = tile[...].astype(jnp.float32).astype(jnp.bfloat16)
    loads[3].wait()


def pack_later_kernel(sizes, x_in, s_cols, s_in, s_out, *refs):
    count, piece, order, ranges = sizes
    x_out, (held, tile, sem) = refs[: len(ranges)], refs[len(ranges) :]
    sources = [(s_cols, held)]
    sources += [(s_in.at[q], s_out.at[pl.ds(q * order, order)]) for q in range(piece)]
    sources += [
        (x_in.at[:, pl.ds(first, height)], out.reshape(count, height, order))
        for (first, height), out in zip(ranges, x_out)
    ]
    loads = [pltpu.make_async_copy(*pair, sem.at[p]) for p, pair in enumerate(sources)]
    for load in loads:
        load.start()
    tile[...] = jnp.zeros_like(tile)
    loads[0].wait()
    write_digits(tile, 0, held[...])
    s_out[piece * order :] = tile[...].astype(jnp.float32).astype(jnp.bfloat16)
    for load in loads[1:]:
        load.wait()


def match(sizes, place, panel_cols, kept_cols, codes):
    width, local_rows, kept = sizes
    right, goal, local = place
    wanted, held = [jnp.zeros_like(right)] * width, [jnp.zeros_like(right)] * kept
    for p in range(panel_cols.shape[0]):
        for s in range(width):
            wanted[s] = jnp.where(right == p * width, panel_cols[p : p + 1, s : s + 1], wanted[s])
    for i in range(local_rows):
        for t in range(kept):
            held[t] = jnp.where(local == i, kept_cols[t : t + 1, i : i + 1], held[t])
    block = lax.broadcasted_iota(jnp.int32, right.shape, 1)
    for s in range(width):
        word = jnp.full_like(right, -1)
        for t in range(kept):
            pair = ((block << FIELD) | (right + s)) << FIELD | (goal + t)
            word = jnp.where(held[t] == wanted[s], pair, word)
        codes[s : s + 1] = word


def list_pairs(sizes, codes, pairs):
    count, width, trash = sizes
    total = jnp.int32(0)
    for n in range(count):
        for s in range(width):
            word = codes[s, n]
            pairs[total] = word
            total += (word >= 0).astype(jnp.int32)
    for g in range(GROUP):
        pairs[total + g] = trash
    return total


def add_products(left, panel, totals, pairs, total):
    height = totals.shape[1]
    mask = (1 << FIELD) - 1

    def one_group(group, carry):
        words = [pairs[group * GROUP + g] for g in range(GROUP)]
        products = []
        for word in words:
            at = pl.multiple_of((word >> (2 * FIELD)) * height, height)
            products.append(
                jnp.dot(
                    left[pl.ds(at, height)],
                    panel[(word >> FIELD) & mask],
                    preferred_element_type=jnp.float32,
                )
            )
        for word, product in zip(words, products):
            totals[word & mask] += product
        return carry

    lax.fori_loop(0, quotient(total + GROUP - 1, GROUP), one_group, 0)


def own_kernel(sizes, ranges, known, *refs):
    rows, count, piece_rows, width, local_rows, kept, order = sizes
    x_in, s_in, refs = refs[: len(ranges)], refs[len(ranges) :][:rows], refs[len(ranges) + rows :]
    totals, panel, panel_cols, codes, numbers, pairs, sem = refs
    piece = piece_rows * width
    for d in range(rows):
        tile = s_in[d][piece * order :].astype(jnp.float32).astype(jnp.int32)
        panel_cols[d * piece_rows : (d + 1) * piece_rows] = (
            tile[:piece_rows] + tile[piece_rows : 2 * piece_rows] * LANES
        )
    place = known[0:1], known[1:2], known[2:3]
    match((width, local_rows, kept), place, panel_cols[...], known[8 : 8 + kept], codes)
    copy = pltpu.make_async_copy(codes, numbers, sem)
    copy.start()
    totals[...] = jnp.zeros_like(totals)
    for d in range(rows):
        for q in range(piece):
            panel[d * piece + q] = s_in[d][q * order : (q + 1) * order]
    copy.wait()
    total = list_pairs((count, width, totals.shape[0] - 1), numbers, pairs)
    for (first, height), blocks in zip(ranges, x_in):
        add_products(blocks, panel, totals.at[:, pl.ds(first, height)], pairs, total)


def peer_kernel(sizes, span, *refs):
    cols, layers, count, width, local_rows, kept = sizes
    first, height = span
    slots = local_rows * kept // layers
    if first == 0:
        known, panel_cols, *refs = refs
    else:
        codes, *refs = refs
    x_in, refs = refs[: cols - 1], refs[cols - 1 :]
    panel, before, own, sent, refs = refs[0], refs[1], refs[2], refs[3 : 2 + layers], refs[2 + layers :]
    if first == 0:
        codes, *refs = refs
        for j in range(cols - 1):
            digits = x_in[j][count * height :].astype(jnp.float32).astype(jnp.int32)
            place = [digits[p : p + 1] + digits[p + 1 : p + 2] * LANES for p in (0, 2, 4)]
            match(
                (width, local_rows, kept), place, panel_cols[...], known[8 : 8 + kept], codes.at[j]
            )
    totals, numbers, pairs, sem = refs
    copy = pltpu.make_async_copy(codes, numbers, sem)
    copy.start()
    totals[...] = before[:, first : first + height]
    copy.wait()
    for j in range(cols - 1):
        total = list_pairs((count, width, layers * slots), numbers.at[j], pairs)
        add_products(x_in[j], panel, totals, pairs, total)

    own[...] = totals[:slots]
    half = height // 2
    sublane = lax.broadcasted_iota(jnp.int32, (8, totals.shape[2]), 0)
    for d in range(1, layers):
        code = sent[d - 1]
        for u in range(slots):
            value = totals[d * slots + u]
            peak = jnp.max(jnp.abs(value), axis=0, keepdims=True)
            power = jnp.floor(jnp.log2(jnp.maximum(peak, 1e-30)) + 1e-3) + 1.0
            whole = jnp.floor(value * jnp.exp2(15.0 - power) + 0.5).astype(jnp.int32)
            word = (whole[:half] << 16) | (whole[half:] & 0xFFFF)
            bits = ((power.astype(jnp.int32) + 128) >> sublane) & 1
            code[pl.ds(u * half, 8)] = (word[:8] & ~1) | bits
            code[pl.ds(u * half + 8, half - 8)] = word[8:]


def finish_kernel(sizes, span, *refs):
    layers, slots = sizes
    first, height = span
    half = height // 2
    sublane = lax.broadcasted_iota(jnp.int32, (8, refs[-1].shape[3]), 0)
    before, own, codes, result = refs[: first > 0], refs[-layers - 1], refs[-layers:-1], refs[-1]
    kept = result.shape[1]
    for done in before:
        result[:, :, :first] = done[...]
    for u in range(slots):
        high, low = own[u, :half], own[u, half:]
        for code in codes:
            word = code[pl.ds(u * half, half)]
            power = jnp.sum((word[:8] & 1) << sublane, axis=0, keepdims=True).astype(jnp.float32)
            scale = jnp.exp2(power - (128.0 + 15.0))
            word = jnp.concatenate([word[:8] & ~1, word[8:]])
            high += (word >> 16).astype(jnp.float32) * scale
            low += ((word << 16) >> 16).astype(jnp.float32) * scale
        result[u // kept, u % kept, first : first + half] = high.astype(jnp.bfloat16)
        result[u // kept, u % kept, first + half : first + height] = low.astype(jnp.bfloat16)


def per_device(a_blocks, a_rows, a_cols, s_blocks, s_cols, c_cols):
    rows, cols, layers = (lax.axis_size(axis) for axis in ("row", "col", "layer"))
    count, order = a_blocks.shape[:2]
    piece_rows, width = s_cols.shape
    local_rows, kept = c_cols.shape
    own_rows = local_rows // layers
    slots = own_rows * kept
    all_slots = layers * slots
    ranges = row_ranges(order)
    piece = piece_rows * width
    panel_size = rows * piece
    block_size = order * order
    flat_s = s_blocks.reshape(piece, order, order)
    note_height = (2 * piece_rows + 15) // 16 * 16
    code_height = (width + 7) // 8 * 8

    vector = pl.BlockSpec(memory_space=pltpu.VMEM)
    far = pl.BlockSpec(memory_space=HBM)

    first_height = ranges[0][1]
    known, x_first = pl.pallas_call(
        functools.partial(
            pack_first_kernel,
            (layers, count, piece_rows, width, local_rows, kept, order, first_height),
        ),
        out_shape=[
            jax.ShapeDtypeStruct((16, LANES), jnp.int32),
            jax.ShapeDtypeStruct((count * first_height + 16, order), jnp.bfloat16),
        ],
        in_specs=[far] * 4,
        out_specs=[vector] * 2,
        scratch_shapes=[
            pltpu.VMEM((1, count), jnp.int32),
            pltpu.VMEM((1, count), jnp.int32),
            pltpu.VMEM((kept, local_rows), jnp.int32),
            pltpu.VMEM((16, LANES), jnp.int32),
            pltpu.SemaphoreType.DMA((4,)),
        ],
        compiler_params=pltpu.CompilerParams(
            vmem_limit_bytes=2 * block_size * (count + 1) + 4 * MIB
        ),
        name="pack_first",
    )(*in_hbm(a_rows.reshape(1, count), a_cols.reshape(1, count), c_cols.T, a_blocks))
    first_piece = [shifted(x_first, "col", j) for j in range(1, cols)]
    later_blocks, later_s_cols, later_s, _ = lax.optimization_barrier(
        (a_blocks, s_cols, flat_s, known)
    )
    s_sent, *x_later = pl.pallas_call(
        functools.partial(pack_later_kernel, (count, piece, order, ranges[1:])),
        out_shape=[jax.ShapeDtypeStruct((piece * order + note_height, order), jnp.bfloat16)]
        + [
            jax.ShapeDtypeStruct((count * height, order), jnp.bfloat16) for _, height in ranges[1:]
        ],
        in_specs=[far] * 3,
        out_specs=[vector] * len(ranges),
        scratch_shapes=[
            pltpu.VMEM((piece_rows, width), jnp.int32),
            pltpu.VMEM((note_height, LANES), jnp.int32),
            pltpu.SemaphoreType.DMA((piece + len(ranges),)),
        ],
        compiler_params=pltpu.CompilerParams(
            vmem_limit_bytes=2 * block_size * (count + piece + 1) + 4 * MIB
        ),
        name="pack_later",
    )(*in_hbm(later_blocks, later_s_cols, later_s))
    x_sent = [x_first, *x_later]
    s_pieces = gathered(s_sent, "row")
    later, _ = lax.optimization_barrier((x_sent[1:], s_pieces))
    x_pieces = [first_piece]
    x_pieces += [[shifted(part, "col", j) for j in range(1, cols)] for part in later]

    moved = block_size * (4 * all_slots + 4 * panel_size + 2 * count)
    totals, panel, panel_cols = pl.pallas_call(
        functools.partial(
            own_kernel, (rows, count, piece_rows, width, local_rows, kept, order), ranges
        ),
        out_shape=[
            jax.ShapeDtypeStruct((all_slots + 1, order, order), jnp.float32),
            jax.ShapeDtypeStruct((panel_size, order, order), jnp.bfloat16),
            jax.ShapeDtypeStruct((rows * piece_rows, LANES), jnp.int32),
        ],
        in_specs=[vector] * (1 + len(ranges) + rows),
        out_specs=[vector] * 3,
        scratch_shapes=[
            pltpu.VMEM((code_height, LANES), jnp.int32),
            pltpu.SMEM((code_height, LANES), jnp.int32),
            pltpu.SMEM((count * width + GROUP,), jnp.int32),
            pltpu.SemaphoreType.DMA,
        ],
        compiler_params=pltpu.CompilerParams(vmem_limit_bytes=moved + 4 * MIB),
        cost_estimate=pl.CostEstimate(
            flops=2 * order**3 * count * width // 4, bytes_accessed=moved, transcendentals=0
        ),
        name="own_products",
    )(known, *x_sent, *s_pieces)

    moved = block_size * (8 * all_slots + 2 * panel_size + 2 * count * (cols - 1))
    code_shape = (cols - 1, code_height, LANES)
    finished, plan = [], []
    for (at, height), pieces in zip(ranges, x_pieces):
        code_rows = slots * (height // 2)
        out_shape = [jax.ShapeDtypeStruct((slots, height, order), jnp.float32)]
        out_shape += [jax.ShapeDtypeStruct((code_rows, order), jnp.int32)] * (layers - 1)
        if at == 0:
            out_shape.append(jax.ShapeDtypeStruct(code_shape, jnp.int32))
        given = plan or (known, panel_cols)
        out = pl.pallas_call(
            functools.partial(
                peer_kernel, (cols, layers, count, width, local_rows, kept), (at, height)
            ),
            out_shape=out_shape,
            in_specs=[vector] * (len(given) + cols + 1),
            out_specs=[vector] * len(out_shape),
            scratch_shapes=[
                pltpu.VMEM((all_slots + 1, height, order), jnp.float32),
                pltpu.SMEM(code_shape, jnp.int32),
                pltpu.SMEM((count * width + GROUP,), jnp.int32),
                pltpu.SemaphoreType.DMA,
            ],
            compiler_params=pltpu.CompilerParams(vmem_limit_bytes=moved + 4 * MIB),
            cost_estimate=pl.CostEstimate(
                flops=2 * order**2 * height * count * width // 4 * (cols - 1),
                bytes_accessed=moved // 2,
                transcendentals=0,
            ),
            name=f"peer_products_{at}",
        )(*given, *pieces, panel, totals)
        plan = plan or out[layers:]
        far = [d for d in range(layers // 2, layers)]
        turn = far + [d for d in range(1, layers) if d not in far]
        if at > 0:
            turn = turn[1:] + turn[:1]
        codes = [flipped(out[d], "layer", d) for d in turn]
        finished = [
            pl.pallas_call(
                functools.partial(finish_kernel, (layers, slots), (at, height)),
                out_shape=jax.ShapeDtypeStruct((own_rows, kept, at + height, order), jnp.bfloat16),
                in_specs=[vector] * (len(finished) + layers),
                out_specs=vector,
                compiler_params=pltpu.CompilerParams(
                    vmem_limit_bytes=16 * slots * block_size + 4 * MIB
                ),
                name=f"finish_{at}",
            )(*finished, out[0], *codes)
        ]
    return finished[0]


def solution(mesh):
    placed = (
        P(("row", "col", "layer"), None, None),
        P(("row", "col", "layer")),
        P(("row", "col", "layer")),
        P(("row", "layer"), "col", None, None),
        P(("row", "layer"), "col"),
        P("row", "col"),
    )
    return jax.shard_map(
        per_device,
        mesh=mesh,
        in_specs=placed,
        out_specs=P(("row", "layer"), "col", None, None),
        check_vma=False,
    )
```

```python
import functools

import jax
import jax.numpy as jnp
from jax import lax
from jax.experimental import pallas as pl
from jax.experimental.pallas import tpu as pltpu
from jax.sharding import PartitionSpec as P

GROUP = 8
LANES = 128
FIELD = 10
MIB = 2**20
HBM = pltpu.MemorySpace.HBM


def row_ranges(order):
    first = order * 5 // 8
    return [(0, first), (first, order - first)]


def in_hbm(*values):
    return [pltpu.with_memory_space_constraint(value, HBM) for value in values]


def flipped(value, axis, bits):
    return lax.ppermute(value, axis, [(i, i ^ bits) for i in range(lax.axis_size(axis))])


def gathered(value, axis):
    values = {0: value}
    bit = lax.axis_size(axis) // 2
    while bit:
        values |= {d ^ bit: flipped(held, axis, bit) for d, held in values.items()}
        bit //= 2
    return [values[d] for d in range(len(values))]


def shifted(value, axis, offset):
    size = lax.axis_size(axis)
    return lax.ppermute(value, axis, [((i + offset) % size, i) for i in range(size)])


def quotient(value, by):
    return value >> (by.bit_length() - 1) if by & (by - 1) == 0 else lax.div(value, by)


def remainder(value, by):
    return value & (by - 1) if by & (by - 1) == 0 else lax.rem(value, by)


def write_digits(tile, at, value):
    height, width = value.shape
    tile[at : at + height, :width] = remainder(value, LANES)
    tile[at + height : at + 2 * height, :width] = quotient(value, LANES)


def pack_first_kernel(sizes, a_rows, a_cols, c_cols, x_in, known, x_out, rows, cols, held, tile, sem):
    layers, count, piece_rows, width, local_rows, kept, order, height = sizes
    spot = x_out.at[pl.ds(0, count * height)].reshape(count, height, order)
    loads = [
        pltpu.make_async_copy(source, goal, sem.at[p])
        for p, (source, goal) in enumerate(
            ((a_rows, rows), (a_cols, cols), (c_cols, held), (x_in.at[:, pl.ds(0, height)], spot))
        )
    ]
    for load in loads:
        load.start()
    known[...] = jnp.zeros_like(known)
    tile[...] = jnp.zeros_like(tile)
    for load in loads[:3]:
        load.wait()
    own_rows = local_rows // layers
    row, col = rows[...], cols[...]
    here = quotient(row[:, :1], local_rows)
    layer = remainder(quotient(col[:, :1], piece_rows), layers)
    owner = quotient(col, piece_rows * layers)
    local = row - here * local_rows
    goal = (quotient(local, own_rows) ^ layer) * own_rows
    place = (
        ((owner ^ here) * piece_rows + remainder(col, piece_rows)) * width,
        (goal + remainder(local, own_rows)) * kept,
        local,
    )
    for p, value in enumerate(place):
        known[p : p + 1, :count] = value
        write_digits(tile, 2 * p, value)
    known[8 : 8 + kept, :local_rows] = held[...]
    x_out[count * height :] = tile[...].astype(jnp.float32).astype(jnp.bfloat16)
    loads[3].wait()


def pack_later_kernel(sizes, x_in, s_cols, s_in, s_out, *refs):
    count, piece, order, ranges = sizes
    x_out, (held, tile, sem) = refs[: len(ranges)], refs[len(ranges) :]
    sources = [(s_cols, held)]
    sources += [(s_in.at[q], s_out.at[pl.ds(q * order, order)]) for q in range(piece)]
    sources += [
        (x_in.at[:, pl.ds(first, height)], out.reshape(count, height, order))
        for (first, height), out in zip(ranges, x_out)
    ]
    loads = [pltpu.make_async_copy(*pair, sem.at[p]) for p, pair in enumerate(sources)]
    for load in loads:
        load.start()
    tile[...] = jnp.zeros_like(tile)
    loads[0].wait()
    write_digits(tile, 0, held[...])
    s_out[piece * order :] = tile[...].astype(jnp.float32).astype(jnp.bfloat16)
    for load in loads[1:]:
        load.wait()


def match(sizes, place, panel_cols, kept_cols, codes):
    width, local_rows, kept = sizes
    right, goal, local = place
    wanted, held = [jnp.zeros_like(right)] * width, [jnp.zeros_like(right)] * kept
    for p in range(panel_cols.shape[0]):
        for s in range(width):
            wanted[s] = jnp.where(right == p * width, panel_cols[p : p + 1, s : s + 1], wanted[s])
    for i in range(local_rows):
        for t in range(kept):
            held[t] = jnp.where(local == i, kept_cols[t : t + 1, i : i + 1], held[t])
    block = lax.broadcasted_iota(jnp.int32, right.shape, 1)
    for s in range(width):
        word = jnp.full_like(right, -1)
        for t in range(kept):
            pair = ((block << FIELD) | (right + s)) << FIELD | (goal + t)
            word = jnp.where(held[t] == wanted[s], pair, word)
        codes[s : s + 1] = word


def list_pairs(sizes, codes, pairs):
    count, width, trash = sizes
    total = jnp.int32(0)
    for n in range(count):
        for s in range(width):
            word = codes[s, n]
            pairs[total] = word
            total += (word >= 0).astype(jnp.int32)
    for g in range(GROUP):
        pairs[total + g] = trash
    return total


def add_products(left, panel, totals, pairs, total):
    height = totals.shape[1]
    mask = (1 << FIELD) - 1

    def one_group(group, carry):
        words = [pairs[group * GROUP + g] for g in range(GROUP)]
        products = []
        for word in words:
            at = pl.multiple_of((word >> (2 * FIELD)) * height, height)
            products.append(
                jnp.dot(
                    left[pl.ds(at, height)],
                    panel[(word >> FIELD) & mask],
                    preferred_element_type=jnp.float32,
                )
            )
        for word, product in zip(words, products):
            totals[word & mask] += product
        return carry

    lax.fori_loop(0, quotient(total + GROUP - 1, GROUP), one_group, 0)


def own_kernel(sizes, ranges, known, *refs):
    rows, count, piece_rows, width, local_rows, kept, order = sizes
    x_in, s_in, refs = refs[: len(ranges)], refs[len(ranges) :][:rows], refs[len(ranges) + rows :]
    totals, panel, panel_cols, codes, numbers, pairs, sem = refs
    piece = piece_rows * width
    for d in range(rows):
        tile = s_in[d][piece * order :].astype(jnp.float32).astype(jnp.int32)
        panel_cols[d * piece_rows : (d + 1) * piece_rows] = (
            tile[:piece_rows] + tile[piece_rows : 2 * piece_rows] * LANES
        )
    place = known[0:1], known[1:2], known[2:3]
    match((width, local_rows, kept), place, panel_cols[...], known[8 : 8 + kept], codes)
    copy = pltpu.make_async_copy(codes, numbers, sem)
    copy.start()
    totals[...] = jnp.zeros_like(totals)
    for d in range(rows):
        for q in range(piece):
            panel[d * piece + q] = s_in[d][q * order : (q + 1) * order]
    copy.wait()
    total = list_pairs((count, width, totals.shape[0] - 1), numbers, pairs)
    for (first, height), blocks in zip(ranges, x_in):
        add_products(blocks, panel, totals.at[:, pl.ds(first, height)], pairs, total)


def peer_kernel(sizes, span, *refs):
    cols, layers, count, width, local_rows, kept = sizes
    first, height = span
    slots = local_rows * kept // layers
    if first == 0:
        known, panel_cols, *refs = refs
    else:
        codes, *refs = refs
    x_in, refs = refs[: cols - 1], refs[cols - 1 :]
    panel, before, own, sent, refs = refs[0], refs[1], refs[2], refs[3 : 2 + layers], refs[2 + layers :]
    if first == 0:
        codes, *refs = refs
        for j in range(cols - 1):
            digits = x_in[j][count * height :].astype(jnp.float32).astype(jnp.int32)
            place = [digits[p : p + 1] + digits[p + 1 : p + 2] * LANES for p in (0, 2, 4)]
            match(
                (width, local_rows, kept), place, panel_cols[...], known[8 : 8 + kept], codes.at[j]
            )
    totals, numbers, pairs, sem = refs
    copy = pltpu.make_async_copy(codes, numbers, sem)
    copy.start()
    totals[...] = before[:, first : first + height]
    copy.wait()
    for j in range(cols - 1):
        total = list_pairs((count, width, layers * slots), numbers.at[j], pairs)
        add_products(x_in[j], panel, totals, pairs, total)

    own[...] = totals[:slots]
    half = height // 2
    sublane = lax.broadcasted_iota(jnp.int32, (8, totals.shape[2]), 0)
    for d in range(1, layers):
        code = sent[d - 1]
        for u in range(slots):
            value = totals[d * slots + u]
            peak = jnp.max(jnp.abs(value), axis=0, keepdims=True)
            power = jnp.floor(jnp.log2(jnp.maximum(peak, 1e-30)) + 1e-3) + 1.0
            whole = jnp.floor(value * jnp.exp2(15.0 - power) + 0.5).astype(jnp.int32)
            word = (whole[:half] << 16) | (whole[half:] & 0xFFFF)
            bits = ((power.astype(jnp.int32) + 128) >> sublane) & 1
            code[pl.ds(u * half, 8)] = (word[:8] & ~1) | bits
            code[pl.ds(u * half + 8, half - 8)] = word[8:]


def finish_kernel(sizes, span, *refs):
    layers, slots = sizes
    first, height = span
    half = height // 2
    sublane = lax.broadcasted_iota(jnp.int32, (8, refs[-1].shape[3]), 0)
    before, own, codes, result = refs[: first > 0], refs[-layers - 1], refs[-layers:-1], refs[-1]
    kept = result.shape[1]
    for done in before:
        result[:, :, :first] = done[...]
    for u in range(slots):
        high, low = own[u, :half], own[u, half:]
        for code in codes:
            word = code[pl.ds(u * half, half)]
            power = jnp.sum((word[:8] & 1) << sublane, axis=0, keepdims=True).astype(jnp.float32)
            scale = jnp.exp2(power - (128.0 + 15.0))
            word = jnp.concatenate([word[:8] & ~1, word[8:]])
            high += (word >> 16).astype(jnp.float32) * scale
            low += ((word << 16) >> 16).astype(jnp.float32) * scale
        result[u // kept, u % kept, first : first + half] = high.astype(jnp.bfloat16)
        result[u // kept, u % kept, first + half : first + height] = low.astype(jnp.bfloat16)


def per_device(a_blocks, a_rows, a_cols, s_blocks, s_cols, c_cols):
    rows, cols, layers = (lax.axis_size(axis) for axis in ("row", "col", "layer"))
    count, order = a_blocks.shape[:2]
    piece_rows, width = s_cols.shape
    local_rows, kept = c_cols.shape
    own_rows = local_rows // layers
    slots = own_rows * kept
    all_slots = layers * slots
    ranges = row_ranges(order)
    piece = piece_rows * width
    panel_size = rows * piece
    block_size = order * order
    flat_s = s_blocks.reshape(piece, order, order)
    note_height = (2 * piece_rows + 15) // 16 * 16
    code_height = (width + 7) // 8 * 8

    vector = pl.BlockSpec(memory_space=pltpu.VMEM)
    far = pl.BlockSpec(memory_space=HBM)

    first_height = ranges[0][1]
    known, x_first = pl.pallas_call(
        functools.partial(
            pack_first_kernel,
            (layers, count, piece_rows, width, local_rows, kept, order, first_height),
        ),
        out_shape=[
            jax.ShapeDtypeStruct((16, LANES), jnp.int32),
            jax.ShapeDtypeStruct((count * first_height + 16, order), jnp.bfloat16),
        ],
        in_specs=[far] * 4,
        out_specs=[vector] * 2,
        scratch_shapes=[
            pltpu.VMEM((1, count), jnp.int32),
            pltpu.VMEM((1, count), jnp.int32),
            pltpu.VMEM((kept, local_rows), jnp.int32),
            pltpu.VMEM((16, LANES), jnp.int32),
            pltpu.SemaphoreType.DMA((4,)),
        ],
        compiler_params=pltpu.CompilerParams(
            vmem_limit_bytes=2 * block_size * (count + 1) + 4 * MIB
        ),
        name="pack_first",
    )(*in_hbm(a_rows.reshape(1, count), a_cols.reshape(1, count), c_cols.T, a_blocks))
    first_piece = [shifted(x_first, "col", j) for j in range(1, cols)]
    later_blocks, later_s_cols, later_s, _ = lax.optimization_barrier(
        (a_blocks, s_cols, flat_s, known)
    )
    s_sent, *x_later = pl.pallas_call(
        functools.partial(pack_later_kernel, (count, piece, order, ranges[1:])),
        out_shape=[jax.ShapeDtypeStruct((piece * order + note_height, order), jnp.bfloat16)]
        + [
            jax.ShapeDtypeStruct((count * height, order), jnp.bfloat16) for _, height in ranges[1:]
        ],
        in_specs=[far] * 3,
        out_specs=[vector] * len(ranges),
        scratch_shapes=[
            pltpu.VMEM((piece_rows, width), jnp.int32),
            pltpu.VMEM((note_height, LANES), jnp.int32),
            pltpu.SemaphoreType.DMA((piece + len(ranges),)),
        ],
        compiler_params=pltpu.CompilerParams(
            vmem_limit_bytes=2 * block_size * (count + piece + 1) + 4 * MIB
        ),
        name="pack_later",
    )(*in_hbm(later_blocks, later_s_cols, later_s))
    x_sent = [x_first, *x_later]
    s_pieces = gathered(s_sent, "row")
    moved = block_size * (4 * all_slots + 4 * panel_size + 2 * count)
    totals, panel, panel_cols = pl.pallas_call(
        functools.partial(
            own_kernel, (rows, count, piece_rows, width, local_rows, kept, order), ranges
        ),
        out_shape=[
            jax.ShapeDtypeStruct((all_slots + 1, order, order), jnp.float32),
            jax.ShapeDtypeStruct((panel_size, order, order), jnp.bfloat16),
            jax.ShapeDtypeStruct((rows * piece_rows, LANES), jnp.int32),
        ],
        in_specs=[vector] * (1 + len(ranges) + rows),
        out_specs=[vector] * 3,
        scratch_shapes=[
            pltpu.VMEM((code_height, LANES), jnp.int32),
            pltpu.SMEM((code_height, LANES), jnp.int32),
            pltpu.SMEM((count * width + GROUP,), jnp.int32),
            pltpu.SemaphoreType.DMA,
        ],
        compiler_params=pltpu.CompilerParams(vmem_limit_bytes=moved + 4 * MIB),
        cost_estimate=pl.CostEstimate(
            flops=2 * order**3 * count * width // 4, bytes_accessed=moved, transcendentals=0
        ),
        name="own_products",
    )(known, *x_sent, *s_pieces)

    moved = block_size * (8 * all_slots + 2 * panel_size + 2 * count * (cols - 1))
    later, panel_cols = lax.optimization_barrier((x_sent[1:], panel_cols))
    x_pieces = [first_piece]
    x_pieces += [[shifted(part, "col", j) for j in range(1, cols)] for part in later]

    code_shape = (cols - 1, code_height, LANES)
    finished, plan = [], []
    for (at, height), pieces in zip(ranges, x_pieces):
        code_rows = slots * (height // 2)
        out_shape = [jax.ShapeDtypeStruct((slots, height, order), jnp.float32)]
        out_shape += [jax.ShapeDtypeStruct((code_rows, order), jnp.int32)] * (layers - 1)
        if at == 0:
            out_shape.append(jax.ShapeDtypeStruct(code_shape, jnp.int32))
        given = plan or (known, panel_cols)
        out = pl.pallas_call(
            functools.partial(
                peer_kernel, (cols, layers, count, width, local_rows, kept), (at, height)
            ),
            out_shape=out_shape,
            in_specs=[vector] * (len(given) + cols + 1),
            out_specs=[vector] * len(out_shape),
            scratch_shapes=[
                pltpu.VMEM((all_slots + 1, height, order), jnp.float32),
                pltpu.SMEM(code_shape, jnp.int32),
                pltpu.SMEM((count * width + GROUP,), jnp.int32),
                pltpu.SemaphoreType.DMA,
            ],
            compiler_params=pltpu.CompilerParams(vmem_limit_bytes=moved + 4 * MIB),
            cost_estimate=pl.CostEstimate(
                flops=2 * order**2 * height * count * width // 4 * (cols - 1),
                bytes_accessed=moved // 2,
                transcendentals=0,
            ),
            name=f"peer_products_{at}",
        )(*given, *pieces, panel, totals)
        plan = plan or out[layers:]
        far = [d for d in range(layers // 2, layers)]
        turn = far + [d for d in range(1, layers) if d not in far]
        if at > 0:
            turn = turn[1:] + turn[:1]
        codes = [flipped(out[d], "layer", d) for d in turn]
        finished = [
            pl.pallas_call(
                functools.partial(finish_kernel, (layers, slots), (at, height)),
                out_shape=jax.ShapeDtypeStruct((own_rows, kept, at + height, order), jnp.bfloat16),
                in_specs=[vector] * (len(finished) + layers),
                out_specs=vector,
                compiler_params=pltpu.CompilerParams(
                    vmem_limit_bytes=16 * slots * block_size + 4 * MIB
                ),
                name=f"finish_{at}",
            )(*finished, out[0], *codes)
        ]
    return finished[0]


def solution(mesh):
    placed = (
        P(("row", "col", "layer"), None, None),
        P(("row", "col", "layer")),
        P(("row", "col", "layer")),
        P(("row", "layer"), "col", None, None),
        P(("row", "layer"), "col"),
        P("row", "col"),
    )
    return jax.shard_map(
        per_device,
        mesh=mesh,
        in_specs=placed,
        out_specs=P(("row", "layer"), "col", None, None),
        check_vma=False,
    )
```

```python
import functools

import jax
import jax.numpy as jnp
from jax import lax
from jax.experimental import pallas as pl
from jax.experimental.pallas import tpu as pltpu
from jax.sharding import PartitionSpec as P

GROUP = 8
LANES = 128
FIELD = 10
MIB = 2**20
HBM = pltpu.MemorySpace.HBM


def row_ranges(order):
    first = order * 5 // 8
    return [(0, first), (first, order - first)]


def in_hbm(*values):
    return [pltpu.with_memory_space_constraint(value, HBM) for value in values]


def flipped(value, axis, bits):
    return lax.ppermute(value, axis, [(i, i ^ bits) for i in range(lax.axis_size(axis))])


def gathered(value, axis):
    values = {0: value}
    bit = lax.axis_size(axis) // 2
    while bit:
        values |= {d ^ bit: flipped(held, axis, bit) for d, held in values.items()}
        bit //= 2
    return [values[d] for d in range(len(values))]


def shifted(value, axis, offset):
    size = lax.axis_size(axis)
    return lax.ppermute(value, axis, [((i + offset) % size, i) for i in range(size)])


def quotient(value, by):
    return value >> (by.bit_length() - 1) if by & (by - 1) == 0 else lax.div(value, by)


def remainder(value, by):
    return value & (by - 1) if by & (by - 1) == 0 else lax.rem(value, by)


def write_digits(tile, at, value):
    height, width = value.shape
    tile[at : at + height, :width] = remainder(value, LANES)
    tile[at + height : at + 2 * height, :width] = quotient(value, LANES)


def copy_step(count):
    return pl.cdiv(count, 6)


def pack_first_kernel(sizes, a_rows, a_cols, c_cols, x_in, known, x_out, rows, cols, held, tile, sem):
    layers, count, piece_rows, width, local_rows, kept, order, height = sizes
    spot = x_out.at[pl.ds(0, count * height)].reshape(count, height, order)
    pairs = [(a_rows, rows), (a_cols, cols), (c_cols, held)]
    step = copy_step(count)
    for n in range(0, count, step):
        some = pl.ds(n, min(step, count - n))
        pairs.append((x_in.at[some, pl.ds(0, height)], spot.at[some]))
    loads = [pltpu.make_async_copy(*pair, sem.at[p]) for p, pair in enumerate(pairs)]
    for load in loads:
        load.start()
    known[...] = jnp.zeros_like(known)
    tile[...] = jnp.zeros_like(tile)
    for load in loads[:3]:
        load.wait()
    own_rows = local_rows // layers
    row, col = rows[...], cols[...]
    here = quotient(row[:, :1], local_rows)
    layer = remainder(quotient(col[:, :1], piece_rows), layers)
    owner = quotient(col, piece_rows * layers)
    local = row - here * local_rows
    goal = (quotient(local, own_rows) ^ layer) * own_rows
    place = (
        ((owner ^ here) * piece_rows + remainder(col, piece_rows)) * width,
        (goal + remainder(local, own_rows)) * kept,
        local,
    )
    for p, value in enumerate(place):
        known[p : p + 1, :count] = value
        write_digits(tile, 2 * p, value)
    known[8 : 8 + kept, :local_rows] = held[...]
    x_out[count * height :] = tile[...].astype(jnp.float32).astype(jnp.bfloat16)
    for load in loads[3:]:
        load.wait()


def pack_later_kernel(sizes, x_in, s_cols, s_in, s_out, *refs):
    count, piece, order, ranges = sizes
    x_out, (held, tile, sem) = refs[: len(ranges)], refs[len(ranges) :]
    sources = [(s_cols, held)]
    sources += [(s_in.at[q], s_out.at[pl.ds(q * order, order)]) for q in range(piece)]
    sources += [
        (x_in.at[:, pl.ds(first, height)], out.reshape(count, height, order))
        for (first, height), out in zip(ranges, x_out)
    ]
    loads = [pltpu.make_async_copy(*pair, sem.at[p]) for p, pair in enumerate(sources)]
    for load in loads:
        load.start()
    tile[...] = jnp.zeros_like(tile)
    loads[0].wait()
    write_digits(tile, 0, held[...])
    s_out[piece * order :] = tile[...].astype(jnp.float32).astype(jnp.bfloat16)
    for load in loads[1:]:
        load.wait()


def match(sizes, place, panel_cols, kept_cols, codes):
    width, local_rows, kept = sizes
    right, goal, local = place
    wanted, held = [jnp.zeros_like(right)] * width, [jnp.zeros_like(right)] * kept
    for p in range(panel_cols.shape[0]):
        for s in range(width):
            wanted[s] = jnp.where(right == p * width, panel_cols[p : p + 1, s : s + 1], wanted[s])
    for i in range(local_rows):
        for t in range(kept):
            held[t] = jnp.where(local == i, kept_cols[t : t + 1, i : i + 1], held[t])
    block = lax.broadcasted_iota(jnp.int32, right.shape, 1)
    for s in range(width):
        word = jnp.full_like(right, -1)
        for t in range(kept):
            pair = ((block << FIELD) | (right + s)) << FIELD | (goal + t)
            word = jnp.where(held[t] == wanted[s], pair, word)
        codes[s : s + 1] = word


def list_height(count, width):
    return (count * width // GROUP + 2 + 7) // 8 * 8


def list_pairs(sizes, codes, pairs):
    count, width, trash = sizes
    total = jnp.int32(0)
    for n in range(count):
        for s in range(width):
            word = codes[s, n]
            pairs[quotient(total, GROUP), remainder(total, GROUP)] = word
            total += (word >= 0).astype(jnp.int32)
    for g in range(GROUP):
        pairs[quotient(total + g, GROUP), remainder(total + g, GROUP)] = trash
    groups = quotient(total + GROUP - 1, GROUP)
    pairs[pairs.shape[0] - 1, 0] = groups
    return groups


def add_products(left, panel, totals, words_of, groups):
    height = totals.shape[1]
    mask = (1 << FIELD) - 1

    def one_group(group, carry):
        words = words_of(group)
        products = []
        for word in words:
            at = pl.multiple_of((word >> (2 * FIELD)) * height, height)
            products.append(
                jnp.dot(
                    left[pl.ds(at, height)],
                    panel[(word >> FIELD) & mask],
                    preferred_element_type=jnp.float32,
                )
            )
        for word, product in zip(words, products):
            totals[word & mask] += product
        return carry

    lax.fori_loop(0, groups, one_group, 0)


def own_kernel(sizes, ranges, known, *refs):
    rows, count, piece_rows, width, local_rows, kept, order = sizes
    x_in, s_in, refs = refs[: len(ranges)], refs[len(ranges) :][:rows], refs[len(ranges) + rows :]
    totals, panel, panel_cols, codes, numbers, pairs, sem = refs
    piece = piece_rows * width
    for d in range(rows):
        tile = s_in[d][piece * order :].astype(jnp.float32).astype(jnp.int32)
        panel_cols[d * piece_rows : (d + 1) * piece_rows] = (
            tile[:piece_rows] + tile[piece_rows : 2 * piece_rows] * LANES
        )
    place = known[0:1], known[1:2], known[2:3]
    match((width, local_rows, kept), place, panel_cols[...], known[8 : 8 + kept], codes)
    copy = pltpu.make_async_copy(codes, numbers, sem)
    copy.start()
    totals[...] = jnp.zeros_like(totals)
    for d in range(rows):
        for q in range(piece):
            panel[d * piece + q] = s_in[d][q * order : (q + 1) * order]
    copy.wait()
    groups = list_pairs((count, width, totals.shape[0] - 1), numbers, pairs)

    def words_of(group):
        return [pairs[group, g] for g in range(GROUP)]

    for (first, height), blocks in zip(ranges, x_in):
        add_products(blocks, panel, totals.at[:, pl.ds(first, height)], words_of, groups)


def peer_kernel(sizes, span, *refs):
    cols, layers, count, width, local_rows, kept = sizes
    first, height = span
    slots = local_rows * kept // layers
    if first == 0:
        known, panel_cols, *refs = refs
    else:
        listed, *refs = refs
    x_in, refs = refs[: cols - 1], refs[cols - 1 :]
    panel, before, own, sent, refs = refs[0], refs[1], refs[2], refs[3 : 2 + layers], refs[2 + layers :]
    totals = refs[-1]
    if first == 0:
        listed, codes, numbers, pairs, sem, list_sem = refs[:-1]
        for j in range(cols - 1):
            digits = x_in[j][count * height :].astype(jnp.float32).astype(jnp.int32)
            place = [digits[p : p + 1] + digits[p + 1 : p + 2] * LANES for p in (0, 2, 4)]
            match(
                (width, local_rows, kept), place, panel_cols[...], known[8 : 8 + kept], codes.at[j]
            )
        copy = pltpu.make_async_copy(codes, numbers, sem)
        copy.start()
        totals[...] = before[:, first : first + height]
        copy.wait()
        counts = [
            list_pairs((count, width, layers * slots), numbers.at[j], pairs.at[j])
            for j in range(cols - 1)
        ]
        copy = pltpu.make_async_copy(pairs, listed, list_sem)
        copy.start()
        for j in range(cols - 1):

            def words_of(group):
                return [pairs[j, group, g] for g in range(GROUP)]

            add_products(x_in[j], panel, totals, words_of, counts[j])
        copy.wait()
    else:
        totals[...] = before[:, first : first + height]
        for j in range(cols - 1):

            def words_of(group):
                row = listed[j, pl.ds(group, 1)]
                return [row[0, g] for g in range(GROUP)]

            add_products(x_in[j], panel, totals, words_of, listed[j, listed.shape[1] - 1 :][0, 0])

    own[...] = totals[:slots]
    half = height // 2
    sublane = lax.broadcasted_iota(jnp.int32, (8, totals.shape[2]), 0)
    for d in range(1, layers):
        code = sent[d - 1]
        for u in range(slots):
            value = totals[d * slots + u]
            peak = jnp.max(jnp.abs(value), axis=0, keepdims=True)
            power = jnp.floor(jnp.log2(jnp.maximum(peak, 1e-30)) + 1e-3) + 1.0
            whole = jnp.floor(value * jnp.exp2(15.0 - power) + 0.5).astype(jnp.int32)
            word = (whole[:half] << 16) | (whole[half:] & 0xFFFF)
            bits = ((power.astype(jnp.int32) + 128) >> sublane) & 1
            code[pl.ds(u * half, 8)] = (word[:8] & ~1) | bits
            code[pl.ds(u * half + 8, half - 8)] = word[8:]


def finish_kernel(sizes, span, *refs):
    layers, slots = sizes
    first, height = span
    half = height // 2
    sublane = lax.broadcasted_iota(jnp.int32, (8, refs[-1].shape[3]), 0)
    before, own, codes, result = refs[: first > 0], refs[-layers - 1], refs[-layers:-1], refs[-1]
    kept = result.shape[1]
    for done in before:
        result[:, :, :first] = done[...]
    for u in range(slots):
        high, low = own[u, :half], own[u, half:]
        for code in codes:
            word = code[pl.ds(u * half, half)]
            power = jnp.sum((word[:8] & 1) << sublane, axis=0, keepdims=True).astype(jnp.float32)
            scale = jnp.exp2(power - (128.0 + 15.0))
            word = jnp.concatenate([word[:8] & ~1, word[8:]])
            high += (word >> 16).astype(jnp.float32) * scale
            low += ((word << 16) >> 16).astype(jnp.float32) * scale
        result[u // kept, u % kept, first : first + half] = high.astype(jnp.bfloat16)
        result[u // kept, u % kept, first + half : first + height] = low.astype(jnp.bfloat16)


def per_device(a_blocks, a_rows, a_cols, s_blocks, s_cols, c_cols):
    rows, cols, layers = (lax.axis_size(axis) for axis in ("row", "col", "layer"))
    count, order = a_blocks.shape[:2]
    piece_rows, width = s_cols.shape
    local_rows, kept = c_cols.shape
    own_rows = local_rows // layers
    slots = own_rows * kept
    all_slots = layers * slots
    ranges = row_ranges(order)
    piece = piece_rows * width
    panel_size = rows * piece
    block_size = order * order
    flat_s = s_blocks.reshape(piece, order, order)
    note_height = (2 * piece_rows + 15) // 16 * 16
    code_height = (width + 7) // 8 * 8

    vector = pl.BlockSpec(memory_space=pltpu.VMEM)
    far = pl.BlockSpec(memory_space=HBM)

    first_height = ranges[0][1]
    known, x_first = pl.pallas_call(
        functools.partial(
            pack_first_kernel,
            (layers, count, piece_rows, width, local_rows, kept, order, first_height),
        ),
        out_shape=[
            jax.ShapeDtypeStruct((16, LANES), jnp.int32),
            jax.ShapeDtypeStruct((count * first_height + 16, order), jnp.bfloat16),
        ],
        in_specs=[far] * 4,
        out_specs=[vector] * 2,
        scratch_shapes=[
            pltpu.VMEM((1, count), jnp.int32),
            pltpu.VMEM((1, count), jnp.int32),
            pltpu.VMEM((kept, local_rows), jnp.int32),
            pltpu.VMEM((16, LANES), jnp.int32),
            pltpu.SemaphoreType.DMA((3 + pl.cdiv(count, copy_step(count)),)),
        ],
        compiler_params=pltpu.CompilerParams(
            vmem_limit_bytes=2 * block_size * (count + 1) + 4 * MIB
        ),
        name="pack_first",
    )(*in_hbm(a_rows.reshape(1, count), a_cols.reshape(1, count), c_cols.T, a_blocks))
    first_piece = [shifted(x_first, "col", j) for j in range(1, cols)]
    later_blocks, later_s_cols, later_s, _ = lax.optimization_barrier(
        (a_blocks, s_cols, flat_s, known)
    )
    s_sent, *x_later = pl.pallas_call(
        functools.partial(pack_later_kernel, (count, piece, order, ranges[1:])),
        out_shape=[jax.ShapeDtypeStruct((piece * order + note_height, order), jnp.bfloat16)]
        + [
            jax.ShapeDtypeStruct((count * height, order), jnp.bfloat16) for _, height in ranges[1:]
        ],
        in_specs=[far] * 3,
        out_specs=[vector] * len(ranges),
        scratch_shapes=[
            pltpu.VMEM((piece_rows, width), jnp.int32),
            pltpu.VMEM((note_height, LANES), jnp.int32),
            pltpu.SemaphoreType.DMA((piece + len(ranges),)),
        ],
        compiler_params=pltpu.CompilerParams(
            vmem_limit_bytes=2 * block_size * (count + piece + 1) + 4 * MIB
        ),
        name="pack_later",
    )(*in_hbm(later_blocks, later_s_cols, later_s))
    x_sent = [x_first, *x_later]
    s_pieces = gathered(s_sent, "row")
    moved = block_size * (4 * all_slots + 4 * panel_size + 2 * count)
    totals, panel, panel_cols = pl.pallas_call(
        functools.partial(
            own_kernel, (rows, count, piece_rows, width, local_rows, kept, order), ranges
        ),
        out_shape=[
            jax.ShapeDtypeStruct((all_slots + 1, order, order), jnp.float32),
            jax.ShapeDtypeStruct((panel_size, order, order), jnp.bfloat16),
            jax.ShapeDtypeStruct((rows * piece_rows, LANES), jnp.int32),
        ],
        in_specs=[vector] * (1 + len(ranges) + rows),
        out_specs=[vector] * 3,
        scratch_shapes=[
            pltpu.VMEM((code_height, LANES), jnp.int32),
            pltpu.SMEM((code_height, LANES), jnp.int32),
            pltpu.SMEM((list_height(count, width), LANES), jnp.int32),
            pltpu.SemaphoreType.DMA,
        ],
        compiler_params=pltpu.CompilerParams(vmem_limit_bytes=moved + 4 * MIB),
        cost_estimate=pl.CostEstimate(
            flops=2 * order**3 * count * width // 4, bytes_accessed=moved, transcendentals=0
        ),
        name="own_products",
    )(known, *x_sent, *s_pieces)

    moved = block_size * (8 * all_slots + 2 * panel_size + 2 * count * (cols - 1))
    later, panel_cols = lax.optimization_barrier((x_sent[1:], panel_cols))
    x_pieces = [first_piece]
    x_pieces += [[shifted(part, "col", j) for j in range(1, cols)] for part in later]

    code_shape = (cols - 1, code_height, LANES)
    list_shape = (cols - 1, list_height(count, width), LANES)
    finished, plan = [], []
    for (at, height), pieces in zip(ranges, x_pieces):
        code_rows = slots * (height // 2)
        out_shape = [jax.ShapeDtypeStruct((slots, height, order), jnp.float32)]
        out_shape += [jax.ShapeDtypeStruct((code_rows, order), jnp.int32)] * (layers - 1)
        scratch = []
        if at == 0:
            out_shape.append(jax.ShapeDtypeStruct(list_shape, jnp.int32))
            scratch = [
                pltpu.VMEM(code_shape, jnp.int32),
                pltpu.SMEM(code_shape, jnp.int32),
                pltpu.SMEM(list_shape, jnp.int32),
                pltpu.SemaphoreType.DMA,
                pltpu.SemaphoreType.DMA,
            ]
        given = plan or (known, panel_cols)
        out = pl.pallas_call(
            functools.partial(
                peer_kernel, (cols, layers, count, width, local_rows, kept), (at, height)
            ),
            out_shape=out_shape,
            in_specs=[vector] * (len(given) + cols + 1),
            out_specs=[vector] * len(out_shape),
            scratch_shapes=[*scratch, pltpu.VMEM((all_slots + 1, height, order), jnp.float32)],
            compiler_params=pltpu.CompilerParams(vmem_limit_bytes=moved + 4 * MIB),
            cost_estimate=pl.CostEstimate(
                flops=2 * order**2 * height * count * width // 4 * (cols - 1),
                bytes_accessed=moved // 2,
                transcendentals=0,
            ),
            name=f"peer_products_{at}",
        )(*given, *pieces, panel, totals)
        plan = plan or out[layers:]
        far = [d for d in range(layers // 2, layers)]
        turn = far + [d for d in range(1, layers) if d not in far]
        if at > 0:
            turn = turn[1:] + turn[:1]
        codes = [flipped(out[d], "layer", d) for d in turn]
        finished = [
            pl.pallas_call(
                functools.partial(finish_kernel, (layers, slots), (at, height)),
                out_shape=jax.ShapeDtypeStruct((own_rows, kept, at + height, order), jnp.bfloat16),
                in_specs=[vector] * (len(finished) + layers),
                out_specs=vector,
                compiler_params=pltpu.CompilerParams(
                    vmem_limit_bytes=16 * slots * block_size + 4 * MIB
                ),
                name=f"finish_{at}",
            )(*finished, out[0], *codes)
        ]
    return finished[0]


def solution(mesh):
    placed = (
        P(("row", "col", "layer"), None, None),
        P(("row", "col", "layer")),
        P(("row", "col", "layer")),
        P(("row", "layer"), "col", None, None),
        P(("row", "layer"), "col"),
        P("row", "col"),
    )
    return jax.shard_map(
        per_device,
        mesh=mesh,
        in_specs=placed,
        out_specs=P(("row", "layer"), "col", None, None),
        check_vma=False,
    )
```

```python
import functools

import jax
import jax.numpy as jnp
from jax import lax
from jax.experimental import pallas as pl
from jax.experimental.pallas import tpu as pltpu
from jax.sharding import PartitionSpec as P

GROUP = 8
LANES = 128
FIELD = 10
MIB = 2**20
HBM = pltpu.MemorySpace.HBM


def row_ranges(order):
    first = order * 5 // 8
    return [(0, first), (first, order - first)]


def in_hbm(*values):
    return [pltpu.with_memory_space_constraint(value, HBM) for value in values]


def flipped(value, axis, bits):
    return lax.ppermute(value, axis, [(i, i ^ bits) for i in range(lax.axis_size(axis))])


def gathered(value, axis):
    values = {0: value}
    bit = lax.axis_size(axis) // 2
    while bit:
        values |= {d ^ bit: flipped(held, axis, bit) for d, held in values.items()}
        bit //= 2
    return [values[d] for d in range(len(values))]


def shifted(value, axis, offset):
    size = lax.axis_size(axis)
    return lax.ppermute(value, axis, [((i + offset) % size, i) for i in range(size)])


def quotient(value, by):
    return value >> (by.bit_length() - 1) if by & (by - 1) == 0 else lax.div(value, by)


def remainder(value, by):
    return value & (by - 1) if by & (by - 1) == 0 else lax.rem(value, by)


def write_digits(tile, at, value):
    height, width = value.shape
    tile[at : at + height, :width] = remainder(value, LANES)
    tile[at + height : at + 2 * height, :width] = quotient(value, LANES)


def pack_first_kernel(sizes, a_rows, a_cols, c_cols, x_in, known, x_out, rows, cols, held, tile, sem):
    layers, count, piece_rows, width, local_rows, kept, order, height = sizes
    spot = x_out.at[pl.ds(0, count * height)].reshape(count, height, order)
    pairs = [(a_rows, rows), (a_cols, cols), (c_cols, held), (x_in.at[:, pl.ds(0, height)], spot)]
    loads = [pltpu.make_async_copy(*pair, sem.at[p]) for p, pair in enumerate(pairs)]
    for load in loads:
        load.start()
    known[...] = jnp.zeros_like(known)
    tile[...] = jnp.zeros_like(tile)
    for load in loads[:3]:
        load.wait()
    own_rows = local_rows // layers
    row, col = rows[...], cols[...]
    here = quotient(row[:, :1], local_rows)
    layer = remainder(quotient(col[:, :1], piece_rows), layers)
    owner = quotient(col, piece_rows * layers)
    local = row - here * local_rows
    goal = (quotient(local, own_rows) ^ layer) * own_rows
    place = (
        ((owner ^ here) * piece_rows + remainder(col, piece_rows)) * width,
        (goal + remainder(local, own_rows)) * kept,
        local,
    )
    for p, value in enumerate(place):
        known[p : p + 1, :count] = value
        write_digits(tile, 2 * p, value)
    known[8 : 8 + kept, :local_rows] = held[...]
    x_out[count * height :] = tile[...].astype(jnp.float32).astype(jnp.bfloat16)
    loads[3].wait()


def pack_later_kernel(sizes, x_in, s_cols, s_in, s_out, *refs):
    count, piece, order, ranges = sizes
    x_out, (held, tile, sem) = refs[: len(ranges)], refs[len(ranges) :]
    sources = [(s_cols, held)]
    sources += [(s_in.at[q], s_out.at[pl.ds(q * order, order)]) for q in range(piece)]
    sources += [
        (x_in.at[:, pl.ds(first, height)], out.reshape(count, height, order))
        for (first, height), out in zip(ranges, x_out)
    ]
    loads = [pltpu.make_async_copy(*pair, sem.at[p]) for p, pair in enumerate(sources)]
    for load in loads:
        load.start()
    tile[...] = jnp.zeros_like(tile)
    loads[0].wait()
    write_digits(tile, 0, held[...])
    s_out[piece * order :] = tile[...].astype(jnp.float32).astype(jnp.bfloat16)
    for load in loads[1:]:
        load.wait()


def match(sizes, place, panel_cols, kept_cols):
    width, local_rows, kept = sizes
    right, goal, local = place
    wanted, held = [jnp.zeros_like(right)] * width, [jnp.zeros_like(right)] * kept
    for p in range(panel_cols.shape[0]):
        for s in range(width):
            wanted[s] = jnp.where(right == p * width, panel_cols[p : p + 1, s : s + 1], wanted[s])
    for i in range(local_rows):
        for t in range(kept):
            held[t] = jnp.where(local == i, kept_cols[t : t + 1, i : i + 1], held[t])
    block = lax.broadcasted_iota(jnp.int32, right.shape, 1)
    codes = []
    for s in range(width):
        word = jnp.full_like(right, -1)
        for t in range(kept):
            pair = ((block << FIELD) | (right + s)) << FIELD | (goal + t)
            word = jnp.where(held[t] == wanted[s], pair, word)
        codes.append(word)
    return codes


def list_height(count, width):
    return (count * width // GROUP + 2 + 7) // 8 * 8


def list_pairs(sizes, codes, pairs):
    count, trash = sizes
    total = jnp.int32(0)
    for n in range(count):
        for code in codes:
            word = code[0, n]
            pairs[total] = word
            total += (word >= 0).astype(jnp.int32)
    for g in range(GROUP):
        pairs[total + g] = trash
    return quotient(total + GROUP - 1, GROUP)


def add_products(left, panel, totals, words_of, groups):
    height = totals.shape[1]
    mask = (1 << FIELD) - 1

    def one_group(group, carry):
        words = words_of(group)
        products = []
        for word in words:
            at = pl.multiple_of((word >> (2 * FIELD)) * height, height)
            products.append(
                jnp.dot(
                    left[pl.ds(at, height)],
                    panel[(word >> FIELD) & mask],
                    preferred_element_type=jnp.float32,
                )
            )
        for word, product in zip(words, products):
            totals[word & mask] += product
        return carry

    lax.fori_loop(0, groups, one_group, 0)


def own_kernel(sizes, ranges, known, *refs):
    rows, count, piece_rows, width, local_rows, kept, order = sizes
    x_in, s_in, refs = refs[: len(ranges)], refs[len(ranges) :][:rows], refs[len(ranges) + rows :]
    totals, panel, panel_cols, pairs = refs
    piece = piece_rows * width
    for d in range(rows):
        tile = s_in[d][piece * order :].astype(jnp.float32).astype(jnp.int32)
        panel_cols[d * piece_rows : (d + 1) * piece_rows] = (
            tile[:piece_rows] + tile[piece_rows : 2 * piece_rows] * LANES
        )
    place = known[0:1], known[1:2], known[2:3]
    codes = match((width, local_rows, kept), place, panel_cols[...], known[8 : 8 + kept])
    totals[...] = jnp.zeros_like(totals)
    for d in range(rows):
        for q in range(piece):
            panel[d * piece + q] = s_in[d][q * order : (q + 1) * order]
    groups = list_pairs((count, totals.shape[0] - 1), codes, pairs)

    def words_of(group):
        return [pairs[group * GROUP + g] for g in range(GROUP)]

    for (first, height), blocks in zip(ranges, x_in):
        add_products(blocks, panel, totals.at[:, pl.ds(first, height)], words_of, groups)


def peer_kernel(sizes, span, *refs):
    cols, layers, count, width, local_rows, kept = sizes
    first, height = span
    slots = local_rows * kept // layers
    if first == 0:
        known, panel_cols, *refs = refs
    else:
        listed, *refs = refs
    x_in, refs = refs[: cols - 1], refs[cols - 1 :]
    panel, before, own, sent, refs = refs[0], refs[1], refs[2], refs[3 : 2 + layers], refs[2 + layers :]
    totals = refs[-1]
    if first == 0:
        listed, pairs = refs[:-1]
        lane = lax.broadcasted_iota(jnp.int32, (1, listed.shape[2]), 1)
        totals[...] = before[:, first : first + height]
        for j in range(cols - 1):
            digits = x_in[j][count * height :].astype(jnp.float32).astype(jnp.int32)
            place = [digits[p : p + 1] + digits[p + 1 : p + 2] * LANES for p in (0, 2, 4)]
            codes = match(
                (width, local_rows, kept), place, panel_cols[...], known[8 : 8 + kept]
            )
            groups = list_pairs((count, layers * slots), codes, pairs)
            listed[j, listed.shape[1] - 1 :] = jnp.full(lane.shape, groups, jnp.int32)

            def words_of(group):
                words = [pairs[group * GROUP + g] for g in range(GROUP)]
                row = jnp.zeros(lane.shape, jnp.int32)
                for g, word in enumerate(words):
                    row = jnp.where(lane == g, word, row)
                listed[j, pl.ds(group, 1)] = row
                return words

            add_products(x_in[j], panel, totals, words_of, groups)
    else:
        totals[...] = before[:, first : first + height]
        for j in range(cols - 1):

            def words_of(group):
                row = listed[j, pl.ds(group, 1)]
                return [row[0, g] for g in range(GROUP)]

            add_products(x_in[j], panel, totals, words_of, listed[j, listed.shape[1] - 1 :][0, 0])

    own[...] = totals[:slots]
    half = height // 2
    sublane = lax.broadcasted_iota(jnp.int32, (8, totals.shape[2]), 0)
    for d in range(1, layers):
        code = sent[d - 1]
        for u in range(slots):
            value = totals[d * slots + u]
            peak = jnp.max(jnp.abs(value), axis=0, keepdims=True)
            power = jnp.floor(jnp.log2(jnp.maximum(peak, 1e-30)) + 1e-3) + 1.0
            whole = jnp.floor(value * jnp.exp2(15.0 - power) + 0.5).astype(jnp.int32)
            word = (whole[:half] << 16) | (whole[half:] & 0xFFFF)
            bits = ((power.astype(jnp.int32) + 128) >> sublane) & 1
            code[pl.ds(u * half, 8)] = (word[:8] & ~1) | bits
            code[pl.ds(u * half + 8, half - 8)] = word[8:]


def finish_kernel(sizes, span, *refs):
    layers, slots = sizes
    first, height = span
    half = height // 2
    sublane = lax.broadcasted_iota(jnp.int32, (8, refs[-1].shape[3]), 0)
    before, own, codes, result = refs[: first > 0], refs[-layers - 1], refs[-layers:-1], refs[-1]
    kept = result.shape[1]
    for done in before:
        result[:, :, :first] = done[...]
    for u in range(slots):
        high, low = own[u, :half], own[u, half:]
        for code in codes:
            word = code[pl.ds(u * half, half)]
            power = jnp.sum((word[:8] & 1) << sublane, axis=0, keepdims=True).astype(jnp.float32)
            scale = jnp.exp2(power - (128.0 + 15.0))
            word = jnp.concatenate([word[:8] & ~1, word[8:]])
            high += (word >> 16).astype(jnp.float32) * scale
            low += ((word << 16) >> 16).astype(jnp.float32) * scale
        result[u // kept, u % kept, first : first + half] = high.astype(jnp.bfloat16)
        result[u // kept, u % kept, first + half : first + height] = low.astype(jnp.bfloat16)


def per_device(a_blocks, a_rows, a_cols, s_blocks, s_cols, c_cols):
    rows, cols, layers = (lax.axis_size(axis) for axis in ("row", "col", "layer"))
    count, order = a_blocks.shape[:2]
    piece_rows, width = s_cols.shape
    local_rows, kept = c_cols.shape
    own_rows = local_rows // layers
    slots = own_rows * kept
    all_slots = layers * slots
    ranges = row_ranges(order)
    piece = piece_rows * width
    panel_size = rows * piece
    block_size = order * order
    flat_s = s_blocks.reshape(piece, order, order)
    note_height = (2 * piece_rows + 15) // 16 * 16

    vector = pl.BlockSpec(memory_space=pltpu.VMEM)
    far = pl.BlockSpec(memory_space=HBM)

    first_height = ranges[0][1]
    known, x_first = pl.pallas_call(
        functools.partial(
            pack_first_kernel,
            (layers, count, piece_rows, width, local_rows, kept, order, first_height),
        ),
        out_shape=[
            jax.ShapeDtypeStruct((16, LANES), jnp.int32),
            jax.ShapeDtypeStruct((count * first_height + 16, order), jnp.bfloat16),
        ],
        in_specs=[far] * 4,
        out_specs=[vector] * 2,
        scratch_shapes=[
            pltpu.VMEM((1, count), jnp.int32),
            pltpu.VMEM((1, count), jnp.int32),
            pltpu.VMEM((kept, local_rows), jnp.int32),
            pltpu.VMEM((16, LANES), jnp.int32),
            pltpu.SemaphoreType.DMA((4,)),
        ],
        compiler_params=pltpu.CompilerParams(
            vmem_limit_bytes=2 * block_size * (count + 1) + 4 * MIB
        ),
        name="pack_first",
    )(*in_hbm(a_rows.reshape(1, count), a_cols.reshape(1, count), c_cols.T, a_blocks))
    first_piece = [shifted(x_first, "col", j) for j in range(1, cols)]
    later_blocks, later_s_cols, later_s, _ = lax.optimization_barrier(
        (a_blocks, s_cols, flat_s, known)
    )
    s_sent, *x_later = pl.pallas_call(
        functools.partial(pack_later_kernel, (count, piece, order, ranges[1:])),
        out_shape=[jax.ShapeDtypeStruct((piece * order + note_height, order), jnp.bfloat16)]
        + [
            jax.ShapeDtypeStruct((count * height, order), jnp.bfloat16) for _, height in ranges[1:]
        ],
        in_specs=[far] * 3,
        out_specs=[vector] * len(ranges),
        scratch_shapes=[
            pltpu.VMEM((piece_rows, width), jnp.int32),
            pltpu.VMEM((note_height, LANES), jnp.int32),
            pltpu.SemaphoreType.DMA((piece + len(ranges),)),
        ],
        compiler_params=pltpu.CompilerParams(
            vmem_limit_bytes=2 * block_size * (count + piece + 1) + 4 * MIB
        ),
        name="pack_later",
    )(*in_hbm(later_blocks, later_s_cols, later_s))
    x_sent = [x_first, *x_later]
    s_pieces = gathered(s_sent, "row")
    moved = block_size * (4 * all_slots + 4 * panel_size + 2 * count)
    totals, panel, panel_cols = pl.pallas_call(
        functools.partial(
            own_kernel, (rows, count, piece_rows, width, local_rows, kept, order), ranges
        ),
        out_shape=[
            jax.ShapeDtypeStruct((all_slots + 1, order, order), jnp.float32),
            jax.ShapeDtypeStruct((panel_size, order, order), jnp.bfloat16),
            jax.ShapeDtypeStruct((rows * piece_rows, LANES), jnp.int32),
        ],
        in_specs=[vector] * (1 + len(ranges) + rows),
        out_specs=[vector] * 3,
        scratch_shapes=[
            pltpu.SMEM((count * width + GROUP,), jnp.int32),
        ],
        compiler_params=pltpu.CompilerParams(vmem_limit_bytes=moved + 4 * MIB),
        cost_estimate=pl.CostEstimate(
            flops=2 * order**3 * count * width // 4, bytes_accessed=moved, transcendentals=0
        ),
        name="own_products",
    )(known, *x_sent, *s_pieces)

    moved = block_size * (8 * all_slots + 2 * panel_size + 2 * count * (cols - 1))
    later, panel_cols = lax.optimization_barrier((x_sent[1:], panel_cols))
    x_pieces = [first_piece]
    x_pieces += [[shifted(part, "col", j) for j in range(1, cols)] for part in later]

    list_shape = (cols - 1, list_height(count, width), LANES)
    finished, plan = [], []
    for (at, height), pieces in zip(ranges, x_pieces):
        code_rows = slots * (height // 2)
        out_shape = [jax.ShapeDtypeStruct((slots, height, order), jnp.float32)]
        out_shape += [jax.ShapeDtypeStruct((code_rows, order), jnp.int32)] * (layers - 1)
        scratch = []
        if at == 0:
            out_shape.append(jax.ShapeDtypeStruct(list_shape, jnp.int32))
            scratch = [pltpu.SMEM((count * width + GROUP,), jnp.int32)]
        given = plan or (known, panel_cols)
        out = pl.pallas_call(
            functools.partial(
                peer_kernel, (cols, layers, count, width, local_rows, kept), (at, height)
            ),
            out_shape=out_shape,
            in_specs=[vector] * (len(given) + cols + 1),
            out_specs=[vector] * len(out_shape),
            scratch_shapes=[*scratch, pltpu.VMEM((all_slots + 1, height, order), jnp.float32)],
            compiler_params=pltpu.CompilerParams(vmem_limit_bytes=moved + 4 * MIB),
            cost_estimate=pl.CostEstimate(
                flops=2 * order**2 * height * count * width // 4 * (cols - 1),
                bytes_accessed=moved // 2,
                transcendentals=0,
            ),
            name=f"peer_products_{at}",
        )(*given, *pieces, panel, totals)
        plan = plan or out[layers:]
        far = [d for d in range(layers // 2, layers)]
        turn = far + [d for d in range(1, layers) if d not in far]
        if at > 0:
            turn = turn[1:] + turn[:1]
        codes = [flipped(out[d], "layer", d) for d in turn]
        finished = [
            pl.pallas_call(
                functools.partial(finish_kernel, (layers, slots), (at, height)),
                out_shape=jax.ShapeDtypeStruct((own_rows, kept, at + height, order), jnp.bfloat16),
                in_specs=[vector] * (len(finished) + layers),
                out_specs=vector,
                compiler_params=pltpu.CompilerParams(
                    vmem_limit_bytes=16 * slots * block_size + 4 * MIB
                ),
                name=f"finish_{at}",
            )(*finished, out[0], *codes)
        ]
    return finished[0]


def solution(mesh):
    placed = (
        P(("row", "col", "layer"), None, None),
        P(("row", "col", "layer")),
        P(("row", "col", "layer")),
        P(("row", "layer"), "col", None, None),
        P(("row", "layer"), "col"),
        P("row", "col"),
    )
    return jax.shard_map(
        per_device,
        mesh=mesh,
        in_specs=placed,
        out_specs=P(("row", "layer"), "col", None, None),
        check_vma=False,
    )
```

```python
import functools

import jax
import jax.numpy as jnp
from jax import lax
from jax.experimental import pallas as pl
from jax.experimental.pallas import tpu as pltpu
from jax.sharding import PartitionSpec as P

GROUP = 8
LANES = 128
FIELD = 10
MIB = 2**20
HBM = pltpu.MemorySpace.HBM


def row_ranges(order):
    first = order * 5 // 8
    return [(0, first), (first, order - first)]


def in_hbm(*values):
    return [pltpu.with_memory_space_constraint(value, HBM) for value in values]


def flipped(value, axis, bits):
    return lax.ppermute(value, axis, [(i, i ^ bits) for i in range(lax.axis_size(axis))])


def gathered(value, axis):
    values = {0: value}
    bit = lax.axis_size(axis) // 2
    while bit:
        values |= {d ^ bit: flipped(held, axis, bit) for d, held in values.items()}
        bit //= 2
    return [values[d] for d in range(len(values))]


def shifted(value, axis, offset):
    size = lax.axis_size(axis)
    return lax.ppermute(value, axis, [((i + offset) % size, i) for i in range(size)])


def quotient(value, by):
    return value >> (by.bit_length() - 1) if by & (by - 1) == 0 else lax.div(value, by)


def remainder(value, by):
    return value & (by - 1) if by & (by - 1) == 0 else lax.rem(value, by)


def write_digits(tile, at, value):
    height, width = value.shape
    tile[at : at + height, :width] = remainder(value, LANES)
    tile[at + height : at + 2 * height, :width] = quotient(value, LANES)


def pack_first_kernel(sizes, a_rows, a_cols, c_cols, x_in, known, x_out, rows, cols, held, tile, sem):
    layers, count, piece_rows, width, local_rows, kept, order, height = sizes
    spot = x_out.at[pl.ds(0, count * height)].reshape(count, height, order)
    pairs = [(a_rows, rows), (a_cols, cols), (c_cols, held), (x_in.at[:, pl.ds(0, height)], spot)]
    loads = [pltpu.make_async_copy(*pair, sem.at[p]) for p, pair in enumerate(pairs)]
    for load in loads:
        load.start()
    known[...] = jnp.zeros_like(known)
    tile[...] = jnp.zeros_like(tile)
    for load in loads[:3]:
        load.wait()
    own_rows = local_rows // layers
    row, col = rows[...], cols[...]
    here = quotient(row[:, :1], local_rows)
    layer = remainder(quotient(col[:, :1], piece_rows), layers)
    owner = quotient(col, piece_rows * layers)
    local = row - here * local_rows
    goal = (quotient(local, own_rows) ^ layer) * own_rows
    place = (
        ((owner ^ here) * piece_rows + remainder(col, piece_rows)) * width,
        (goal + remainder(local, own_rows)) * kept,
        local,
    )
    for p, value in enumerate(place):
        known[p : p + 1, :count] = value
        write_digits(tile, 2 * p, value)
    known[8 : 8 + kept, :local_rows] = held[...]
    x_out[count * height :] = tile[...].astype(jnp.float32).astype(jnp.bfloat16)
    loads[3].wait()


def pack_later_kernel(sizes, x_in, s_cols, s_in, s_out, *refs):
    count, piece, order, ranges = sizes
    x_out, (held, tile, sem) = refs[: len(ranges)], refs[len(ranges) :]
    sources = [(s_cols, held)]
    sources += [(s_in.at[q], s_out.at[pl.ds(q * order, order)]) for q in range(piece)]
    sources += [
        (x_in.at[:, pl.ds(first, height)], out.reshape(count, height, order))
        for (first, height), out in zip(ranges, x_out)
    ]
    loads = [pltpu.make_async_copy(*pair, sem.at[p]) for p, pair in enumerate(sources)]
    for load in loads:
        load.start()
    tile[...] = jnp.zeros_like(tile)
    loads[0].wait()
    write_digits(tile, 0, held[...])
    s_out[piece * order :] = tile[...].astype(jnp.float32).astype(jnp.bfloat16)
    for load in loads[1:]:
        load.wait()


def match(sizes, place, panel_cols, kept_cols):
    width, local_rows, kept = sizes
    right, goal, local = place
    wanted, held = [jnp.zeros_like(right)] * width, [jnp.zeros_like(right)] * kept
    for p in range(panel_cols.shape[0]):
        for s in range(width):
            wanted[s] = jnp.where(right == p * width, panel_cols[p : p + 1, s : s + 1], wanted[s])
    for i in range(local_rows):
        for t in range(kept):
            held[t] = jnp.where(local == i, kept_cols[t : t + 1, i : i + 1], held[t])
    block = lax.broadcasted_iota(jnp.int32, right.shape, 1)
    codes = []
    for s in range(width):
        word = jnp.full_like(right, -1)
        for t in range(kept):
            pair = ((block << FIELD) | (right + s)) << FIELD | (goal + t)
            word = jnp.where(held[t] == wanted[s], pair, word)
        codes.append(word)
    return codes


def list_height(count, width):
    return (count * width // GROUP + 2 + 7) // 8 * 8


def list_pairs(sizes, codes, pairs):
    count, trash = sizes
    total = jnp.int32(0)
    for n in range(count):
        for code in codes:
            word = code[0, n]
            pairs[total] = word
            total += (word >= 0).astype(jnp.int32)
    for g in range(GROUP):
        pairs[total + g] = trash
    return quotient(total + GROUP - 1, GROUP)


def add_products(left, panel, totals, words_of, groups):
    height = totals.shape[1]
    mask = (1 << FIELD) - 1

    def one_group(group, carry):
        words = words_of(group)
        products = []
        for word in words:
            at = pl.multiple_of((word >> (2 * FIELD)) * height, height)
            products.append(
                jnp.dot(
                    left[pl.ds(at, height)],
                    panel[(word >> FIELD) & mask],
                    preferred_element_type=jnp.float32,
                )
            )
        for word, product in zip(words, products):
            totals[word & mask] += product
        return carry

    lax.fori_loop(0, groups, one_group, 0)


def own_kernel(sizes, ranges, known, *refs):
    rows, count, piece_rows, width, local_rows, kept, order = sizes
    x_in, s_in, refs = refs[: len(ranges)], refs[len(ranges) :][:rows], refs[len(ranges) + rows :]
    totals, panel, panel_cols, pairs = refs
    piece = piece_rows * width
    for d in range(rows):
        tile = s_in[d][piece * order :].astype(jnp.float32).astype(jnp.int32)
        panel_cols[d * piece_rows : (d + 1) * piece_rows] = (
            tile[:piece_rows] + tile[piece_rows : 2 * piece_rows] * LANES
        )
    place = known[0:1], known[1:2], known[2:3]
    codes = match((width, local_rows, kept), place, panel_cols[...], known[8 : 8 + kept])
    totals[...] = jnp.zeros_like(totals)
    for d in range(rows):
        for q in range(piece):
            panel[d * piece + q] = s_in[d][q * order : (q + 1) * order]
    groups = list_pairs((count, totals.shape[0] - 1), codes, pairs)

    def words_of(group):
        return [pairs[group * GROUP + g] for g in range(GROUP)]

    for (first, height), blocks in zip(ranges, x_in):
        add_products(blocks, panel, totals.at[:, pl.ds(first, height)], words_of, groups)


def peer_kernel(sizes, span, *refs):
    cols, layers, count, width, local_rows, kept = sizes
    first, height = span
    slots = local_rows * kept // layers
    if first == 0:
        known, panel_cols, *refs = refs
    else:
        listed, *refs = refs
    x_in, refs = refs[: cols - 1], refs[cols - 1 :]
    panel, before, own, sent, refs = refs[0], refs[1], refs[2], refs[3 : 2 + layers], refs[2 + layers :]
    totals = refs[-1]
    if first == 0:
        listed, pairs = refs[:-1]
        lane = lax.broadcasted_iota(jnp.int32, (1, listed.shape[2]), 1)
        totals[...] = before[:, first : first + height]
        for j in range(cols - 1):
            digits = x_in[j][count * height :].astype(jnp.float32).astype(jnp.int32)
            place = [digits[p : p + 1] + digits[p + 1 : p + 2] * LANES for p in (0, 2, 4)]
            codes = match(
                (width, local_rows, kept), place, panel_cols[...], known[8 : 8 + kept]
            )
            groups = list_pairs((count, layers * slots), codes, pairs)
            listed[j, listed.shape[1] - 1 :] = jnp.full(lane.shape, groups, jnp.int32)

            def words_of(group):
                words = [pairs[group * GROUP + g] for g in range(GROUP)]
                row = jnp.zeros(lane.shape, jnp.int32)
                for g, word in enumerate(words):
                    row = jnp.where(lane == g, word, row)
                listed[j, pl.ds(group, 1)] = row
                return words

            add_products(x_in[j], panel, totals, words_of, groups)
    else:
        totals[...] = before[:, first : first + height]
        for j in range(cols - 1):

            def words_of(group):
                row = listed[j, pl.ds(group, 1)]
                return [row[0, g] for g in range(GROUP)]

            add_products(x_in[j], panel, totals, words_of, listed[j, listed.shape[1] - 1 :][0, 0])

    own[...] = totals[:slots]
    half = height // 2
    sublane = lax.broadcasted_iota(jnp.int32, (8, totals.shape[2]), 0)
    for d in range(1, layers):
        code = sent[d - 1]
        for u in range(slots):
            value = totals[d * slots + u]
            peak = jnp.max(jnp.abs(value), axis=0, keepdims=True)
            power = jnp.floor(jnp.log2(jnp.maximum(peak, 1e-36)) + 1e-3) + 1.0
            whole = jnp.floor(value * jnp.exp2(-power) * 32768.0 + 0.5).astype(jnp.int32)
            word = (whole[:half] << 16) | (whole[half:] & 0xFFFF)
            bits = ((power.astype(jnp.int32) + 128) >> sublane) & 1
            code[pl.ds(u * half, 8)] = (word[:8] & ~1) | bits
            code[pl.ds(u * half + 8, half - 8)] = word[8:]


def finish_kernel(sizes, span, *refs):
    layers, slots = sizes
    first, height = span
    half = height // 2
    sublane = lax.broadcasted_iota(jnp.int32, (8, refs[-1].shape[3]), 0)
    before, own, codes, result = refs[: first > 0], refs[-layers - 1], refs[-layers:-1], refs[-1]
    kept = result.shape[1]
    for done in before:
        result[:, :, :first] = done[...]
    for u in range(slots):
        high, low = own[u, :half], own[u, half:]
        for code in codes:
            word = code[pl.ds(u * half, half)]
            power = jnp.sum((word[:8] & 1) << sublane, axis=0, keepdims=True).astype(jnp.float32)
            scale = jnp.exp2(power - 128.0)
            word = jnp.concatenate([word[:8] & ~1, word[8:]])
            high += (word >> 16).astype(jnp.float32) * (1 / 32768) * scale
            low += ((word << 16) >> 16).astype(jnp.float32) * (1 / 32768) * scale
        result[u // kept, u % kept, first : first + half] = high.astype(jnp.bfloat16)
        result[u // kept, u % kept, first + half : first + height] = low.astype(jnp.bfloat16)


def per_device(a_blocks, a_rows, a_cols, s_blocks, s_cols, c_cols):
    rows, cols, layers = (lax.axis_size(axis) for axis in ("row", "col", "layer"))
    count, order = a_blocks.shape[:2]
    piece_rows, width = s_cols.shape
    local_rows, kept = c_cols.shape
    own_rows = local_rows // layers
    slots = own_rows * kept
    all_slots = layers * slots
    ranges = row_ranges(order)
    piece = piece_rows * width
    panel_size = rows * piece
    block_size = order * order
    flat_s = s_blocks.reshape(piece, order, order)
    note_height = (2 * piece_rows + 15) // 16 * 16

    vector = pl.BlockSpec(memory_space=pltpu.VMEM)
    far = pl.BlockSpec(memory_space=HBM)

    first_height = ranges[0][1]
    known, x_first = pl.pallas_call(
        functools.partial(
            pack_first_kernel,
            (layers, count, piece_rows, width, local_rows, kept, order, first_height),
        ),
        out_shape=[
            jax.ShapeDtypeStruct((16, LANES), jnp.int32),
            jax.ShapeDtypeStruct((count * first_height + 16, order), jnp.bfloat16),
        ],
        in_specs=[far] * 4,
        out_specs=[vector] * 2,
        scratch_shapes=[
            pltpu.VMEM((1, count), jnp.int32),
            pltpu.VMEM((1, count), jnp.int32),
            pltpu.VMEM((kept, local_rows), jnp.int32),
            pltpu.VMEM((16, LANES), jnp.int32),
            pltpu.SemaphoreType.DMA((4,)),
        ],
        compiler_params=pltpu.CompilerParams(
            vmem_limit_bytes=2 * block_size * (count + 1) + 4 * MIB
        ),
        name="pack_first",
    )(*in_hbm(a_rows.reshape(1, count), a_cols.reshape(1, count), c_cols.T, a_blocks))
    first_piece = [shifted(x_first, "col", j) for j in range(1, cols)]
    later_blocks, later_s_cols, later_s, _ = lax.optimization_barrier(
        (a_blocks, s_cols, flat_s, known)
    )
    s_sent, *x_later = pl.pallas_call(
        functools.partial(pack_later_kernel, (count, piece, order, ranges[1:])),
        out_shape=[jax.ShapeDtypeStruct((piece * order + note_height, order), jnp.bfloat16)]
        + [
            jax.ShapeDtypeStruct((count * height, order), jnp.bfloat16) for _, height in ranges[1:]
        ],
        in_specs=[far] * 3,
        out_specs=[vector] * len(ranges),
        scratch_shapes=[
            pltpu.VMEM((piece_rows, width), jnp.int32),
            pltpu.VMEM((note_height, LANES), jnp.int32),
            pltpu.SemaphoreType.DMA((piece + len(ranges),)),
        ],
        compiler_params=pltpu.CompilerParams(
            vmem_limit_bytes=2 * block_size * (count + piece + 1) + 4 * MIB
        ),
        name="pack_later",
    )(*in_hbm(later_blocks, later_s_cols, later_s))
    x_sent = [x_first, *x_later]
    s_pieces = gathered(s_sent, "row")
    moved = block_size * (4 * all_slots + 4 * panel_size + 2 * count)
    totals, panel, panel_cols = pl.pallas_call(
        functools.partial(
            own_kernel, (rows, count, piece_rows, width, local_rows, kept, order), ranges
        ),
        out_shape=[
            jax.ShapeDtypeStruct((all_slots + 1, order, order), jnp.float32),
            jax.ShapeDtypeStruct((panel_size, order, order), jnp.bfloat16),
            jax.ShapeDtypeStruct((rows * piece_rows, LANES), jnp.int32),
        ],
        in_specs=[vector] * (1 + len(ranges) + rows),
        out_specs=[vector] * 3,
        scratch_shapes=[
            pltpu.SMEM((count * width + GROUP,), jnp.int32),
        ],
        compiler_params=pltpu.CompilerParams(vmem_limit_bytes=moved + 4 * MIB),
        cost_estimate=pl.CostEstimate(
            flops=2 * order**3 * count * width // 4, bytes_accessed=moved, transcendentals=0
        ),
        name="own_products",
    )(known, *x_sent, *s_pieces)

    moved = block_size * (8 * all_slots + 2 * panel_size + 2 * count * (cols - 1))
    later, panel_cols = lax.optimization_barrier((x_sent[1:], panel_cols))
    x_pieces = [first_piece]
    x_pieces += [[shifted(part, "col", j) for j in range(1, cols)] for part in later]

    list_shape = (cols - 1, list_height(count, width), LANES)
    finished, plan = [], []
    for (at, height), pieces in zip(ranges, x_pieces):
        code_rows = slots * (height // 2)
        out_shape = [jax.ShapeDtypeStruct((slots, height, order), jnp.float32)]
        out_shape += [jax.ShapeDtypeStruct((code_rows, order), jnp.int32)] * (layers - 1)
        scratch = []
        if at == 0:
            out_shape.append(jax.ShapeDtypeStruct(list_shape, jnp.int32))
            scratch = [pltpu.SMEM((count * width + GROUP,), jnp.int32)]
        given = plan or (known, panel_cols)
        out = pl.pallas_call(
            functools.partial(
                peer_kernel, (cols, layers, count, width, local_rows, kept), (at, height)
            ),
            out_shape=out_shape,
            in_specs=[vector] * (len(given) + cols + 1),
            out_specs=[vector] * len(out_shape),
            scratch_shapes=[*scratch, pltpu.VMEM((all_slots + 1, height, order), jnp.float32)],
            compiler_params=pltpu.CompilerParams(vmem_limit_bytes=moved + 4 * MIB),
            cost_estimate=pl.CostEstimate(
                flops=2 * order**2 * height * count * width // 4 * (cols - 1),
                bytes_accessed=moved // 2,
                transcendentals=0,
            ),
            name=f"peer_products_{at}",
        )(*given, *pieces, panel, totals)
        plan = plan or out[layers:]
        far = [d for d in range(layers // 2, layers)]
        turn = far + [d for d in range(1, layers) if d not in far]
        if at > 0:
            turn = turn[1:] + turn[:1]
        codes = [flipped(out[d], "layer", d) for d in turn]
        finished = [
            pl.pallas_call(
                functools.partial(finish_kernel, (layers, slots), (at, height)),
                out_shape=jax.ShapeDtypeStruct((own_rows, kept, at + height, order), jnp.bfloat16),
                in_specs=[vector] * (len(finished) + layers),
                out_specs=vector,
                compiler_params=pltpu.CompilerParams(
                    vmem_limit_bytes=16 * slots * block_size + 4 * MIB
                ),
                name=f"finish_{at}",
            )(*finished, out[0], *codes)
        ]
    return finished[0]


def solution(mesh):
    placed = (
        P(("row", "col", "layer"), None, None),
        P(("row", "col", "layer")),
        P(("row", "col", "layer")),
        P(("row", "layer"), "col", None, None),
        P(("row", "layer"), "col"),
        P("row", "col"),
    )
    return jax.shard_map(
        per_device,
        mesh=mesh,
        in_specs=placed,
        out_specs=P(("row", "layer"), "col", None, None),
        check_vma=False,
    )
```

```python
import functools

import jax
import jax.numpy as jnp
from jax import lax
from jax.experimental import pallas as pl
from jax.experimental.pallas import tpu as pltpu
from jax.sharding import PartitionSpec as P

GROUP = 8
LANES = 128
FIELD = 10
MIB = 2**20
HBM = pltpu.MemorySpace.HBM


def row_ranges(order):
    first = order * 5 // 8
    return [(0, first), (first, order - first)]


def in_hbm(*values):
    return [pltpu.with_memory_space_constraint(value, HBM) for value in values]


def flipped(value, axis, bits):
    return lax.ppermute(value, axis, [(i, i ^ bits) for i in range(lax.axis_size(axis))])


def gathered(value, axis):
    values = {0: value}
    bit = lax.axis_size(axis) // 2
    while bit:
        values |= {d ^ bit: flipped(held, axis, bit) for d, held in values.items()}
        bit //= 2
    return [values[d] for d in range(len(values))]


def shifted(value, axis, offset):
    size = lax.axis_size(axis)
    return lax.ppermute(value, axis, [((i + offset) % size, i) for i in range(size)])


def quotient(value, by):
    return value >> (by.bit_length() - 1) if by & (by - 1) == 0 else lax.div(value, by)


def remainder(value, by):
    return value & (by - 1) if by & (by - 1) == 0 else lax.rem(value, by)


def write_digits(tile, at, value):
    height, width = value.shape
    tile[at : at + height, :width] = remainder(value, LANES)
    tile[at + height : at + 2 * height, :width] = quotient(value, LANES)


def pack_first_kernel(sizes, a_rows, a_cols, c_cols, x_in, known, x_out, rows, cols, held, tile, sem):
    layers, count, piece_rows, width, local_rows, kept, order, height = sizes
    spot = x_out.at[pl.ds(0, count * height)].reshape(count, height, order)
    pairs = [(a_rows, rows), (a_cols, cols), (c_cols, held), (x_in.at[:, pl.ds(0, height)], spot)]
    loads = [pltpu.make_async_copy(*pair, sem.at[p]) for p, pair in enumerate(pairs)]
    for load in loads:
        load.start()
    known[...] = jnp.zeros_like(known)
    tile[...] = jnp.zeros_like(tile)
    for load in loads[:3]:
        load.wait()
    own_rows = local_rows // layers
    row, col = rows[...], cols[...]
    here = quotient(row[:, :1], local_rows)
    layer = remainder(quotient(col[:, :1], piece_rows), layers)
    owner = quotient(col, piece_rows * layers)
    local = row - here * local_rows
    goal = (quotient(local, own_rows) ^ layer) * own_rows
    place = (
        ((owner ^ here) * piece_rows + remainder(col, piece_rows)) * width,
        (goal + remainder(local, own_rows)) * kept,
        local,
    )
    for p, value in enumerate(place):
        known[p : p + 1, :count] = value
        write_digits(tile, 2 * p, value)
    known[8 : 8 + kept, :local_rows] = held[...]
    x_out[count * height :] = tile[...].astype(jnp.float32).astype(jnp.bfloat16)
    loads[3].wait()


def pack_later_kernel(sizes, x_in, s_cols, s_in, s_out, *refs):
    count, piece, order, ranges = sizes
    x_out, (held, tile, sem) = refs[: len(ranges)], refs[len(ranges) :]
    sources = [(s_cols, held)]
    sources += [(s_in.at[q], s_out.at[pl.ds(q * order, order)]) for q in range(piece)]
    sources += [
        (x_in.at[:, pl.ds(first, height)], out.reshape(count, height, order))
        for (first, height), out in zip(ranges, x_out)
    ]
    loads = [pltpu.make_async_copy(*pair, sem.at[p]) for p, pair in enumerate(sources)]
    for load in loads:
        load.start()
    tile[...] = jnp.zeros_like(tile)
    loads[0].wait()
    write_digits(tile, 0, held[...])
    s_out[piece * order :] = tile[...].astype(jnp.float32).astype(jnp.bfloat16)
    for load in loads[1:]:
        load.wait()


def match(sizes, place, panel_cols, kept_cols):
    width, local_rows, kept = sizes
    right, goal, local = place
    wanted, held = [jnp.zeros_like(right)] * width, [jnp.zeros_like(right)] * kept
    for p in range(panel_cols.shape[0]):
        for s in range(width):
            wanted[s] = jnp.where(right == p * width, panel_cols[p : p + 1, s : s + 1], wanted[s])
    for i in range(local_rows):
        for t in range(kept):
            held[t] = jnp.where(local == i, kept_cols[t : t + 1, i : i + 1], held[t])
    block = lax.broadcasted_iota(jnp.int32, right.shape, 1)
    codes = []
    for s in range(width):
        word = jnp.full_like(right, -1)
        for t in range(kept):
            pair = ((block << FIELD) | (right + s)) << FIELD | (goal + t)
            word = jnp.where(held[t] == wanted[s], pair, word)
        codes.append(word)
    return codes


def list_height(count, width):
    return (count * width // GROUP + 2 + 7) // 8 * 8


def list_pairs(sizes, codes, pairs):
    count, trash = sizes
    total = jnp.int32(0)
    for n in range(count):
        for code in codes:
            word = code[0, n]
            pairs[total] = word
            total += (word >= 0).astype(jnp.int32)
    for g in range(GROUP):
        pairs[total + g] = trash
    return quotient(total + GROUP - 1, GROUP)


def add_products(left, panel, totals, words_of, groups):
    height = totals.shape[1]
    mask = (1 << FIELD) - 1

    def one_group(group, carry):
        words = words_of(group)
        products = []
        for word in words:
            at = pl.multiple_of((word >> (2 * FIELD)) * height, height)
            products.append(
                jnp.dot(
                    left[pl.ds(at, height)],
                    panel[(word >> FIELD) & mask],
                    preferred_element_type=jnp.float32,
                )
            )
        for word, product in zip(words, products):
            totals[word & mask] += product
        return carry

    lax.fori_loop(0, groups, one_group, 0)


def own_kernel(sizes, ranges, known, *refs):
    rows, count, piece_rows, width, local_rows, kept, order = sizes
    x_in, s_in, refs = refs[: len(ranges)], refs[len(ranges) :][:rows], refs[len(ranges) + rows :]
    totals, panel, panel_cols, pairs = refs
    piece = piece_rows * width
    for d in range(rows):
        tile = s_in[d][piece * order :].astype(jnp.float32).astype(jnp.int32)
        panel_cols[d * piece_rows : (d + 1) * piece_rows] = (
            tile[:piece_rows] + tile[piece_rows : 2 * piece_rows] * LANES
        )
    place = known[0:1], known[1:2], known[2:3]
    codes = match((width, local_rows, kept), place, panel_cols[...], known[8 : 8 + kept])
    totals[...] = jnp.zeros_like(totals)
    for d in range(rows):
        for q in range(piece):
            panel[d * piece + q] = s_in[d][q * order : (q + 1) * order]
    groups = list_pairs((count, totals.shape[0] - 1), codes, pairs)

    def words_of(group):
        return [pairs[group * GROUP + g] for g in range(GROUP)]

    for (first, height), blocks in zip(ranges, x_in):
        add_products(blocks, panel, totals.at[:, pl.ds(first, height)], words_of, groups)


def peer_kernel(sizes, span, *refs):
    cols, layers, count, width, local_rows, kept = sizes
    first, height = span
    slots = local_rows * kept // layers
    if first == 0:
        known, panel_cols, *refs = refs
    else:
        listed, *refs = refs
    x_in, refs = refs[: cols - 1], refs[cols - 1 :]
    panel, before, own, sent, refs = refs[0], refs[1], refs[2], refs[3 : 2 + layers], refs[2 + layers :]
    totals = refs[-1]
    if first == 0:
        listed, pairs = refs[:-1]
        lane = lax.broadcasted_iota(jnp.int32, (1, listed.shape[2]), 1)
        totals[...] = before[:, first : first + height]
        for j in range(cols - 1):
            digits = x_in[j][count * height :].astype(jnp.float32).astype(jnp.int32)
            place = [digits[p : p + 1] + digits[p + 1 : p + 2] * LANES for p in (0, 2, 4)]
            codes = match(
                (width, local_rows, kept), place, panel_cols[...], known[8 : 8 + kept]
            )
            groups = list_pairs((count, layers * slots), codes, pairs)
            listed[j, listed.shape[1] - 1 :] = jnp.full(lane.shape, groups, jnp.int32)

            def words_of(group):
                words = [pairs[group * GROUP + g] for g in range(GROUP)]
                row = jnp.zeros(lane.shape, jnp.int32)
                for g, word in enumerate(words):
                    row = jnp.where(lane == g, word, row)
                listed[j, pl.ds(group, 1)] = row
                return words

            add_products(x_in[j], panel, totals, words_of, groups)
    else:
        totals[...] = before[:, first : first + height]
        for j in range(cols - 1):

            def words_of(group):
                row = listed[j, pl.ds(group, 1)]
                return [row[0, g] for g in range(GROUP)]

            add_products(x_in[j], panel, totals, words_of, listed[j, listed.shape[1] - 1 :][0, 0])

    own[...] = totals[:slots]
    half = height // 2
    sublane = lax.broadcasted_iota(jnp.int32, (8, totals.shape[2]), 0)
    for d in range(1, layers):
        code = sent[d - 1]
        for u in range(slots):
            value = totals[d * slots + u]
            peak = jnp.max(jnp.abs(value), axis=0, keepdims=True)
            power = jnp.floor(jnp.log2(jnp.maximum(peak, 1e-36)) + 1e-3) + 1.0
            whole = jnp.floor(value * jnp.exp2(-power) * 32768.0 + 0.5).astype(jnp.int32)
            word = (whole[:half] << 16) | (whole[half:] & 0xFFFF)
            bits = ((power.astype(jnp.int32) + 128) >> sublane) & 1
            code[pl.ds(u * half, 8)] = (word[:8] & ~1) | bits
            code[pl.ds(u * half + 8, half - 8)] = word[8:]


def finish_kernel(sizes, span, *refs):
    layers, slots = sizes
    first, height = span
    half = height // 2
    sublane = lax.broadcasted_iota(jnp.int32, (8, refs[-1].shape[3]), 0)
    before, own, codes, result = refs[: first > 0], refs[-layers - 1], refs[-layers:-1], refs[-1]
    kept = result.shape[1]
    for done in before:
        result[:, :, :first] = done[...]
    for u in range(slots):
        high, low = own[u, :half], own[u, half:]
        for code in codes:
            word = code[pl.ds(u * half, half)]
            power = jnp.sum((word[:8] & 1) << sublane, axis=0, keepdims=True).astype(jnp.float32)
            scale = jnp.exp2(power - 128.0)
            word = jnp.concatenate([word[:8] & ~1, word[8:]])
            high += (word >> 16).astype(jnp.float32) * (1 / 32768) * scale
            low += ((word << 16) >> 16).astype(jnp.float32) * (1 / 32768) * scale
        result[u // kept, u % kept, first : first + half] = high.astype(jnp.bfloat16)
        result[u // kept, u % kept, first + half : first + height] = low.astype(jnp.bfloat16)


def per_device(a_blocks, a_rows, a_cols, s_blocks, s_cols, c_cols):
    rows, cols, layers = (lax.axis_size(axis) for axis in ("row", "col", "layer"))
    count, order = a_blocks.shape[:2]
    piece_rows, width = s_cols.shape
    local_rows, kept = c_cols.shape
    own_rows = local_rows // layers
    slots = own_rows * kept
    all_slots = layers * slots
    ranges = row_ranges(order)
    piece = piece_rows * width
    panel_size = rows * piece
    block_size = order * order
    flat_s = s_blocks.reshape(piece, order, order)
    note_height = (2 * piece_rows + 15) // 16 * 16

    vector = pl.BlockSpec(memory_space=pltpu.VMEM)
    far = pl.BlockSpec(memory_space=HBM)

    first_height = ranges[0][1]
    known, x_first = pl.pallas_call(
        functools.partial(
            pack_first_kernel,
            (layers, count, piece_rows, width, local_rows, kept, order, first_height),
        ),
        out_shape=[
            jax.ShapeDtypeStruct((16, LANES), jnp.int32),
            jax.ShapeDtypeStruct((count * first_height + 16, order), jnp.bfloat16),
        ],
        in_specs=[far] * 4,
        out_specs=[vector] * 2,
        scratch_shapes=[
            pltpu.VMEM((1, count), jnp.int32),
            pltpu.VMEM((1, count), jnp.int32),
            pltpu.VMEM((kept, local_rows), jnp.int32),
            pltpu.VMEM((16, LANES), jnp.int32),
            pltpu.SemaphoreType.DMA((4,)),
        ],
        compiler_params=pltpu.CompilerParams(
            vmem_limit_bytes=2 * block_size * (count + 1) + 4 * MIB
        ),
        name="pack_first",
    )(*in_hbm(a_rows.reshape(1, count), a_cols.reshape(1, count), c_cols.T, a_blocks))
    first_piece = [shifted(x_first, "col", j) for j in range(1, cols)]
    later_blocks, later_s_cols, later_s, _ = lax.optimization_barrier(
        (a_blocks, s_cols, flat_s, known)
    )
    s_sent, *x_later = pl.pallas_call(
        functools.partial(pack_later_kernel, (count, piece, order, ranges[1:])),
        out_shape=[jax.ShapeDtypeStruct((piece * order + note_height, order), jnp.bfloat16)]
        + [
            jax.ShapeDtypeStruct((count * height, order), jnp.bfloat16) for _, height in ranges[1:]
        ],
        in_specs=[far] * 3,
        out_specs=[vector] * len(ranges),
        scratch_shapes=[
            pltpu.VMEM((piece_rows, width), jnp.int32),
            pltpu.VMEM((note_height, LANES), jnp.int32),
            pltpu.SemaphoreType.DMA((piece + len(ranges),)),
        ],
        compiler_params=pltpu.CompilerParams(
            vmem_limit_bytes=2 * block_size * (count + piece + 1) + 4 * MIB
        ),
        name="pack_later",
    )(*in_hbm(later_blocks, later_s_cols, later_s))
    x_sent = [x_first, *x_later]
    s_pieces = gathered(s_sent, "row")
    moved = block_size * (4 * all_slots + 4 * panel_size + 2 * count)
    totals, panel, panel_cols = pl.pallas_call(
        functools.partial(
            own_kernel, (rows, count, piece_rows, width, local_rows, kept, order), ranges
        ),
        out_shape=[
            jax.ShapeDtypeStruct((all_slots + 1, order, order), jnp.float32),
            jax.ShapeDtypeStruct((panel_size, order, order), jnp.bfloat16),
            jax.ShapeDtypeStruct((rows * piece_rows, LANES), jnp.int32),
        ],
        in_specs=[vector] * (1 + len(ranges) + rows),
        out_specs=[vector] * 3,
        scratch_shapes=[
            pltpu.SMEM((count * width + GROUP,), jnp.int32),
        ],
        compiler_params=pltpu.CompilerParams(vmem_limit_bytes=moved + 4 * MIB),
        cost_estimate=pl.CostEstimate(
            flops=2 * order**3 * count * width // 4, bytes_accessed=moved, transcendentals=0
        ),
        name="own_products",
    )(known, *x_sent, *s_pieces)

    moved = block_size * (8 * all_slots + 2 * panel_size + 2 * count * (cols - 1))
    later, panel_cols = lax.optimization_barrier((x_sent[1:], panel_cols))
    x_pieces = [first_piece]
    x_pieces += [[shifted(part, "col", j) for j in range(1, cols)] for part in later]

    list_shape = (cols - 1, list_height(count, width), LANES)
    finished, plan = [], []
    for (at, height), pieces in zip(ranges, x_pieces):
        code_rows = slots * (height // 2)
        out_shape = [jax.ShapeDtypeStruct((slots, height, order), jnp.float32)]
        out_shape += [jax.ShapeDtypeStruct((code_rows, order), jnp.int32)] * (layers - 1)
        scratch = []
        if at == 0:
            out_shape.append(jax.ShapeDtypeStruct(list_shape, jnp.int32))
            scratch = [pltpu.SMEM((count * width + GROUP,), jnp.int32)]
        given = plan or (known, panel_cols)
        out = pl.pallas_call(
            functools.partial(
                peer_kernel, (cols, layers, count, width, local_rows, kept), (at, height)
            ),
            out_shape=out_shape,
            in_specs=[vector] * (len(given) + cols + 1),
            out_specs=[vector] * len(out_shape),
            scratch_shapes=[*scratch, pltpu.VMEM((all_slots + 1, height, order), jnp.float32)],
            compiler_params=pltpu.CompilerParams(vmem_limit_bytes=moved + 4 * MIB),
            cost_estimate=pl.CostEstimate(
                flops=2 * order**2 * height * count * width // 4 * (cols - 1),
                bytes_accessed=moved // 2,
                transcendentals=0,
            ),
            name=f"peer_products_{at}",
        )(*given, *pieces, panel, totals)
        plan = plan or out[layers:]
        far, near = list(range(layers // 2, layers)), list(range(1, layers // 2))
        turn = far + near if at == 0 else far[:-1] + near + far[-1:]
        codes = [flipped(out[d], "layer", d) for d in turn]
        finished = [
            pl.pallas_call(
                functools.partial(finish_kernel, (layers, slots), (at, height)),
                out_shape=jax.ShapeDtypeStruct((own_rows, kept, at + height, order), jnp.bfloat16),
                in_specs=[vector] * (len(finished) + layers),
                out_specs=vector,
                compiler_params=pltpu.CompilerParams(
                    vmem_limit_bytes=16 * slots * block_size + 4 * MIB
                ),
                name=f"finish_{at}",
            )(*finished, out[0], *codes)
        ]
    return finished[0]


def solution(mesh):
    placed = (
        P(("row", "col", "layer"), None, None),
        P(("row", "col", "layer")),
        P(("row", "col", "layer")),
        P(("row", "layer"), "col", None, None),
        P(("row", "layer"), "col"),
        P("row", "col"),
    )
    return jax.shard_map(
        per_device,
        mesh=mesh,
        in_specs=placed,
        out_specs=P(("row", "layer"), "col", None, None),
        check_vma=False,
    )
```

```python
import functools

import jax
import jax.numpy as jnp
from jax import lax
from jax.experimental import pallas as pl
from jax.experimental.pallas import tpu as pltpu
from jax.sharding import PartitionSpec as P

GROUP = 8
LANES = 128
FIELD = 10
MIB = 2**20
HBM = pltpu.MemorySpace.HBM


def row_ranges(order):
    first = order * 3 // 4
    return [(0, first), (first, order - first)]


def in_hbm(*values):
    return [pltpu.with_memory_space_constraint(value, HBM) for value in values]


def flipped(value, axis, bits):
    return lax.ppermute(value, axis, [(i, i ^ bits) for i in range(lax.axis_size(axis))])


def gathered(value, axis):
    values = {0: value}
    bit = lax.axis_size(axis) // 2
    while bit:
        values |= {d ^ bit: flipped(held, axis, bit) for d, held in values.items()}
        bit //= 2
    return [values[d] for d in range(len(values))]


def shifted(value, axis, offset):
    size = lax.axis_size(axis)
    return lax.ppermute(value, axis, [((i + offset) % size, i) for i in range(size)])


def quotient(value, by):
    return value >> (by.bit_length() - 1) if by & (by - 1) == 0 else lax.div(value, by)


def remainder(value, by):
    return value & (by - 1) if by & (by - 1) == 0 else lax.rem(value, by)


def write_digits(tile, at, value):
    height, width = value.shape
    tile[at : at + height, :width] = remainder(value, LANES)
    tile[at + height : at + 2 * height, :width] = quotient(value, LANES)


def pack_first_kernel(sizes, a_rows, a_cols, c_cols, x_in, known, x_out, rows, cols, held, tile, sem):
    layers, count, piece_rows, width, local_rows, kept, order, height = sizes
    spot = x_out.at[pl.ds(0, count * height)].reshape(count, height, order)
    pairs = [(a_rows, rows), (a_cols, cols), (c_cols, held), (x_in.at[:, pl.ds(0, height)], spot)]
    loads = [pltpu.make_async_copy(*pair, sem.at[p]) for p, pair in enumerate(pairs)]
    for load in loads:
        load.start()
    known[...] = jnp.zeros_like(known)
    tile[...] = jnp.zeros_like(tile)
    for load in loads[:3]:
        load.wait()
    own_rows = local_rows // layers
    row, col = rows[...], cols[...]
    here = quotient(row[:, :1], local_rows)
    layer = remainder(quotient(col[:, :1], piece_rows), layers)
    owner = quotient(col, piece_rows * layers)
    local = row - here * local_rows
    goal = (quotient(local, own_rows) ^ layer) * own_rows
    place = (
        ((owner ^ here) * piece_rows + remainder(col, piece_rows)) * width,
        (goal + remainder(local, own_rows)) * kept,
        local,
    )
    for p, value in enumerate(place):
        known[p : p + 1, :count] = value
        write_digits(tile, 2 * p, value)
    known[8 : 8 + kept, :local_rows] = held[...]
    x_out[count * height :] = tile[...].astype(jnp.float32).astype(jnp.bfloat16)
    loads[3].wait()


def pack_later_kernel(sizes, x_in, s_cols, s_in, s_out, *refs):
    count, piece, order, ranges = sizes
    x_out, (held, tile, sem) = refs[: len(ranges)], refs[len(ranges) :]
    sources = [(s_cols, held)]
    sources += [(s_in.at[q], s_out.at[pl.ds(q * order, order)]) for q in range(piece)]
    sources += [
        (x_in.at[:, pl.ds(first, height)], out.reshape(count, height, order))
        for (first, height), out in zip(ranges, x_out)
    ]
    loads = [pltpu.make_async_copy(*pair, sem.at[p]) for p, pair in enumerate(sources)]
    for load in loads:
        load.start()
    tile[...] = jnp.zeros_like(tile)
    loads[0].wait()
    write_digits(tile, 0, held[...])
    s_out[piece * order :] = tile[...].astype(jnp.float32).astype(jnp.bfloat16)
    for load in loads[1:]:
        load.wait()


def match(sizes, place, panel_cols, kept_cols):
    width, local_rows, kept = sizes
    right, goal, local = place
    wanted, held = [jnp.zeros_like(right)] * width, [jnp.zeros_like(right)] * kept
    for p in range(panel_cols.shape[0]):
        for s in range(width):
            wanted[s] = jnp.where(right == p * width, panel_cols[p : p + 1, s : s + 1], wanted[s])
    for i in range(local_rows):
        for t in range(kept):
            held[t] = jnp.where(local == i, kept_cols[t : t + 1, i : i + 1], held[t])
    block = lax.broadcasted_iota(jnp.int32, right.shape, 1)
    codes = []
    for s in range(width):
        word = jnp.full_like(right, -1)
        for t in range(kept):
            pair = ((block << FIELD) | (right + s)) << FIELD | (goal + t)
            word = jnp.where(held[t] == wanted[s], pair, word)
        codes.append(word)
    return codes


def list_height(count, width):
    return (count * width // GROUP + 2 + 7) // 8 * 8


def list_pairs(sizes, codes, pairs):
    count, trash = sizes
    total = jnp.int32(0)
    for n in range(count):
        for code in codes:
            word = code[0, n]
            pairs[total] = word
            total += (word >= 0).astype(jnp.int32)
    for g in range(GROUP):
        pairs[total + g] = trash
    return quotient(total + GROUP - 1, GROUP)


def add_products(left, panel, totals, words_of, groups):
    height = totals.shape[1]
    mask = (1 << FIELD) - 1

    def one_group(group, carry):
        words = words_of(group)
        products = []
        for word in words:
            at = pl.multiple_of((word >> (2 * FIELD)) * height, height)
            products.append(
                jnp.dot(
                    left[pl.ds(at, height)],
                    panel[(word >> FIELD) & mask],
                    preferred_element_type=jnp.float32,
                )
            )
        for word, product in zip(words, products):
            totals[word & mask] += product
        return carry

    lax.fori_loop(0, groups, one_group, 0)


def own_kernel(sizes, ranges, known, *refs):
    rows, count, piece_rows, width, local_rows, kept, order = sizes
    x_in, s_in, refs = refs[: len(ranges)], refs[len(ranges) :][:rows], refs[len(ranges) + rows :]
    totals, panel, panel_cols, pairs = refs
    piece = piece_rows * width
    for d in range(rows):
        tile = s_in[d][piece * order :].astype(jnp.float32).astype(jnp.int32)
        panel_cols[d * piece_rows : (d + 1) * piece_rows] = (
            tile[:piece_rows] + tile[piece_rows : 2 * piece_rows] * LANES
        )
    place = known[0:1], known[1:2], known[2:3]
    codes = match((width, local_rows, kept), place, panel_cols[...], known[8 : 8 + kept])
    totals[...] = jnp.zeros_like(totals)
    for d in range(rows):
        for q in range(piece):
            panel[d * piece + q] = s_in[d][q * order : (q + 1) * order]
    groups = list_pairs((count, totals.shape[0] - 1), codes, pairs)

    def words_of(group):
        return [pairs[group * GROUP + g] for g in range(GROUP)]

    for (first, height), blocks in zip(ranges, x_in):
        add_products(blocks, panel, totals.at[:, pl.ds(first, height)], words_of, groups)


def peer_kernel(sizes, span, *refs):
    cols, layers, count, width, local_rows, kept = sizes
    first, height = span
    slots = local_rows * kept // layers
    if first == 0:
        known, panel_cols, *refs = refs
    else:
        listed, *refs = refs
    x_in, refs = refs[: cols - 1], refs[cols - 1 :]
    panel, before, own, sent, refs = refs[0], refs[1], refs[2], refs[3 : 2 + layers], refs[2 + layers :]
    totals = refs[-1]
    if first == 0:
        listed, pairs = refs[:-1]
        lane = lax.broadcasted_iota(jnp.int32, (1, listed.shape[2]), 1)
        totals[...] = before[:, first : first + height]
        for j in range(cols - 1):
            digits = x_in[j][count * height :].astype(jnp.float32).astype(jnp.int32)
            place = [digits[p : p + 1] + digits[p + 1 : p + 2] * LANES for p in (0, 2, 4)]
            codes = match(
                (width, local_rows, kept), place, panel_cols[...], known[8 : 8 + kept]
            )
            groups = list_pairs((count, layers * slots), codes, pairs)
            listed[j, listed.shape[1] - 1 :] = jnp.full(lane.shape, groups, jnp.int32)

            def words_of(group):
                words = [pairs[group * GROUP + g] for g in range(GROUP)]
                row = jnp.zeros(lane.shape, jnp.int32)
                for g, word in enumerate(words):
                    row = jnp.where(lane == g, word, row)
                listed[j, pl.ds(group, 1)] = row
                return words

            add_products(x_in[j], panel, totals, words_of, groups)
    else:
        totals[...] = before[:, first : first + height]
        for j in range(cols - 1):

            def words_of(group):
                row = listed[j, pl.ds(group, 1)]
                return [row[0, g] for g in range(GROUP)]

            add_products(x_in[j], panel, totals, words_of, listed[j, listed.shape[1] - 1 :][0, 0])

    own[...] = totals[:slots]
    half = height // 2
    sublane = lax.broadcasted_iota(jnp.int32, (8, totals.shape[2]), 0)
    for d in range(1, layers):
        code = sent[d - 1]
        for u in range(slots):
            value = totals[d * slots + u]
            peak = jnp.max(jnp.abs(value), axis=0, keepdims=True)
            power = jnp.floor(jnp.log2(jnp.maximum(peak, 1e-36)) + 1e-3) + 1.0
            whole = jnp.floor(value * jnp.exp2(-power) * 32768.0 + 0.5).astype(jnp.int32)
            word = (whole[:half] << 16) | (whole[half:] & 0xFFFF)
            bits = ((power.astype(jnp.int32) + 128) >> sublane) & 1
            code[pl.ds(u * half, 8)] = (word[:8] & ~1) | bits
            code[pl.ds(u * half + 8, half - 8)] = word[8:]


def finish_kernel(sizes, span, *refs):
    layers, slots = sizes
    first, height = span
    half = height // 2
    sublane = lax.broadcasted_iota(jnp.int32, (8, refs[-1].shape[3]), 0)
    before, own, codes, result = refs[: first > 0], refs[-layers - 1], refs[-layers:-1], refs[-1]
    kept = result.shape[1]
    for done in before:
        result[:, :, :first] = done[...]
    for u in range(slots):
        high, low = own[u, :half], own[u, half:]
        for code in codes:
            word = code[pl.ds(u * half, half)]
            power = jnp.sum((word[:8] & 1) << sublane, axis=0, keepdims=True).astype(jnp.float32)
            scale = jnp.exp2(power - 128.0)
            word = jnp.concatenate([word[:8] & ~1, word[8:]])
            high += (word >> 16).astype(jnp.float32) * (1 / 32768) * scale
            low += ((word << 16) >> 16).astype(jnp.float32) * (1 / 32768) * scale
        result[u // kept, u % kept, first : first + half] = high.astype(jnp.bfloat16)
        result[u // kept, u % kept, first + half : first + height] = low.astype(jnp.bfloat16)


def per_device(a_blocks, a_rows, a_cols, s_blocks, s_cols, c_cols):
    rows, cols, layers = (lax.axis_size(axis) for axis in ("row", "col", "layer"))
    count, order = a_blocks.shape[:2]
    piece_rows, width = s_cols.shape
    local_rows, kept = c_cols.shape
    own_rows = local_rows // layers
    slots = own_rows * kept
    all_slots = layers * slots
    ranges = row_ranges(order)
    piece = piece_rows * width
    panel_size = rows * piece
    block_size = order * order
    flat_s = s_blocks.reshape(piece, order, order)
    note_height = (2 * piece_rows + 15) // 16 * 16

    vector = pl.BlockSpec(memory_space=pltpu.VMEM)
    far = pl.BlockSpec(memory_space=HBM)

    first_height = ranges[0][1]
    known, x_first = pl.pallas_call(
        functools.partial(
            pack_first_kernel,
            (layers, count, piece_rows, width, local_rows, kept, order, first_height),
        ),
        out_shape=[
            jax.ShapeDtypeStruct((16, LANES), jnp.int32),
            jax.ShapeDtypeStruct((count * first_height + 16, order), jnp.bfloat16),
        ],
        in_specs=[far] * 4,
        out_specs=[vector] * 2,
        scratch_shapes=[
            pltpu.VMEM((1, count), jnp.int32),
            pltpu.VMEM((1, count), jnp.int32),
            pltpu.VMEM((kept, local_rows), jnp.int32),
            pltpu.VMEM((16, LANES), jnp.int32),
            pltpu.SemaphoreType.DMA((4,)),
        ],
        compiler_params=pltpu.CompilerParams(
            vmem_limit_bytes=2 * block_size * (count + 1) + 4 * MIB
        ),
        name="pack_first",
    )(*in_hbm(a_rows.reshape(1, count), a_cols.reshape(1, count), c_cols.T, a_blocks))
    first_piece = [shifted(x_first, "col", j) for j in range(1, cols)]
    later_blocks, later_s_cols, later_s, _ = lax.optimization_barrier(
        (a_blocks, s_cols, flat_s, known)
    )
    s_sent, *x_later = pl.pallas_call(
        functools.partial(pack_later_kernel, (count, piece, order, ranges[1:])),
        out_shape=[jax.ShapeDtypeStruct((piece * order + note_height, order), jnp.bfloat16)]
        + [
            jax.ShapeDtypeStruct((count * height, order), jnp.bfloat16) for _, height in ranges[1:]
        ],
        in_specs=[far] * 3,
        out_specs=[vector] * len(ranges),
        scratch_shapes=[
            pltpu.VMEM((piece_rows, width), jnp.int32),
            pltpu.VMEM((note_height, LANES), jnp.int32),
            pltpu.SemaphoreType.DMA((piece + len(ranges),)),
        ],
        compiler_params=pltpu.CompilerParams(
            vmem_limit_bytes=2 * block_size * (count + piece + 1) + 4 * MIB
        ),
        name="pack_later",
    )(*in_hbm(later_blocks, later_s_cols, later_s))
    x_sent = [x_first, *x_later]
    s_pieces = gathered(s_sent, "row")
    moved = block_size * (4 * all_slots + 4 * panel_size + 2 * count)
    totals, panel, panel_cols = pl.pallas_call(
        functools.partial(
            own_kernel, (rows, count, piece_rows, width, local_rows, kept, order), ranges
        ),
        out_shape=[
            jax.ShapeDtypeStruct((all_slots + 1, order, order), jnp.float32),
            jax.ShapeDtypeStruct((panel_size, order, order), jnp.bfloat16),
            jax.ShapeDtypeStruct((rows * piece_rows, LANES), jnp.int32),
        ],
        in_specs=[vector] * (1 + len(ranges) + rows),
        out_specs=[vector] * 3,
        scratch_shapes=[
            pltpu.SMEM((count * width + GROUP,), jnp.int32),
        ],
        compiler_params=pltpu.CompilerParams(vmem_limit_bytes=moved + 4 * MIB),
        cost_estimate=pl.CostEstimate(
            flops=2 * order**3 * count * width // 4, bytes_accessed=moved, transcendentals=0
        ),
        name="own_products",
    )(known, *x_sent, *s_pieces)

    moved = block_size * (8 * all_slots + 2 * panel_size + 2 * count * (cols - 1))
    later, panel_cols = lax.optimization_barrier((x_sent[1:], panel_cols))
    x_pieces = [first_piece]
    x_pieces += [[shifted(part, "col", j) for j in range(1, cols)] for part in later]

    list_shape = (cols - 1, list_height(count, width), LANES)
    finished, plan = [], []
    for (at, height), pieces in zip(ranges, x_pieces):
        code_rows = slots * (height // 2)
        out_shape = [jax.ShapeDtypeStruct((slots, height, order), jnp.float32)]
        out_shape += [jax.ShapeDtypeStruct((code_rows, order), jnp.int32)] * (layers - 1)
        scratch = []
        if at == 0:
            out_shape.append(jax.ShapeDtypeStruct(list_shape, jnp.int32))
            scratch = [pltpu.SMEM((count * width + GROUP,), jnp.int32)]
        given = plan or (known, panel_cols)
        out = pl.pallas_call(
            functools.partial(
                peer_kernel, (cols, layers, count, width, local_rows, kept), (at, height)
            ),
            out_shape=out_shape,
            in_specs=[vector] * (len(given) + cols + 1),
            out_specs=[vector] * len(out_shape),
            scratch_shapes=[*scratch, pltpu.VMEM((all_slots + 1, height, order), jnp.float32)],
            compiler_params=pltpu.CompilerParams(vmem_limit_bytes=moved + 4 * MIB),
            cost_estimate=pl.CostEstimate(
                flops=2 * order**2 * height * count * width // 4 * (cols - 1),
                bytes_accessed=moved // 2,
                transcendentals=0,
            ),
            name=f"peer_products_{at}",
        )(*given, *pieces, panel, totals)
        plan = plan or out[layers:]
        far, near = list(range(layers // 2, layers)), list(range(1, layers // 2))
        turn = far + near if at == 0 else far[:-1] + near + far[-1:]
        codes = [flipped(out[d], "layer", d) for d in turn]
        finished = [
            pl.pallas_call(
                functools.partial(finish_kernel, (layers, slots), (at, height)),
                out_shape=jax.ShapeDtypeStruct((own_rows, kept, at + height, order), jnp.bfloat16),
                in_specs=[vector] * (len(finished) + layers),
                out_specs=vector,
                compiler_params=pltpu.CompilerParams(
                    vmem_limit_bytes=16 * slots * block_size + 4 * MIB
                ),
                name=f"finish_{at}",
            )(*finished, out[0], *codes)
        ]
    return finished[0]


def solution(mesh):
    placed = (
        P(("row", "col", "layer"), None, None),
        P(("row", "col", "layer")),
        P(("row", "col", "layer")),
        P(("row", "layer"), "col", None, None),
        P(("row", "layer"), "col"),
        P("row", "col"),
    )
    return jax.shard_map(
        per_device,
        mesh=mesh,
        in_specs=placed,
        out_specs=P(("row", "layer"), "col", None, None),
        check_vma=False,
    )
```

```python
import functools

import jax
import jax.numpy as jnp
from jax import lax
from jax.experimental import pallas as pl
from jax.experimental.pallas import tpu as pltpu
from jax.sharding import PartitionSpec as P

GROUP = 8
LANES = 128
FIELD = 10
MIB = 2**20
HBM = pltpu.MemorySpace.HBM


def row_ranges(order):
    first = order * 5 // 8
    return [(0, first), (first, order - first)]


def in_hbm(*values):
    return [pltpu.with_memory_space_constraint(value, HBM) for value in values]


def flipped(value, axis, bits):
    return lax.ppermute(value, axis, [(i, i ^ bits) for i in range(lax.axis_size(axis))])


def gathered(value, axis):
    values = {0: value}
    bit = lax.axis_size(axis) // 2
    while bit:
        values |= {d ^ bit: flipped(held, axis, bit) for d, held in values.items()}
        bit //= 2
    return [values[d] for d in range(len(values))]


def shifted(value, axis, offset):
    size = lax.axis_size(axis)
    return lax.ppermute(value, axis, [((i + offset) % size, i) for i in range(size)])


def quotient(value, by):
    return value >> (by.bit_length() - 1) if by & (by - 1) == 0 else lax.div(value, by)


def remainder(value, by):
    return value & (by - 1) if by & (by - 1) == 0 else lax.rem(value, by)


def write_digits(tile, at, value):
    height, width = value.shape
    tile[at : at + height, :width] = remainder(value, LANES)
    tile[at + height : at + 2 * height, :width] = quotient(value, LANES)


def pack_first_kernel(sizes, a_rows, a_cols, c_cols, x_in, known, x_out, rows, cols, held, tile, sem):
    layers, count, piece_rows, width, local_rows, kept, order, height = sizes
    spot = x_out.at[pl.ds(0, count * height)].reshape(count, height, order)
    pairs = [(a_rows, rows), (a_cols, cols), (c_cols, held), (x_in.at[:, pl.ds(0, height)], spot)]
    loads = [pltpu.make_async_copy(*pair, sem.at[p]) for p, pair in enumerate(pairs)]
    for load in loads:
        load.start()
    known[...] = jnp.zeros_like(known)
    tile[...] = jnp.zeros_like(tile)
    for load in loads[:3]:
        load.wait()
    own_rows = local_rows // layers
    row, col = rows[...], cols[...]
    here = quotient(row[:, :1], local_rows)
    layer = remainder(quotient(col[:, :1], piece_rows), layers)
    owner = quotient(col, piece_rows * layers)
    local = row - here * local_rows
    goal = (quotient(local, own_rows) ^ layer) * own_rows
    place = (
        ((owner ^ here) * piece_rows + remainder(col, piece_rows)) * width,
        (goal + remainder(local, own_rows)) * kept,
        local,
    )
    for p, value in enumerate(place):
        known[p : p + 1, :count] = value
        write_digits(tile, 2 * p, value)
    known[8 : 8 + kept, :local_rows] = held[...]
    x_out[count * height :] = tile[...].astype(jnp.float32).astype(jnp.bfloat16)
    loads[3].wait()


def pack_later_kernel(sizes, x_in, s_cols, s_in, s_out, *refs):
    count, piece, order, ranges = sizes
    x_out, (held, tile, sem) = refs[: len(ranges)], refs[len(ranges) :]
    sources = [(s_cols, held)]
    sources += [(s_in.at[q], s_out.at[pl.ds(q * order, order)]) for q in range(piece)]
    sources += [
        (x_in.at[:, pl.ds(first, height)], out.reshape(count, height, order))
        for (first, height), out in zip(ranges, x_out)
    ]
    loads = [pltpu.make_async_copy(*pair, sem.at[p]) for p, pair in enumerate(sources)]
    for load in loads:
        load.start()
    tile[...] = jnp.zeros_like(tile)
    loads[0].wait()
    write_digits(tile, 0, held[...])
    s_out[piece * order :] = tile[...].astype(jnp.float32).astype(jnp.bfloat16)
    for load in loads[1:]:
        load.wait()


def range_kernel(span, x_in, out, sem):
    first, height = span
    spot = out.reshape(x_in.shape[0], height, x_in.shape[2])
    load = pltpu.make_async_copy(x_in.at[:, pl.ds(first, height)], spot, sem)
    load.start()
    load.wait()


def match(sizes, place, panel_cols, kept_cols):
    width, local_rows, kept = sizes
    right, goal, local = place
    wanted, held = [jnp.zeros_like(right)] * width, [jnp.zeros_like(right)] * kept
    for p in range(panel_cols.shape[0]):
        for s in range(width):
            wanted[s] = jnp.where(right == p * width, panel_cols[p : p + 1, s : s + 1], wanted[s])
    for i in range(local_rows):
        for t in range(kept):
            held[t] = jnp.where(local == i, kept_cols[t : t + 1, i : i + 1], held[t])
    block = lax.broadcasted_iota(jnp.int32, right.shape, 1)
    codes = []
    for s in range(width):
        word = jnp.full_like(right, -1)
        for t in range(kept):
            pair = ((block << FIELD) | (right + s)) << FIELD | (goal + t)
            word = jnp.where(held[t] == wanted[s], pair, word)
        codes.append(word)
    return codes


def list_height(count, width):
    return (count * width // GROUP + 2 + 7) // 8 * 8


def list_pairs(sizes, codes, pairs):
    count, trash = sizes
    total = jnp.int32(0)
    for n in range(count):
        for code in codes:
            word = code[0, n]
            pairs[total] = word
            total += (word >= 0).astype(jnp.int32)
    for g in range(GROUP):
        pairs[total + g] = trash
    return quotient(total + GROUP - 1, GROUP)


def add_products(left, panel, totals, words_of, groups):
    height = totals.shape[1]
    mask = (1 << FIELD) - 1

    def one_group(group, carry):
        words = words_of(group)
        products = []
        for word in words:
            at = pl.multiple_of((word >> (2 * FIELD)) * height, height)
            products.append(
                jnp.dot(
                    left[pl.ds(at, height)],
                    panel[(word >> FIELD) & mask],
                    preferred_element_type=jnp.float32,
                )
            )
        for word, product in zip(words, products):
            totals[word & mask] += product
        return carry

    lax.fori_loop(0, groups, one_group, 0)


def own_kernel(sizes, ranges, known, *refs):
    rows, count, piece_rows, width, local_rows, kept, order = sizes
    x_in, s_in, refs = refs[: len(ranges)], refs[len(ranges) :][:rows], refs[len(ranges) + rows :]
    totals, panel, panel_cols, pairs = refs
    piece = piece_rows * width
    for d in range(rows):
        tile = s_in[d][piece * order :].astype(jnp.float32).astype(jnp.int32)
        panel_cols[d * piece_rows : (d + 1) * piece_rows] = (
            tile[:piece_rows] + tile[piece_rows : 2 * piece_rows] * LANES
        )
    place = known[0:1], known[1:2], known[2:3]
    codes = match((width, local_rows, kept), place, panel_cols[...], known[8 : 8 + kept])
    totals[...] = jnp.zeros_like(totals)
    for d in range(rows):
        for q in range(piece):
            panel[d * piece + q] = s_in[d][q * order : (q + 1) * order]
    groups = list_pairs((count, totals.shape[0] - 1), codes, pairs)

    def words_of(group):
        return [pairs[group * GROUP + g] for g in range(GROUP)]

    for (first, height), blocks in zip(ranges, x_in):
        add_products(blocks, panel, totals.at[:, pl.ds(first, height)], words_of, groups)


def peer_kernel(sizes, span, *refs):
    cols, layers, count, width, local_rows, kept = sizes
    first, height = span
    slots = local_rows * kept // layers
    if first == 0:
        known, panel_cols, *refs = refs
    else:
        listed, *refs = refs
    x_in, refs = refs[: cols - 1], refs[cols - 1 :]
    panel, before, own, sent, refs = refs[0], refs[1], refs[2], refs[3 : 2 + layers], refs[2 + layers :]
    totals = refs[-1]
    if first == 0:
        listed, pairs = refs[:-1]
        lane = lax.broadcasted_iota(jnp.int32, (1, listed.shape[2]), 1)
        totals[...] = before[:, first : first + height]
        for j in range(cols - 1):
            digits = x_in[j][count * height :].astype(jnp.float32).astype(jnp.int32)
            place = [digits[p : p + 1] + digits[p + 1 : p + 2] * LANES for p in (0, 2, 4)]
            codes = match(
                (width, local_rows, kept), place, panel_cols[...], known[8 : 8 + kept]
            )
            groups = list_pairs((count, layers * slots), codes, pairs)
            listed[j, listed.shape[1] - 1 :] = jnp.full(lane.shape, groups, jnp.int32)

            def words_of(group):
                words = [pairs[group * GROUP + g] for g in range(GROUP)]
                row = jnp.zeros(lane.shape, jnp.int32)
                for g, word in enumerate(words):
                    row = jnp.where(lane == g, word, row)
                listed[j, pl.ds(group, 1)] = row
                return words

            add_products(x_in[j], panel, totals, words_of, groups)
    else:
        totals[...] = before[:, first : first + height]
        for j in range(cols - 1):

            def words_of(group):
                row = listed[j, pl.ds(group, 1)]
                return [row[0, g] for g in range(GROUP)]

            add_products(x_in[j], panel, totals, words_of, listed[j, listed.shape[1] - 1 :][0, 0])

    own[...] = totals[:slots]
    half = height // 2
    sublane = lax.broadcasted_iota(jnp.int32, (8, totals.shape[2]), 0)
    for d in range(1, layers):
        code = sent[d - 1]
        for u in range(slots):
            value = totals[d * slots + u]
            peak = jnp.max(jnp.abs(value), axis=0, keepdims=True)
            power = jnp.floor(jnp.log2(jnp.maximum(peak, 1e-36)) + 1e-3) + 1.0
            whole = jnp.floor(value * jnp.exp2(-power) * 32768.0 + 0.5).astype(jnp.int32)
            word = (whole[:half] << 16) | (whole[half:] & 0xFFFF)
            bits = ((power.astype(jnp.int32) + 128) >> sublane) & 1
            code[pl.ds(u * half, 8)] = (word[:8] & ~1) | bits
            code[pl.ds(u * half + 8, half - 8)] = word[8:]


def finish_kernel(sizes, span, *refs):
    layers, slots = sizes
    first, height = span
    half = height // 2
    sublane = lax.broadcasted_iota(jnp.int32, (8, refs[-1].shape[3]), 0)
    before, own, codes, result = refs[: first > 0], refs[-layers - 1], refs[-layers:-1], refs[-1]
    kept = result.shape[1]
    for done in before:
        result[:, :, :first] = done[...]
    for u in range(slots):
        high, low = own[u, :half], own[u, half:]
        for code in codes:
            word = code[pl.ds(u * half, half)]
            power = jnp.sum((word[:8] & 1) << sublane, axis=0, keepdims=True).astype(jnp.float32)
            scale = jnp.exp2(power - 128.0)
            word = jnp.concatenate([word[:8] & ~1, word[8:]])
            high += (word >> 16).astype(jnp.float32) * (1 / 32768) * scale
            low += ((word << 16) >> 16).astype(jnp.float32) * (1 / 32768) * scale
        result[u // kept, u % kept, first : first + half] = high.astype(jnp.bfloat16)
        result[u // kept, u % kept, first + half : first + height] = low.astype(jnp.bfloat16)


def per_device(a_blocks, a_rows, a_cols, s_blocks, s_cols, c_cols):
    rows, cols, layers = (lax.axis_size(axis) for axis in ("row", "col", "layer"))
    count, order = a_blocks.shape[:2]
    piece_rows, width = s_cols.shape
    local_rows, kept = c_cols.shape
    own_rows = local_rows // layers
    slots = own_rows * kept
    all_slots = layers * slots
    ranges = row_ranges(order)
    piece = piece_rows * width
    panel_size = rows * piece
    block_size = order * order
    flat_s = s_blocks.reshape(piece, order, order)
    note_height = (2 * piece_rows + 15) // 16 * 16

    vector = pl.BlockSpec(memory_space=pltpu.VMEM)
    far = pl.BlockSpec(memory_space=HBM)

    first_height = ranges[0][1]
    known, x_first = pl.pallas_call(
        functools.partial(
            pack_first_kernel,
            (layers, count, piece_rows, width, local_rows, kept, order, first_height),
        ),
        out_shape=[
            jax.ShapeDtypeStruct((16, LANES), jnp.int32),
            jax.ShapeDtypeStruct((count * first_height + 16, order), jnp.bfloat16),
        ],
        in_specs=[far] * 4,
        out_specs=[vector] * 2,
        scratch_shapes=[
            pltpu.VMEM((1, count), jnp.int32),
            pltpu.VMEM((1, count), jnp.int32),
            pltpu.VMEM((kept, local_rows), jnp.int32),
            pltpu.VMEM((16, LANES), jnp.int32),
            pltpu.SemaphoreType.DMA((4,)),
        ],
        compiler_params=pltpu.CompilerParams(
            vmem_limit_bytes=2 * block_size * (count + 1) + 4 * MIB
        ),
        name="pack_first",
    )(*in_hbm(a_rows.reshape(1, count), a_cols.reshape(1, count), c_cols.T, a_blocks))
    first_piece = [shifted(x_first, "col", j) for j in range(1, cols)]
    later_blocks, later_s_cols, later_s, _ = lax.optimization_barrier(
        (a_blocks, s_cols, flat_s, known)
    )
    s_sent, *x_later = pl.pallas_call(
        functools.partial(pack_later_kernel, (count, piece, order, ranges[1:])),
        out_shape=[jax.ShapeDtypeStruct((piece * order + note_height, order), jnp.bfloat16)]
        + [
            jax.ShapeDtypeStruct((count * height, order), jnp.bfloat16) for _, height in ranges[1:]
        ],
        in_specs=[far] * 3,
        out_specs=[vector] * len(ranges),
        scratch_shapes=[
            pltpu.VMEM((piece_rows, width), jnp.int32),
            pltpu.VMEM((note_height, LANES), jnp.int32),
            pltpu.SemaphoreType.DMA((piece + len(ranges),)),
        ],
        compiler_params=pltpu.CompilerParams(
            vmem_limit_bytes=2 * block_size * (count + piece + 1) + 4 * MIB
        ),
        name="pack_later",
    )(*in_hbm(later_blocks, later_s_cols, later_s))
    x_sent = [x_first, *x_later]
    s_pieces = gathered(s_sent, "row")
    moved = block_size * (4 * all_slots + 4 * panel_size + 2 * count)
    totals, panel, panel_cols = pl.pallas_call(
        functools.partial(
            own_kernel, (rows, count, piece_rows, width, local_rows, kept, order), ranges
        ),
        out_shape=[
            jax.ShapeDtypeStruct((all_slots + 1, order, order), jnp.float32),
            jax.ShapeDtypeStruct((panel_size, order, order), jnp.bfloat16),
            jax.ShapeDtypeStruct((rows * piece_rows, LANES), jnp.int32),
        ],
        in_specs=[vector] * (1 + len(ranges) + rows),
        out_specs=[vector] * 3,
        scratch_shapes=[
            pltpu.SMEM((count * width + GROUP,), jnp.int32),
        ],
        compiler_params=pltpu.CompilerParams(vmem_limit_bytes=moved + 4 * MIB),
        cost_estimate=pl.CostEstimate(
            flops=2 * order**3 * count * width // 4, bytes_accessed=moved, transcendentals=0
        ),
        name="own_products",
    )(known, *x_sent, *s_pieces)

    moved = block_size * (8 * all_slots + 2 * panel_size + 2 * count * (cols - 1))
    late_blocks, panel_cols = lax.optimization_barrier((a_blocks, panel_cols))
    later = [
        pl.pallas_call(
            functools.partial(range_kernel, span),
            out_shape=jax.ShapeDtypeStruct((count * span[1], order), jnp.bfloat16),
            in_specs=[far],
            out_specs=vector,
            scratch_shapes=[pltpu.SemaphoreType.DMA],
            compiler_params=pltpu.CompilerParams(
                vmem_limit_bytes=2 * block_size * count + 4 * MIB
            ),
            name=f"pack_{span[0]}",
        )(*in_hbm(late_blocks))
        for span in ranges[1:]
    ]
    x_pieces = [first_piece]
    x_pieces += [[shifted(part, "col", j) for j in range(1, cols)] for part in later]

    list_shape = (cols - 1, list_height(count, width), LANES)
    finished, plan = [], []
    for (at, height), pieces in zip(ranges, x_pieces):
        code_rows = slots * (height // 2)
        out_shape = [jax.ShapeDtypeStruct((slots, height, order), jnp.float32)]
        out_shape += [jax.ShapeDtypeStruct((code_rows, order), jnp.int32)] * (layers - 1)
        scratch = []
        if at == 0:
            out_shape.append(jax.ShapeDtypeStruct(list_shape, jnp.int32))
            scratch = [pltpu.SMEM((count * width + GROUP,), jnp.int32)]
        given = plan or (known, panel_cols)
        out = pl.pallas_call(
            functools.partial(
                peer_kernel, (cols, layers, count, width, local_rows, kept), (at, height)
            ),
            out_shape=out_shape,
            in_specs=[vector] * (len(given) + cols + 1),
            out_specs=[vector] * len(out_shape),
            scratch_shapes=[*scratch, pltpu.VMEM((all_slots + 1, height, order), jnp.float32)],
            compiler_params=pltpu.CompilerParams(vmem_limit_bytes=moved + 4 * MIB),
            cost_estimate=pl.CostEstimate(
                flops=2 * order**2 * height * count * width // 4 * (cols - 1),
                bytes_accessed=moved // 2,
                transcendentals=0,
            ),
            name=f"peer_products_{at}",
        )(*given, *pieces, panel, totals)
        plan = plan or out[layers:]
        far, near = list(range(layers // 2, layers)), list(range(1, layers // 2))
        turn = far + near if at == 0 else far[:-1] + near + far[-1:]
        codes = [flipped(out[d], "layer", d) for d in turn]
        finished = [
            pl.pallas_call(
                functools.partial(finish_kernel, (layers, slots), (at, height)),
                out_shape=jax.ShapeDtypeStruct((own_rows, kept, at + height, order), jnp.bfloat16),
                in_specs=[vector] * (len(finished) + layers),
                out_specs=vector,
                compiler_params=pltpu.CompilerParams(
                    vmem_limit_bytes=16 * slots * block_size + 4 * MIB
                ),
                name=f"finish_{at}",
            )(*finished, out[0], *codes)
        ]
    return finished[0]


def solution(mesh):
    placed = (
        P(("row", "col", "layer"), None, None),
        P(("row", "col", "layer")),
        P(("row", "col", "layer")),
        P(("row", "layer"), "col", None, None),
        P(("row", "layer"), "col"),
        P("row", "col"),
    )
    return jax.shard_map(
        per_device,
        mesh=mesh,
        in_specs=placed,
        out_specs=P(("row", "layer"), "col", None, None),
        check_vma=False,
    )
```

```python
import functools

import jax
import jax.numpy as jnp
from jax import lax
from jax.experimental import pallas as pl
from jax.experimental.pallas import tpu as pltpu
from jax.sharding import PartitionSpec as P

GROUP = 8
LANES = 128
FIELD = 10
MIB = 2**20
HBM = pltpu.MemorySpace.HBM


def row_ranges(order):
    first = order * 5 // 8
    return [(0, first), (first, order - first)]


def in_hbm(*values):
    return [pltpu.with_memory_space_constraint(value, HBM) for value in values]


def flipped(value, axis, bits):
    return lax.ppermute(value, axis, [(i, i ^ bits) for i in range(lax.axis_size(axis))])


def gathered(value, axis):
    values = {0: value}
    bit = lax.axis_size(axis) // 2
    while bit:
        values |= {d ^ bit: flipped(held, axis, bit) for d, held in values.items()}
        bit //= 2
    return [values[d] for d in range(len(values))]


def shifted(value, axis, offset):
    size = lax.axis_size(axis)
    return lax.ppermute(value, axis, [((i + offset) % size, i) for i in range(size)])


def quotient(value, by):
    return value >> (by.bit_length() - 1) if by & (by - 1) == 0 else lax.div(value, by)


def remainder(value, by):
    return value & (by - 1) if by & (by - 1) == 0 else lax.rem(value, by)


def write_digits(tile, at, value):
    height, width = value.shape
    tile[at : at + height, :width] = remainder(value, LANES)
    tile[at + height : at + 2 * height, :width] = quotient(value, LANES)


def pack_first_kernel(sizes, a_rows, a_cols, c_cols, x_in, known, x_out, rows, cols, held, tile, sem):
    layers, count, piece_rows, width, local_rows, kept, order, height = sizes
    spot = x_out.at[pl.ds(0, count * height)].reshape(count, height, order)
    pairs = [(a_rows, rows), (a_cols, cols), (c_cols, held), (x_in.at[:, pl.ds(0, height)], spot)]
    loads = [pltpu.make_async_copy(*pair, sem.at[p]) for p, pair in enumerate(pairs)]
    for load in loads:
        load.start()
    known[...] = jnp.zeros_like(known)
    tile[...] = jnp.zeros_like(tile)
    for load in loads[:3]:
        load.wait()
    own_rows = local_rows // layers
    row, col = rows[...], cols[...]
    here = quotient(row[:, :1], local_rows)
    layer = remainder(quotient(col[:, :1], piece_rows), layers)
    owner = quotient(col, piece_rows * layers)
    local = row - here * local_rows
    goal = (quotient(local, own_rows) ^ layer) * own_rows
    place = (
        ((owner ^ here) * piece_rows + remainder(col, piece_rows)) * width,
        (goal + remainder(local, own_rows)) * kept,
        local,
    )
    for p, value in enumerate(place):
        known[p : p + 1, :count] = value
        write_digits(tile, 2 * p, value)
    known[8 : 8 + kept, :local_rows] = held[...]
    x_out[count * height :] = tile[...].astype(jnp.float32).astype(jnp.bfloat16)
    loads[3].wait()


def pack_later_kernel(sizes, x_in, s_cols, s_in, s_out, *refs):
    count, piece, order, ranges = sizes
    x_out, (held, tile, sem) = refs[: len(ranges)], refs[len(ranges) :]
    sources = [(s_cols, held)]
    sources += [(s_in.at[q], s_out.at[pl.ds(q * order, order)]) for q in range(piece)]
    sources += [
        (x_in.at[:, pl.ds(first, height)], out.reshape(count, height, order))
        for (first, height), out in zip(ranges, x_out)
    ]
    loads = [pltpu.make_async_copy(*pair, sem.at[p]) for p, pair in enumerate(sources)]
    for load in loads:
        load.start()
    tile[...] = jnp.zeros_like(tile)
    loads[0].wait()
    write_digits(tile, 0, held[...])
    s_out[piece * order :] = tile[...].astype(jnp.float32).astype(jnp.bfloat16)
    for load in loads[1:]:
        load.wait()


def match(sizes, place, panel_cols, kept_cols):
    width, local_rows, kept = sizes
    right, goal, local = place
    wanted, held = [jnp.zeros_like(right)] * width, [jnp.zeros_like(right)] * kept
    for p in range(panel_cols.shape[0]):
        for s in range(width):
            wanted[s] = jnp.where(right == p * width, panel_cols[p : p + 1, s : s + 1], wanted[s])
    for i in range(local_rows):
        for t in range(kept):
            held[t] = jnp.where(local == i, kept_cols[t : t + 1, i : i + 1], held[t])
    block = lax.broadcasted_iota(jnp.int32, right.shape, 1)
    codes = []
    for s in range(width):
        word = jnp.full_like(right, -1)
        for t in range(kept):
            pair = ((block << FIELD) | (right + s)) << FIELD | (goal + t)
            word = jnp.where(held[t] == wanted[s], pair, word)
        codes.append(word)
    return codes


def list_height(count, width):
    return (count * width // GROUP + 2 + 7) // 8 * 8


def list_pairs(sizes, codes, pairs):
    count, trash = sizes
    total = jnp.int32(0)
    for n in range(count):
        for code in codes:
            word = code[0, n]
            pairs[total] = word
            total += (word >= 0).astype(jnp.int32)
    for g in range(GROUP):
        pairs[total + g] = trash
    return quotient(total + GROUP - 1, GROUP)


def add_products(left, panel, totals, words_of, groups):
    height = totals.shape[1]
    mask = (1 << FIELD) - 1

    def one_group(group, carry):
        words = words_of(group)
        products = []
        for word in words:
            at = pl.multiple_of((word >> (2 * FIELD)) * height, height)
            products.append(
                jnp.dot(
                    left[pl.ds(at, height)],
                    panel[(word >> FIELD) & mask],
                    preferred_element_type=jnp.float32,
                )
            )
        for word, product in zip(words, products):
            totals[word & mask] += product
        return carry

    lax.fori_loop(0, groups, one_group, 0)


def own_kernel(sizes, ranges, known, *refs):
    rows, count, piece_rows, width, local_rows, kept, order = sizes
    x_in, s_in, refs = refs[: len(ranges)], refs[len(ranges) :][:rows], refs[len(ranges) + rows :]
    totals, panel, panel_cols, pairs = refs
    piece = piece_rows * width
    for d in range(rows):
        tile = s_in[d][piece * order :].astype(jnp.float32).astype(jnp.int32)
        panel_cols[d * piece_rows : (d + 1) * piece_rows] = (
            tile[:piece_rows] + tile[piece_rows : 2 * piece_rows] * LANES
        )
    place = known[0:1], known[1:2], known[2:3]
    codes = match((width, local_rows, kept), place, panel_cols[...], known[8 : 8 + kept])
    totals[...] = jnp.zeros_like(totals)
    for d in range(rows):
        for q in range(piece):
            panel[d * piece + q] = s_in[d][q * order : (q + 1) * order]
    groups = list_pairs((count, totals.shape[0] - 1), codes, pairs)

    def words_of(group):
        return [pairs[group * GROUP + g] for g in range(GROUP)]

    for (first, height), blocks in zip(ranges, x_in):
        add_products(blocks, panel, totals.at[:, pl.ds(first, height)], words_of, groups)


def peer_kernel(sizes, span, *refs):
    cols, layers, count, width, local_rows, kept = sizes
    first, height = span
    slots = local_rows * kept // layers
    if first == 0:
        known, panel_cols, *refs = refs
    else:
        listed, *refs = refs
    x_in, refs = refs[: cols - 1], refs[cols - 1 :]
    panel, before, own, sent, refs = refs[0], refs[1], refs[2], refs[3 : 2 + layers], refs[2 + layers :]
    totals = refs[-1]
    if first == 0:
        listed, pairs = refs[:-1]
        lane = lax.broadcasted_iota(jnp.int32, (1, listed.shape[2]), 1)
        totals[...] = before[:, first : first + height]
        for j in range(cols - 1):
            digits = x_in[j][count * height :].astype(jnp.float32).astype(jnp.int32)
            place = [digits[p : p + 1] + digits[p + 1 : p + 2] * LANES for p in (0, 2, 4)]
            codes = match(
                (width, local_rows, kept), place, panel_cols[...], known[8 : 8 + kept]
            )
            groups = list_pairs((count, layers * slots), codes, pairs)
            listed[j, listed.shape[1] - 1 :] = jnp.full(lane.shape, groups, jnp.int32)

            def words_of(group):
                words = [pairs[group * GROUP + g] for g in range(GROUP)]
                row = jnp.zeros(lane.shape, jnp.int32)
                for g, word in enumerate(words):
                    row = jnp.where(lane == g, word, row)
                listed[j, pl.ds(group, 1)] = row
                return words

            add_products(x_in[j], panel, totals, words_of, groups)
    else:
        totals[...] = before[:, first : first + height]
        for j in range(cols - 1):

            def words_of(group):
                row = listed[j, pl.ds(group, 1)]
                return [row[0, g] for g in range(GROUP)]

            add_products(x_in[j], panel, totals, words_of, listed[j, listed.shape[1] - 1 :][0, 0])

    own[...] = totals[:slots]
    half = height // 2
    sublane = lax.broadcasted_iota(jnp.int32, (8, totals.shape[2]), 0)
    for d in range(1, layers):
        code = sent[d - 1]
        for u in range(slots):
            value = totals[d * slots + u]
            peak = jnp.max(jnp.abs(value), axis=0, keepdims=True)
            power = jnp.floor(jnp.log2(jnp.maximum(peak, 1e-36)) + 1e-3) + 1.0
            whole = jnp.floor(value * jnp.exp2(-power) * 32768.0 + 0.5).astype(jnp.int32)
            word = (whole[:half] << 16) | (whole[half:] & 0xFFFF)
            bits = ((power.astype(jnp.int32) + 128) >> sublane) & 1
            code[pl.ds(u * half, 8)] = (word[:8] & ~1) | bits
            code[pl.ds(u * half + 8, half - 8)] = word[8:]


def finish_kernel(sizes, span, *refs):
    layers, slots = sizes
    first, height = span
    half = height // 2
    sublane = lax.broadcasted_iota(jnp.int32, (8, refs[-1].shape[3]), 0)
    before, own, codes, result = refs[: first > 0], refs[-layers - 1], refs[-layers:-1], refs[-1]
    kept = result.shape[1]
    for done in before:
        result[:, :, :first] = done[...]
    for u in range(slots):
        high, low = own[u, :half], own[u, half:]
        for code in codes:
            word = code[pl.ds(u * half, half)]
            power = jnp.sum((word[:8] & 1) << sublane, axis=0, keepdims=True).astype(jnp.float32)
            scale = jnp.exp2(power - 128.0)
            word = jnp.concatenate([word[:8] & ~1, word[8:]])
            high += (word >> 16).astype(jnp.float32) * (1 / 32768) * scale
            low += ((word << 16) >> 16).astype(jnp.float32) * (1 / 32768) * scale
        result[u // kept, u % kept, first : first + half] = high.astype(jnp.bfloat16)
        result[u // kept, u % kept, first + half : first + height] = low.astype(jnp.bfloat16)


def per_device(a_blocks, a_rows, a_cols, s_blocks, s_cols, c_cols):
    rows, cols, layers = (lax.axis_size(axis) for axis in ("row", "col", "layer"))
    count, order = a_blocks.shape[:2]
    piece_rows, width = s_cols.shape
    local_rows, kept = c_cols.shape
    own_rows = local_rows // layers
    slots = own_rows * kept
    all_slots = layers * slots
    ranges = row_ranges(order)
    piece = piece_rows * width
    panel_size = rows * piece
    block_size = order * order
    flat_s = s_blocks.reshape(piece, order, order)
    note_height = (2 * piece_rows + 15) // 16 * 16

    vector = pl.BlockSpec(memory_space=pltpu.VMEM)
    far = pl.BlockSpec(memory_space=HBM)

    first_height = ranges[0][1]
    known, x_first = pl.pallas_call(
        functools.partial(
            pack_first_kernel,
            (layers, count, piece_rows, width, local_rows, kept, order, first_height),
        ),
        out_shape=[
            jax.ShapeDtypeStruct((16, LANES), jnp.int32),
            jax.ShapeDtypeStruct((count * first_height + 16, order), jnp.bfloat16),
        ],
        in_specs=[far] * 4,
        out_specs=[vector] * 2,
        scratch_shapes=[
            pltpu.VMEM((1, count), jnp.int32),
            pltpu.VMEM((1, count), jnp.int32),
            pltpu.VMEM((kept, local_rows), jnp.int32),
            pltpu.VMEM((16, LANES), jnp.int32),
            pltpu.SemaphoreType.DMA((4,)),
        ],
        compiler_params=pltpu.CompilerParams(
            vmem_limit_bytes=2 * block_size * (count + 1) + 4 * MIB
        ),
        name="pack_first",
    )(*in_hbm(a_rows.reshape(1, count), a_cols.reshape(1, count), c_cols.T, a_blocks))
    first_piece = [shifted(x_first, "col", j) for j in range(1, cols)]
    later_blocks, later_s_cols, later_s, _ = lax.optimization_barrier(
        (a_blocks, s_cols, flat_s, known)
    )
    s_sent, *x_later = pl.pallas_call(
        functools.partial(pack_later_kernel, (count, piece, order, ranges[1:])),
        out_shape=[jax.ShapeDtypeStruct((piece * order + note_height, order), jnp.bfloat16)]
        + [
            jax.ShapeDtypeStruct((count * height, order), jnp.bfloat16) for _, height in ranges[1:]
        ],
        in_specs=[far] * 3,
        out_specs=[vector] * len(ranges),
        scratch_shapes=[
            pltpu.VMEM((piece_rows, width), jnp.int32),
            pltpu.VMEM((note_height, LANES), jnp.int32),
            pltpu.SemaphoreType.DMA((piece + len(ranges),)),
        ],
        compiler_params=pltpu.CompilerParams(
            vmem_limit_bytes=2 * block_size * (count + piece + 1) + 4 * MIB
        ),
        name="pack_later",
    )(*in_hbm(later_blocks, later_s_cols, later_s))
    x_sent = [x_first, *x_later]
    s_pieces = gathered(s_sent, "row")
    moved = block_size * (4 * all_slots + 4 * panel_size + 2 * count)
    totals, panel, panel_cols = pl.pallas_call(
        functools.partial(
            own_kernel, (rows, count, piece_rows, width, local_rows, kept, order), ranges
        ),
        out_shape=[
            jax.ShapeDtypeStruct((all_slots + 1, order, order), jnp.float32),
            jax.ShapeDtypeStruct((panel_size, order, order), jnp.bfloat16),
            jax.ShapeDtypeStruct((rows * piece_rows, LANES), jnp.int32),
        ],
        in_specs=[vector] * (1 + len(ranges) + rows),
        out_specs=[vector] * 3,
        scratch_shapes=[
            pltpu.SMEM((count * width + GROUP,), jnp.int32),
        ],
        compiler_params=pltpu.CompilerParams(vmem_limit_bytes=moved + 4 * MIB),
        cost_estimate=pl.CostEstimate(
            flops=2 * order**3 * count * width // 4, bytes_accessed=moved, transcendentals=0
        ),
        name="own_products",
    )(known, *x_sent, *s_pieces)

    moved = block_size * (8 * all_slots + 2 * panel_size + 2 * count * (cols - 1))
    later, _ = lax.optimization_barrier((x_sent[1:], s_pieces))
    x_pieces = [first_piece]
    x_pieces += [[shifted(part, "col", j) for j in range(1, cols)] for part in later]

    list_shape = (cols - 1, list_height(count, width), LANES)
    finished, plan = [], []
    for (at, height), pieces in zip(ranges, x_pieces):
        code_rows = slots * (height // 2)
        out_shape = [jax.ShapeDtypeStruct((slots, height, order), jnp.float32)]
        out_shape += [jax.ShapeDtypeStruct((code_rows, order), jnp.int32)] * (layers - 1)
        scratch = []
        if at == 0:
            out_shape.append(jax.ShapeDtypeStruct(list_shape, jnp.int32))
            scratch = [pltpu.SMEM((count * width + GROUP,), jnp.int32)]
        given = plan or (known, panel_cols)
        out = pl.pallas_call(
            functools.partial(
                peer_kernel, (cols, layers, count, width, local_rows, kept), (at, height)
            ),
            out_shape=out_shape,
            in_specs=[vector] * (len(given) + cols + 1),
            out_specs=[vector] * len(out_shape),
            scratch_shapes=[*scratch, pltpu.VMEM((all_slots + 1, height, order), jnp.float32)],
            compiler_params=pltpu.CompilerParams(vmem_limit_bytes=moved + 4 * MIB),
            cost_estimate=pl.CostEstimate(
                flops=2 * order**2 * height * count * width // 4 * (cols - 1),
                bytes_accessed=moved // 2,
                transcendentals=0,
            ),
            name=f"peer_products_{at}",
        )(*given, *pieces, panel, totals)
        plan = plan or out[layers:]
        far, near = list(range(layers // 2, layers)), list(range(1, layers // 2))
        turn = far + near if at == 0 else far[:-1] + near + far[-1:]
        codes = [flipped(out[d], "layer", d) for d in turn]
        finished = [
            pl.pallas_call(
                functools.partial(finish_kernel, (layers, slots), (at, height)),
                out_shape=jax.ShapeDtypeStruct((own_rows, kept, at + height, order), jnp.bfloat16),
                in_specs=[vector] * (len(finished) + layers),
                out_specs=vector,
                compiler_params=pltpu.CompilerParams(
                    vmem_limit_bytes=16 * slots * block_size + 4 * MIB
                ),
                name=f"finish_{at}",
            )(*finished, out[0], *codes)
        ]
    return finished[0]


def solution(mesh):
    placed = (
        P(("row", "col", "layer"), None, None),
        P(("row", "col", "layer")),
        P(("row", "col", "layer")),
        P(("row", "layer"), "col", None, None),
        P(("row", "layer"), "col"),
        P("row", "col"),
    )
    return jax.shard_map(
        per_device,
        mesh=mesh,
        in_specs=placed,
        out_specs=P(("row", "layer"), "col", None, None),
        check_vma=False,
    )
```

```python
import functools

import jax
import jax.numpy as jnp
from jax import lax
from jax.experimental import pallas as pl
from jax.experimental.pallas import tpu as pltpu
from jax.sharding import PartitionSpec as P

GROUP = 8
LANES = 128
FIELD = 10
MIB = 2**20
HBM = pltpu.MemorySpace.HBM


def row_ranges(order):
    first = order * 5 // 8
    return [(0, first), (first, order - first)]


def in_hbm(*values):
    return [pltpu.with_memory_space_constraint(value, HBM) for value in values]


def flipped(value, axis, bits):
    return lax.ppermute(value, axis, [(i, i ^ bits) for i in range(lax.axis_size(axis))])


def gathered(value, axis):
    values = {0: value}
    bit = lax.axis_size(axis) // 2
    while bit:
        values |= {d ^ bit: flipped(held, axis, bit) for d, held in values.items()}
        bit //= 2
    return [values[d] for d in range(len(values))]


def shifted(value, axis, offset):
    size = lax.axis_size(axis)
    return lax.ppermute(value, axis, [((i + offset) % size, i) for i in range(size)])


def quotient(value, by):
    return value >> (by.bit_length() - 1) if by & (by - 1) == 0 else lax.div(value, by)


def remainder(value, by):
    return value & (by - 1) if by & (by - 1) == 0 else lax.rem(value, by)


def write_digits(tile, at, value):
    height, width = value.shape
    tile[at : at + height, :width] = remainder(value, LANES)
    tile[at + height : at + 2 * height, :width] = quotient(value, LANES)


def pack_first_kernel(sizes, a_rows, a_cols, c_cols, x_in, known, x_out, rows, cols, held, tile, sem):
    layers, count, piece_rows, width, local_rows, kept, order, height = sizes
    spot = x_out.at[pl.ds(0, count * height)].reshape(count, height, order)
    pairs = [(a_rows, rows), (a_cols, cols), (c_cols, held), (x_in.at[:, pl.ds(0, height)], spot)]
    loads = [pltpu.make_async_copy(*pair, sem.at[p]) for p, pair in enumerate(pairs)]
    for load in loads:
        load.start()
    known[...] = jnp.zeros_like(known)
    tile[...] = jnp.zeros_like(tile)
    for load in loads[:3]:
        load.wait()
    own_rows = local_rows // layers
    row, col = rows[...], cols[...]
    here = quotient(row[:, :1], local_rows)
    layer = remainder(quotient(col[:, :1], piece_rows), layers)
    owner = quotient(col, piece_rows * layers)
    local = row - here * local_rows
    goal = (quotient(local, own_rows) ^ layer) * own_rows
    place = (
        ((owner ^ here) * piece_rows + remainder(col, piece_rows)) * width,
        (goal + remainder(local, own_rows)) * kept,
        local,
    )
    for p, value in enumerate(place):
        known[p : p + 1, :count] = value
        write_digits(tile, 2 * p, value)
    known[8 : 8 + kept, :local_rows] = held[...]
    x_out[count * height :] = tile[...].astype(jnp.float32).astype(jnp.bfloat16)
    loads[3].wait()


def pack_later_kernel(sizes, x_in, s_cols, s_in, s_out, *refs):
    count, piece, order, ranges = sizes
    x_out, (held, tile, sem) = refs[: len(ranges)], refs[len(ranges) :]
    sources = [(s_cols, held)]
    sources += [(s_in.at[q], s_out.at[pl.ds(q * order, order)]) for q in range(piece)]
    sources += [
        (x_in.at[:, pl.ds(first, height)], out.reshape(count, height, order))
        for (first, height), out in zip(ranges, x_out)
    ]
    loads = [pltpu.make_async_copy(*pair, sem.at[p]) for p, pair in enumerate(sources)]
    for load in loads:
        load.start()
    tile[...] = jnp.zeros_like(tile)
    loads[0].wait()
    write_digits(tile, 0, held[...])
    s_out[piece * order :] = tile[...].astype(jnp.float32).astype(jnp.bfloat16)
    for load in loads[1:]:
        load.wait()


def match(sizes, place, panel_cols, kept_cols):
    width, local_rows, kept = sizes
    right, goal, local = place
    wanted, held = [jnp.zeros_like(right)] * width, [jnp.zeros_like(right)] * kept
    for p in range(panel_cols.shape[0]):
        for s in range(width):
            wanted[s] = jnp.where(right == p * width, panel_cols[p : p + 1, s : s + 1], wanted[s])
    for i in range(local_rows):
        for t in range(kept):
            held[t] = jnp.where(local == i, kept_cols[t : t + 1, i : i + 1], held[t])
    block = lax.broadcasted_iota(jnp.int32, right.shape, 1)
    codes = []
    for s in range(width):
        word = jnp.full_like(right, -1)
        for t in range(kept):
            pair = ((block << FIELD) | (right + s)) << FIELD | (goal + t)
            word = jnp.where(held[t] == wanted[s], pair, word)
        codes.append(word)
    return codes


def list_height(count, width):
    return (count * width // GROUP + 2 + 7) // 8 * 8


def list_pairs(sizes, codes, pairs):
    count, trash = sizes
    total = jnp.int32(0)
    for n in range(count):
        for code in codes:
            word = code[0, n]
            pairs[total] = word
            total += (word >= 0).astype(jnp.int32)
    for g in range(GROUP):
        pairs[total + g] = trash
    return quotient(total + GROUP - 1, GROUP)


def add_products(left, panel, totals, words_of, groups):
    height = totals.shape[1]
    mask = (1 << FIELD) - 1

    def one_group(group, carry):
        words = words_of(group)
        products = []
        for word in words:
            at = pl.multiple_of((word >> (2 * FIELD)) * height, height)
            products.append(
                jnp.dot(
                    left[pl.ds(at, height)],
                    panel[(word >> FIELD) & mask],
                    preferred_element_type=jnp.float32,
                )
            )
        for word, product in zip(words, products):
            totals[word & mask] += product
        return carry

    lax.fori_loop(0, groups, one_group, 0)


def own_kernel(sizes, ranges, known, *refs):
    rows, count, piece_rows, width, local_rows, kept, order = sizes
    x_in, s_in, refs = refs[: len(ranges)], refs[len(ranges) :][:rows], refs[len(ranges) + rows :]
    totals, panel, panel_cols, pairs = refs
    piece = piece_rows * width
    for d in range(rows):
        tile = s_in[d][piece * order :].astype(jnp.float32).astype(jnp.int32)
        panel_cols[d * piece_rows : (d + 1) * piece_rows] = (
            tile[:piece_rows] + tile[piece_rows : 2 * piece_rows] * LANES
        )
    place = known[0:1], known[1:2], known[2:3]
    codes = match((width, local_rows, kept), place, panel_cols[...], known[8 : 8 + kept])
    totals[...] = jnp.zeros_like(totals)
    for d in range(rows):
        for q in range(piece):
            panel[d * piece + q] = s_in[d][q * order : (q + 1) * order]
    groups = list_pairs((count, totals.shape[0] - 1), codes, pairs)

    def words_of(group):
        return [pairs[group * GROUP + g] for g in range(GROUP)]

    for (first, height), blocks in zip(ranges, x_in):
        add_products(blocks, panel, totals.at[:, pl.ds(first, height)], words_of, groups)


def peer_kernel(sizes, span, *refs):
    cols, layers, count, width, local_rows, kept = sizes
    first, height = span
    slots = local_rows * kept // layers
    if first == 0:
        known, panel_cols, *refs = refs
    else:
        listed, *refs = refs
    x_in, refs = refs[: cols - 1], refs[cols - 1 :]
    panel, before, own, sent, refs = refs[0], refs[1], refs[2], refs[3 : 2 + layers], refs[2 + layers :]
    totals = refs[-1]
    if first == 0:
        listed, pairs = refs[:-1]
        lane = lax.broadcasted_iota(jnp.int32, (1, listed.shape[2]), 1)
        totals[...] = before[:, first : first + height]
        for j in range(cols - 1):
            digits = x_in[j][count * height :].astype(jnp.float32).astype(jnp.int32)
            place = [digits[p : p + 1] + digits[p + 1 : p + 2] * LANES for p in (0, 2, 4)]
            codes = match(
                (width, local_rows, kept), place, panel_cols[...], known[8 : 8 + kept]
            )
            groups = list_pairs((count, layers * slots), codes, pairs)
            listed[j, listed.shape[1] - 1 :] = jnp.full(lane.shape, groups, jnp.int32)

            def words_of(group):
                words = [pairs[group * GROUP + g] for g in range(GROUP)]
                row = jnp.zeros(lane.shape, jnp.int32)
                for g, word in enumerate(words):
                    row = jnp.where(lane == g, word, row)
                listed[j, pl.ds(group, 1)] = row
                return words

            add_products(x_in[j], panel, totals, words_of, groups)
    else:
        totals[...] = before[:, first : first + height]
        for j in range(cols - 1):

            def words_of(group):
                row = listed[j, pl.ds(group, 1)]
                return [row[0, g] for g in range(GROUP)]

            add_products(x_in[j], panel, totals, words_of, listed[j, listed.shape[1] - 1 :][0, 0])

    own[...] = totals[:slots]
    half = height // 2
    sublane = lax.broadcasted_iota(jnp.int32, (8, totals.shape[2]), 0)
    for d in range(1, layers):
        code = sent[d - 1]
        for u in range(slots):
            value = totals[d * slots + u]
            peak = jnp.max(jnp.abs(value), axis=0, keepdims=True)
            power = jnp.floor(jnp.log2(jnp.maximum(peak, 1e-36)) + 1e-3) + 1.0
            whole = jnp.floor(value * jnp.exp2(-power) * 32768.0 + 0.5).astype(jnp.int32)
            word = (whole[:half] << 16) | (whole[half:] & 0xFFFF)
            bits = ((power.astype(jnp.int32) + 128) >> sublane) & 1
            code[pl.ds(u * half, 8)] = (word[:8] & ~1) | bits
            code[pl.ds(u * half + 8, half - 8)] = word[8:]


def finish_kernel(sizes, span, *refs):
    layers, slots = sizes
    first, height = span
    half = height // 2
    sublane = lax.broadcasted_iota(jnp.int32, (8, refs[-1].shape[3]), 0)
    before, own, codes, result = refs[: first > 0], refs[-layers - 1], refs[-layers:-1], refs[-1]
    kept = result.shape[1]
    for done in before:
        result[:, :, :first] = done[...]
    for u in range(slots):
        high, low = own[u, :half], own[u, half:]
        for code in codes:
            word = code[pl.ds(u * half, half)]
            power = jnp.sum((word[:8] & 1) << sublane, axis=0, keepdims=True).astype(jnp.float32)
            scale = jnp.exp2(power - 128.0)
            word = jnp.concatenate([word[:8] & ~1, word[8:]])
            high += (word >> 16).astype(jnp.float32) * (1 / 32768) * scale
            low += ((word << 16) >> 16).astype(jnp.float32) * (1 / 32768) * scale
        result[u // kept, u % kept, first : first + half] = high.astype(jnp.bfloat16)
        result[u // kept, u % kept, first + half : first + height] = low.astype(jnp.bfloat16)


def per_device(a_blocks, a_rows, a_cols, s_blocks, s_cols, c_cols):
    rows, cols, layers = (lax.axis_size(axis) for axis in ("row", "col", "layer"))
    count, order = a_blocks.shape[:2]
    piece_rows, width = s_cols.shape
    local_rows, kept = c_cols.shape
    own_rows = local_rows // layers
    slots = own_rows * kept
    all_slots = layers * slots
    ranges = row_ranges(order)
    piece = piece_rows * width
    panel_size = rows * piece
    block_size = order * order
    flat_s = s_blocks.reshape(piece, order, order)
    note_height = (2 * piece_rows + 15) // 16 * 16

    vector = pl.BlockSpec(memory_space=pltpu.VMEM)
    far = pl.BlockSpec(memory_space=HBM)

    first_height = ranges[0][1]
    known, x_first = pl.pallas_call(
        functools.partial(
            pack_first_kernel,
            (layers, count, piece_rows, width, local_rows, kept, order, first_height),
        ),
        out_shape=[
            jax.ShapeDtypeStruct((16, LANES), jnp.int32),
            jax.ShapeDtypeStruct((count * first_height + 16, order), jnp.bfloat16),
        ],
        in_specs=[far] * 4,
        out_specs=[vector] * 2,
        scratch_shapes=[
            pltpu.VMEM((1, count), jnp.int32),
            pltpu.VMEM((1, count), jnp.int32),
            pltpu.VMEM((kept, local_rows), jnp.int32),
            pltpu.VMEM((16, LANES), jnp.int32),
            pltpu.SemaphoreType.DMA((4,)),
        ],
        compiler_params=pltpu.CompilerParams(
            vmem_limit_bytes=2 * block_size * (count + 1) + 4 * MIB
        ),
        name="pack_first",
    )(*in_hbm(a_rows.reshape(1, count), a_cols.reshape(1, count), c_cols.T, a_blocks))
    first_piece = [shifted(x_first, "col", j) for j in range(1, cols)]
    later_blocks, later_s_cols, later_s, _ = lax.optimization_barrier(
        (a_blocks, s_cols, flat_s, known)
    )
    s_sent, *x_later = pl.pallas_call(
        functools.partial(pack_later_kernel, (count, piece, order, ranges[1:])),
        out_shape=[jax.ShapeDtypeStruct((piece * order + note_height, order), jnp.bfloat16)]
        + [
            jax.ShapeDtypeStruct((count * height, order), jnp.bfloat16) for _, height in ranges[1:]
        ],
        in_specs=[far] * 3,
        out_specs=[vector] * len(ranges),
        scratch_shapes=[
            pltpu.VMEM((piece_rows, width), jnp.int32),
            pltpu.VMEM((note_height, LANES), jnp.int32),
            pltpu.SemaphoreType.DMA((piece + len(ranges),)),
        ],
        compiler_params=pltpu.CompilerParams(
            vmem_limit_bytes=2 * block_size * (count + piece + 1) + 4 * MIB
        ),
        name="pack_later",
    )(*in_hbm(later_blocks, later_s_cols, later_s))
    x_sent = [x_first, *x_later]
    s_pieces = gathered(s_sent, "row")
    moved = block_size * (4 * all_slots + 4 * panel_size + 2 * count)
    totals, panel, panel_cols = pl.pallas_call(
        functools.partial(
            own_kernel, (rows, count, piece_rows, width, local_rows, kept, order), ranges
        ),
        out_shape=[
            jax.ShapeDtypeStruct((all_slots + 1, order, order), jnp.float32),
            jax.ShapeDtypeStruct((panel_size, order, order), jnp.bfloat16),
            jax.ShapeDtypeStruct((rows * piece_rows, LANES), jnp.int32),
        ],
        in_specs=[vector] * (1 + len(ranges) + rows),
        out_specs=[vector] * 3,
        scratch_shapes=[
            pltpu.SMEM((count * width + GROUP,), jnp.int32),
        ],
        compiler_params=pltpu.CompilerParams(vmem_limit_bytes=moved + 4 * MIB),
        cost_estimate=pl.CostEstimate(
            flops=2 * order**3 * count * width // 4, bytes_accessed=moved, transcendentals=0
        ),
        name="own_products",
    )(known, *x_sent, *s_pieces)

    moved = block_size * (8 * all_slots + 2 * panel_size + 2 * count * (cols - 1))
    later = x_sent[1:]
    x_pieces = [first_piece]
    x_pieces += [[shifted(part, "col", j) for j in range(1, cols)] for part in later]

    list_shape = (cols - 1, list_height(count, width), LANES)
    finished, plan = [], []
    for (at, height), pieces in zip(ranges, x_pieces):
        code_rows = slots * (height // 2)
        out_shape = [jax.ShapeDtypeStruct((slots, height, order), jnp.float32)]
        out_shape += [jax.ShapeDtypeStruct((code_rows, order), jnp.int32)] * (layers - 1)
        scratch = []
        if at == 0:
            out_shape.append(jax.ShapeDtypeStruct(list_shape, jnp.int32))
            scratch = [pltpu.SMEM((count * width + GROUP,), jnp.int32)]
        given = plan or (known, panel_cols)
        out = pl.pallas_call(
            functools.partial(
                peer_kernel, (cols, layers, count, width, local_rows, kept), (at, height)
            ),
            out_shape=out_shape,
            in_specs=[vector] * (len(given) + cols + 1),
            out_specs=[vector] * len(out_shape),
            scratch_shapes=[*scratch, pltpu.VMEM((all_slots + 1, height, order), jnp.float32)],
            compiler_params=pltpu.CompilerParams(vmem_limit_bytes=moved + 4 * MIB),
            cost_estimate=pl.CostEstimate(
                flops=2 * order**2 * height * count * width // 4 * (cols - 1),
                bytes_accessed=moved // 2,
                transcendentals=0,
            ),
            name=f"peer_products_{at}",
        )(*given, *pieces, panel, totals)
        plan = plan or out[layers:]
        far, near = list(range(layers // 2, layers)), list(range(1, layers // 2))
        turn = far + near if at == 0 else far[:-1] + near + far[-1:]
        codes = [flipped(out[d], "layer", d) for d in turn]
        finished = [
            pl.pallas_call(
                functools.partial(finish_kernel, (layers, slots), (at, height)),
                out_shape=jax.ShapeDtypeStruct((own_rows, kept, at + height, order), jnp.bfloat16),
                in_specs=[vector] * (len(finished) + layers),
                out_specs=vector,
                compiler_params=pltpu.CompilerParams(
                    vmem_limit_bytes=16 * slots * block_size + 4 * MIB
                ),
                name=f"finish_{at}",
            )(*finished, out[0], *codes)
        ]
    return finished[0]


def solution(mesh):
    placed = (
        P(("row", "col", "layer"), None, None),
        P(("row", "col", "layer")),
        P(("row", "col", "layer")),
        P(("row", "layer"), "col", None, None),
        P(("row", "layer"), "col"),
        P("row", "col"),
    )
    return jax.shard_map(
        per_device,
        mesh=mesh,
        in_specs=placed,
        out_specs=P(("row", "layer"), "col", None, None),
        check_vma=False,
    )
```
